32 devices in a mesh: lat: 4 (over z), lon: 4 (over y, x), batch: 2 (over core).
Axes of the slice: x: 2, y: 2, z: 4, core: 2. Of those that a mesh axis runs over, the one named last changes fastest.
Arguments:
- fields: bfloat16 [18, 16, 128, 114], P('batch', 'lat', 'lon'), may hold values from -20 to 20
- targets: float32 [18, 16, 128, 2], P('batch', 'lat', 'lon'), may hold values from -6 to 6
- land_mask: int32 [18, 16, 128], P('batch', 'lat', 'lon'), may hold values from 0 to 1
- input_kernel: float32 [715008], P(('lat', 'lon', 'batch')), may hold values from -0.078125 to 0.078125
- input_first: float32 [715008], P(('lat', 'lon', 'batch'))
- input_second: float32 [715008], P(('lat', 'lon', 'batch'))
- block_kernels: float32 [6, 147456], P(None, ('lat', 'lon', 'batch')), may hold values from -0.1875 to 0.1875
- block_first: float32 [6, 147456], P(None, ('lat', 'lon', 'batch'))
- block_second: float32 [6, 147456], P(None, ('lat', 'lon', 'batch'))
- head_weight: float32 [128, 2], replicated, may hold values from -0.5 to 0.5
- head_first: float32 [128, 2], replicated
- head_second: float32 [128, 2], replicated
- norm_params: float32 [6, 2, 128], replicated, may hold values from -1.2 to 2, as said below
- norm_first: float32 [6, 2, 128], replicated
- norm_second: float32 [6, 2, 128], replicated
Outputs:
- loss_sum: float32 [1], replicated
- loss_weight: float32 [1], replicated
- input_momentum: float32 [715008], P(('lat', 'lon', 'batch'))
- input_variance: float32 [715008], P(('lat', 'lon', 'batch'))
- input_updated: float32 [715008], P(('lat', 'lon', 'batch'))
- block_momentum: float32 [6, 147456], P(None, ('lat', 'lon', 'batch'))
- block_variance: float32 [6, 147456], P(None, ('lat', 'lon', 'batch'))
- block_updated: float32 [6, 147456], P(None, ('lat', 'lon', 'batch'))
- head_momentum: float32 [128, 2], replicated
- head_variance: float32 [128, 2], replicated
- head_updated: float32 [128, 2], replicated
- norm_momentum: float32 [6, 2, 128], replicated
- norm_variance: float32 [6, 2, 128], replicated
- norm_updated: float32 [6, 2, 128], replicated
The draws below stay inside these ranges and needn't reach their ends.
Inputs may be any that keep to these rules, and one draw needn't show every extreme that they name: Gains in norm_params[:, 0] lie in 0.5 to 2.
All inputs are finite; a program needn't handle non-finite values.
Results may differ from the reference program's by a relative error of at most 0.03.
Values may be sent and summed in bfloat16 or wider, within the bound.
No kernel may reach another device: no remote copies, remote signals or barrier semaphores. Data moves between devices by JAX's collectives and lax.ppermute only.
A program may use at most 192 MiB of HBM per device.

```python
import math
import jax
import jax.numpy as jnp
from jax import lax

IN = 114
C = 128
OUT = 2
BLOCKS = 3
STEP = 10
SAMPLES = 18
LAT = 16
LON = 128


def grad_size():
    return 2.0 * math.sqrt(SAMPLES / (LAT * LON))


def first_moment(key, extent, factor):
    noise = jnp.clip(jax.random.normal(key, extent, jnp.float32), -4.0, 4.0)
    return 0.11 * factor * grad_size() * noise


def second_moment(key, extent, factor):
    level = factor * grad_size()
    spread = jax.random.uniform(key, extent, jnp.float32, math.log(0.5), math.log(8.0))
    return 0.001 * level * level * jnp.exp(spread)


def linear_ramp(length, start_value, end_value):
    places = (jnp.arange(length).astype(jnp.float32) + 0.5) / length
    return start_value + (end_value - start_value) * places


def draw_fields(key, part):
    key = jax.random.fold_in(key, 1)
    extent = (SAMPLES, LAT, LON, IN)
    noise = jnp.clip(jax.random.normal(key, extent, jnp.float32), -4.0, 4.0)
    start_value, end_value = (0.6, 1.8)
    row_scale = linear_ramp(LAT, start_value, end_value)
    col_scale = linear_ramp(LON, start_value, end_value)
    sample_scale = linear_ramp(SAMPLES, 0.75, 1.5)
    return (noise * sample_scale[:, None, None, None] * row_scale[None, :, None, None] * col_scale[None, None, :, None]).astype(jnp.bfloat16)


def draw_land_mask(key, part):
    key = jax.random.fold_in(key, 2)
    row_index = jnp.arange(LAT)[:, None]
    col_index = jnp.arange(LON)[None, :]
    cutoff = 150 + 800 * (2 * row_index + 1) * (2 * LON + 2 * col_index + 1) // (8 * LAT * LON)
    picks = jax.random.randint(key, (SAMPLES, LAT, LON), 0, 1000)
    return (picks < cutoff[None, :, :]).astype(jnp.int32)


def draw_norm_params(key, part):
    key = jax.random.fold_in(key, 3)
    gain_key, shift_key = jax.random.split(key)
    gains = 0.5 * jnp.exp(jax.random.uniform(gain_key, (2 * BLOCKS, 1, C), jnp.float32, 0.0, math.log(4.0)))
    shifts = 0.3 * jnp.clip(jax.random.normal(shift_key, (2 * BLOCKS, 1, C), jnp.float32), -4.0, 4.0)
    return jnp.concatenate([gains, shifts], axis=1)


def draw_input_first(key, part):
    key = jax.random.fold_in(key, 4)
    return first_moment(key, (49 * IN * C,), 1.0)


def draw_input_second(key, part):
    key = jax.random.fold_in(key, 5)
    return second_moment(key, (49 * IN * C,), 1.0)


def draw_block_first(key, part):
    key = jax.random.fold_in(key, 6)
    return first_moment(key, (2 * BLOCKS, 9 * C * C), 1.0)


def draw_block_second(key, part):
    key = jax.random.fold_in(key, 7)
    return second_moment(key, (2 * BLOCKS, 9 * C * C), 1.0)


def draw_head_first(key, part):
    key = jax.random.fold_in(key, 8)
    return first_moment(key, (C, OUT), 4.0)


def draw_head_second(key, part):
    key = jax.random.fold_in(key, 9)
    return second_moment(key, (C, OUT), 4.0)


def draw_norm_first(key, part):
    key = jax.random.fold_in(key, 10)
    return first_moment(key, (2 * BLOCKS, 2, C), 2.0)


def draw_norm_second(key, part):
    key = jax.random.fold_in(key, 11)
    return second_moment(key, (2 * BLOCKS, 2, C), 2.0)


def block_scale(stream_key, shape, pieces, smallest, top_value):
    def one(axis_at, shards_of):
        draws = jax.random.uniform(jax.random.fold_in(jax.random.fold_in(stream_key, 6), axis_at), (shards_of,), jnp.float32, smallest / len(pieces), top_value / len(pieces))
        return jnp.repeat(jnp.exp(draws), shape[axis_at] // shards_of).reshape((-1,) + (1,) * (len(shape) - axis_at - 1))

    gain = one(*pieces[0])
    for cut in pieces[1:]:
        gain = gain * one(*cut)
    return gain


def scatter_about(rng, shape, scale, bound, cuts=(), dtype=jnp.bfloat16):
    entries = scale * jax.random.normal(rng, shape, jnp.float32)
    if cuts:
        entries = entries * block_scale(rng, shape, cuts, -0.22, 0.18)
    return jnp.clip(entries, -bound, bound).astype(dtype)


def setup_inputs(seed: int = 0) -> dict:
    arg_keys = jax.random.split(jax.random.key(seed), 16)
    return {
        "fields": draw_fields(jax.random.fold_in(arg_keys[15], 71), 0),
        "targets": scatter_about(arg_keys[1], (SAMPLES, LAT, LON, OUT), 1.0, 6.0, ((0, 2), (1, 4), (2, 4)), jnp.float32),
        "land_mask": draw_land_mask(jax.random.fold_in(arg_keys[15], 71), 0),
        "input_kernel": scatter_about(arg_keys[3], (49 * IN * C,), (49 * IN) ** -0.5, 0.078125, ((0, 32),), jnp.float32),
        "input_first": draw_input_first(jax.random.fold_in(arg_keys[15], 71), 0),
        "input_second": draw_input_second(jax.random.fold_in(arg_keys[15], 71), 0),
        "block_kernels": scatter_about(arg_keys[6], (2 * BLOCKS, 9 * C * C), (9 * C) ** -0.5, 0.1875, ((1, 32),), jnp.float32),
        "block_first": draw_block_first(jax.random.fold_in(arg_keys[15], 71), 0),
        "block_second": draw_block_second(jax.random.fold_in(arg_keys[15], 71), 0),
        "head_weight": scatter_about(arg_keys[9], (C, OUT), C ** -0.5, 0.5, (), jnp.float32),
        "head_first": draw_head_first(jax.random.fold_in(arg_keys[15], 71), 0),
        "head_second": draw_head_second(jax.random.fold_in(arg_keys[15], 71), 0),
        "norm_params": draw_norm_params(jax.random.fold_in(arg_keys[15], 71), 0),
        "norm_first": draw_norm_first(jax.random.fold_in(arg_keys[15], 71), 0),
        "norm_second": draw_norm_second(jax.random.fold_in(arg_keys[15], 71), 0),
    }


@jax.custom_vjp
def low(v):
    return lax.optimization_barrier(v.astype(jnp.bfloat16)).astype(jnp.float32)

@jax.custom_vjp
def low_back(v):
    return v

def low_keep(v):
    return (low(v), None)

def low_pass(kept, grad):
    return (grad,)

def back_keep(v):
    return (v, None)

def back_low(kept, grad):
    return (low(grad),)
low.defvjp(low_keep, low_pass)
low_back.defvjp(back_keep, back_low)
NORM_EPSILON = 1e-05

def conv_same(source, kernel, reach):
    return lax.conv_general_dilated(source, kernel, (1, 1), ((reach, reach), (reach, reach)), dimension_numbers=('NHWC', 'HWIO', 'NHWC'), precision=lax.Precision.HIGHEST)

def conv_unit(source, kernel, norm_pair):
    preact = low_back(conv_same(low(source), kernel, 1))
    fired = low_back(low(jax.nn.gelu(preact)))
    average = lax.optimization_barrier(jnp.mean(fired, axis=(0, 1, 2)))
    spread = lax.optimization_barrier(jnp.mean(fired * fired, axis=(0, 1, 2))) - average * average
    normed = norm_pair[0] * (fired - average) * lax.rsqrt(spread + NORM_EPSILON) + norm_pair[1]
    return low_back(low(normed))

def block_pass(stream, kernels, pairs):
    middle = conv_unit(stream, kernels[0], pairs[0])
    branch = conv_unit(middle, kernels[1], pairs[1])
    return stream + branch

def forward(input_kernel, block_kernels, head_weight, norm_params, fields, targets, pixel_weight):
    kernel_in = low(input_kernel).reshape(7, 7, IN, C)
    kernels = low(block_kernels).reshape(2 * BLOCKS, 3, 3, C, C)
    stream = jax.nn.gelu(low_back(conv_same(fields, kernel_in, 3)))
    residual_block = jax.checkpoint(block_pass)
    for layer in range(BLOCKS):
        stream = residual_block(stream, kernels[2 * layer:2 * layer + 2], norm_params[2 * layer:2 * layer + 2])
    predicted = low_back(jnp.einsum('nhwc,co->nhwo', low(stream), low(head_weight), precision=lax.Precision.HIGHEST))
    misfit = predicted - targets
    return jnp.sum(pixel_weight[..., None] * misfit * misfit)

def adamw_update(weight, gradient, momentum, variance, step_rate):
    momentum = 0.9 * momentum + 0.1 * gradient
    variance = 0.999 * variance + 0.001 * gradient * gradient
    corrected = momentum / (1.0 - 0.9 ** STEP)
    scaled = jnp.sqrt(variance / (1.0 - 0.999 ** STEP)) + 1e-08
    return (momentum, variance, weight - step_rate * (corrected / scaled + 0.01 * weight))

def reference(fields, targets, land_mask, input_kernel, input_first, input_second, block_kernels, block_first, block_second, head_weight, head_first, head_second, norm_params, norm_first, norm_second):
    latitude = (jnp.arange(LAT).astype(jnp.float32) + 0.5) / LAT * jnp.pi - jnp.pi / 2
    pixel_weight = jnp.cos(latitude)[None, :, None] * land_mask.astype(jnp.float32)
    loss_weight = jnp.sum(pixel_weight) / SAMPLES
    inputs_wide = fields.astype(jnp.float32)

    def loss_of(kernel_in, kernels, head, pairs):
        return forward(kernel_in, kernels, head, pairs, inputs_wide, targets, pixel_weight)
    loss_sum, pullback = jax.vjp(loss_of, input_kernel, block_kernels, head_weight, norm_params)
    input_grad, block_grad, head_grad, norm_grad = pullback(1.0 / loss_weight)
    input_out = adamw_update(input_kernel, input_grad, input_first, input_second, 0.015)
    block_out = adamw_update(block_kernels, block_grad, block_first, block_second, 0.03)
    head_out = adamw_update(head_weight, head_grad, head_first, head_second, 0.15)
    norm_out = adamw_update(norm_params, norm_grad, norm_first, norm_second, 0.8)
    return (jnp.reshape(loss_sum, (1,)), jnp.reshape(loss_weight, (1,)), input_out[0], input_out[1], input_out[2], block_out[0], block_out[1], block_out[2], head_out[0], head_out[1], head_out[2], norm_out[0], norm_out[1], norm_out[2])
```

```python
import functools

import jax
import jax.numpy as jnp
from jax import lax
from jax.experimental import pallas as pl
from jax.experimental.pallas import tpu as pltpu
from jax.sharding import PartitionSpec as P

STEP = 10


NORM_EPSILON = 1e-05
GELU_SCALE = 0.7978845608028654
GELU_CUBE = 0.044715
GROUP = 4
VMEM_LIMIT = 48 << 20
MOST_PIXELS = 4096


def shortened(shard):

    def short(part):
        return part.astype(jnp.bfloat16) if part.dtype == jnp.float32 else part

    return jax.tree.map(short, shard)


def with_halo(cells, sides, width):
    for axis, dim in sides:
        count = lax.axis_size(axis)
        ends = count - 1
        head = lax.slice_in_dim(cells, 0, width, axis=dim)
        tail = lax.slice_in_dim(cells, cells.shape[dim] - width, cells.shape[dim], axis=dim)
        cells = jnp.concatenate(
            [
                lax.ppermute(tail, axis, [(i, (i + 1) % count) for i in range(ends)]),
                cells,
                lax.ppermute(head, axis, [((i + 1) % count, i) for i in range(ends)]),
            ],
            axis=dim,
        )
    return cells


def conv_valid(padded, kernel):
    return lax.conv_general_dilated(
        padded,
        kernel,
        (1, 1),
        "VALID",
        dimension_numbers=("NHWC", "HWIO", "NHWC"),
        preferred_element_type=jnp.float32,
    )


def kernel_grad(padded, gradient):
    summed = lax.conv_general_dilated(
        padded,
        gradient,
        (1, 1),
        "VALID",
        dimension_numbers=("CHWN", "IHWO", "NHWC"),
        preferred_element_type=jnp.float32,
    )
    return summed.transpose(1, 2, 0, 3)


def rim_cells(values):
    return with_halo(shortened(values), (("lat", 1), ("lon", 2)), 1).astype(values.dtype)


def to_channels(values):
    return jax.tree.map(
        lambda part, own: part.astype(own.dtype),
        lax.all_to_all(shortened(values), "lat", split_axis=3, concat_axis=0, tiled=True),
        values,
    )


def to_pixels(values):
    return lax.all_to_all(values, "lat", split_axis=0, concat_axis=3, tiled=True)


def spread_sums(summed, squares):
    return lax.psum((summed, squares), ("lon", "batch"))


def own_channels(norm_pair, width):
    return lax.dynamic_slice_in_dim(norm_pair, lax.axis_index("lat") * width, width, 1)


def norm_forward(fired, norm_pair, pixel_count):
    values = to_channels(fired)
    norm_pair = own_channels(norm_pair, values.shape[3])
    widened = values.astype(jnp.float32)
    summed, squares = spread_sums(
        jnp.sum(widened, axis=(0, 1, 2)), jnp.sum(widened * widened, axis=(0, 1, 2))
    )
    average = summed / pixel_count
    inverse_std = lax.rsqrt(squares / pixel_count - average * average + NORM_EPSILON)
    centred = (widened - average) * inverse_std
    normed = (norm_pair[0] * centred + norm_pair[1]).astype(jnp.bfloat16)
    normed = to_pixels(normed)
    return (normed, (centred, inverse_std, norm_pair))


def norm_backward(gradient, kept, pixel_count):
    centred, inverse_std, norm_pair = kept
    gradient = to_channels(gradient)
    widened = gradient.astype(jnp.float32)
    shift_grad, gain_grad = spread_sums(
        jnp.sum(widened, axis=(0, 1, 2)), jnp.sum(widened * centred, axis=(0, 1, 2))
    )
    scaled = norm_pair[0] * inverse_std
    fired_grad = (
        scaled * (widened - shift_grad / pixel_count - centred * gain_grad / pixel_count)
    ).astype(jnp.bfloat16)
    fired_grad = to_pixels(fired_grad)
    return (fired_grad, jnp.stack([gain_grad, shift_grad]))


def gelu_pullback(preact, gradient):
    unused, pullback = jax.vjp(jax.nn.gelu, preact)
    return pullback(gradient)[0]


def conv_forward(source, kernel, norm_pair, pixel_count):
    padded = rim_cells(source)
    preact = conv_valid(padded, kernel)
    fired = jax.nn.gelu(preact).astype(jnp.bfloat16)
    normed, kept = norm_forward(fired, norm_pair, pixel_count)
    return (normed, (padded, preact, kept))


def conv_backward(gradient, kernel, record, pixel_count):
    padded, preact, kept = record
    fired_grad, pair_grad = norm_backward(gradient, kept, pixel_count)
    preact_grad = gelu_pullback(preact, fired_grad.astype(jnp.float32)).astype(jnp.bfloat16)
    kernel_gradient = kernel_grad(padded, preact_grad)
    flipped = kernel[::-1, ::-1].transpose(0, 1, 3, 2)
    source_grad = conv_valid(rim_cells(preact_grad), flipped)
    return (source_grad, kernel_gradient, pair_grad)


def block_forward(stream, kernels, norm_pairs, pixel_count):
    middle, first_record = conv_forward(
        stream.astype(jnp.bfloat16), kernels[0], norm_pairs[0], pixel_count
    )
    branch, second_record = conv_forward(middle, kernels[1], norm_pairs[1], pixel_count)
    return (stream + branch.astype(jnp.float32), (first_record, second_record))


def block_backward(stream_grad, stream, kernels, norm_pairs, pixel_count):
    unused, records = block_forward(stream, kernels, norm_pairs, pixel_count)
    middle_grad, second_kernel, second_pair = conv_backward(
        stream_grad.astype(jnp.bfloat16), kernels[1], records[1], pixel_count
    )
    source_grad, first_kernel, first_pair = conv_backward(
        middle_grad.astype(jnp.bfloat16), kernels[0], records[0], pixel_count
    )
    return (stream_grad + source_grad, (first_kernel, second_kernel), (first_pair, second_pair))


def adamw_update(weight, gradient, momentum, variance, step_rate):
    momentum = 0.9 * momentum + 0.1 * gradient
    variance = 0.999 * variance + 0.001 * gradient * gradient
    corrected = momentum / (1.0 - 0.9**STEP)
    scaled = jnp.sqrt(variance / (1.0 - 0.999**STEP)) + 1e-08
    return (momentum, variance, weight - step_rate * (corrected / scaled + 0.01 * weight))


def finished(
    loss_sum, loss_weight, input_grad, block_grad, head_grad, norm_grad,
    input_state, block_state, head_state, norm_state,
):
    outputs = [jnp.reshape(loss_sum, (1,)), jnp.reshape(loss_weight, (1,))]
    for state, gradient, step_rate in (
        (input_state, input_grad, 0.015),
        (block_state, block_grad, 0.03),
        (head_state, head_grad, 0.15),
        (norm_state, norm_grad, 0.8),
    ):
        weight, first, second = state
        outputs.extend(adamw_update(weight, gradient, first, second, step_rate))
    return tuple(outputs)


def tile_body(
    fields,
    targets,
    land_mask,
    input_kernel,
    input_first,
    input_second,
    block_kernels,
    block_first,
    block_second,
    head_weight,
    head_first,
    head_second,
    norm_params,
    norm_first,
    norm_second,
):
    samples_here, rows_here, cols_here, in_width = fields.shape
    channels = norm_params.shape[2]
    conv_count = block_kernels.shape[0]
    full_input, full_blocks = (
        lax.all_gather(
            input_kernel.astype(jnp.bfloat16), ("lat", "lon", "batch"), axis=0, tiled=True
        ),
        lax.all_gather(
            block_kernels.astype(jnp.bfloat16), ("lat", "lon", "batch"), axis=1, tiled=True
        ),
    )
    kernel_in = full_input.reshape(7, 7, in_width, channels)
    kernels = full_blocks.reshape(conv_count, 3, 3, channels, channels)
    head_low = head_weight.astype(jnp.bfloat16)
    sample_count = samples_here * lax.axis_size("batch")
    pixel_count = float(
        sample_count * rows_here * lax.axis_size("lat") * cols_here * lax.axis_size("lon")
    )
    row_global = (lax.axis_index("lat") * rows_here + jnp.arange(rows_here)).astype(jnp.float32)
    latitude = (row_global + 0.5) / (rows_here * lax.axis_size("lat")) * jnp.pi - jnp.pi / 2
    pixel_weight = jnp.cos(latitude)[None, :, None] * land_mask.astype(jnp.float32)
    valid_sum = lax.psum(jnp.sum(pixel_weight), ("lat", "lon", "batch"))
    loss_weight = valid_sum / sample_count
    padded_in = with_halo(fields, (("lat", 1), ("lon", 2)), 3)
    preact_in = conv_valid(padded_in, kernel_in)
    streams = [jax.nn.gelu(preact_in)]
    for layer in range(conv_count // 2):
        advanced, unused = block_forward(
            streams[-1],
            kernels[2 * layer : 2 * layer + 2],
            norm_params[2 * layer : 2 * layer + 2],
            pixel_count,
        )
        streams.append(advanced)
    top_stream = streams[-1].astype(jnp.bfloat16)
    predicted = jnp.einsum(
        "nhwc,co->nhwo", top_stream, head_low, preferred_element_type=jnp.float32
    )
    misfit = predicted - targets
    loss_local = jnp.sum(pixel_weight[..., None] * misfit * misfit)
    pred_grad = (2.0 * pixel_weight[..., None] * misfit / loss_weight).astype(jnp.bfloat16)
    head_local = jnp.einsum(
        "nhwc,nhwo->co", top_stream, pred_grad, preferred_element_type=jnp.float32
    )
    stream_grad = jnp.einsum(
        "nhwo,co->nhwc", pred_grad, head_low, preferred_element_type=jnp.float32
    )
    kernel_grads = [None] * conv_count
    pair_grads = [None] * conv_count
    for layer in reversed(range(conv_count // 2)):
        stream_grad, kernel_pair, norm_pair = block_backward(
            stream_grad,
            streams[layer],
            kernels[2 * layer : 2 * layer + 2],
            norm_params[2 * layer : 2 * layer + 2],
            pixel_count,
        )
        kernel_grads[2 * layer], kernel_grads[2 * layer + 1] = kernel_pair
        pair_grads[2 * layer], pair_grads[2 * layer + 1] = norm_pair
    pre_in_grad = gelu_pullback(preact_in, stream_grad).astype(jnp.bfloat16)
    input_local = kernel_grad(padded_in, pre_in_grad).reshape(-1)
    block_local = jnp.stack(kernel_grads).reshape(conv_count, -1)
    input_grad, block_grad = (
        lax.psum_scatter(input_local, ("lat", "lon", "batch"), scatter_dimension=0, tiled=True),
        lax.psum_scatter(block_local, ("lat", "lon", "batch"), scatter_dimension=1, tiled=True),
    )
    head_grad, loss_sum = lax.psum((head_local, loss_local), ("lat", "lon", "batch"))
    norm_grad = jnp.stack(pair_grads)
    norm_grad = lax.all_gather(norm_grad, "lat", axis=2, tiled=True)
    return finished(
        loss_sum, loss_weight, input_grad, block_grad, head_grad, norm_grad,
        (input_kernel, input_first, input_second), (block_kernels, block_first, block_second),
        (head_weight, head_first, head_second), (norm_params, norm_first, norm_second),
    )


ALL = ("lat", "lon", "batch")
TILE = ("lat", "lon")
PIECES = 3
SPREAD = 16


def vmem_spec():
    return pl.BlockSpec(memory_space=pltpu.VMEM)


def smem_spec():
    return pl.BlockSpec(memory_space=pltpu.SMEM)


def call(kernel, outs, args, scratch=(), flags=None, cost=0):
    specs = [vmem_spec()] * len(args)
    if flags is not None:
        specs = [smem_spec()] + specs
        args = (flags,) + tuple(args)
    return pl.pallas_call(
        kernel,
        out_shape=[jax.ShapeDtypeStruct(shape, dtype) for shape, dtype in outs],
        in_specs=specs,
        out_specs=[vmem_spec()] * len(outs),
        scratch_shapes=list(scratch),
        compiler_params=pltpu.CompilerParams(vmem_limit_bytes=VMEM_LIMIT),
        cost_estimate=pl.CostEstimate(flops=cost, bytes_accessed=4 << 20, transcendentals=0),
    )(*args)


def dot(left, right, dims=((1,), (0,))):
    return lax.dot_general(left, right, (dims, ((), ())), preferred_element_type=jnp.float32)


def gelu_value(x):
    return x * (0.5 * (1.0 + jnp.tanh(GELU_SCALE * (x + GELU_CUBE * (x * x * x)))))


def gelu_both(x):
    square = x * x
    level = jnp.tanh(GELU_SCALE * (x + GELU_CUBE * (x * square)))
    half = 0.5 * (1.0 + level)
    slope = half + 0.5 * x * (1.0 - level * level) * (GELU_SCALE * (1.0 + 3.0 * GELU_CUBE * square))
    return x * half, slope


def shifted(cells, step):
    count = cells.shape[0]
    if step == 0:
        return cells
    column = lax.broadcasted_iota(jnp.int32, cells.shape, 0) + step
    rolled = pltpu.roll(cells, (-step) % count, 0)
    return jnp.where((column >= 0) & (column < count), rolled, 0.0)


def spread_pair(pair, cells, shifts_ref, sizes):
    cols, width, pairs = sizes
    for b in range(3):
        moved = shifted(cells, b - 1).astype(jnp.bfloat16)
        shifts_ref[(pair + 1) * cols : (pair + 2) * cols, b * width : (b + 1) * width] = moved[:, width:]
        shifts_ref[pair * cols : (pair + 1) * cols, (3 + b) * width : (4 + b) * width] = moved[:, :width]


def clear_rim(shifts_ref, sizes):
    cols, width, pairs = sizes
    zero = jnp.zeros((cols, 3 * width), jnp.bfloat16)
    shifts_ref[0:cols, 0 : 3 * width] = zero
    shifts_ref[pairs * cols : (pairs + 1) * cols, 3 * width : 6 * width] = zero


def taps_forward(weight_ref, taps_ref, width):
    for k in range(2):
        for rr in range(2):
            for b in range(3):
                for q in range(2):
                    a = 2 * k + rr - q
                    at = (rr * 3 + b) * width
                    if 0 <= a <= 2:
                        block = weight_ref[(a * 3 + b) * width : (a * 3 + b + 1) * width, :]
                    else:
                        block = jnp.zeros((width, width), jnp.bfloat16)
                    taps_ref[k, at : at + width, q * width : (q + 1) * width] = block


def taps_backward(weight_ref, taps_ref, width):
    for k in range(2):
        for rr in range(2):
            for b in range(3):
                for q in range(2):
                    a = 2 - (2 * k + rr - q)
                    at = (rr * 3 + b) * width
                    if 0 <= a <= 2:
                        tap = a * 3 + 2 - b
                        block = weight_ref[tap * width : (tap + 1) * width, :]
                    else:
                        block = jnp.zeros((width, width), jnp.bfloat16)
                    taps_ref[k, q * width : (q + 1) * width, at : at + width] = block


def pair_conv(shifts_ref, taps_ref, group, cols, dims=((1,), (0,))):
    rows = GROUP * cols
    first = shifts_ref[group * rows : (group + 1) * rows, :]
    second = shifts_ref[group * rows + cols : (group + 1) * rows + cols, :]
    return dot(first, taps_ref[0], dims) + dot(second, taps_ref[1], dims)


def folded(sums, width):
    return sums[:, :width] + sums[:, width:]


def total_of(parts_ref):
    return jnp.sum(parts_ref[...], axis=0)


def twice(row):
    return jnp.concatenate([row, row], axis=1)


def norm_of(parts_ref, pixel_count):
    total = total_of(parts_ref)
    average = total[0:1] / pixel_count
    inverse_std = lax.rsqrt(total[1:2] / pixel_count - average * average + NORM_EPSILON)
    return twice(average), twice(inverse_std)


def conv_and_sums(flags_ref, shifts_ref, taps_ref, preact_ref, fired_ref, sums_ref, sizes, more=None):
    cols, width, pairs = sizes
    total = jnp.zeros((1, 2 * width), jnp.float32)
    squares = jnp.zeros((1, 2 * width), jnp.float32)
    for group in range(pairs // GROUP):
        preact = pair_conv(shifts_ref, taps_ref, group, cols)
        rows = slice(group * GROUP * cols, (group + 1) * GROUP * cols)
        preact_ref[rows, :] = preact
        fired = gelu_value(preact).astype(jnp.bfloat16)
        fired_ref[rows, :] = fired
        wide = fired.astype(jnp.float32)
        total = total + jnp.sum(wide, axis=0, keepdims=True)
        squares = squares + jnp.sum(wide * wide, axis=0, keepdims=True)
    active = flags_ref[0].astype(jnp.float32)
    parts = [folded(total, width) * active, folded(squares, width) * active]
    put_sums(sums_ref, parts + (more or []))


def put_sums(sums_ref, parts):
    shape = sums_ref.shape[1:]
    row = lax.broadcasted_iota(jnp.int32, shape, 0)
    block = jnp.zeros(shape, jnp.float32)
    at = 0
    for part in parts:
        for i in range(part.shape[0]):
            block = jnp.where(row == at, jnp.broadcast_to(part[i : i + 1], shape), block)
            at += 1
    sums_ref[...] = jnp.broadcast_to(block[None], sums_ref.shape)


def field_row(fields_ref, row, tiles):
    nl, no, rows_here, cols_here = tiles
    lat, inner = row // rows_here, row % rows_here
    return jnp.concatenate([fields_ref[lat * no + lon, inner] for lon in range(no)], axis=0)


def wide_shifts(fields_ref, shifts_ref, tiles, sizes):
    cols, width, pairs = sizes
    rows = 2 * pairs
    for row in range(-3, rows + 3):
        at, rr = (row + 3) // 2, (row + 3) % 2
        if 0 <= row < rows:
            cells = field_row(fields_ref, row, tiles).astype(jnp.float32)
        for b in range(7):
            if 0 <= row < rows:
                moved = shifted(cells, b - 3).astype(jnp.bfloat16)
            else:
                moved = jnp.zeros((cols, width), jnp.bfloat16)
            spot = (rr * 7 + b) * width
            shifts_ref[at * cols : (at + 1) * cols, spot : spot + width] = moved


def input_taps_kernel(frames_ref, taps_ref, flat_ref, *, starts, in_width):
    width = flat_ref.shape[1]
    rows = frames_ref.shape[1]
    flat_ref[...] = jnp.zeros(flat_ref.shape, jnp.float32)
    for device, start in enumerate(starts):
        flat_ref[start : start + rows, :] += frames_ref[device].astype(jnp.float32)
    inside = lax.broadcasted_iota(jnp.int32, (width, width), 0) < in_width
    zero = jnp.zeros((width, width), jnp.bfloat16)
    for b in range(7):
        taps_ref[3, (7 + b) * width : (8 + b) * width, 0:width] = zero
        taps_ref[0, b * width : (b + 1) * width, width : 2 * width] = zero
        for a in range(7):
            tap = a * 7 + b
            block = flat_ref[tap * in_width : tap * in_width + width, :]
            block = jnp.where(inside, block, 0.0).astype(jnp.bfloat16)
            for q in range(2):
                k, rr = (a + q) // 2, (a + q) % 2
                spot = (rr * 7 + b) * width
                taps_ref[k, spot : spot + width, q * width : (q + 1) * width] = block


def block_kernel_rows_kernel(pieces_ref, whole_ref, flat_ref):
    devices, count, rows, width = pieces_ref.shape
    for index in range(count):
        for device in range(devices):
            flat_ref[device * rows : (device + 1) * rows, :] = pieces_ref[device, index].astype(jnp.float32)
        whole_ref[index] = flat_ref[...].astype(jnp.bfloat16)


def first_kernel(
    flags_ref, fields_ref, in_taps_ref, weight_ref,
    in_preact_ref, stream_ref, source_ref, preact_ref, fired_ref, sums_ref,
    wide_ref, shifts_ref, taps_ref, *, tiles, sizes, in_width,
):
    cols, width, pairs = sizes
    wide_shifts(fields_ref, wide_ref, tiles, sizes)
    taps_forward(weight_ref, taps_ref, width)
    clear_rim(shifts_ref, sizes)
    rows = GROUP * cols
    for group in range(pairs // GROUP):
        preact = dot(wide_ref[group * rows : (group + 1) * rows, :], in_taps_ref[0])
        for k in range(1, 4):
            preact += dot(
                wide_ref[group * rows + k * cols : (group + 1) * rows + k * cols, :], in_taps_ref[k]
            )
        in_preact_ref[group * rows : (group + 1) * rows, :] = preact
        stream = gelu_value(preact)
        stream_ref[group * rows : (group + 1) * rows, :] = stream
        source = stream.astype(jnp.bfloat16)
        source_ref[group * rows : (group + 1) * rows, :] = source
        for pair in range(GROUP):
            cells = source[pair * cols : (pair + 1) * cols].astype(jnp.float32)
            spread_pair(group * GROUP + pair, cells, shifts_ref, sizes)
    weight_sum = jnp.zeros((1, width), jnp.float32)
    for row in range(2 * pairs):
        low = field_row(fields_ref, row, tiles).astype(jnp.float32)
        weight_sum += jnp.sum(low, axis=0, keepdims=True)
    lane = lax.broadcasted_iota(jnp.int32, (1, width), 1) - in_width
    chosen = (lane >= 2 * PIECES) & (lane < 3 * PIECES)
    weight_sum = jnp.sum(jnp.where(chosen, weight_sum, 0.0), axis=1, keepdims=True)
    conv_and_sums(
        flags_ref, shifts_ref, taps_ref, preact_ref, fired_ref, sums_ref, sizes,
        [jnp.broadcast_to(weight_sum, (1, width))],
    )


def unit_kernel(
    flags_ref, fired_in_ref, parts_ref, pair_ref, weight_ref, *rest, sizes, pixel_count, residual
):
    cols, width, pairs = sizes
    if residual:
        stream_in_ref, stream_ref, *rest = rest
    source_ref, preact_ref, fired_ref, sums_ref, shifts_ref, taps_ref = rest
    average, inverse_std = norm_of(parts_ref, pixel_count)
    gain, shift = twice(pair_ref[0:1]), twice(pair_ref[1:2])
    taps_forward(weight_ref, taps_ref, width)
    clear_rim(shifts_ref, sizes)
    for pair in range(pairs):
        rows = slice(pair * cols, (pair + 1) * cols)
        fired = fired_in_ref[rows, :].astype(jnp.float32)
        normed = (gain * ((fired - average) * inverse_std) + shift).astype(jnp.bfloat16)
        if residual:
            stream = stream_in_ref[rows, :] + normed.astype(jnp.float32)
            stream_ref[rows, :] = stream
            normed = stream.astype(jnp.bfloat16)
        source_ref[rows, :] = normed
        spread_pair(pair, normed.astype(jnp.float32), shifts_ref, sizes)
    conv_and_sums(flags_ref, shifts_ref, taps_ref, preact_ref, fired_ref, sums_ref, sizes)


def head_kernel(
    flags_ref, fired_ref, parts_ref, first_parts_ref, pair_ref, stream_in_ref, fields_ref, head_ref,
    grad_ref, sums_ref, *, tiles, sizes, pixel_count, sample_count, in_width,
):
    cols, width, pairs = sizes
    average, inverse_std = norm_of(parts_ref, pixel_count)
    average, inverse_std = average[:, :width], inverse_std[:, :width]
    gain, shift = pair_ref[0:1], pair_ref[1:2]
    loss_weight = total_of(first_parts_ref)[2:3] / sample_count
    head = head_ref[...]
    outs = 2
    lane_from = lax.broadcasted_iota(jnp.int32, (width, width), 0) - in_width
    lane_to = lax.broadcasted_iota(jnp.int32, (width, width), 1)
    within = lane_from - PIECES * lane_to
    picks = (within >= 0) & (within < PIECES) & (lane_to < outs)
    pick_target = jnp.where(picks, 1.0, 0.0).astype(jnp.bfloat16)
    picks = (lane_from >= outs * PIECES) & (lane_from < (outs + 1) * PIECES) & (lane_to < outs)
    pick_weight = jnp.where(picks, 1.0, 0.0).astype(jnp.bfloat16)
    zero = jnp.zeros((1, width), jnp.float32)
    loss, shift_grad, gain_grad = zero, zero, zero
    head_grad = jnp.zeros((width, width), jnp.float32)
    for row in range(2 * pairs):
        pair, q = row // 2, row % 2
        rows, lanes = slice(pair * cols, (pair + 1) * cols), slice(q * width, (q + 1) * width)
        centred = (fired_ref[rows, lanes].astype(jnp.float32) - average) * inverse_std
        normed = (gain * centred + shift).astype(jnp.bfloat16)
        top = (stream_in_ref[rows, lanes] + normed.astype(jnp.float32)).astype(jnp.bfloat16)
        fields = field_row(fields_ref, row, tiles)
        misfit = dot(top, head) - dot(fields, pick_target)
        weight = dot(fields, pick_weight)
        loss += jnp.sum(weight * misfit * misfit, axis=0, keepdims=True)
        pred_grad = (2.0 * weight * misfit / loss_weight).astype(jnp.bfloat16)
        head_grad += dot(pred_grad, top, ((0,), (0,)))
        grad = dot(pred_grad, head, ((1,), (1,)))
        grad_ref[rows, lanes] = grad
        low = grad.astype(jnp.bfloat16).astype(jnp.float32)
        shift_grad += jnp.sum(low, axis=0, keepdims=True)
        gain_grad += jnp.sum(low * centred, axis=0, keepdims=True)
    loss = jnp.broadcast_to(jnp.sum(loss, axis=1, keepdims=True), (1, width))
    put_sums(sums_ref, [shift_grad, gain_grad, head_grad[0:outs], loss])


def back_kernel(
    flags_ref, parts_ref, grad_ref, preact_ref, norm_parts_ref, pair_ref, weight_ref, *rest,
    sizes, pixel_count, second, last,
):
    cols, width, pairs = sizes
    below_ref, *rest = rest
    if not last:
        below_parts_ref, *rest = rest
    if not second:
        kept_ref, *rest = rest
    if last:
        pre_ref, out_ref, pair_grad_ref, shifts_ref, taps_ref = rest
    else:
        pre_ref, out_ref, sums_ref, pair_grad_ref, shifts_ref, taps_ref = rest
    total = total_of(parts_ref)
    shift_grad, gain_grad = total[0:1], total[1:2]
    pair_grad_ref[0:1, :] = gain_grad
    pair_grad_ref[1:2, :] = shift_grad
    average, inverse_std = norm_of(norm_parts_ref, pixel_count)
    scaled = twice(pair_ref[0:1]) * inverse_std
    shift_mean, gain_mean = twice(shift_grad / pixel_count), twice(gain_grad / pixel_count)
    active = flags_ref[0].astype(jnp.float32)
    taps_backward(weight_ref, taps_ref, width)
    clear_rim(shifts_ref, sizes)
    for pair in range(pairs):
        rows = slice(pair * cols, (pair + 1) * cols)
        fired, slope = gelu_both(preact_ref[rows, :])
        centred = (fired.astype(jnp.bfloat16).astype(jnp.float32) - average) * inverse_std
        grad = grad_ref[rows, :].astype(jnp.bfloat16).astype(jnp.float32)
        fired_grad = (scaled * (grad - shift_mean - centred * gain_mean)).astype(jnp.bfloat16)
        pre = (fired_grad.astype(jnp.float32) * slope * active).astype(jnp.bfloat16)
        pre_ref[rows, :] = pre
        spread_pair(pair, pre.astype(jnp.float32), shifts_ref, sizes)
    if not last:
        below_average, below_inverse = norm_of(below_parts_ref, pixel_count)
    shift_sum = jnp.zeros((1, 2 * width), jnp.float32)
    gain_sum = jnp.zeros((1, 2 * width), jnp.float32)
    for group in range(pairs // GROUP):
        rows = slice(group * GROUP * cols, (group + 1) * GROUP * cols)
        source = pair_conv(shifts_ref, taps_ref, group, cols, ((1,), (1,)))
        if not second:
            source = source + kept_ref[rows, :]
        fired, slope = gelu_both(below_ref[rows, :])
        if last:
            out_ref[rows, :] = (source * slope).astype(jnp.bfloat16)
            continue
        out_ref[rows, :] = source.astype(out_ref.dtype)
        low = source.astype(jnp.bfloat16).astype(jnp.float32)
        centred = (fired.astype(jnp.bfloat16).astype(jnp.float32) - below_average) * below_inverse
        shift_sum += jnp.sum(low, axis=0, keepdims=True)
        gain_sum += jnp.sum(low * centred, axis=0, keepdims=True)
    if not last:
        put_sums(sums_ref, [folded(shift_sum, width) * active, folded(gain_sum, width) * active])


def kernel_grad_kernel(source_ref, pre_ref, shards_ref, shifts_ref, flat_ref, *, sizes):
    cols, width, pairs = sizes
    clear_rim(shifts_ref, sizes)
    for pair in range(pairs):
        cells = source_ref[pair * cols : (pair + 1) * cols, :].astype(jnp.float32)
        spread_pair(pair, cells, shifts_ref, sizes)
    for a in range(4):
        k, rr = a // 2, a % 2
        block = shifts_ref[k * cols : (k + pairs) * cols, rr * 3 * width : (rr + 1) * 3 * width]
        grad = dot(block, pre_ref[...], ((0,), (0,)))
        if a < 3:
            flat_ref[a * 3 * width : (a + 1) * 3 * width, :] = grad[:, :width]
        if a > 0:
            flat_ref[(a - 1) * 3 * width : a * 3 * width, :] += grad[:, width:]
    devices, rows, unused = shards_ref.shape
    for device in range(devices):
        shards_ref[device] = flat_ref[device * rows : (device + 1) * rows, :].astype(shards_ref.dtype)


def input_grad_kernel(
    flags_ref, fields_ref, pre_ref, mine_ref, theirs_ref, wide_ref, flat_ref, *,
    tiles, sizes, starts, in_width,
):
    cols, width, pairs = sizes
    wide_shifts(fields_ref, wide_ref, tiles, sizes)
    for a in range(8):
        k, rr = a // 2, a % 2
        for b in range(7):
            spot = (rr * 7 + b) * width
            block = wide_ref[k * cols : (k + pairs) * cols, spot : spot + width]
            grad = dot(block, pre_ref[...], ((0,), (0,)))[:in_width]
            if a < 7:
                tap = a * 7 + b
                flat_ref[tap * in_width : (tap + 1) * in_width, :] = grad[:, :width]
            if a > 0:
                tap = (a - 1) * 7 + b
                flat_ref[tap * in_width : (tap + 1) * in_width, :] += grad[:, width:]
    rows = mine_ref.shape[1]
    for place in range(mine_ref.shape[0]):
        even, odd = starts[2 * place], starts[2 * place + 1]
        for target, first, other in ((mine_ref, even, odd), (theirs_ref, odd, even)):
            start = jnp.where(flags_ref[1] == 0, first, other)
            start = pl.multiple_of(start, SPREAD)
            target[place] = flat_ref[pl.ds(start, rows), :].astype(jnp.bfloat16)


def split_pieces(values):
    pieces = []
    for unused in range(PIECES - 1):
        piece = lax.reduce_precision(values, 8, 7)
        pieces.append(piece)
        values = values - piece
    pieces.append(values)
    return [piece.astype(jnp.bfloat16) for piece in pieces]


def spread_all(values, axes):
    return lax.all_to_all(values, axes, 0, 0, tiled=True)


def whole_sample_body(
    fields,
    targets,
    land_mask,
    input_kernel,
    input_first,
    input_second,
    block_kernels,
    block_first,
    block_second,
    head_weight,
    head_first,
    head_second,
    norm_params,
    norm_first,
    norm_second,
):
    samples_here, rows_here, cols_here, in_width = fields.shape
    width = norm_params.shape[2]
    conv_count = block_kernels.shape[0]
    nl, no, nb = (lax.axis_size(axis) for axis in ALL)
    places, devices = nl * no, nl * no * nb
    tiles = (nl, no, rows_here, cols_here)
    cols, pairs = cols_here * no, rows_here * nl // 2
    sizes = (cols, width, pairs)
    pixels = pairs * cols
    sample_count = samples_here * nb
    pixel_count = float(sample_count * 2 * pixels)
    place = lax.axis_index(TILE)
    core = lax.axis_index("batch")
    flags = jnp.stack([(place < samples_here).astype(jnp.int32), core.astype(jnp.int32)])
    bf16, f32 = jnp.bfloat16, jnp.float32

    device = lax.axis_index(ALL)
    shard = input_kernel.shape[0]
    unit = SPREAD * width
    starts = [d * shard // unit * SPREAD for d in range(devices)]
    frame = max(-(-((d + 1) * shard) // unit) * SPREAD - starts[d] for d in range(devices))
    flat_rows = max(starts[-1] + frame, (49 - 1) * in_width + width)
    flat_rows = -(-flat_rows // 8) * 8
    offset = device * shard % unit

    row_global = (lax.axis_index("lat") * rows_here + jnp.arange(rows_here)).astype(f32)
    latitude = (row_global + 0.5) / (rows_here * nl) * jnp.pi - jnp.pi / 2
    pixel_weight = jnp.cos(latitude)[None, :, None] * land_mask.astype(f32)
    extra = split_pieces(targets[..., 0]) + split_pieces(targets[..., 1]) + split_pieces(pixel_weight)
    packed = jnp.concatenate([fields, jnp.stack(extra, axis=-1)], axis=-1)
    packed = jnp.pad(
        packed, ((0, places - samples_here), (0, 0), (0, 0), (0, width - packed.shape[-1]))
    )
    packed = spread_all(packed, TILE)

    framed = lax.dynamic_update_slice(
        jnp.zeros((frame * width,), bf16), input_kernel.astype(bf16), (offset,)
    ).reshape(frame, width)
    frames = gather_all(framed)
    (in_taps,) = call(
        functools.partial(input_taps_kernel, starts=starts, in_width=in_width),
        [((4, 14 * width, 2 * width), bf16)],
        (frames,),
        [pltpu.VMEM((flat_rows, width), f32)],
    )
    piece_rows = block_kernels.shape[1] // width
    pieces = gather_all(block_kernels.astype(bf16).reshape(conv_count, piece_rows, width))
    (weights,) = call(
        block_kernel_rows_kernel,
        [((conv_count, 9 * width, width), bf16)],
        (pieces,),
        [pltpu.VMEM((9 * width, width), f32)],
    )
    weights = [weights[k] for k in range(conv_count)]
    head_low = jnp.pad(head_weight.astype(bf16), ((0, 0), (0, width - head_weight.shape[1])))

    wide_scratch = pltpu.VMEM(((pairs + 3) * cols, 14 * width), bf16)
    shift_scratch = pltpu.VMEM(((pairs + 1) * cols, 6 * width), bf16)
    forward_scratch = [shift_scratch, pltpu.VMEM((2, 6 * width, 2 * width), bf16)]
    backward_scratch = [shift_scratch, pltpu.VMEM((2, 2 * width, 6 * width), bf16)]
    plane = (pixels, 2 * width)
    sums_shape = ((devices, 4, width), f32)
    unit_cost = 2 * 2 * pixels * 9 * width * width

    in_preact, stream, source, preact, fired, sums = call(
        functools.partial(first_kernel, tiles=tiles, sizes=sizes, in_width=in_width),
        [(plane, f32), (plane, f32), (plane, bf16), (plane, f32), (plane, bf16), sums_shape],
        (packed, in_taps, weights[0]),
        [wide_scratch] + forward_scratch,
        flags,
        6 * unit_cost,
    )
    sources, preacts, parts = [source], [preact], [spread_all(sums, ALL)]
    for k in range(1, conv_count):
        residual = k % 2 == 0
        kept = (stream,) if residual else ()
        out = call(
            functools.partial(unit_kernel, sizes=sizes, pixel_count=pixel_count, residual=residual),
            [(plane, f32)] * residual + [(plane, bf16), (plane, f32), (plane, bf16), sums_shape],
            (fired, parts[-1], norm_params[k - 1], weights[k]) + kept,
            forward_scratch,
            flags,
            unit_cost,
        )
        if residual:
            stream, *out = out
        source, preact, fired, sums = out
        sources.append(source)
        preacts.append(preact)
        parts.append(spread_all(sums, ALL))

    grad, sums = call(
        functools.partial(
            head_kernel,
            tiles=tiles, sizes=sizes, pixel_count=pixel_count, sample_count=sample_count, in_width=in_width,
        ),
        [(plane, f32), ((devices, 8, width), f32)],
        (fired, parts[-1], parts[0], norm_params[-1], stream, packed, head_low),
        (),
        flags,
        unit_cost // 4,
    )
    head_parts = back_parts = spread_all(sums, ALL)
    pair_grads, shards = [None] * conv_count, [None] * conv_count
    for k in reversed(range(conv_count)):
        second, last = k % 2 == 1, k == 0
        out_type = bf16 if second or last else f32
        below = (in_preact,) if last else (preacts[k - 1], parts[k - 1])
        if second:
            kept_grad = grad
        else:
            below = below + (kept_grad,)
        pre, grad, *rest = call(
            functools.partial(
                back_kernel, sizes=sizes, pixel_count=pixel_count, second=second, last=last
            ),
            [(plane, bf16), (plane, out_type)] + [sums_shape] * (not last) + [((2, width), f32)],
            (back_parts, grad, preacts[k], parts[k], norm_params[k], weights[k]) + below,
            backward_scratch,
            flags,
            unit_cost,
        )
        pair_grads[k] = rest[-1]
        if not last:
            back_parts = spread_all(rest[0], ALL)
        (shard_grads,) = call(
            functools.partial(kernel_grad_kernel, sizes=sizes),
            [((devices, piece_rows, width), bf16)],
            (sources[k], pre),
            [shift_scratch, pltpu.VMEM((9 * width, width), f32)],
            None,
            unit_cost,
        )
        shards[k] = jnp.sum(spread_all(shard_grads, ALL).astype(f32), axis=0)
    mine, theirs = call(
        functools.partial(
            input_grad_kernel, tiles=tiles, sizes=sizes, starts=starts, in_width=in_width
        ),
        [((places, frame, width), bf16)] * 2,
        (packed, grad),
        [wide_scratch, pltpu.VMEM((flat_rows, width), f32)],
        flags,
        6 * unit_cost,
    )
    theirs = lax.ppermute(theirs, "batch", [(i, nb - 1 - i) for i in range(nb)])
    own = spread_all((mine.astype(f32) + theirs.astype(f32)).astype(bf16), TILE)
    own = jnp.sum(own.astype(f32), axis=0).reshape(-1)
    input_grad = lax.dynamic_slice(own, (offset,), (shard,))
    block_grad = jnp.stack(shards).reshape(conv_count, -1)
    head_total = jnp.sum(head_parts, axis=0)
    head_grad = head_total[2:4].T
    loss_sum = head_total[4, 0]
    loss_weight = jnp.sum(parts[0], axis=0)[2, 0] / sample_count
    norm_grad = jnp.stack(pair_grads)
    return finished(
        loss_sum, loss_weight, input_grad, block_grad, head_grad, norm_grad,
        (input_kernel, input_first, input_second), (block_kernels, block_first, block_second),
        (head_weight, head_first, head_second), (norm_params, norm_first, norm_second),
    )


def gather_all(values):
    places = lax.axis_size(TILE)
    mine = lax.all_to_all(
        jnp.broadcast_to(values[None], (places,) + values.shape), TILE, 0, 0, tiled=True
    )
    count = lax.axis_size("batch")
    theirs = lax.ppermute(mine, "batch", [(i, count - 1 - i) for i in range(count)])
    first = lax.axis_index("batch") == 0
    both = jnp.stack([jnp.where(first, mine, theirs), jnp.where(first, theirs, mine)], axis=1)
    return both.reshape((places * count,) + values.shape)


def one_device_takes_a_sample(fields, block_kernels, head_weight, norm_params):
    samples_here, rows_here, cols_here, in_width = fields.shape
    nl, no, nb = (lax.axis_size(axis) for axis in ALL)
    rows, cols, width = rows_here * nl, cols_here * no, norm_params.shape[2]
    return (
        samples_here <= nl * no
        and nb == 2
        and rows * cols <= MOST_PIXELS
        and rows % (2 * GROUP) == 0
        and cols % 128 == 0
        and cols_here % 8 == 0
        and width == 128
        and head_weight.shape[1] == 2
        and in_width + 3 * PIECES <= width
        and block_kernels.shape[1] % width == 0
    )


def body(*args):
    fields, block_kernels, head_weight, norm_params = args[0], args[6], args[9], args[12]
    if one_device_takes_a_sample(fields, block_kernels, head_weight, norm_params):
        return whole_sample_body(*args)
    return tile_body(*args)


def solution(mesh):
    in_specs = (
        P("batch", "lat", "lon", None),
        P("batch", "lat", "lon", None),
        P("batch", "lat", "lon"),
        P(("lat", "lon", "batch")),
        P(("lat", "lon", "batch")),
        P(("lat", "lon", "batch")),
        P(None, ("lat", "lon", "batch")),
        P(None, ("lat", "lon", "batch")),
        P(None, ("lat", "lon", "batch")),
        P(),
        P(),
        P(),
        P(),
        P(),
        P(),
    )
    out_specs = (
        P(),
        P(),
        P(("lat", "lon", "batch")),
        P(("lat", "lon", "batch")),
        P(("lat", "lon", "batch")),
        P(None, ("lat", "lon", "batch")),
        P(None, ("lat", "lon", "batch")),
        P(None, ("lat", "lon", "batch")),
        P(),
        P(),
        P(),
        P(),
        P(),
        P(),
    )
    return jax.shard_map(body, mesh=mesh, in_specs=in_specs, out_specs=out_specs, check_vma=False)
```

```python
import functools

import jax
import jax.numpy as jnp
from jax import lax
from jax.experimental import pallas as pl
from jax.experimental.pallas import tpu as pltpu
from jax.sharding import PartitionSpec as P

STEP = 10


NORM_EPSILON = 1e-05
GELU_SCALE = 0.7978845608028654
GELU_CUBE = 0.044715
GROUP = 4
SMALL_ROOM = 14 << 20
LARGE_ROOM = 32 << 20
COPIES = 24
FORWARD, BACKWARD = 1, 2
NEAR = 3
LATE = 3
MOST_PIXELS = 4096


def shortened(shard):

    def short(part):
        return part.astype(jnp.bfloat16) if part.dtype == jnp.float32 else part

    return jax.tree.map(short, shard)


def with_halo(cells, sides, width):
    for axis, dim in sides:
        count = lax.axis_size(axis)
        ends = count - 1
        head = lax.slice_in_dim(cells, 0, width, axis=dim)
        tail = lax.slice_in_dim(cells, cells.shape[dim] - width, cells.shape[dim], axis=dim)
        cells = jnp.concatenate(
            [
                lax.ppermute(tail, axis, [(i, (i + 1) % count) for i in range(ends)]),
                cells,
                lax.ppermute(head, axis, [((i + 1) % count, i) for i in range(ends)]),
            ],
            axis=dim,
        )
    return cells


def conv_valid(padded, kernel):
    return lax.conv_general_dilated(
        padded,
        kernel,
        (1, 1),
        "VALID",
        dimension_numbers=("NHWC", "HWIO", "NHWC"),
        preferred_element_type=jnp.float32,
    )


def kernel_grad(padded, gradient):
    summed = lax.conv_general_dilated(
        padded,
        gradient,
        (1, 1),
        "VALID",
        dimension_numbers=("CHWN", "IHWO", "NHWC"),
        preferred_element_type=jnp.float32,
    )
    return summed.transpose(1, 2, 0, 3)


def rim_cells(values):
    return with_halo(shortened(values), (("lat", 1), ("lon", 2)), 1).astype(values.dtype)


def to_channels(values):
    return jax.tree.map(
        lambda part, own: part.astype(own.dtype),
        lax.all_to_all(shortened(values), "lat", split_axis=3, concat_axis=0, tiled=True),
        values,
    )


def to_pixels(values):
    return lax.all_to_all(values, "lat", split_axis=0, concat_axis=3, tiled=True)


def spread_sums(summed, squares):
    return lax.psum((summed, squares), ("lon", "batch"))


def own_channels(norm_pair, width):
    return lax.dynamic_slice_in_dim(norm_pair, lax.axis_index("lat") * width, width, 1)


def norm_forward(fired, norm_pair, pixel_count):
    values = to_channels(fired)
    norm_pair = own_channels(norm_pair, values.shape[3])
    widened = values.astype(jnp.float32)
    summed, squares = spread_sums(
        jnp.sum(widened, axis=(0, 1, 2)), jnp.sum(widened * widened, axis=(0, 1, 2))
    )
    average = summed / pixel_count
    inverse_std = lax.rsqrt(squares / pixel_count - average * average + NORM_EPSILON)
    centred = (widened - average) * inverse_std
    normed = (norm_pair[0] * centred + norm_pair[1]).astype(jnp.bfloat16)
    normed = to_pixels(normed)
    return (normed, (centred, inverse_std, norm_pair))


def norm_backward(gradient, kept, pixel_count):
    centred, inverse_std, norm_pair = kept
    gradient = to_channels(gradient)
    widened = gradient.astype(jnp.float32)
    shift_grad, gain_grad = spread_sums(
        jnp.sum(widened, axis=(0, 1, 2)), jnp.sum(widened * centred, axis=(0, 1, 2))
    )
    scaled = norm_pair[0] * inverse_std
    fired_grad = (
        scaled * (widened - shift_grad / pixel_count - centred * gain_grad / pixel_count)
    ).astype(jnp.bfloat16)
    fired_grad = to_pixels(fired_grad)
    return (fired_grad, jnp.stack([gain_grad, shift_grad]))


def gelu_pullback(preact, gradient):
    unused, pullback = jax.vjp(jax.nn.gelu, preact)
    return pullback(gradient)[0]


def conv_forward(source, kernel, norm_pair, pixel_count):
    padded = rim_cells(source)
    preact = conv_valid(padded, kernel)
    fired = jax.nn.gelu(preact).astype(jnp.bfloat16)
    normed, kept = norm_forward(fired, norm_pair, pixel_count)
    return (normed, (padded, preact, kept))


def conv_backward(gradient, kernel, record, pixel_count):
    padded, preact, kept = record
    fired_grad, pair_grad = norm_backward(gradient, kept, pixel_count)
    preact_grad = gelu_pullback(preact, fired_grad.astype(jnp.float32)).astype(jnp.bfloat16)
    kernel_gradient = kernel_grad(padded, preact_grad)
    flipped = kernel[::-1, ::-1].transpose(0, 1, 3, 2)
    source_grad = conv_valid(rim_cells(preact_grad), flipped)
    return (source_grad, kernel_gradient, pair_grad)


def block_forward(stream, kernels, norm_pairs, pixel_count):
    middle, first_record = conv_forward(
        stream.astype(jnp.bfloat16), kernels[0], norm_pairs[0], pixel_count
    )
    branch, second_record = conv_forward(middle, kernels[1], norm_pairs[1], pixel_count)
    return (stream + branch.astype(jnp.float32), (first_record, second_record))


def block_backward(stream_grad, stream, kernels, norm_pairs, pixel_count):
    unused, records = block_forward(stream, kernels, norm_pairs, pixel_count)
    middle_grad, second_kernel, second_pair = conv_backward(
        stream_grad.astype(jnp.bfloat16), kernels[1], records[1], pixel_count
    )
    source_grad, first_kernel, first_pair = conv_backward(
        middle_grad.astype(jnp.bfloat16), kernels[0], records[0], pixel_count
    )
    return (stream_grad + source_grad, (first_kernel, second_kernel), (first_pair, second_pair))


def adamw_update(weight, gradient, momentum, variance, step_rate):
    momentum = 0.9 * momentum + 0.1 * gradient
    variance = 0.999 * variance + 0.001 * gradient * gradient
    corrected = momentum / (1.0 - 0.9**STEP)
    scaled = jnp.sqrt(variance / (1.0 - 0.999**STEP)) + 1e-08
    return (momentum, variance, weight - step_rate * (corrected / scaled + 0.01 * weight))


def finished(
    loss_sum, loss_weight, input_grad, block_grad, head_grad, norm_grad,
    input_state, block_state, head_state, norm_state,
):
    outputs = [jnp.reshape(loss_sum, (1,)), jnp.reshape(loss_weight, (1,))]
    for state, gradient, step_rate in (
        (input_state, input_grad, 0.015),
        (block_state, block_grad, 0.03),
        (head_state, head_grad, 0.15),
        (norm_state, norm_grad, 0.8),
    ):
        weight, first, second = state
        outputs.extend(adamw_update(weight, gradient, first, second, step_rate))
    return tuple(outputs)


def tile_body(
    fields,
    targets,
    land_mask,
    input_kernel,
    input_first,
    input_second,
    block_kernels,
    block_first,
    block_second,
    head_weight,
    head_first,
    head_second,
    norm_params,
    norm_first,
    norm_second,
):
    samples_here, rows_here, cols_here, in_width = fields.shape
    channels = norm_params.shape[2]
    conv_count = block_kernels.shape[0]
    full_input, full_blocks = (
        lax.all_gather(
            input_kernel.astype(jnp.bfloat16), ("lat", "lon", "batch"), axis=0, tiled=True
        ),
        lax.all_gather(
            block_kernels.astype(jnp.bfloat16), ("lat", "lon", "batch"), axis=1, tiled=True
        ),
    )
    kernel_in = full_input.reshape(7, 7, in_width, channels)
    kernels = full_blocks.reshape(conv_count, 3, 3, channels, channels)
    head_low = head_weight.astype(jnp.bfloat16)
    sample_count = samples_here * lax.axis_size("batch")
    pixel_count = float(
        sample_count * rows_here * lax.axis_size("lat") * cols_here * lax.axis_size("lon")
    )
    row_global = (lax.axis_index("lat") * rows_here + jnp.arange(rows_here)).astype(jnp.float32)
    latitude = (row_global + 0.5) / (rows_here * lax.axis_size("lat")) * jnp.pi - jnp.pi / 2
    pixel_weight = jnp.cos(latitude)[None, :, None] * land_mask.astype(jnp.float32)
    valid_sum = lax.psum(jnp.sum(pixel_weight), ("lat", "lon", "batch"))
    loss_weight = valid_sum / sample_count
    padded_in = with_halo(fields, (("lat", 1), ("lon", 2)), 3)
    preact_in = conv_valid(padded_in, kernel_in)
    streams = [jax.nn.gelu(preact_in)]
    for layer in range(conv_count // 2):
        advanced, unused = block_forward(
            streams[-1],
            kernels[2 * layer : 2 * layer + 2],
            norm_params[2 * layer : 2 * layer + 2],
            pixel_count,
        )
        streams.append(advanced)
    top_stream = streams[-1].astype(jnp.bfloat16)
    predicted = jnp.einsum(
        "nhwc,co->nhwo", top_stream, head_low, preferred_element_type=jnp.float32
    )
    misfit = predicted - targets
    loss_local = jnp.sum(pixel_weight[..., None] * misfit * misfit)
    pred_grad = (2.0 * pixel_weight[..., None] * misfit / loss_weight).astype(jnp.bfloat16)
    head_local = jnp.einsum(
        "nhwc,nhwo->co", top_stream, pred_grad, preferred_element_type=jnp.float32
    )
    stream_grad = jnp.einsum(
        "nhwo,co->nhwc", pred_grad, head_low, preferred_element_type=jnp.float32
    )
    kernel_grads = [None] * conv_count
    pair_grads = [None] * conv_count
    for layer in reversed(range(conv_count // 2)):
        stream_grad, kernel_pair, norm_pair = block_backward(
            stream_grad,
            streams[layer],
            kernels[2 * layer : 2 * layer + 2],
            norm_params[2 * layer : 2 * layer + 2],
            pixel_count,
        )
        kernel_grads[2 * layer], kernel_grads[2 * layer + 1] = kernel_pair
        pair_grads[2 * layer], pair_grads[2 * layer + 1] = norm_pair
    pre_in_grad = gelu_pullback(preact_in, stream_grad).astype(jnp.bfloat16)
    input_local = kernel_grad(padded_in, pre_in_grad).reshape(-1)
    block_local = jnp.stack(kernel_grads).reshape(conv_count, -1)
    input_grad, block_grad = (
        lax.psum_scatter(input_local, ("lat", "lon", "batch"), scatter_dimension=0, tiled=True),
        lax.psum_scatter(block_local, ("lat", "lon", "batch"), scatter_dimension=1, tiled=True),
    )
    head_grad, loss_sum = lax.psum((head_local, loss_local), ("lat", "lon", "batch"))
    norm_grad = jnp.stack(pair_grads)
    norm_grad = lax.all_gather(norm_grad, "lat", axis=2, tiled=True)
    return finished(
        loss_sum, loss_weight, input_grad, block_grad, head_grad, norm_grad,
        (input_kernel, input_first, input_second), (block_kernels, block_first, block_second),
        (head_weight, head_first, head_second), (norm_params, norm_first, norm_second),
    )


ALL = ("lat", "lon", "batch")
TILE = ("lat", "lon")
PIECES = 3
SPREAD = 16


VECTOR, WIDE = "vector", "wide"
SPACES = {VECTOR: pltpu.VMEM, WIDE: pltpu.HBM}


def call(kernel, ins, outs, scratch=(), flags=None, cost=0, room=SMALL_ROOM):
    specs = [pl.BlockSpec(memory_space=SPACES[space]) for unused, space in ins]
    args = [
        pltpu.with_memory_space_constraint(array, pltpu.HBM) if space == WIDE else array
        for array, space in ins
    ]
    if flags is not None:
        specs, args = [pl.BlockSpec(memory_space=pltpu.SMEM)] + specs, [flags] + args
    return pl.pallas_call(
        kernel,
        out_shape=[
            pltpu.HBM(shape, dtype) if space == WIDE else jax.ShapeDtypeStruct(shape, dtype)
            for shape, dtype, space in outs
        ],
        in_specs=specs,
        out_specs=[pl.BlockSpec(memory_space=SPACES[space]) for *unused, space in outs],
        scratch_shapes=list(scratch) + [pltpu.SemaphoreType.DMA((COPIES,))],
        compiler_params=pltpu.CompilerParams(vmem_limit_bytes=room),
        cost_estimate=pl.CostEstimate(flops=cost, bytes_accessed=4 << 20, transcendentals=0),
    )(*args)


class Mover:
    def __init__(self, semaphores):
        self.semaphores, self.used, self.sent = semaphores, 0, []

    def start(self, source, target):
        copy = pltpu.make_async_copy(source, target, self.semaphores.at[self.used])
        self.used += 1
        copy.start()
        return copy

    def fetch(self, source, target, parts=1):
        step = target.shape[0] // parts
        return [
            self.start(source.at[pl.ds(i * step, step)], target.at[pl.ds(i * step, step)])
            for i in range(parts)
        ]

    def send(self, source, target):
        self.sent.append(self.start(source, target))

    def finish(self):
        for copy in self.sent:
            copy.wait()


def dot(left, right, dims=((1,), (0,))):
    return lax.dot_general(left, right, (dims, ((), ())), preferred_element_type=jnp.float32)


def gelu_value(x):
    return x * (0.5 * (1.0 + jnp.tanh(GELU_SCALE * (x + GELU_CUBE * (x * x * x)))))


def gelu_both(x):
    square = x * x
    level = jnp.tanh(GELU_SCALE * (x + GELU_CUBE * (x * square)))
    half = 0.5 * (1.0 + level)
    slope = half + 0.5 * x * (1.0 - level * level) * (GELU_SCALE * (1.0 + 3.0 * GELU_CUBE * square))
    return x * half, slope


def shifted(cells, step):
    count = cells.shape[0]
    if step == 0:
        return cells
    column = lax.broadcasted_iota(jnp.int32, cells.shape, 0) + step
    rolled = pltpu.roll(cells, (-step) % count, 0)
    return jnp.where((column >= 0) & (column < count), rolled, 0.0)


def spread_pair(pair, cells, shifts_ref, sizes):
    cols, width, pairs = sizes
    for b in range(3):
        moved = shifted(cells, b - 1).astype(jnp.bfloat16)
        shifts_ref[(pair + 1) * cols : (pair + 2) * cols, b * width : (b + 1) * width] = moved[:, width:]
        shifts_ref[pair * cols : (pair + 1) * cols, (3 + b) * width : (4 + b) * width] = moved[:, :width]


def clear_rim(shifts_ref, sizes):
    cols, width, pairs = sizes
    zero = jnp.zeros((cols, 3 * width), jnp.bfloat16)
    shifts_ref[0:cols, 0 : 3 * width] = zero
    shifts_ref[pairs * cols : (pairs + 1) * cols, 3 * width : 6 * width] = zero


def taps_forward(weight_ref, taps_ref, width):
    for k in range(2):
        for rr in range(2):
            for b in range(3):
                for q in range(2):
                    a = 2 * k + rr - q
                    at = (rr * 3 + b) * width
                    if 0 <= a <= 2:
                        block = weight_ref[(a * 3 + b) * width : (a * 3 + b + 1) * width, :]
                    else:
                        block = jnp.zeros((width, width), jnp.bfloat16)
                    taps_ref[k, at : at + width, q * width : (q + 1) * width] = block


def taps_backward(weight_ref, taps_ref, width):
    for k in range(2):
        for rr in range(2):
            for b in range(3):
                for q in range(2):
                    a = 2 - (2 * k + rr - q)
                    at = (rr * 3 + b) * width
                    if 0 <= a <= 2:
                        tap = a * 3 + 2 - b
                        block = weight_ref[tap * width : (tap + 1) * width, :]
                    else:
                        block = jnp.zeros((width, width), jnp.bfloat16)
                    taps_ref[k, q * width : (q + 1) * width, at : at + width] = block


def pair_conv(shifts_ref, taps_ref, group, cols, dims=((1,), (0,))):
    rows = GROUP * cols
    first = shifts_ref[group * rows : (group + 1) * rows, :]
    second = shifts_ref[group * rows + cols : (group + 1) * rows + cols, :]
    return dot(first, taps_ref[0], dims) + dot(second, taps_ref[1], dims)


def folded(sums, width):
    return sums[:, :width] + sums[:, width:]


def total_of(parts_ref):
    return jnp.sum(parts_ref[...], axis=0)


def twice(row):
    return jnp.concatenate([row, row], axis=1)


def norm_of(total, pixel_count):
    average = total[0:1] / pixel_count
    return average, lax.rsqrt(total[1:2] / pixel_count - average * average + NORM_EPSILON)


def conv_and_sums(flags_ref, shifts_ref, taps_ref, fired_ref, slope_ref, sums_ref, sizes, more=None):
    cols, width, pairs = sizes
    total = jnp.zeros((1, 2 * width), jnp.float32)
    squares = jnp.zeros((1, 2 * width), jnp.float32)
    step = GROUP * cols
    for group in range(pairs // GROUP):
        fired, slope = gelu_both(pair_conv(shifts_ref, taps_ref, group, cols))
        rows = pl.ds(group * step, step)
        fired = fired.astype(jnp.bfloat16)
        fired_ref[rows, :] = fired
        slope_ref[rows, :] = slope.astype(jnp.bfloat16)
        wide = fired.astype(jnp.float32)
        total = total + jnp.sum(wide, axis=0, keepdims=True)
        squares = squares + jnp.sum(wide * wide, axis=0, keepdims=True)
    active = flags_ref[0].astype(jnp.float32)
    parts = [folded(total, width) * active, folded(squares, width) * active]
    put_sums(sums_ref, parts + (more or []))


def put_sums(sums_ref, parts):
    shape = sums_ref.shape[1:]
    row = lax.broadcasted_iota(jnp.int32, shape, 0)
    block = jnp.zeros(shape, jnp.float32)
    at = 0
    for part in parts:
        for i in range(part.shape[0]):
            block = jnp.where(row == at, jnp.broadcast_to(part[i : i + 1], shape), block)
            at += 1
    sums_ref[...] = jnp.broadcast_to(block[None], sums_ref.shape)


def field_row(fields_ref, row, tiles):
    nl, no, rows_here, cols_here = tiles
    lat, inner = row // rows_here, row % rows_here
    return jnp.concatenate([fields_ref[lat * no + lon, inner] for lon in range(no)], axis=0)


def wide_shifts(fields_ref, shifts_ref, tiles, sizes):
    cols, width, pairs = sizes
    rows = 2 * pairs
    for row in range(-3, rows + 3):
        at, rr = (row + 3) // 2, (row + 3) % 2
        if 0 <= row < rows:
            cells = field_row(fields_ref, row, tiles).astype(jnp.float32)
        for b in range(7):
            if 0 <= row < rows:
                moved = shifted(cells, b - 3).astype(jnp.bfloat16)
            else:
                moved = jnp.zeros((cols, width), jnp.bfloat16)
            spot = (rr * 7 + b) * width
            shifts_ref[at * cols : (at + 1) * cols, spot : spot + width] = moved


def first_row(device, shard, width, grain):
    return lax.div(device * shard, grain * width) * grain


def frame_rows(shard, devices, width, grain):
    unit = grain * width
    rows = max(-(-(d + 1) * shard // unit) - d * shard // unit for d in range(devices)) * grain
    return -(-rows // SPREAD) * SPREAD


def device_at(flags_ref, lon_step, lat_step, core_step, tiles):
    lat = flags_ref[2] ^ lat_step
    lon = flags_ref[3] ^ lon_step
    return (lat * tiles[1] + lon) * 2 + (flags_ref[1] ^ core_step)


def pack_kernel(fields_ref, targets_ref, weights_ref, packed_ref, pieces_ref, unused_ref, *, in_width):
    samples, rows, cols, unused = fields_ref.shape
    width = packed_ref.shape[3]
    outs = targets_ref.shape[0]
    many = pieces_ref.shape[0]
    pieces_ref[...] = jnp.zeros(pieces_ref.shape, jnp.float32)
    packed_ref[samples:] = jnp.zeros((packed_ref.shape[0] - samples, rows, cols, width), jnp.bfloat16)
    take_from = lax.broadcasted_iota(jnp.int32, (many, width), 0)
    put_to = lax.broadcasted_iota(jnp.int32, (many, width), 1) - in_width
    picks = [
        jnp.where((put_to >= 0) & (take_from == put_to * rows + row), 1.0, 0.0).astype(jnp.bfloat16)
        for row in range(rows)
    ]
    for sample in range(samples):
        for source in range(outs + 1):
            left = targets_ref[source, sample] if source < outs else weights_ref[sample]
            for piece in range(PIECES):
                low = left.astype(jnp.bfloat16).astype(jnp.float32)
                left = left - low
                at = (source * PIECES + piece) * rows
                pieces_ref[at : at + rows, :] = low
        pieces = pieces_ref[...].astype(jnp.bfloat16)
        for row in range(rows):
            placed = dot(pieces, picks[row], ((0,), (0,))).astype(jnp.bfloat16)
            packed_ref[sample, row] = placed
            packed_ref[sample, row, :, 0:in_width] = fields_ref[sample, row]


def place_blocks(part, at, count, rows, device, stage_ref, flat_refs):
    stage_ref[...] = part[at : at + stage_ref.shape[0], :].astype(jnp.float32)
    for index in range(count):
        flat_refs[index][pl.ds(device * rows, rows), :] = stage_ref[index * rows : (index + 1) * rows, :]


def near_kernels(
    flags_ref, parts, arrivals, taps_ref, flat_ref, stage_ref, flat_block_refs, tiles, shards, in_width
):
    nl, no = tiles[0], tiles[1]
    width = flat_ref.shape[1]
    in_shard, block_rows = shards
    rows = frame_rows(in_shard, 2 * nl * no, width, 1)
    flat_ref[...] = jnp.zeros(flat_ref.shape, jnp.float32)
    for lon_step in range(no):
        for core_step in range(2):
            part = parts.at[lon_step * 2 + core_step]
            arrivals[lon_step * 2 + core_step].wait()
            for lat_step in range(nl):
                device = device_at(flags_ref, lon_step, lat_step, core_step, tiles)
                spot = pl.ds(first_row(device, in_shard, width, 1), rows)
                flat_ref[spot, :] += part[lat_step, 0:rows, :].astype(jnp.float32)
                place_blocks(
                    part.at[lat_step], rows, len(flat_block_refs), block_rows, device, stage_ref, flat_block_refs
                )
    inside = lax.broadcasted_iota(jnp.int32, (width, width), 0) < in_width
    zero = jnp.zeros((width, width), jnp.bfloat16)
    for b in range(7):
        taps_ref[3, (7 + b) * width : (8 + b) * width, 0:width] = zero
        taps_ref[0, b * width : (b + 1) * width, width : 2 * width] = zero
        for a in range(7):
            tap = a * 7 + b
            block = flat_ref[tap * in_width : tap * in_width + width, :]
            block = jnp.where(inside, block, 0.0).astype(jnp.bfloat16)
            for q in range(2):
                k, rr = (a + q) // 2, (a + q) % 2
                spot = (rr * 7 + b) * width
                taps_ref[k, spot : spot + width, q * width : (q + 1) * width] = block


def far_kernels_kernel(flags_ref, *refs, tiles, block_rows, count):
    nl, no = tiles[0], tiles[1]
    parts, outs, refs = refs[: 2 * no], refs[2 * no : 2 * no + count], refs[2 * no + count :]
    stage_ref, *flat_refs, whole_ref, semaphores = refs
    mover = Mover(semaphores)
    for lon_step in range(no):
        for core_step in range(2):
            part = parts[lon_step * 2 + core_step]
            for lat_step in range(nl):
                device = device_at(flags_ref, lon_step, lat_step, core_step, tiles)
                place_blocks(part.at[lat_step], 0, count, block_rows, device, stage_ref, flat_refs)
    for index in range(count):
        whole_ref[index] = flat_refs[index][...].astype(jnp.bfloat16)
        mover.send(whole_ref.at[index], outs[index])
    mover.finish()


def first_kernel(flags_ref, *refs, tiles, sizes, shards, in_width, count):
    cols, width, pairs = sizes
    nl, no = tiles[0], tiles[1]
    near, refs = refs[: 2 * no], refs[2 * no :]
    fields_in, *refs = refs
    weight_outs, refs = refs[:count], refs[count:]
    slope_in_out, stream_out, source_out, wide_out, fired_ref, slope_ref, sums_ref, next_weight_ref, *refs = refs
    flat_block_refs, refs = refs[:count], refs[count:]
    (
        near_ref, fields_ref, weights_ref, stage_ref, in_taps_ref, flat_ref, wide_ref,
        slope_in_ref, stream_ref, source_ref, shifts_ref, taps_ref, semaphores,
    ) = refs
    mover = Mover(semaphores)
    fetched = mover.fetch(fields_in, fields_ref)
    arrivals = [mover.start(part, near_ref.at[i]) for i, part in enumerate(near)]
    clear_rim(shifts_ref, sizes)
    fetched[0].wait()
    wide_shifts(fields_ref, wide_ref, tiles, sizes)
    mover.send(wide_ref, wide_out)
    near_kernels(
        flags_ref, near_ref, arrivals, in_taps_ref, flat_ref, stage_ref, flat_block_refs, tiles, shards, in_width
    )
    for index in range(count):
        weight = flat_block_refs[index][...].astype(jnp.bfloat16)
        weights_ref[index] = weight
        if index == 1:
            next_weight_ref[...] = weight
        mover.send(weights_ref.at[index], weight_outs[index])
    taps_forward(weights_ref.at[0], taps_ref, width)
    step = GROUP * cols
    for group in range(pairs // GROUP):
        at = group * step
        preact = dot(wide_ref[at : at + step, :], in_taps_ref[0])
        for k in range(1, 4):
            preact += dot(wide_ref[at + k * cols : at + step + k * cols, :], in_taps_ref[k])
        rows = pl.ds(at, step)
        stream, slope = gelu_both(preact)
        slope_in_ref[rows, :] = slope.astype(jnp.bfloat16)
        mover.send(slope_in_ref.at[rows], slope_in_out.at[rows])
        stream_ref[rows, :] = stream
        mover.send(stream_ref.at[rows], stream_out.at[rows])
        source = stream.astype(jnp.bfloat16)
        source_ref[rows, :] = source
        mover.send(source_ref.at[rows], source_out.at[rows])
        for pair in range(GROUP):
            cells = source[pair * cols : (pair + 1) * cols].astype(jnp.float32)
            spread_pair(group * GROUP + pair, cells, shifts_ref, sizes)
    weight_sum = jnp.zeros((1, width), jnp.float32)
    for row in range(2 * pairs):
        low = field_row(fields_ref, row, tiles).astype(jnp.float32)
        weight_sum += jnp.sum(low, axis=0, keepdims=True)
    lane = lax.broadcasted_iota(jnp.int32, (1, width), 1) - in_width
    chosen = (lane >= 2 * PIECES) & (lane < 3 * PIECES)
    weight_sum = jnp.sum(jnp.where(chosen, weight_sum, 0.0), axis=1, keepdims=True)
    conv_and_sums(
        flags_ref, shifts_ref, taps_ref, fired_ref, slope_ref, sums_ref, sizes,
        [jnp.broadcast_to(weight_sum, (1, width))],
    )
    mover.finish()


def keep_norm(stats_ref, total, average, inverse_std):
    stats_ref[0:1, :] = average
    stats_ref[1:2, :] = inverse_std
    stats_ref[2:3, :] = total[2:3]


def unit_kernel(
    flags_ref, fired_in_ref, parts_ref, norms_ref, weight_ref, slope_in_ref, *refs,
    sizes, pixel_count, index, residual, fetches,
):
    cols, width, pairs = sizes
    if residual:
        stream_in_ref, *refs = refs
    fetched_from, refs = refs[:fetches], refs[fetches:]
    if residual:
        stream_out, *refs = refs
    source_out, stats_out, fired_out, slope_out, fired_ref, slope_ref, sums_ref, *refs = refs
    fetched_to, refs = refs[:fetches], refs[fetches:]
    if residual:
        stream_ref, *refs = refs
    source_ref, stats_ref, shifts_ref, taps_ref, semaphores = refs
    mover = Mover(semaphores)
    mover.send(fired_in_ref, fired_out)
    mover.send(slope_in_ref, slope_out)
    for source, target in zip(fetched_from, fetched_to):
        mover.send(source, target)
    total = total_of(parts_ref)
    average, inverse_std = norm_of(total, pixel_count)
    keep_norm(stats_ref, total, average, inverse_std)
    mover.send(stats_ref, stats_out)
    average, inverse_std = twice(average), twice(inverse_std)
    gain, shift = twice(norms_ref[index, 0:1]), twice(norms_ref[index, 1:2])
    taps_forward(weight_ref, taps_ref, width)
    clear_rim(shifts_ref, sizes)
    for pair in range(pairs):
        rows = pl.ds(pair * cols, cols)
        fired = fired_in_ref[rows, :].astype(jnp.float32)
        normed = (gain * ((fired - average) * inverse_std) + shift).astype(jnp.bfloat16)
        if residual:
            stream = stream_in_ref[rows, :] + normed.astype(jnp.float32)
            stream_ref[rows, :] = stream
            normed = stream.astype(jnp.bfloat16)
        source_ref[rows, :] = normed
        spread_pair(pair, normed.astype(jnp.float32), shifts_ref, sizes)
    mover.send(source_ref, source_out)
    if residual:
        mover.send(stream_ref, stream_out)
    conv_and_sums(flags_ref, shifts_ref, taps_ref, fired_ref, slope_ref, sums_ref, sizes)
    mover.finish()


def head_kernel(
    flags_ref, fired_ref, parts_ref, norms_ref, head_ref, stream_ref, fields_ref, first_stats_ref,
    grad_ref, sums_ref, stats_ref, unused, *,
    tiles, sizes, pixel_count, sample_count, in_width, index,
):
    cols, width, pairs = sizes
    total = total_of(parts_ref)
    average, inverse_std = norm_of(total, pixel_count)
    keep_norm(stats_ref, total, average, inverse_std)
    gain, shift = norms_ref[index, 0:1], norms_ref[index, 1:2]
    head = head_ref[...]
    outs = 2
    lane_from = lax.broadcasted_iota(jnp.int32, (width, width), 0) - in_width
    lane_to = lax.broadcasted_iota(jnp.int32, (width, width), 1)
    within = lane_from - PIECES * lane_to
    picks = (within >= 0) & (within < PIECES) & (lane_to < outs)
    pick_target = jnp.where(picks, 1.0, 0.0).astype(jnp.bfloat16)
    picks = (lane_from >= outs * PIECES) & (lane_from < (outs + 1) * PIECES) & (lane_to < outs)
    pick_weight = jnp.where(picks, 1.0, 0.0).astype(jnp.bfloat16)
    zero = jnp.zeros((1, width), jnp.float32)
    loss, shift_grad, gain_grad = zero, zero, zero
    head_grad = jnp.zeros((width, width), jnp.float32)
    loss_weight = first_stats_ref[2:3, :] / sample_count
    for row in range(2 * pairs):
        pair, q = row // 2, row % 2
        rows, lanes = slice(pair * cols, (pair + 1) * cols), slice(q * width, (q + 1) * width)
        centred = (fired_ref[rows, lanes].astype(jnp.float32) - average) * inverse_std
        normed = (gain * centred + shift).astype(jnp.bfloat16)
        top = (stream_ref[rows, lanes] + normed.astype(jnp.float32)).astype(jnp.bfloat16)
        fields = field_row(fields_ref, row, tiles)
        misfit = dot(top, head) - dot(fields, pick_target)
        weight = dot(fields, pick_weight)
        loss += jnp.sum(weight * misfit * misfit, axis=0, keepdims=True)
        pred_grad = (2.0 * weight * misfit / loss_weight).astype(jnp.bfloat16)
        head_grad += dot(pred_grad, top, ((0,), (0,)))
        grad = dot(pred_grad, head, ((1,), (1,)))
        grad_ref[rows, lanes] = grad
        low = grad.astype(jnp.bfloat16).astype(jnp.float32)
        shift_grad += jnp.sum(low, axis=0, keepdims=True)
        gain_grad += jnp.sum(low * centred, axis=0, keepdims=True)
    loss = jnp.broadcast_to(jnp.sum(loss, axis=1, keepdims=True), (1, width))
    put_sums(sums_ref, [shift_grad, gain_grad, head_grad[0:outs], loss])


def back_to_preact(parts_ref, stats_ref, norms_ref, index, flags_ref, refs, pixel_count, sizes):
    grad_ref, fired_ref, slope_ref, pre_ref, pair_grad_ref, shifts_ref = refs
    cols, width, pairs = sizes
    total = total_of(parts_ref)
    shift_grad, gain_grad = total[0:1], total[1:2]
    pair_grad_ref[0:1, :] = gain_grad
    pair_grad_ref[1:2, :] = shift_grad
    clear_rim(shifts_ref, sizes)
    average, inverse_std = twice(stats_ref[0:1, :]), twice(stats_ref[1:2, :])
    scaled = twice(norms_ref[index, 0:1]) * inverse_std * flags_ref[0].astype(jnp.float32)
    shift_mean, gain_mean = twice(shift_grad / pixel_count), twice(gain_grad / pixel_count)
    for pair in range(pairs):
        rows = pl.ds(pair * cols, cols)
        centred = (fired_ref[rows, :].astype(jnp.float32) - average) * inverse_std
        grad = grad_ref[rows, :].astype(jnp.bfloat16).astype(jnp.float32)
        fired_grad = (scaled * (grad - shift_mean - centred * gain_mean)).astype(jnp.bfloat16)
        pre = (fired_grad.astype(jnp.float32) * slope_ref[rows, :].astype(jnp.float32)).astype(jnp.bfloat16)
        pre_ref[rows, :] = pre
        spread_pair(pair, pre.astype(jnp.float32), shifts_ref, sizes)


def back_kernel(
    flags_ref, parts_ref, norms_ref, grad_ref, fired_ref, slope_ref, stats_ref, *refs,
    sizes, pixel_count, index, second,
):
    cols, width, pairs = sizes
    below_in, below_slope_in, below_stats_in, weight_in, *refs = refs
    if not second:
        kept_in, *refs = refs
    pre_out, pair_grad_out, *refs = refs
    if second:
        kept_out, *refs = refs
    out_ref, sums_ref, below_ref, below_slope_ref, below_stats_ref, *refs = refs
    if not second:
        kept_ref, *refs = refs
    weight_ref, pre_ref, pair_grad_ref, shifts_ref, taps_ref, semaphores = refs
    mover = Mover(semaphores)
    groups = pairs // GROUP
    weight = mover.fetch(weight_in, weight_ref)
    below_stats = mover.fetch(below_stats_in, below_stats_ref)
    if second:
        mover.send(grad_ref, kept_out)
    else:
        kept = mover.fetch(kept_in, kept_ref, groups)
    belows = mover.fetch(below_in, below_ref, groups)
    mover.send(below_slope_in, below_slope_ref)
    refs = (grad_ref, fired_ref, slope_ref, pre_ref, pair_grad_ref, shifts_ref)
    back_to_preact(parts_ref, stats_ref, norms_ref, index, flags_ref, refs, pixel_count, sizes)
    mover.send(pre_ref, pre_out)
    mover.send(pair_grad_ref, pair_grad_out)
    weight[0].wait()
    taps_backward(weight_ref, taps_ref, width)
    below_stats[0].wait()
    average, inverse_std = twice(below_stats_ref[0:1, :]), twice(below_stats_ref[1:2, :])
    shift_sum = jnp.zeros((1, 2 * width), jnp.float32)
    gain_sum = jnp.zeros((1, 2 * width), jnp.float32)
    step = GROUP * cols
    for group in range(groups):
        rows = pl.ds(group * step, step)
        source = pair_conv(shifts_ref, taps_ref, group, cols, ((1,), (1,)))
        if not second:
            kept[group].wait()
            source = source + kept_ref[rows, :]
        belows[group].wait()
        below = below_ref[rows, :].astype(jnp.float32)
        out_ref[rows, :] = source.astype(out_ref.dtype)
        low = source.astype(jnp.bfloat16).astype(jnp.float32)
        shift_sum += jnp.sum(low, axis=0, keepdims=True)
        gain_sum += jnp.sum(low * ((below - average) * inverse_std), axis=0, keepdims=True)
    active = flags_ref[0].astype(jnp.float32)
    put_sums(sums_ref, [folded(shift_sum, width) * active, folded(gain_sum, width) * active])
    mover.finish()


def cut_frames(flags_ref, flat_ref, mine_ref, theirs_ref, tiles, shard, grain):
    width = flat_ref.shape[1]
    nl, no = tiles[0], tiles[1]
    rows = mine_ref.shape[2]
    for lon_step in range(no):
        for lat_step in range(nl):
            for core_step, target in ((0, mine_ref), (1, theirs_ref)):
                device = device_at(flags_ref, lon_step, lat_step, core_step, tiles)
                start = first_row(device, shard, width, grain)
                if grain > 1:
                    start = pl.multiple_of(start, grain)
                target[lon_step, lat_step] = flat_ref[pl.ds(start, rows), :].astype(jnp.bfloat16)


def block_kernel_grad(shifts_ref, pre_ref, flat_ref, sizes):
    cols, width, pairs = sizes
    for a in range(4):
        k, rr = a // 2, a % 2
        block = shifts_ref[k * cols : (k + pairs) * cols, rr * 3 * width : (rr + 1) * 3 * width]
        grad = dot(block, pre_ref[...], ((0,), (0,)))
        if a < 3:
            flat_ref[a * 3 * width : (a + 1) * 3 * width, :] = grad[:, :width]
        if a > 0:
            flat_ref[(a - 1) * 3 * width : a * 3 * width, :] += grad[:, width:]


def kernel_grad_kernel(
    flags_ref, source_in, pre_in, mine_ref, theirs_ref, source_ref, pre_ref, shifts_ref, flat_ref, semaphores, *,
    tiles, sizes, shard,
):
    mover = Mover(semaphores)
    source, pre = mover.fetch(source_in, source_ref), mover.fetch(pre_in, pre_ref)
    clear_rim(shifts_ref, sizes)
    source[0].wait()
    spread_all_pairs(source_ref, shifts_ref, sizes)
    pre[0].wait()
    block_kernel_grad(shifts_ref, pre_ref, flat_ref, sizes)
    cut_frames(flags_ref, flat_ref, mine_ref, theirs_ref, tiles, shard, SPREAD)


def spread_all_pairs(source_ref, shifts_ref, sizes):
    cols, width, pairs = sizes
    for pair in range(pairs):
        cells = source_ref[pair * cols : (pair + 1) * cols, :].astype(jnp.float32)
        spread_pair(pair, cells, shifts_ref, sizes)


def last_kernel(
    flags_ref, parts_ref, norms_ref, grad_ref, fired_ref, slope_ref, stats_ref,
    weight_in, kept_in, in_slope_in, source_in, wide_in,
    pair_grad_out, mine_ref, theirs_ref, mine_first_ref, theirs_first_ref,
    weight_ref, kept_ref, in_slope_ref, source_ref, wide_ref, pre_ref, in_pre_ref, pair_grad_ref,
    shifts_ref, taps_ref, flat_ref, flat_first_ref, semaphores, *,
    tiles, sizes, shards, in_width, pixel_count,
):
    cols, width, pairs = sizes
    mover = Mover(semaphores)
    weight = mover.fetch(weight_in, weight_ref)
    kept = mover.fetch(kept_in, kept_ref)
    in_slope = mover.fetch(in_slope_in, in_slope_ref)
    source = mover.fetch(source_in, source_ref)
    wide = mover.fetch(wide_in, wide_ref)
    refs = (grad_ref, fired_ref, slope_ref, pre_ref, pair_grad_ref, shifts_ref)
    back_to_preact(parts_ref, stats_ref, norms_ref, 0, flags_ref, refs, pixel_count, sizes)
    mover.send(pair_grad_ref, pair_grad_out)
    weight[0].wait()
    taps_backward(weight_ref, taps_ref, width)
    kept[0].wait()
    in_slope[0].wait()
    step = GROUP * cols
    for group in range(pairs // GROUP):
        rows = pl.ds(group * step, step)
        grad = pair_conv(shifts_ref, taps_ref, group, cols, ((1,), (1,))) + kept_ref[rows, :]
        in_pre_ref[rows, :] = (grad * in_slope_ref[rows, :].astype(jnp.float32)).astype(jnp.bfloat16)
    source[0].wait()
    spread_all_pairs(source_ref, shifts_ref, sizes)
    block_kernel_grad(shifts_ref, pre_ref, flat_first_ref, sizes)
    cut_frames(flags_ref, flat_first_ref, mine_first_ref, theirs_first_ref, tiles, shards[1], SPREAD)
    wide[0].wait()
    for a in range(8):
        k, rr = a // 2, a % 2
        block = wide_ref[k * cols : (k + pairs) * cols, rr * 7 * width : (rr + 1) * 7 * width]
        grads = dot(block, in_pre_ref[...], ((0,), (0,)))
        for b in range(7):
            grad = grads[b * width : b * width + in_width]
            if a < 7:
                tap = a * 7 + b
                flat_ref[tap * in_width : (tap + 1) * in_width, :] = grad[:, :width]
            if a > 0:
                tap = (a - 1) * 7 + b
                flat_ref[tap * in_width : (tap + 1) * in_width, :] += grad[:, width:]
    cut_frames(flags_ref, flat_ref, mine_ref, theirs_ref, tiles, shards[0], 1)
    mover.finish()


def swap(values, axis, step):
    return lax.ppermute(values, axis, [(i, i ^ step) for i in range(lax.axis_size(axis))])


def low_sum(*values):
    return sum(part.astype(jnp.float32) for part in values).astype(jnp.bfloat16)


def summed_frames(pairs):
    halves = [low_sum(mine, swap(theirs, "batch", 1)) for mine, theirs in pairs]
    total = jnp.concatenate(halves, axis=2)
    total = low_sum(total[0], *(swap(total[k], "lon", k) for k in range(1, total.shape[0])))
    return sum(
        part.astype(jnp.float32)
        for part in [total[0]] + [swap(total[k], "lat", k) for k in range(1, total.shape[0])]
    )


def spread_all(values, axes):
    return lax.all_to_all(values, axes, 0, 0, tiled=True)


def whole_sample_body(
    fields,
    targets,
    land_mask,
    input_kernel,
    input_first,
    input_second,
    block_kernels,
    block_first,
    block_second,
    head_weight,
    head_first,
    head_second,
    norm_params,
    norm_first,
    norm_second,
):
    samples_here, rows_here, cols_here, in_width = fields.shape
    width = norm_params.shape[2]
    conv_count = block_kernels.shape[0]
    nl, no, nb = (lax.axis_size(axis) for axis in ALL)
    places, devices = nl * no, nl * no * nb
    tiles = (nl, no, rows_here, cols_here)
    cols, pairs = cols_here * no, rows_here * nl // 2
    sizes = (cols, width, pairs)
    pixels = pairs * cols
    sample_count = samples_here * nb
    pixel_count = float(sample_count * 2 * pixels)
    place = lax.axis_index(TILE)
    core = lax.axis_index("batch")
    flags = jnp.stack(
        [
            (place < samples_here).astype(jnp.int32),
            lax.axis_index("batch"),
            lax.axis_index("lat"),
            lax.axis_index("lon"),
        ]
    )
    bf16, f32 = jnp.bfloat16, jnp.float32
    device = lax.axis_index(ALL)
    in_shard, block_shard = input_kernel.shape[0], block_kernels.shape[1]
    in_frame = frame_rows(in_shard, devices, width, 1)
    block_frame = frame_rows(block_shard, devices, width, SPREAD)
    in_offset = device * in_shard % width
    block_offset = device * block_shard % (SPREAD * width)
    flat_rows = max((devices - 1) * in_shard // width + in_frame, 48 * in_width + width)
    flat_rows = -(-flat_rows // 8) * 8
    block_rows = block_shard // width

    def shard_rows(shards):
        count = shards.shape[0] * block_rows
        rows = shards.astype(bf16).reshape(count, width)
        return jnp.pad(rows, ((0, -count % SPREAD), (0, 0)))

    def along(values, axis, count):
        return [values] + [swap(values, axis, k) for k in range(1, count)]

    framed = lax.dynamic_update_slice(
        jnp.zeros((in_frame * width,), bf16), input_kernel.astype(bf16), (in_offset,)
    ).reshape(in_frame, width)
    near = jnp.concatenate([framed, shard_rows(block_kernels[:NEAR])], axis=0)
    near = jnp.stack(along(near, "lat", nl))

    row_global = (lax.axis_index("lat") * rows_here + jnp.arange(rows_here)).astype(f32)
    latitude = (row_global + 0.5) / (rows_here * nl) * jnp.pi - jnp.pi / 2
    pixel_weight = jnp.cos(latitude)[None, :, None] * land_mask.astype(f32)
    (packed,) = call(
        functools.partial(pack_kernel, in_width=in_width),
        [(fields, VECTOR), (targets.transpose(3, 0, 1, 2), VECTOR), (pixel_weight, VECTOR)],
        [((places, rows_here, cols_here, width), bf16, VECTOR)],
        [pltpu.VMEM((-(-3 * PIECES * rows_here // 16) * 16, cols_here), f32)],
    )
    packed, near = lax.optimization_barrier((packed, near))
    near = along(near, "lon", no)
    packed = spread_all(packed, TILE)
    near = [part for values in near for part in (values, swap(values, "batch", 1))]
    head_low = jnp.pad(head_weight.astype(bf16), ((0, 0), (0, width - head_weight.shape[1])))

    plane = (pixels, 2 * width)
    weight_shape = (9 * width, width)
    flat_weight = pltpu.VMEM(weight_shape, f32)
    wide_shape = ((pairs + 3) * cols, 14 * width)
    shift_shape = ((pairs + 1) * cols, 6 * width)
    shift_scratch = pltpu.VMEM(shift_shape, bf16)
    forward_taps, backward_taps = (2, 6 * width, 2 * width), (2, 2 * width, 6 * width)
    sums_shape = ((devices, 4, width), f32, VECTOR)
    stats_shape, pair_shape = (8, width), (2, width)
    low_plane, wide_plane = pltpu.VMEM(plane, bf16), pltpu.VMEM(plane, f32)
    weight_scratch, stats_scratch = pltpu.VMEM(weight_shape, bf16), pltpu.VMEM(stats_shape, f32)
    pair_scratch = pltpu.VMEM(pair_shape, f32)
    unit_cost = 2 * 2 * pixels * 9 * width * width

    def kept_outs(*kinds):
        return [(shape, dtype, WIDE) for shape, dtype in kinds]

    out = call(
        functools.partial(
            first_kernel, tiles=tiles, sizes=sizes, shards=[in_shard, block_rows], in_width=in_width, count=NEAR
        ),
        [(part, WIDE) for part in near] + [(packed, WIDE)],
        kept_outs(*[(weight_shape, bf16)] * NEAR, (plane, bf16), (plane, f32), (plane, bf16), (wide_shape, bf16))
        + [(plane, bf16, VECTOR), (plane, bf16, VECTOR), sums_shape, (weight_shape, bf16, VECTOR)],
        [flat_weight] * NEAR
        + [pltpu.VMEM((len(near), *near[0].shape), bf16), pltpu.VMEM(packed.shape, bf16)]
        + [pltpu.VMEM((NEAR, *weight_shape), bf16)]
        + [pltpu.VMEM((-(-NEAR * block_rows // SPREAD) * SPREAD, width), f32)]
        + [pltpu.VMEM((4, 14 * width, 2 * width), bf16), pltpu.VMEM((flat_rows, width), f32)]
        + [pltpu.VMEM(wide_shape, bf16), low_plane, wide_plane, low_plane]
        + [shift_scratch, pltpu.VMEM(forward_taps, bf16)],
        flags,
        6 * unit_cost,
        LARGE_ROOM,
    )
    weights, out = list(out[:NEAR]), out[NEAR:]
    in_slope, stream, source, wide, fired, slope, sums, weight = out
    far = shard_rows(block_kernels[NEAR:])
    far, sums = lax.optimization_barrier((far, sums))
    parts = spread_all(sums, ALL)
    far = along(jnp.stack(along(far, "lat", nl)), "lon", no)
    far = [part for values in far for part in (values, swap(values, "batch", 1))]
    far_count = conv_count - NEAR
    weights += call(
        functools.partial(far_kernels_kernel, tiles=tiles, block_rows=block_rows, count=far_count),
        [(part, VECTOR) for part in far],
        [(weight_shape, bf16, WIDE)] * far_count,
        [pltpu.VMEM((-(-far_count * block_rows // SPREAD) * SPREAD, width), f32)]
        + [flat_weight] * far_count
        + [pltpu.VMEM((far_count, *weight_shape), bf16)],
        flags,
        unit_cost,
    )

    sources, fireds, slopes, stats = [source], [], [], []
    fetched = []
    for k in range(1, conv_count):
        residual = k % 2 == 0
        fetches = [weights[k + 1]] if k + 1 < conv_count else []
        if not residual:
            fetches.append(stream)
        if k + 1 == conv_count:
            fetches += [packed, stats[0]]
        out = call(
            functools.partial(
                unit_kernel, sizes=sizes, pixel_count=pixel_count, index=k - 1, residual=residual,
                fetches=len(fetches),
            ),
            [(array, VECTOR) for array in (fired, parts, norm_params, weight, slope, *fetched)]
            + [(array, WIDE) for array in fetches],
            kept_outs(*[(plane, f32)] * residual, (plane, bf16), (stats_shape, f32), (plane, bf16), (plane, bf16))
            + [(plane, bf16, VECTOR), (plane, bf16, VECTOR), sums_shape]
            + [(array.shape, array.dtype, VECTOR) for array in fetches],
            [wide_plane] * residual
            + [low_plane, stats_scratch, shift_scratch, pltpu.VMEM(forward_taps, bf16)],
            flags,
            unit_cost,
        )
        if residual:
            stream, *out = out
        source, stat, saved_fired, saved_slope, fired, slope, sums, *fetched = out
        sources.append(source)
        stats.append(stat)
        fireds.append(saved_fired)
        slopes.append(saved_slope)
        if k + 1 < conv_count:
            weight, *fetched = fetched
        parts = spread_all(sums, ALL)

    grad, sums, stat = call(
        functools.partial(
            head_kernel, tiles=tiles, sizes=sizes, pixel_count=pixel_count, sample_count=sample_count,
            in_width=in_width, index=conv_count - 1,
        ),
        [(array, VECTOR) for array in (fired, parts, norm_params, head_low, *fetched)],
        [(plane, f32, VECTOR), ((devices, 8, width), f32, VECTOR), (stats_shape, f32, VECTOR)],
        (),
        flags,
        unit_cost // 4,
    )
    head_parts = parts = spread_all(sums, ALL)

    pair_grads, frames = [None] * conv_count, [None] * conv_count
    for k in range(conv_count - 1, 0, -1):
        second = k % 2 == 1
        pre, pair_grads[k], *out = call(
            functools.partial(back_kernel, sizes=sizes, pixel_count=pixel_count, index=k, second=second),
            [(array, VECTOR) for array in (parts, norm_params, grad, fired, slope, stat)]
            + [(array, WIDE) for array in (fireds[k - 1], slopes[k - 1], stats[k - 1], weights[k])]
            + [(array, WIDE) for array in (() if second else (kept_grad,))],
            kept_outs((plane, bf16), (pair_shape, f32), *[(plane, f32)] * second)
            + [(plane, bf16 if second else f32, VECTOR), sums_shape]
            + [(plane, bf16, VECTOR), (plane, bf16, VECTOR), (stats_shape, f32, VECTOR)],
            [wide_plane] * (not second)
            + [weight_scratch, low_plane, pair_scratch, shift_scratch, pltpu.VMEM(backward_taps, bf16)],
            flags,
            unit_cost,
        )
        if second:
            kept_grad, *out = out
        grad, sums, fired, slope, stat = out
        parts = spread_all(sums, ALL)
        frames[k] = call(
            functools.partial(kernel_grad_kernel, tiles=tiles, sizes=sizes, shard=block_shard),
            [(sources[k], WIDE), (pre, WIDE)],
            [((no, nl, block_frame, width), bf16, VECTOR)] * 2,
            [low_plane, low_plane, shift_scratch, flat_weight],
            flags,
            unit_cost,
        )
    pair_grads[0], *out = call(
        functools.partial(
            last_kernel, tiles=tiles, sizes=sizes, shards=[in_shard, block_shard], in_width=in_width,
            pixel_count=pixel_count,
        ),
        [(array, VECTOR) for array in (parts, norm_params, grad, fired, slope, stat)]
        + [(array, WIDE) for array in (weights[0], kept_grad, in_slope, sources[0], wide)],
        kept_outs((pair_shape, f32))
        + [((no, nl, in_frame, width), bf16, VECTOR)] * 2
        + [((no, nl, block_frame, width), bf16, VECTOR)] * 2,
        [weight_scratch, wide_plane, low_plane, low_plane, pltpu.VMEM(wide_shape, bf16), low_plane, low_plane]
        + [pair_scratch, shift_scratch, pltpu.VMEM(backward_taps, bf16)]
        + [pltpu.VMEM((flat_rows, width), f32), flat_weight],
        flags,
        6 * unit_cost,
        LARGE_ROOM,
    )
    in_frames, frames[0] = out[:2], out[2:]
    early = summed_frames(frames[LATE:])
    late = summed_frames([in_frames] + frames[:LATE])

    def own_shard(rows, offset, shard):
        return lax.dynamic_slice(rows.reshape(-1), (offset,), (shard,))

    input_grad = own_shard(late[:in_frame], in_offset, in_shard)
    rows = jnp.concatenate([late[in_frame:], early], axis=0).reshape(conv_count, -1)
    block_grad = lax.dynamic_slice(rows, (0, block_offset), (conv_count, block_shard))
    head_total = jnp.sum(head_parts, axis=0)
    head_grad = head_total[2:4].T
    loss_sum = head_total[4, 0]
    loss_weight = stats[0][2, 0] / sample_count
    norm_grad = jnp.stack(pair_grads)
    return finished(
        loss_sum, loss_weight, input_grad, block_grad, head_grad, norm_grad,
        (input_kernel, input_first, input_second), (block_kernels, block_first, block_second),
        (head_weight, head_first, head_second), (norm_params, norm_first, norm_second),
    )


def one_device_takes_a_sample(fields, block_kernels, head_weight, norm_params):
    samples_here, rows_here, cols_here, in_width = fields.shape
    nl, no, nb = (lax.axis_size(axis) for axis in ALL)
    rows, cols, width = rows_here * nl, cols_here * no, norm_params.shape[2]
    return (
        samples_here <= nl * no
        and nb == 2
        and nl & (nl - 1) == 0
        and no & (no - 1) == 0
        and rows * cols <= MOST_PIXELS
        and rows % (2 * GROUP) == 0
        and cols % 128 == 0
        and cols_here % 8 == 0
        and width == 128
        and head_weight.shape[1] == 2
        and in_width + 3 * PIECES <= width
        and block_kernels.shape[1] % width == 0
        and block_kernels.shape[0] > max(NEAR, LATE)
    )


def body(*args):
    fields, block_kernels, head_weight, norm_params = args[0], args[6], args[9], args[12]
    if one_device_takes_a_sample(fields, block_kernels, head_weight, norm_params):
        return whole_sample_body(*args)
    return tile_body(*args)


def solution(mesh):
    in_specs = (
        P("batch", "lat", "lon", None),
        P("batch", "lat", "lon", None),
        P("batch", "lat", "lon"),
        P(("lat", "lon", "batch")),
        P(("lat", "lon", "batch")),
        P(("lat", "lon", "batch")),
        P(None, ("lat", "lon", "batch")),
        P(None, ("lat", "lon", "batch")),
        P(None, ("lat", "lon", "batch")),
        P(),
        P(),
        P(),
        P(),
        P(),
        P(),
    )
    out_specs = (
        P(),
        P(),
        P(("lat", "lon", "batch")),
        P(("lat", "lon", "batch")),
        P(("lat", "lon", "batch")),
        P(None, ("lat", "lon", "batch")),
        P(None, ("lat", "lon", "batch")),
        P(None, ("lat", "lon", "batch")),
        P(),
        P(),
        P(),
        P(),
        P(),
        P(),
    )
    return jax.shard_map(body, mesh=mesh, in_specs=in_specs, out_specs=out_specs, check_vma=False)
```

```python
import functools

import jax
import jax.numpy as jnp
from jax import lax
from jax.experimental import pallas as pl
from jax.experimental.pallas import tpu as pltpu
from jax.sharding import PartitionSpec as P

STEP = 10


NORM_EPSILON = 1e-05
GELU_SCALE = 0.7978845608028654
GELU_CUBE = 0.044715
GROUP = 4
SMALL_ROOM = 14 << 20
LARGE_ROOM = 36 << 20
COPIES = 32
FORWARD, BACKWARD = 1, 2
NEAR = 1
MOST_PIXELS = 4096


def shortened(shard):

    def short(part):
        return part.astype(jnp.bfloat16) if part.dtype == jnp.float32 else part

    return jax.tree.map(short, shard)


def with_halo(cells, sides, width):
    for axis, dim in sides:
        count = lax.axis_size(axis)
        ends = count - 1
        head = lax.slice_in_dim(cells, 0, width, axis=dim)
        tail = lax.slice_in_dim(cells, cells.shape[dim] - width, cells.shape[dim], axis=dim)
        cells = jnp.concatenate(
            [
                lax.ppermute(tail, axis, [(i, (i + 1) % count) for i in range(ends)]),
                cells,
                lax.ppermute(head, axis, [((i + 1) % count, i) for i in range(ends)]),
            ],
            axis=dim,
        )
    return cells


def conv_valid(padded, kernel):
    return lax.conv_general_dilated(
        padded,
        kernel,
        (1, 1),
        "VALID",
        dimension_numbers=("NHWC", "HWIO", "NHWC"),
        preferred_element_type=jnp.float32,
    )


def kernel_grad(padded, gradient):
    summed = lax.conv_general_dilated(
        padded,
        gradient,
        (1, 1),
        "VALID",
        dimension_numbers=("CHWN", "IHWO", "NHWC"),
        preferred_element_type=jnp.float32,
    )
    return summed.transpose(1, 2, 0, 3)


def rim_cells(values):
    return with_halo(shortened(values), (("lat", 1), ("lon", 2)), 1).astype(values.dtype)


def to_channels(values):
    return jax.tree.map(
        lambda part, own: part.astype(own.dtype),
        lax.all_to_all(shortened(values), "lat", split_axis=3, concat_axis=0, tiled=True),
        values,
    )


def to_pixels(values):
    return lax.all_to_all(values, "lat", split_axis=0, concat_axis=3, tiled=True)


def spread_sums(summed, squares):
    return lax.psum((summed, squares), ("lon", "batch"))


def own_channels(norm_pair, width):
    return lax.dynamic_slice_in_dim(norm_pair, lax.axis_index("lat") * width, width, 1)


def norm_forward(fired, norm_pair, pixel_count):
    values = to_channels(fired)
    norm_pair = own_channels(norm_pair, values.shape[3])
    widened = values.astype(jnp.float32)
    summed, squares = spread_sums(
        jnp.sum(widened, axis=(0, 1, 2)), jnp.sum(widened * widened, axis=(0, 1, 2))
    )
    average = summed / pixel_count
    inverse_std = lax.rsqrt(squares / pixel_count - average * average + NORM_EPSILON)
    centred = (widened - average) * inverse_std
    normed = (norm_pair[0] * centred + norm_pair[1]).astype(jnp.bfloat16)
    normed = to_pixels(normed)
    return (normed, (centred, inverse_std, norm_pair))


def norm_backward(gradient, kept, pixel_count):
    centred, inverse_std, norm_pair = kept
    gradient = to_channels(gradient)
    widened = gradient.astype(jnp.float32)
    shift_grad, gain_grad = spread_sums(
        jnp.sum(widened, axis=(0, 1, 2)), jnp.sum(widened * centred, axis=(0, 1, 2))
    )
    scaled = norm_pair[0] * inverse_std
    fired_grad = (
        scaled * (widened - shift_grad / pixel_count - centred * gain_grad / pixel_count)
    ).astype(jnp.bfloat16)
    fired_grad = to_pixels(fired_grad)
    return (fired_grad, jnp.stack([gain_grad, shift_grad]))


def gelu_pullback(preact, gradient):
    unused, pullback = jax.vjp(jax.nn.gelu, preact)
    return pullback(gradient)[0]


def conv_forward(source, kernel, norm_pair, pixel_count):
    padded = rim_cells(source)
    preact = conv_valid(padded, kernel)
    fired = jax.nn.gelu(preact).astype(jnp.bfloat16)
    normed, kept = norm_forward(fired, norm_pair, pixel_count)
    return (normed, (padded, preact, kept))


def conv_backward(gradient, kernel, record, pixel_count):
    padded, preact, kept = record
    fired_grad, pair_grad = norm_backward(gradient, kept, pixel_count)
    preact_grad = gelu_pullback(preact, fired_grad.astype(jnp.float32)).astype(jnp.bfloat16)
    kernel_gradient = kernel_grad(padded, preact_grad)
    flipped = kernel[::-1, ::-1].transpose(0, 1, 3, 2)
    source_grad = conv_valid(rim_cells(preact_grad), flipped)
    return (source_grad, kernel_gradient, pair_grad)


def block_forward(stream, kernels, norm_pairs, pixel_count):
    middle, first_record = conv_forward(
        stream.astype(jnp.bfloat16), kernels[0], norm_pairs[0], pixel_count
    )
    branch, second_record = conv_forward(middle, kernels[1], norm_pairs[1], pixel_count)
    return (stream + branch.astype(jnp.float32), (first_record, second_record))


def block_backward(stream_grad, stream, kernels, norm_pairs, pixel_count):
    unused, records = block_forward(stream, kernels, norm_pairs, pixel_count)
    middle_grad, second_kernel, second_pair = conv_backward(
        stream_grad.astype(jnp.bfloat16), kernels[1], records[1], pixel_count
    )
    source_grad, first_kernel, first_pair = conv_backward(
        middle_grad.astype(jnp.bfloat16), kernels[0], records[0], pixel_count
    )
    return (stream_grad + source_grad, (first_kernel, second_kernel), (first_pair, second_pair))


def adamw_update(weight, gradient, momentum, variance, step_rate):
    momentum = 0.9 * momentum + 0.1 * gradient
    variance = 0.999 * variance + 0.001 * gradient * gradient
    corrected = momentum / (1.0 - 0.9**STEP)
    scaled = jnp.sqrt(variance / (1.0 - 0.999**STEP)) + 1e-08
    return (momentum, variance, weight - step_rate * (corrected / scaled + 0.01 * weight))


def finished(
    loss_sum, loss_weight, input_grad, block_grad, head_grad, norm_grad,
    input_state, block_state, head_state, norm_state,
):
    outputs = [jnp.reshape(loss_sum, (1,)), jnp.reshape(loss_weight, (1,))]
    for state, gradient, step_rate in (
        (input_state, input_grad, 0.015),
        (block_state, block_grad, 0.03),
        (head_state, head_grad, 0.15),
        (norm_state, norm_grad, 0.8),
    ):
        weight, first, second = state
        outputs.extend(adamw_update(weight, gradient, first, second, step_rate))
    return tuple(outputs)


def tile_body(
    fields,
    targets,
    land_mask,
    input_kernel,
    input_first,
    input_second,
    block_kernels,
    block_first,
    block_second,
    head_weight,
    head_first,
    head_second,
    norm_params,
    norm_first,
    norm_second,
):
    samples_here, rows_here, cols_here, in_width = fields.shape
    channels = norm_params.shape[2]
    conv_count = block_kernels.shape[0]
    full_input, full_blocks = (
        lax.all_gather(
            input_kernel.astype(jnp.bfloat16), ("lat", "lon", "batch"), axis=0, tiled=True
        ),
        lax.all_gather(
            block_kernels.astype(jnp.bfloat16), ("lat", "lon", "batch"), axis=1, tiled=True
        ),
    )
    kernel_in = full_input.reshape(7, 7, in_width, channels)
    kernels = full_blocks.reshape(conv_count, 3, 3, channels, channels)
    head_low = head_weight.astype(jnp.bfloat16)
    sample_count = samples_here * lax.axis_size("batch")
    pixel_count = float(
        sample_count * rows_here * lax.axis_size("lat") * cols_here * lax.axis_size("lon")
    )
    row_global = (lax.axis_index("lat") * rows_here + jnp.arange(rows_here)).astype(jnp.float32)
    latitude = (row_global + 0.5) / (rows_here * lax.axis_size("lat")) * jnp.pi - jnp.pi / 2
    pixel_weight = jnp.cos(latitude)[None, :, None] * land_mask.astype(jnp.float32)
    valid_sum = lax.psum(jnp.sum(pixel_weight), ("lat", "lon", "batch"))
    loss_weight = valid_sum / sample_count
    padded_in = with_halo(fields, (("lat", 1), ("lon", 2)), 3)
    preact_in = conv_valid(padded_in, kernel_in)
    streams = [jax.nn.gelu(preact_in)]
    for layer in range(conv_count // 2):
        advanced, unused = block_forward(
            streams[-1],
            kernels[2 * layer : 2 * layer + 2],
            norm_params[2 * layer : 2 * layer + 2],
            pixel_count,
        )
        streams.append(advanced)
    top_stream = streams[-1].astype(jnp.bfloat16)
    predicted = jnp.einsum(
        "nhwc,co->nhwo", top_stream, head_low, preferred_element_type=jnp.float32
    )
    misfit = predicted - targets
    loss_local = jnp.sum(pixel_weight[..., None] * misfit * misfit)
    pred_grad = (2.0 * pixel_weight[..., None] * misfit / loss_weight).astype(jnp.bfloat16)
    head_local = jnp.einsum(
        "nhwc,nhwo->co", top_stream, pred_grad, preferred_element_type=jnp.float32
    )
    stream_grad = jnp.einsum(
        "nhwo,co->nhwc", pred_grad, head_low, preferred_element_type=jnp.float32
    )
    kernel_grads = [None] * conv_count
    pair_grads = [None] * conv_count
    for layer in reversed(range(conv_count // 2)):
        stream_grad, kernel_pair, norm_pair = block_backward(
            stream_grad,
            streams[layer],
            kernels[2 * layer : 2 * layer + 2],
            norm_params[2 * layer : 2 * layer + 2],
            pixel_count,
        )
        kernel_grads[2 * layer], kernel_grads[2 * layer + 1] = kernel_pair
        pair_grads[2 * layer], pair_grads[2 * layer + 1] = norm_pair
    pre_in_grad = gelu_pullback(preact_in, stream_grad).astype(jnp.bfloat16)
    input_local = kernel_grad(padded_in, pre_in_grad).reshape(-1)
    block_local = jnp.stack(kernel_grads).reshape(conv_count, -1)
    input_grad, block_grad = (
        lax.psum_scatter(input_local, ("lat", "lon", "batch"), scatter_dimension=0, tiled=True),
        lax.psum_scatter(block_local, ("lat", "lon", "batch"), scatter_dimension=1, tiled=True),
    )
    head_grad, loss_sum = lax.psum((head_local, loss_local), ("lat", "lon", "batch"))
    norm_grad = jnp.stack(pair_grads)
    norm_grad = lax.all_gather(norm_grad, "lat", axis=2, tiled=True)
    return finished(
        loss_sum, loss_weight, input_grad, block_grad, head_grad, norm_grad,
        (input_kernel, input_first, input_second), (block_kernels, block_first, block_second),
        (head_weight, head_first, head_second), (norm_params, norm_first, norm_second),
    )


ALL = ("lat", "lon", "batch")
TILE = ("lat", "lon")
PIECES = 3
SPREAD = 16


VECTOR, WIDE = "vector", "wide"
SPACES = {VECTOR: pltpu.VMEM, WIDE: pltpu.HBM}


def call(kernel, ins, outs, scratch=(), flags=None, cost=0, room=SMALL_ROOM, aliases=()):
    specs = [pl.BlockSpec(memory_space=SPACES[space]) for unused, space in ins]
    args = [
        pltpu.with_memory_space_constraint(array, pltpu.HBM) if space == WIDE else array
        for array, space in ins
    ]
    if flags is not None:
        specs, args = [pl.BlockSpec(memory_space=pltpu.SMEM)] + specs, [flags] + args
    return pl.pallas_call(
        kernel,
        out_shape=[
            pltpu.HBM(shape, dtype) if space == WIDE else jax.ShapeDtypeStruct(shape, dtype)
            for shape, dtype, space in outs
        ],
        in_specs=specs,
        out_specs=[pl.BlockSpec(memory_space=SPACES[space]) for *unused, space in outs],
        scratch_shapes=list(scratch) + [pltpu.SemaphoreType.DMA((COPIES,))],
        input_output_aliases=dict(aliases),
        compiler_params=pltpu.CompilerParams(vmem_limit_bytes=room),
        cost_estimate=pl.CostEstimate(flops=cost, bytes_accessed=4 << 20, transcendentals=0),
    )(*args)


class Mover:
    def __init__(self, semaphores):
        self.semaphores, self.used, self.sent = semaphores, 0, []

    def start(self, source, target):
        copy = pltpu.make_async_copy(source, target, self.semaphores.at[self.used])
        self.used += 1
        copy.start()
        return copy

    def fetch(self, source, target, parts=1):
        step = target.shape[0] // parts
        return [
            self.start(source.at[pl.ds(i * step, step)], target.at[pl.ds(i * step, step)])
            for i in range(parts)
        ]

    def send(self, source, target):
        self.sent.append(self.start(source, target))

    def finish(self):
        for copy in self.sent:
            copy.wait()


def dot(left, right, dims=((1,), (0,))):
    return lax.dot_general(left, right, (dims, ((), ())), preferred_element_type=jnp.float32)


def gelu_value(x):
    return x * (0.5 * (1.0 + jnp.tanh(GELU_SCALE * (x + GELU_CUBE * (x * x * x)))))


def gelu_both(x):
    square = x * x
    level = jnp.tanh(GELU_SCALE * (x + GELU_CUBE * (x * square)))
    half = 0.5 * (1.0 + level)
    slope = half + 0.5 * x * (1.0 - level * level) * (GELU_SCALE * (1.0 + 3.0 * GELU_CUBE * square))
    return x * half, slope


def shifted(cells, step):
    count = cells.shape[0]
    if step == 0:
        return cells
    column = lax.broadcasted_iota(jnp.int32, cells.shape, 0) + step
    rolled = pltpu.roll(cells, (-step) % count, 0)
    return jnp.where((column >= 0) & (column < count), rolled, 0.0)


def spread_pair(pair, cells, shifts_ref, sizes):
    cols, width, pairs = sizes
    for b in range(3):
        moved = shifted(cells, b - 1).astype(jnp.bfloat16)
        shifts_ref[(pair + 1) * cols : (pair + 2) * cols, b * width : (b + 1) * width] = moved[:, width:]
        shifts_ref[pair * cols : (pair + 1) * cols, (3 + b) * width : (4 + b) * width] = moved[:, :width]


def clear_rim(shifts_ref, sizes):
    cols, width, pairs = sizes
    zero = jnp.zeros((cols, 3 * width), jnp.bfloat16)
    shifts_ref[0:cols, 0 : 3 * width] = zero
    shifts_ref[pairs * cols : (pairs + 1) * cols, 3 * width : 6 * width] = zero


def taps_forward(weight_ref, taps_ref, width):
    for k in range(2):
        for rr in range(2):
            for b in range(3):
                for q in range(2):
                    a = 2 * k + rr - q
                    at = (rr * 3 + b) * width
                    if 0 <= a <= 2:
                        block = weight_ref[(a * 3 + b) * width : (a * 3 + b + 1) * width, :]
                    else:
                        block = jnp.zeros((width, width), jnp.bfloat16)
                    taps_ref[k, at : at + width, q * width : (q + 1) * width] = block


def taps_backward(weight_ref, taps_ref, width):
    for k in range(2):
        for rr in range(2):
            for b in range(3):
                for q in range(2):
                    a = 2 - (2 * k + rr - q)
                    at = (rr * 3 + b) * width
                    if 0 <= a <= 2:
                        tap = a * 3 + 2 - b
                        block = weight_ref[tap * width : (tap + 1) * width, :]
                    else:
                        block = jnp.zeros((width, width), jnp.bfloat16)
                    taps_ref[k, q * width : (q + 1) * width, at : at + width] = block


def pair_conv(shifts_ref, taps_ref, group, cols, dims=((1,), (0,))):
    rows = GROUP * cols
    first = shifts_ref[group * rows : (group + 1) * rows, :]
    second = shifts_ref[group * rows + cols : (group + 1) * rows + cols, :]
    return dot(first, taps_ref[0], dims) + dot(second, taps_ref[1], dims)


def folded(sums, width):
    return sums[:, :width] + sums[:, width:]


def total_of(parts_ref):
    return jnp.sum(parts_ref[...], axis=0)


def twice(row):
    return jnp.concatenate([row, row], axis=1)


def norm_of(total, pixel_count):
    average = total[0:1] / pixel_count
    return average, lax.rsqrt(total[1:2] / pixel_count - average * average + NORM_EPSILON)


def conv_and_sums(flags_ref, shifts_ref, taps_ref, fired_ref, slope_ref, sums_ref, sizes, more=None):
    cols, width, pairs = sizes
    total = jnp.zeros((1, 2 * width), jnp.float32)
    squares = jnp.zeros((1, 2 * width), jnp.float32)
    step = GROUP * cols
    for group in range(pairs // GROUP):
        fired, slope = gelu_both(pair_conv(shifts_ref, taps_ref, group, cols))
        rows = pl.ds(group * step, step)
        fired = fired.astype(jnp.bfloat16)
        fired_ref[rows, :] = fired
        slope_ref[rows, :] = slope.astype(jnp.bfloat16)
        wide = fired.astype(jnp.float32)
        total = total + jnp.sum(wide, axis=0, keepdims=True)
        squares = squares + jnp.sum(wide * wide, axis=0, keepdims=True)
    active = flags_ref[0].astype(jnp.float32)
    parts = [folded(total, width) * active, folded(squares, width) * active]
    put_sums(sums_ref, parts + (more or []))


def put_sums(sums_ref, parts):
    shape = sums_ref.shape[1:]
    row = lax.broadcasted_iota(jnp.int32, shape, 0)
    block = jnp.zeros(shape, jnp.float32)
    at = 0
    for part in parts:
        for i in range(part.shape[0]):
            block = jnp.where(row == at, jnp.broadcast_to(part[i : i + 1], shape), block)
            at += 1
    sums_ref[...] = jnp.broadcast_to(block[None], sums_ref.shape)


def field_row(fields_ref, row, tiles):
    nl, no, rows_here, cols_here = tiles
    lat, inner = row // rows_here, row % rows_here
    return jnp.concatenate([fields_ref[lat * no + lon, inner] for lon in range(no)], axis=0)


def wide_shifts(row_of, shifts_ref, sizes, done=None):
    cols, width, pairs = sizes
    rows = 2 * pairs
    for row in range(-3, rows + 3):
        at, rr = (row + 3) // 2, (row + 3) % 2
        if 0 <= row < rows:
            cells = row_of(row).astype(jnp.float32)
        for b in range(7):
            if 0 <= row < rows:
                moved = shifted(cells, b - 3).astype(jnp.bfloat16)
            else:
                moved = jnp.zeros((cols, width), jnp.bfloat16)
            spot = (rr * 7 + b) * width
            shifts_ref[at * cols : (at + 1) * cols, spot : spot + width] = moved
        if rr == 1 and done is not None:
            done(pl.ds(at * cols, cols))


def first_row(device, shard, width):
    return lax.div(device * shard, width)


def frame_rows(shard, devices, width, grain):
    rows = max(-(-(d + 1) * shard // width) - d * shard // width for d in range(devices))
    return -(-rows // grain) * grain


def device_at(flags_ref, lon_step, lat_step, core_step, tiles):
    lat = flags_ref[2] ^ lat_step
    lon = flags_ref[3] ^ lon_step
    return (lat * tiles[1] + lon) * 2 + (flags_ref[1] ^ core_step)


def pack_kernel(fields_ref, targets_ref, weights_ref, packed_ref, pieces_ref, unused_ref, *, in_width):
    samples, rows, cols, unused = fields_ref.shape
    width = packed_ref.shape[3]
    outs = targets_ref.shape[0]
    many = pieces_ref.shape[0]
    pieces_ref[...] = jnp.zeros(pieces_ref.shape, jnp.float32)
    packed_ref[samples:] = jnp.zeros((packed_ref.shape[0] - samples, rows, cols, width), jnp.bfloat16)
    take_from = lax.broadcasted_iota(jnp.int32, (many, width), 0)
    put_to = lax.broadcasted_iota(jnp.int32, (many, width), 1) - in_width
    picks = [
        jnp.where((put_to >= 0) & (take_from == put_to * rows + row), 1.0, 0.0).astype(jnp.bfloat16)
        for row in range(rows)
    ]
    for sample in range(samples):
        for source in range(outs + 1):
            left = targets_ref[source, sample] if source < outs else weights_ref[sample]
            for piece in range(PIECES):
                low = left.astype(jnp.bfloat16).astype(jnp.float32)
                left = left - low
                at = (source * PIECES + piece) * rows
                pieces_ref[at : at + rows, :] = low
        pieces = pieces_ref[...].astype(jnp.bfloat16)
        for row in range(rows):
            placed = dot(pieces, picks[row], ((0,), (0,))).astype(jnp.bfloat16)
            packed_ref[sample, row] = placed
            packed_ref[sample, row, :, 0:in_width] = fields_ref[sample, row]


def place_blocks(part, at, count, rows, device, stage_ref, flat_refs):
    stage_ref[...] = part[at : at + stage_ref.shape[0], :].astype(jnp.float32)
    for index in range(count):
        flat_refs[index][pl.ds(device * rows, rows), :] = stage_ref[index * rows : (index + 1) * rows, :]


def near_kernels(
    flags_ref, parts, taps_ref, flat_ref, stage_ref, flat_block_refs, tiles, shards, in_width
):
    nl, no = tiles[0], tiles[1]
    width = flat_ref.shape[1]
    in_shard, block_rows = shards
    rows = frame_rows(in_shard, 2 * nl * no, width, SPREAD)
    flat_ref[...] = jnp.zeros(flat_ref.shape, jnp.float32)
    for lon_step in range(no):
        for core_step in range(2):
            part = parts[lon_step * 2 + core_step]
            for lat_step in range(nl):
                device = device_at(flags_ref, lon_step, lat_step, core_step, tiles)
                spot = pl.ds(first_row(device, in_shard, width), rows)
                flat_ref[spot, :] += part[lat_step, 0:rows, :].astype(jnp.float32)
                place_blocks(
                    part.at[lat_step], rows, len(flat_block_refs), block_rows, device, stage_ref, flat_block_refs
                )
    inside = lax.broadcasted_iota(jnp.int32, (width, width), 0) < in_width
    zero = jnp.zeros((width, width), jnp.bfloat16)
    for b in range(7):
        taps_ref[3, (7 + b) * width : (8 + b) * width, 0:width] = zero
        taps_ref[0, b * width : (b + 1) * width, width : 2 * width] = zero
        for a in range(7):
            tap = a * 7 + b
            block = flat_ref[tap * in_width : tap * in_width + width, :]
            block = jnp.where(inside, block, 0.0).astype(jnp.bfloat16)
            for q in range(2):
                k, rr = (a + q) // 2, (a + q) % 2
                spot = (rr * 7 + b) * width
                taps_ref[k, spot : spot + width, q * width : (q + 1) * width] = block


def far_kernels_kernel(flags_ref, *refs, tiles, block_rows, count):
    nl, no = tiles[0], tiles[1]
    parts, outs, next_ref, refs = refs[: 2 * no], refs[2 * no : 2 * no + count], refs[2 * no + count], refs[2 * no + count + 1 :]
    near_ref, stage_ref, *flat_refs, whole_ref, semaphores = refs
    mover = Mover(semaphores)
    arrivals = [mover.start(part, near_ref.at[i]) for i, part in enumerate(parts)]
    for lon_step in range(no):
        for core_step in range(2):
            at = lon_step * 2 + core_step
            arrivals[at].wait()
            for lat_step in range(nl):
                device = device_at(flags_ref, lon_step, lat_step, core_step, tiles)
                place_blocks(near_ref.at[at, lat_step], 0, count, block_rows, device, stage_ref, flat_refs)
    for index in range(count):
        weight = flat_refs[index][0 : whole_ref.shape[1], :].astype(jnp.bfloat16)
        whole_ref[index] = weight
        if index == 0:
            next_ref[...] = weight
        mover.send(whole_ref.at[index], outs[index])
    mover.finish()


def wide_kernel(flags_ref, fields_in, wide_out, fields_ref, wide_ref, semaphores, *, sizes):
    cols, width, pairs = sizes
    mover = Mover(semaphores)
    mover.fetch(fields_in, fields_ref)[0].wait()

    def row_of(row):
        pair, q = row // 2, row % 2
        return fields_ref[pair * cols : (pair + 1) * cols, q * width : (q + 1) * width]

    def done(rows):
        mover.send(wide_ref.at[rows], wide_out.at[rows])

    wide_shifts(row_of, wide_ref, sizes, done)
    mover.finish()


def first_kernel(flags_ref, *refs, tiles, sizes, shards, in_width, count):
    cols, width, pairs = sizes
    nl, no = tiles[0], tiles[1]
    near, refs = refs[: 2 * no], refs[2 * no :]
    fields_ref, *refs = refs
    weight_outs, refs = refs[:count], refs[count:]
    pairs_out, slope_in_out, stream_out, source_out, fired_ref, slope_ref, sums_ref, *refs = refs
    flat_block_refs, refs = refs[:count], refs[count:]
    (
        pairs_ref, weights_ref, stage_ref, in_taps_ref, flat_ref, wide_ref,
        slope_in_ref, stream_ref, source_ref, shifts_ref, taps_ref, semaphores,
    ) = refs
    mover = Mover(semaphores)
    clear_rim(shifts_ref, sizes)

    def row_of(row):
        cells = field_row(fields_ref, row, tiles)
        pair, q = row // 2, row % 2
        pairs_ref[pair * cols : (pair + 1) * cols, q * width : (q + 1) * width] = cells
        return cells

    wide_shifts(row_of, wide_ref, sizes)
    mover.send(pairs_ref, pairs_out)
    near_kernels(
        flags_ref, near, in_taps_ref, flat_ref, stage_ref, flat_block_refs, tiles, shards, in_width
    )
    for index in range(count):
        weight = flat_block_refs[index][0 : weights_ref.shape[1], :].astype(jnp.bfloat16)
        weights_ref[index] = weight
        mover.send(weights_ref.at[index], weight_outs[index])
    taps_forward(weights_ref.at[0], taps_ref, width)
    step = GROUP * cols
    for group in range(pairs // GROUP):
        at = group * step
        preact = dot(wide_ref[at : at + step, :], in_taps_ref[0])
        for k in range(1, 4):
            preact += dot(wide_ref[at + k * cols : at + step + k * cols, :], in_taps_ref[k])
        rows = pl.ds(at, step)
        stream, slope = gelu_both(preact)
        slope_in_ref[rows, :] = slope.astype(jnp.bfloat16)
        mover.send(slope_in_ref.at[rows], slope_in_out.at[rows])
        stream_ref[rows, :] = stream
        mover.send(stream_ref.at[rows], stream_out.at[rows])
        source = stream.astype(jnp.bfloat16)
        source_ref[rows, :] = source
        mover.send(source_ref.at[rows], source_out.at[rows])
        for pair in range(GROUP):
            cells = source[pair * cols : (pair + 1) * cols].astype(jnp.float32)
            spread_pair(group * GROUP + pair, cells, shifts_ref, sizes)
    weight_sum = folded(jnp.sum(pairs_ref[...].astype(jnp.float32), axis=0, keepdims=True), width)
    lane = lax.broadcasted_iota(jnp.int32, (1, width), 1) - in_width
    chosen = (lane >= 2 * PIECES) & (lane < 3 * PIECES)
    weight_sum = jnp.sum(jnp.where(chosen, weight_sum, 0.0), axis=1, keepdims=True)
    conv_and_sums(
        flags_ref, shifts_ref, taps_ref, fired_ref, slope_ref, sums_ref, sizes,
        [jnp.broadcast_to(weight_sum, (1, width))],
    )
    mover.finish()


def keep_norm(stats_ref, total, average, inverse_std):
    stats_ref[0:1, :] = average
    stats_ref[1:2, :] = inverse_std
    stats_ref[2:3, :] = total[2:3]


def unit_kernel(
    flags_ref, fired_in_ref, parts_ref, norms_ref, weight_ref, slope_in_ref, *refs,
    sizes, pixel_count, index, residual, fetches,
):
    cols, width, pairs = sizes
    if residual:
        stream_in_ref, *refs = refs
    fetched_from, refs = refs[:fetches], refs[fetches:]
    if residual:
        stream_out, *refs = refs
    source_out, stats_out, fired_out, slope_out, fired_ref, slope_ref, sums_ref, *refs = refs
    fetched_to, refs = refs[:fetches], refs[fetches:]
    if residual:
        stream_ref, *refs = refs
    source_ref, stats_ref, shifts_ref, taps_ref, semaphores = refs
    mover = Mover(semaphores)
    mover.send(fired_in_ref, fired_out)
    mover.send(slope_in_ref, slope_out)
    for source, target in zip(fetched_from, fetched_to):
        mover.send(source, target)
    total = total_of(parts_ref)
    average, inverse_std = norm_of(total, pixel_count)
    keep_norm(stats_ref, total, average, inverse_std)
    mover.send(stats_ref, stats_out)
    average, inverse_std = twice(average), twice(inverse_std)
    gain, shift = twice(norms_ref[index, 0:1]), twice(norms_ref[index, 1:2])
    taps_forward(weight_ref, taps_ref, width)
    clear_rim(shifts_ref, sizes)
    for pair in range(pairs):
        rows = pl.ds(pair * cols, cols)
        fired = fired_in_ref[rows, :].astype(jnp.float32)
        normed = (gain * ((fired - average) * inverse_std) + shift).astype(jnp.bfloat16)
        if residual:
            stream = stream_in_ref[rows, :] + normed.astype(jnp.float32)
            stream_ref[rows, :] = stream
            normed = stream.astype(jnp.bfloat16)
        source_ref[rows, :] = normed
        spread_pair(pair, normed.astype(jnp.float32), shifts_ref, sizes)
    mover.send(source_ref, source_out)
    if residual:
        mover.send(stream_ref, stream_out)
    conv_and_sums(flags_ref, shifts_ref, taps_ref, fired_ref, slope_ref, sums_ref, sizes)
    mover.finish()


def head_kernel(
    flags_ref, fired_ref, parts_ref, norms_ref, head_ref, stream_ref, fields_in, first_stats_in,
    grad_ref, sums_ref, stats_ref, fields_ref, first_stats_ref, top_ref, semaphores, *,
    sizes, pixel_count, sample_count, in_width, index,
):
    cols, width, pairs = sizes
    mover = Mover(semaphores)
    first_stats = mover.fetch(first_stats_in, first_stats_ref)
    fetched = mover.fetch(fields_in, fields_ref)
    total = total_of(parts_ref)
    average, inverse_std = norm_of(total, pixel_count)
    keep_norm(stats_ref, total, average, inverse_std)
    average, inverse_std = twice(average), twice(inverse_std)
    gain, shift = twice(norms_ref[index, 0:1]), twice(norms_ref[index, 1:2])
    head = head_ref[...]
    outs = 2
    lane_from = lax.broadcasted_iota(jnp.int32, (width, 2 * width), 0) - in_width
    lane_to = lax.broadcasted_iota(jnp.int32, (width, 2 * width), 1)
    within = lane_from - PIECES * lane_to
    picks = (within >= 0) & (within < PIECES) & (lane_to < outs)
    lane_to = lane_to - width
    weighs = (lane_from >= outs * PIECES) & (lane_from < (outs + 1) * PIECES)
    picks = picks | (weighs & (lane_to >= 0) & (lane_to < outs))
    picks = jnp.where(picks, 1.0, 0.0).astype(jnp.bfloat16)
    for pair in range(pairs):
        rows = pl.ds(pair * cols, cols)
        centred = (fired_ref[rows, :].astype(jnp.float32) - average) * inverse_std
        normed = (gain * centred + shift).astype(jnp.bfloat16)
        top_ref[rows, :] = (stream_ref[rows, :] + normed.astype(jnp.float32)).astype(jnp.bfloat16)
    first_stats[0].wait()
    loss_weight = first_stats_ref[2:3, :] / sample_count
    loss = jnp.zeros((1, width), jnp.float32)
    shift_grad = jnp.zeros((1, 2 * width), jnp.float32)
    gain_grad = jnp.zeros((1, 2 * width), jnp.float32)
    head_grad = jnp.zeros((width, width), jnp.float32)
    fetched[0].wait()
    step = GROUP * cols
    for group in range(pairs // GROUP):
        rows = pl.ds(group * step, step)
        for q in range(2):
            lanes = slice(q * width, (q + 1) * width)
            top = top_ref[rows, lanes]
            picked = dot(fields_ref[rows, lanes], picks)
            misfit, weight = dot(top, head) - picked[:, :width], picked[:, width:]
            loss += jnp.sum(weight * misfit * misfit, axis=0, keepdims=True)
            pred_grad = (2.0 * weight * misfit / loss_weight).astype(jnp.bfloat16)
            head_grad += dot(pred_grad, top, ((0,), (0,)))
            grad_ref[rows, lanes] = dot(pred_grad, head, ((1,), (1,)))
        low = grad_ref[rows, :].astype(jnp.bfloat16).astype(jnp.float32)
        centred = (fired_ref[rows, :].astype(jnp.float32) - average) * inverse_std
        shift_grad += jnp.sum(low, axis=0, keepdims=True)
        gain_grad += jnp.sum(low * centred, axis=0, keepdims=True)
    loss = jnp.broadcast_to(jnp.sum(loss, axis=1, keepdims=True), (1, width))
    put_sums(sums_ref, [folded(shift_grad, width), folded(gain_grad, width), head_grad[0:outs], loss])


def back_to_preact(parts_ref, stats_ref, norms_ref, index, flags_ref, refs, pixel_count, sizes):
    grad_ref, fired_ref, slope_ref, pre_ref, pair_grad_ref, shifts_ref = refs
    cols, width, pairs = sizes
    total = total_of(parts_ref)
    shift_grad, gain_grad = total[0:1], total[1:2]
    pair_grad_ref[0:1, :] = gain_grad
    pair_grad_ref[1:2, :] = shift_grad
    average, inverse_std = twice(stats_ref[0:1, :]), twice(stats_ref[1:2, :])
    scaled = twice(norms_ref[index, 0:1]) * inverse_std * flags_ref[0].astype(jnp.float32)
    shift_mean, gain_mean = twice(shift_grad / pixel_count), twice(gain_grad / pixel_count)
    for pair in range(pairs):
        rows = pl.ds(pair * cols, cols)
        centred = (fired_ref[rows, :].astype(jnp.float32) - average) * inverse_std
        grad = grad_ref[rows, :].astype(jnp.bfloat16).astype(jnp.float32)
        fired_grad = (scaled * (grad - shift_mean - centred * gain_mean)).astype(jnp.bfloat16)
        pre = (fired_grad.astype(jnp.float32) * slope_ref[rows, :].astype(jnp.float32)).astype(jnp.bfloat16)
        pre_ref[rows, :] = pre
        spread_pair(pair, pre.astype(jnp.float32), shifts_ref, sizes)


def back_kernel(
    flags_ref, parts_ref, norms_ref, grad_ref, weight_ref, fired_ref, slope_ref, stats_ref, below_in, below_stats_in,
    *refs, sizes, pixel_count, index, second,
):
    cols, width, pairs = sizes
    if not second:
        kept_in, *refs = refs
    pre_out, pair_grad_out, *refs = refs
    if second:
        kept_out, *refs = refs
    out_ref, sums_ref, *refs = refs
    if not second:
        kept_ref, *refs = refs
    below_ref, below_stats_ref, pre_ref, pair_grad_ref, shifts_ref, taps_ref, semaphores = refs
    mover = Mover(semaphores)
    groups = pairs // GROUP
    below_stats = mover.fetch(below_stats_in, below_stats_ref)
    below = mover.fetch(below_in, below_ref)
    if second:
        mover.send(grad_ref, kept_out)
    else:
        kept = mover.fetch(kept_in, kept_ref)
    clear_rim(shifts_ref, sizes)
    taps_backward(weight_ref, taps_ref, width)
    refs = (grad_ref, fired_ref, slope_ref, pre_ref, pair_grad_ref, shifts_ref)
    back_to_preact(parts_ref, stats_ref, norms_ref, index, flags_ref, refs, pixel_count, sizes)
    mover.send(pre_ref, pre_out)
    mover.send(pair_grad_ref, pair_grad_out)
    below_stats[0].wait()
    average, inverse_std = twice(below_stats_ref[0:1, :]), twice(below_stats_ref[1:2, :])
    shift_sum = jnp.zeros((1, 2 * width), jnp.float32)
    gain_sum = jnp.zeros((1, 2 * width), jnp.float32)
    step = GROUP * cols
    if not second:
        kept[0].wait()
    below[0].wait()
    for group in range(groups):
        rows = pl.ds(group * step, step)
        source = pair_conv(shifts_ref, taps_ref, group, cols, ((1,), (1,)))
        if not second:
            source = source + kept_ref[rows, :]
        out_ref[rows, :] = source.astype(out_ref.dtype)
        low = source.astype(jnp.bfloat16).astype(jnp.float32)
        shift_sum += jnp.sum(low, axis=0, keepdims=True)
        gain_sum += jnp.sum(low * ((below_ref[rows, :].astype(jnp.float32) - average) * inverse_std), axis=0, keepdims=True)
    active = flags_ref[0].astype(jnp.float32)
    put_sums(sums_ref, [folded(shift_sum, width) * active, folded(gain_sum, width) * active])
    mover.finish()


def cut_frames(flags_ref, flat_ref, mine_ref, theirs_ref, tiles, shard):
    width = flat_ref.shape[1]
    nl, no = tiles[0], tiles[1]
    rows = mine_ref.shape[2]
    for lon_step in range(no):
        for lat_step in range(nl):
            for core_step, target in ((0, mine_ref), (1, theirs_ref)):
                device = device_at(flags_ref, lon_step, lat_step, core_step, tiles)
                start = first_row(device, shard, width)
                target[lon_step, lat_step] = flat_ref[pl.ds(start, rows), :].astype(jnp.bfloat16)


def block_kernel_grad(shifts_ref, pre_ref, flat_ref, sizes):
    cols, width, pairs = sizes
    for a in range(4):
        k, rr = a // 2, a % 2
        block = shifts_ref[k * cols : (k + pairs) * cols, rr * 3 * width : (rr + 1) * 3 * width]
        grad = dot(block, pre_ref[...], ((0,), (0,)))
        if a < 3:
            flat_ref[a * 3 * width : (a + 1) * 3 * width, :] = grad[:, :width]
        if a > 0:
            flat_ref[(a - 1) * 3 * width : a * 3 * width, :] += grad[:, width:]


def kernel_grad_kernel(flags_ref, *refs, tiles, sizes, shard, fetches):
    fetched_from, refs = refs[:fetches], refs[fetches:]
    source_in, pre_in, *refs = refs
    fetched_to, refs = refs[:fetches], refs[fetches:]
    mine_out, theirs_ref, mine_ref, source_ref, pre_ref, shifts_ref, flat_ref, semaphores = refs
    mover = Mover(semaphores)
    source, pre = mover.fetch(source_in, source_ref), mover.fetch(pre_in, pre_ref)
    for wide, near in zip(fetched_from, fetched_to):
        mover.send(wide, near)
    clear_rim(shifts_ref, sizes)
    source[0].wait()
    spread_all_pairs(source_ref, shifts_ref, sizes)
    pre[0].wait()
    block_kernel_grad(shifts_ref, pre_ref, flat_ref, sizes)
    cut_frames(flags_ref, flat_ref, mine_ref, theirs_ref, tiles, shard)
    mover.send(mine_ref, mine_out)
    mover.finish()


def spread_all_pairs(source_ref, shifts_ref, sizes):
    cols, width, pairs = sizes
    for pair in range(pairs):
        cells = source_ref[pair * cols : (pair + 1) * cols, :].astype(jnp.float32)
        spread_pair(pair, cells, shifts_ref, sizes)


def last_kernel(
    flags_ref, parts_ref, norms_ref, grad_ref, fired_in, slope_in, stats_in, weight_in, kept_in, in_slope_in,
    source_in, wide_in, *refs, tiles, sizes, shards, in_width, pixel_count, others,
):
    cols, width, pairs = sizes
    nl, no = tiles[0], tiles[1]
    near_ins, other_ins, refs = refs[:2], refs[2 : 2 + 2 * others], refs[2 + 2 * others :]
    (
        pair_grad_out, mine_ref, theirs_ref,
        fired_ref, slope_ref, stats_ref, weight_ref, kept_ref, in_slope_ref, source_ref, wide_ref, pre_ref, in_pre_ref, pair_grad_ref,
        shifts_ref, taps_ref, flat_ref, flat_first_ref, others_ref, semaphores,
    ) = refs
    mover = Mover(semaphores)
    groups = pairs // GROUP
    early = mover.fetch(stats_in, stats_ref) + mover.fetch(weight_in, weight_ref)
    early += mover.fetch(fired_in, fired_ref) + mover.fetch(slope_in, slope_ref)
    clear_rim(shifts_ref, sizes)
    for arrival in early:
        arrival.wait()
    kept = mover.fetch(kept_in, kept_ref)
    in_slope = mover.fetch(in_slope_in, in_slope_ref)
    source = mover.fetch(source_in, source_ref)
    wide = mover.fetch(wide_in, wide_ref)
    arrivals = [mover.start(other, others_ref.at[i]) for i, other in enumerate(near_ins + other_ins)]
    taps_backward(weight_ref, taps_ref, width)
    refs = (grad_ref, fired_ref, slope_ref, pre_ref, pair_grad_ref, shifts_ref)
    back_to_preact(parts_ref, stats_ref, norms_ref, 0, flags_ref, refs, pixel_count, sizes)
    mover.send(pair_grad_ref, pair_grad_out)
    kept[0].wait()
    in_slope[0].wait()
    step = GROUP * cols
    for group in range(groups):
        rows = pl.ds(group * step, step)
        grad = pair_conv(shifts_ref, taps_ref, group, cols, ((1,), (1,))) + kept_ref[rows, :]
        in_pre_ref[rows, :] = (grad * in_slope_ref[rows, :].astype(jnp.float32)).astype(jnp.bfloat16)
    source[0].wait()
    spread_all_pairs(source_ref, shifts_ref, sizes)
    block_kernel_grad(shifts_ref, pre_ref, flat_first_ref, sizes)
    for arrival in arrivals:
        arrival.wait()
    wide[0].wait()
    for a in range(8):
        k, rr = a // 2, a % 2
        block = wide_ref[k * cols : (k + pairs) * cols, rr * 7 * width : (rr + 1) * 7 * width]
        grads = dot(block, in_pre_ref[...], ((0,), (0,)))
        for b in range(7):
            grad = grads[b * width : b * width + in_width]
            if a < 7:
                tap = a * 7 + b
                flat_ref[tap * in_width : (tap + 1) * in_width, :] = grad[:, :width]
            if a > 0:
                tap = (a - 1) * 7 + b
                flat_ref[tap * in_width : (tap + 1) * in_width, :] += grad[:, width:]
    rows = others_ref.shape[3]
    in_rows = mine_ref.shape[2] - (others + 2) * rows
    for lon_step in range(no):
        for lat_step in range(nl):
            for core_step, target in ((0, mine_ref), (1, theirs_ref)):
                device = device_at(flags_ref, lon_step, lat_step, core_step, tiles)
                spot = pl.ds(first_row(device, shards[0], width), in_rows)
                target[lon_step, lat_step, 0:in_rows, :] = flat_ref[spot, :].astype(jnp.bfloat16)
                spot = pl.ds(first_row(device, shards[1], width), rows)
                block = flat_first_ref[spot, :].astype(jnp.bfloat16)
                target[lon_step, lat_step, in_rows : in_rows + rows, :] = block
                at = in_rows + rows
                target[lon_step, lat_step, at : at + rows, :] = others_ref[core_step, lon_step, lat_step]
            for other in range(1, others + 1):
                at = in_rows + (other + 1) * rows
                mine_ref[lon_step, lat_step, at : at + rows, :] = low_sum(
                    others_ref[2 * other, lon_step, lat_step], others_ref[2 * other + 1, lon_step, lat_step]
                )
    mover.finish()


def add_kernel(flags_ref, mine_ref, theirs_ref, total_ref, unused):
    rows = theirs_ref.shape[2]
    for lon_step in range(mine_ref.shape[0]):
        for lat_step in range(mine_ref.shape[1]):
            mine = mine_ref[lon_step, lat_step, 0:rows, :].astype(jnp.float32)
            total = mine + theirs_ref[lon_step, lat_step].astype(jnp.float32)
            total_ref[lon_step, lat_step, 0:rows, :] = total.astype(jnp.bfloat16)


def swap(values, axis, step):
    return lax.ppermute(values, axis, [(i, i ^ step) for i in range(lax.axis_size(axis))])


def low_sum(*values):
    return sum(part.astype(jnp.float32) for part in values).astype(jnp.bfloat16)


def along_lon(frames):
    return [frames[0]] + [swap(frames[k], "lon", k) for k in range(1, frames.shape[0])]


def summed_along_lat(total):
    parts = [total[0]] + [swap(total[k], "lat", k) for k in range(1, total.shape[0])]
    return sum(part.astype(jnp.float32) for part in parts)


def spread_all(values, axes):
    return lax.all_to_all(values, axes, 0, 0, tiled=True)


def whole_sample_body(
    fields,
    targets,
    land_mask,
    input_kernel,
    input_first,
    input_second,
    block_kernels,
    block_first,
    block_second,
    head_weight,
    head_first,
    head_second,
    norm_params,
    norm_first,
    norm_second,
):
    samples_here, rows_here, cols_here, in_width = fields.shape
    width = norm_params.shape[2]
    conv_count = block_kernels.shape[0]
    nl, no, nb = (lax.axis_size(axis) for axis in ALL)
    places, devices = nl * no, nl * no * nb
    tiles = (nl, no, rows_here, cols_here)
    cols, pairs = cols_here * no, rows_here * nl // 2
    sizes = (cols, width, pairs)
    pixels = pairs * cols
    sample_count = samples_here * nb
    pixel_count = float(sample_count * 2 * pixels)
    place = lax.axis_index(TILE)
    core = lax.axis_index("batch")
    flags = jnp.stack(
        [
            (place < samples_here).astype(jnp.int32),
            lax.axis_index("batch"),
            lax.axis_index("lat"),
            lax.axis_index("lon"),
        ]
    )
    bf16, f32 = jnp.bfloat16, jnp.float32
    device = lax.axis_index(ALL)
    in_shard, block_shard = input_kernel.shape[0], block_kernels.shape[1]
    in_frame = frame_rows(in_shard, devices, width, SPREAD)
    block_frame = frame_rows(block_shard, devices, width, 8)
    in_offset = device * in_shard % width
    flat_rows = max((devices - 1) * in_shard // width + in_frame, 48 * in_width + width)
    flat_rows = -(-flat_rows // 8) * 8
    block_rows = block_shard // width

    def shard_rows(shards):
        count = shards.shape[0] * block_rows
        rows = shards.astype(bf16).reshape(count, width)
        return jnp.pad(rows, ((0, -count % SPREAD), (0, 0)))

    def along(values, axis, count):
        return [values] + [swap(values, axis, k) for k in range(1, count)]

    framed = lax.dynamic_update_slice(
        jnp.zeros((in_frame * width,), bf16), input_kernel.astype(bf16), (in_offset,)
    ).reshape(in_frame, width)
    near = jnp.concatenate([framed, shard_rows(block_kernels[:NEAR])], axis=0)
    near_rows = near.shape[0]
    both = jnp.stack(along(jnp.concatenate([near, shard_rows(block_kernels[NEAR:])], axis=0), "lat", nl))

    row_global = (lax.axis_index("lat") * rows_here + jnp.arange(rows_here)).astype(f32)
    latitude = (row_global + 0.5) / (rows_here * nl) * jnp.pi - jnp.pi / 2
    pixel_weight = jnp.cos(latitude)[None, :, None] * land_mask.astype(f32)
    (packed,) = call(
        functools.partial(pack_kernel, in_width=in_width),
        [(fields, VECTOR), (targets.transpose(3, 0, 1, 2), VECTOR), (pixel_weight, VECTOR)],
        [((places, rows_here, cols_here, width), bf16, VECTOR)],
        [pltpu.VMEM((-(-3 * PIECES * rows_here // 16) * 16, cols_here), f32)],
    )
    near, far = both[:, :near_rows], both[:, near_rows:]
    packed, near, far = lax.optimization_barrier((packed, near, far))
    near = along(near, "lon", no)
    packed = spread_all(packed, TILE)
    head_low = jnp.pad(head_weight.astype(bf16), ((0, 0), (0, width - head_weight.shape[1])))

    plane = (pixels, 2 * width)
    weight_shape = (9 * width, width)
    flat_weight = pltpu.VMEM((9 * width + block_frame + 8, width), f32)
    wide_shape = ((pairs + 3) * cols, 14 * width)
    shift_shape = ((pairs + 1) * cols, 6 * width)
    shift_scratch = pltpu.VMEM(shift_shape, bf16)
    forward_taps, backward_taps = (2, 6 * width, 2 * width), (2, 2 * width, 6 * width)
    sums_shape = ((devices, 4, width), f32, VECTOR)
    stats_shape, pair_shape = (8, width), (2, width)
    frame_shape = (no, nl, block_frame, width)
    low_plane, wide_plane = pltpu.VMEM(plane, bf16), pltpu.VMEM(plane, f32)
    weight_scratch, stats_scratch = pltpu.VMEM(weight_shape, bf16), pltpu.VMEM(stats_shape, f32)
    pair_scratch = pltpu.VMEM(pair_shape, f32)
    unit_cost = 2 * 2 * pixels * 9 * width * width

    def kept_outs(*kinds):
        return [(shape, dtype, WIDE) for shape, dtype in kinds]

    far = along(far, "lon", no)
    near = [part for values in near for part in (values, swap(values, "batch", 1))]
    near_count, far_count = NEAR, conv_count - NEAR
    out = call(
        functools.partial(
            first_kernel, tiles=tiles, sizes=sizes, shards=[in_shard, block_rows], in_width=in_width, count=near_count
        ),
        [(part, VECTOR) for part in near] + [(packed, VECTOR)],
        kept_outs(*[(weight_shape, bf16)] * near_count, (plane, bf16), (plane, bf16), (plane, f32), (plane, bf16))
        + [(plane, bf16, VECTOR), (plane, bf16, VECTOR), sums_shape],
        [flat_weight] * near_count
        + [low_plane, pltpu.VMEM((near_count, *weight_shape), bf16)]
        + [pltpu.VMEM((-(-near_count * block_rows // SPREAD) * SPREAD, width), f32)]
        + [pltpu.VMEM((4, 14 * width, 2 * width), bf16), pltpu.VMEM((flat_rows, width), f32)]
        + [pltpu.VMEM(wide_shape, bf16), low_plane, wide_plane, low_plane]
        + [shift_scratch, pltpu.VMEM(forward_taps, bf16)],
        flags,
        6 * unit_cost,
        LARGE_ROOM,
    )
    weights, out = list(out[:near_count]), out[near_count:]
    fields, in_slope, stream, source, fired, slope, sums = out
    far, sums = lax.optimization_barrier((far, sums))
    parts = spread_all(sums, ALL)
    far = [part for values in far for part in (values, swap(values, "batch", 1))]
    *far_weights, weight = call(
        functools.partial(far_kernels_kernel, tiles=tiles, block_rows=block_rows, count=far_count),
        [(part, WIDE) for part in far],
        kept_outs(*[(weight_shape, bf16)] * far_count) + [(weight_shape, bf16, VECTOR)],
        [pltpu.VMEM((len(far), *far[0].shape), bf16)]
        + [pltpu.VMEM((-(-far_count * block_rows // SPREAD) * SPREAD, width), f32)]
        + [flat_weight] * far_count
        + [pltpu.VMEM((far_count, *weight_shape), bf16)],
        flags,
        unit_cost,
    )
    weights += far_weights

    sources, fireds, slopes, stats = [source], [], [], []
    fetched = []
    for k in range(1, conv_count):
        residual = k % 2 == 0
        fetches = [weights[k + 1]] if k + 1 < conv_count else []
        if not residual:
            fetches.append(stream)
        out = call(
            functools.partial(
                unit_kernel, sizes=sizes, pixel_count=pixel_count, index=k - 1, residual=residual,
                fetches=len(fetches),
            ),
            [(array, VECTOR) for array in (fired, parts, norm_params, weight, slope, *fetched)]
            + [(array, WIDE) for array in fetches],
            kept_outs(*[(plane, f32)] * residual, (plane, bf16), (stats_shape, f32), (plane, bf16), (plane, bf16))
            + [(plane, bf16, VECTOR), (plane, bf16, VECTOR), sums_shape]
            + [(array.shape, array.dtype, VECTOR) for array in fetches],
            [wide_plane] * residual
            + [low_plane, stats_scratch, shift_scratch, pltpu.VMEM(forward_taps, bf16)],
            flags,
            unit_cost,
        )
        if residual:
            stream, *out = out
        source, stat, saved_fired, saved_slope, fired, slope, sums, *fetched = out
        sources.append(source)
        stats.append(stat)
        fireds.append(saved_fired)
        slopes.append(saved_slope)
        if k + 1 < conv_count:
            weight, *fetched = fetched
        parts = spread_all(sums, ALL)

    (wide,) = call(
        functools.partial(wide_kernel, sizes=sizes),
        [(fields, WIDE)],
        kept_outs((wide_shape, bf16)),
        [low_plane, pltpu.VMEM(wide_shape, bf16)],
        flags,
        unit_cost,
        LARGE_ROOM,
    )
    wide, parts = lax.optimization_barrier((wide, parts))
    grad, sums, stat = call(
        functools.partial(
            head_kernel, sizes=sizes, pixel_count=pixel_count, sample_count=sample_count, in_width=in_width,
            index=conv_count - 1,
        ),
        [(array, VECTOR) for array in (fired, parts, norm_params, head_low, *fetched)]
        + [(fields, WIDE), (stats[0], WIDE)],
        [(plane, f32, VECTOR), ((devices, 8, width), f32, VECTOR), (stats_shape, f32, VECTOR)],
        [low_plane, stats_scratch, low_plane],
        flags,
        unit_cost // 4,
    )
    parts = spread_all(sums, ALL)
    head_parts = parts

    pair_grads, frames = [None] * conv_count, [None] * conv_count
    for k in range(conv_count - 1, 0, -1):
        second = k % 2 == 1
        pre, pair_grads[k], *out = call(
            functools.partial(back_kernel, sizes=sizes, pixel_count=pixel_count, index=k, second=second),
            [(array, VECTOR) for array in (parts, norm_params, grad, weight, fired, slope, stat)]
            + [(array, WIDE) for array in (fireds[k - 1], stats[k - 1])]
            + [(array, WIDE) for array in (() if second else (kept_grad,))],
            kept_outs((plane, bf16), (pair_shape, f32), *[(plane, f32)] * second)
            + [(plane, bf16 if second else f32, VECTOR), sums_shape],
            [wide_plane] * (not second)
            + [low_plane, stats_scratch, low_plane, pair_scratch, shift_scratch, pltpu.VMEM(backward_taps, bf16)],
            flags,
            unit_cost,
        )
        if second:
            kept_grad, *out = out
        grad, sums = out
        parts = spread_all(sums, ALL)
        fetches = (weights[k - 1], fireds[k - 1], slopes[k - 1], stats[k - 1]) if k > 1 else ()
        *fetched, mine, theirs = call(
            functools.partial(
                kernel_grad_kernel, tiles=tiles, sizes=sizes, shard=block_shard, fetches=len(fetches)
            ),
            [(array, WIDE) for array in (*fetches, sources[k], pre)],
            [(array.shape, array.dtype, VECTOR) for array in fetches]
            + [(frame_shape, bf16, WIDE), (frame_shape, bf16, VECTOR)],
            [pltpu.VMEM(frame_shape, bf16), low_plane, low_plane, shift_scratch, flat_weight],
            flags,
            unit_cost,
        )
        frames[k] = [mine, theirs]
        if k > 1:
            weight, fired, slope, stat = fetched
        if k + 1 < conv_count:
            frames[k + 1][1] = swap(frames[k + 1][1], "batch", 1)
        parts, frames[k:] = lax.optimization_barrier((parts, frames[k:]))
    others = [part for pair in frames[1:] for part in pair]
    pair_grads[0], mine, theirs = call(
        functools.partial(
            last_kernel, tiles=tiles, sizes=sizes, shards=[in_shard, block_shard], in_width=in_width,
            pixel_count=pixel_count, others=conv_count - 2,
        ),
        [(array, VECTOR) for array in (parts, norm_params, grad)]
        + [(array, WIDE) for array in (fireds[0], slopes[0], stats[0], weights[0])]
        + [(array, WIDE) for array in (kept_grad, in_slope, sources[0], wide, *others)],
        kept_outs((pair_shape, f32))
        + [((no, nl, in_frame + rows, width), bf16, VECTOR) for rows in (conv_count * block_frame, 2 * block_frame)],
        [low_plane, low_plane, stats_scratch, weight_scratch, wide_plane, low_plane, low_plane]
        + [pltpu.VMEM(wide_shape, bf16), low_plane, low_plane]
        + [pair_scratch, shift_scratch, pltpu.VMEM(backward_taps, bf16)]
        + [pltpu.VMEM((flat_rows, width), f32), flat_weight]
        + [pltpu.VMEM((len(others), *frame_shape), bf16)],
        flags,
        6 * unit_cost,
        LARGE_ROOM,
    )
    theirs, head_parts, first_stats = lax.optimization_barrier((theirs, head_parts, stats[0]))
    (mine,) = call(
        add_kernel,
        [(mine, VECTOR), (swap(theirs, "batch", 1), VECTOR)],
        [(mine.shape, bf16, VECTOR)],
        (),
        flags,
        unit_cost // 8,
        SMALL_ROOM,
        {1: 0},
    )
    grads = along_lon(mine)
    grads = summed_along_lat(low_sum(*grads))
    input_grad = lax.dynamic_slice(grads[:in_frame].reshape(-1), (in_offset,), (in_shard,))
    block_grad = grads[in_frame:].reshape(conv_count, block_frame, width)[:, :block_rows]
    block_grad = block_grad.reshape(conv_count, block_shard)
    head_total = jnp.sum(head_parts, axis=0)
    head_grad = head_total[2:4].T
    loss_sum = head_total[4, 0]
    loss_weight = first_stats[2, 0] / sample_count
    norm_grad = jnp.stack(pair_grads)
    return finished(
        loss_sum, loss_weight, input_grad, block_grad, head_grad, norm_grad,
        (input_kernel, input_first, input_second), (block_kernels, block_first, block_second),
        (head_weight, head_first, head_second), (norm_params, norm_first, norm_second),
    )


def one_device_takes_a_sample(fields, block_kernels, head_weight, norm_params):
    samples_here, rows_here, cols_here, in_width = fields.shape
    nl, no, nb = (lax.axis_size(axis) for axis in ALL)
    rows, cols, width = rows_here * nl, cols_here * no, norm_params.shape[2]
    return (
        samples_here <= nl * no
        and nb == 2
        and nl & (nl - 1) == 0
        and no & (no - 1) == 0
        and rows * cols <= MOST_PIXELS
        and rows % (2 * GROUP) == 0
        and cols % 128 == 0
        and cols_here % 8 == 0
        and width == 128
        and head_weight.shape[1] == 2
        and in_width + 3 * PIECES <= width
        and block_kernels.shape[1] % width == 0
        and block_kernels.shape[0] > NEAR
    )


def body(*args):
    fields, block_kernels, head_weight, norm_params = args[0], args[6], args[9], args[12]
    if one_device_takes_a_sample(fields, block_kernels, head_weight, norm_params):
        return whole_sample_body(*args)
    return tile_body(*args)


def solution(mesh):
    in_specs = (
        P("batch", "lat", "lon", None),
        P("batch", "lat", "lon", None),
        P("batch", "lat", "lon"),
        P(("lat", "lon", "batch")),
        P(("lat", "lon", "batch")),
        P(("lat", "lon", "batch")),
        P(None, ("lat", "lon", "batch")),
        P(None, ("lat", "lon", "batch")),
        P(None, ("lat", "lon", "batch")),
        P(),
        P(),
        P(),
        P(),
        P(),
        P(),
    )
    out_specs = (
        P(),
        P(),
        P(("lat", "lon", "batch")),
        P(("lat", "lon", "batch")),
        P(("lat", "lon", "batch")),
        P(None, ("lat", "lon", "batch")),
        P(None, ("lat", "lon", "batch")),
        P(None, ("lat", "lon", "batch")),
        P(),
        P(),
        P(),
        P(),
        P(),
        P(),
    )
    return jax.shard_map(body, mesh=mesh, in_specs=in_specs, out_specs=out_specs, check_vma=False)
```

```python
import functools

import jax
import jax.numpy as jnp
from jax import lax
from jax.experimental import pallas as pl
from jax.experimental.pallas import tpu as pltpu
from jax.sharding import PartitionSpec as P

STEP = 10


NORM_EPSILON = 1e-05
GELU_SCALE = 0.7978845608028654
GELU_CUBE = 0.044715
GROUP = 4
UNROLL = False
SMALL_ROOM = 14 << 20
LARGE_ROOM = 36 << 20
COPIES = 32
FORWARD, BACKWARD = 1, 2
NEAR = 1
MOST_PIXELS = 4096


def shortened(shard):

    def short(part):
        return part.astype(jnp.bfloat16) if part.dtype == jnp.float32 else part

    return jax.tree.map(short, shard)


def with_halo(cells, sides, width):
    for axis, dim in sides:
        count = lax.axis_size(axis)
        ends = count - 1
        head = lax.slice_in_dim(cells, 0, width, axis=dim)
        tail = lax.slice_in_dim(cells, cells.shape[dim] - width, cells.shape[dim], axis=dim)
        cells = jnp.concatenate(
            [
                lax.ppermute(tail, axis, [(i, (i + 1) % count) for i in range(ends)]),
                cells,
                lax.ppermute(head, axis, [((i + 1) % count, i) for i in range(ends)]),
            ],
            axis=dim,
        )
    return cells


def conv_valid(padded, kernel):
    return lax.conv_general_dilated(
        padded,
        kernel,
        (1, 1),
        "VALID",
        dimension_numbers=("NHWC", "HWIO", "NHWC"),
        preferred_element_type=jnp.float32,
    )


def kernel_grad(padded, gradient):
    summed = lax.conv_general_dilated(
        padded,
        gradient,
        (1, 1),
        "VALID",
        dimension_numbers=("CHWN", "IHWO", "NHWC"),
        preferred_element_type=jnp.float32,
    )
    return summed.transpose(1, 2, 0, 3)


def rim_cells(values):
    return with_halo(shortened(values), (("lat", 1), ("lon", 2)), 1).astype(values.dtype)


def to_channels(values):
    return jax.tree.map(
        lambda part, own: part.astype(own.dtype),
        lax.all_to_all(shortened(values), "lat", split_axis=3, concat_axis=0, tiled=True),
        values,
    )


def to_pixels(values):
    return lax.all_to_all(values, "lat", split_axis=0, concat_axis=3, tiled=True)


def spread_sums(summed, squares):
    return lax.psum((summed, squares), ("lon", "batch"))


def own_channels(norm_pair, width):
    return lax.dynamic_slice_in_dim(norm_pair, lax.axis_index("lat") * width, width, 1)


def norm_forward(fired, norm_pair, pixel_count):
    values = to_channels(fired)
    norm_pair = own_channels(norm_pair, values.shape[3])
    widened = values.astype(jnp.float32)
    summed, squares = spread_sums(
        jnp.sum(widened, axis=(0, 1, 2)), jnp.sum(widened * widened, axis=(0, 1, 2))
    )
    average = summed / pixel_count
    inverse_std = lax.rsqrt(squares / pixel_count - average * average + NORM_EPSILON)
    centred = (widened - average) * inverse_std
    normed = (norm_pair[0] * centred + norm_pair[1]).astype(jnp.bfloat16)
    normed = to_pixels(normed)
    return (normed, (centred, inverse_std, norm_pair))


def norm_backward(gradient, kept, pixel_count):
    centred, inverse_std, norm_pair = kept
    gradient = to_channels(gradient)
    widened = gradient.astype(jnp.float32)
    shift_grad, gain_grad = spread_sums(
        jnp.sum(widened, axis=(0, 1, 2)), jnp.sum(widened * centred, axis=(0, 1, 2))
    )
    scaled = norm_pair[0] * inverse_std
    fired_grad = (
        scaled * (widened - shift_grad / pixel_count - centred * gain_grad / pixel_count)
    ).astype(jnp.bfloat16)
    fired_grad = to_pixels(fired_grad)
    return (fired_grad, jnp.stack([gain_grad, shift_grad]))


def gelu_pullback(preact, gradient):
    unused, pullback = jax.vjp(jax.nn.gelu, preact)
    return pullback(gradient)[0]


def conv_forward(source, kernel, norm_pair, pixel_count):
    padded = rim_cells(source)
    preact = conv_valid(padded, kernel)
    fired = jax.nn.gelu(preact).astype(jnp.bfloat16)
    normed, kept = norm_forward(fired, norm_pair, pixel_count)
    return (normed, (padded, preact, kept))


def conv_backward(gradient, kernel, record, pixel_count):
    padded, preact, kept = record
    fired_grad, pair_grad = norm_backward(gradient, kept, pixel_count)
    preact_grad = gelu_pullback(preact, fired_grad.astype(jnp.float32)).astype(jnp.bfloat16)
    kernel_gradient = kernel_grad(padded, preact_grad)
    flipped = kernel[::-1, ::-1].transpose(0, 1, 3, 2)
    source_grad = conv_valid(rim_cells(preact_grad), flipped)
    return (source_grad, kernel_gradient, pair_grad)


def block_forward(stream, kernels, norm_pairs, pixel_count):
    middle, first_record = conv_forward(
        stream.astype(jnp.bfloat16), kernels[0], norm_pairs[0], pixel_count
    )
    branch, second_record = conv_forward(middle, kernels[1], norm_pairs[1], pixel_count)
    return (stream + branch.astype(jnp.float32), (first_record, second_record))


def block_backward(stream_grad, stream, kernels, norm_pairs, pixel_count):
    unused, records = block_forward(stream, kernels, norm_pairs, pixel_count)
    middle_grad, second_kernel, second_pair = conv_backward(
        stream_grad.astype(jnp.bfloat16), kernels[1], records[1], pixel_count
    )
    source_grad, first_kernel, first_pair = conv_backward(
        middle_grad.astype(jnp.bfloat16), kernels[0], records[0], pixel_count
    )
    return (stream_grad + source_grad, (first_kernel, second_kernel), (first_pair, second_pair))


def adamw_update(weight, gradient, momentum, variance, step_rate):
    momentum = 0.9 * momentum + 0.1 * gradient
    variance = 0.999 * variance + 0.001 * gradient * gradient
    corrected = momentum / (1.0 - 0.9**STEP)
    scaled = jnp.sqrt(variance / (1.0 - 0.999**STEP)) + 1e-08
    return (momentum, variance, weight - step_rate * (corrected / scaled + 0.01 * weight))


def finished(
    loss_sum, loss_weight, input_grad, block_grad, head_grad, norm_grad,
    input_state, block_state, head_state, norm_state,
):
    outputs = [jnp.reshape(loss_sum, (1,)), jnp.reshape(loss_weight, (1,))]
    for state, gradient, step_rate in (
        (input_state, input_grad, 0.015),
        (block_state, block_grad, 0.03),
        (head_state, head_grad, 0.15),
        (norm_state, norm_grad, 0.8),
    ):
        weight, first, second = state
        outputs.extend(adamw_update(weight, gradient, first, second, step_rate))
    return tuple(outputs)


def tile_body(
    fields,
    targets,
    land_mask,
    input_kernel,
    input_first,
    input_second,
    block_kernels,
    block_first,
    block_second,
    head_weight,
    head_first,
    head_second,
    norm_params,
    norm_first,
    norm_second,
):
    samples_here, rows_here, cols_here, in_width = fields.shape
    channels = norm_params.shape[2]
    conv_count = block_kernels.shape[0]
    full_input, full_blocks = (
        lax.all_gather(
            input_kernel.astype(jnp.bfloat16), ("lat", "lon", "batch"), axis=0, tiled=True
        ),
        lax.all_gather(
            block_kernels.astype(jnp.bfloat16), ("lat", "lon", "batch"), axis=1, tiled=True
        ),
    )
    kernel_in = full_input.reshape(7, 7, in_width, channels)
    kernels = full_blocks.reshape(conv_count, 3, 3, channels, channels)
    head_low = head_weight.astype(jnp.bfloat16)
    sample_count = samples_here * lax.axis_size("batch")
    pixel_count = float(
        sample_count * rows_here * lax.axis_size("lat") * cols_here * lax.axis_size("lon")
    )
    row_global = (lax.axis_index("lat") * rows_here + jnp.arange(rows_here)).astype(jnp.float32)
    latitude = (row_global + 0.5) / (rows_here * lax.axis_size("lat")) * jnp.pi - jnp.pi / 2
    pixel_weight = jnp.cos(latitude)[None, :, None] * land_mask.astype(jnp.float32)
    valid_sum = lax.psum(jnp.sum(pixel_weight), ("lat", "lon", "batch"))
    loss_weight = valid_sum / sample_count
    padded_in = with_halo(fields, (("lat", 1), ("lon", 2)), 3)
    preact_in = conv_valid(padded_in, kernel_in)
    streams = [jax.nn.gelu(preact_in)]
    for layer in range(conv_count // 2):
        advanced, unused = block_forward(
            streams[-1],
            kernels[2 * layer : 2 * layer + 2],
            norm_params[2 * layer : 2 * layer + 2],
            pixel_count,
        )
        streams.append(advanced)
    top_stream = streams[-1].astype(jnp.bfloat16)
    predicted = jnp.einsum(
        "nhwc,co->nhwo", top_stream, head_low, preferred_element_type=jnp.float32
    )
    misfit = predicted - targets
    loss_local = jnp.sum(pixel_weight[..., None] * misfit * misfit)
    pred_grad = (2.0 * pixel_weight[..., None] * misfit / loss_weight).astype(jnp.bfloat16)
    head_local = jnp.einsum(
        "nhwc,nhwo->co", top_stream, pred_grad, preferred_element_type=jnp.float32
    )
    stream_grad = jnp.einsum(
        "nhwo,co->nhwc", pred_grad, head_low, preferred_element_type=jnp.float32
    )
    kernel_grads = [None] * conv_count
    pair_grads = [None] * conv_count
    for layer in reversed(range(conv_count // 2)):
        stream_grad, kernel_pair, norm_pair = block_backward(
            stream_grad,
            streams[layer],
            kernels[2 * layer : 2 * layer + 2],
            norm_params[2 * layer : 2 * layer + 2],
            pixel_count,
        )
        kernel_grads[2 * layer], kernel_grads[2 * layer + 1] = kernel_pair
        pair_grads[2 * layer], pair_grads[2 * layer + 1] = norm_pair
    pre_in_grad = gelu_pullback(preact_in, stream_grad).astype(jnp.bfloat16)
    input_local = kernel_grad(padded_in, pre_in_grad).reshape(-1)
    block_local = jnp.stack(kernel_grads).reshape(conv_count, -1)
    input_grad, block_grad = (
        lax.psum_scatter(input_local, ("lat", "lon", "batch"), scatter_dimension=0, tiled=True),
        lax.psum_scatter(block_local, ("lat", "lon", "batch"), scatter_dimension=1, tiled=True),
    )
    head_grad, loss_sum = lax.psum((head_local, loss_local), ("lat", "lon", "batch"))
    norm_grad = jnp.stack(pair_grads)
    norm_grad = lax.all_gather(norm_grad, "lat", axis=2, tiled=True)
    return finished(
        loss_sum, loss_weight, input_grad, block_grad, head_grad, norm_grad,
        (input_kernel, input_first, input_second), (block_kernels, block_first, block_second),
        (head_weight, head_first, head_second), (norm_params, norm_first, norm_second),
    )


ALL = ("lat", "lon", "batch")
TILE = ("lat", "lon")
PIECES = 3
SPREAD = 16


VECTOR, WIDE = "vector", "wide"
SPACES = {VECTOR: pltpu.VMEM, WIDE: pltpu.HBM}


def call(kernel, ins, outs, scratch=(), flags=None, cost=0, room=SMALL_ROOM, aliases=()):
    specs = [pl.BlockSpec(memory_space=SPACES[space]) for unused, space in ins]
    args = [
        pltpu.with_memory_space_constraint(array, pltpu.HBM) if space == WIDE else array
        for array, space in ins
    ]
    if flags is not None:
        specs, args = [pl.BlockSpec(memory_space=pltpu.SMEM)] + specs, [flags] + args
    return pl.pallas_call(
        kernel,
        out_shape=[
            pltpu.HBM(shape, dtype) if space == WIDE else jax.ShapeDtypeStruct(shape, dtype)
            for shape, dtype, space in outs
        ],
        in_specs=specs,
        out_specs=[pl.BlockSpec(memory_space=SPACES[space]) for *unused, space in outs],
        scratch_shapes=list(scratch) + [pltpu.SemaphoreType.DMA((COPIES,))],
        input_output_aliases=dict(aliases),
        compiler_params=pltpu.CompilerParams(vmem_limit_bytes=room),
        cost_estimate=pl.CostEstimate(flops=cost, bytes_accessed=4 << 20, transcendentals=0),
    )(*args)


class Mover:
    def __init__(self, semaphores):
        self.semaphores, self.used, self.sent = semaphores, 0, []

    def start(self, source, target):
        copy = pltpu.make_async_copy(source, target, self.semaphores.at[self.used])
        self.used += 1
        copy.start()
        return copy

    def fetch(self, source, target, parts=1):
        step = target.shape[0] // parts
        return [
            self.start(source.at[pl.ds(i * step, step)], target.at[pl.ds(i * step, step)])
            for i in range(parts)
        ]

    def send(self, source, target):
        self.sent.append(self.start(source, target))

    def finish(self):
        for copy in self.sent:
            copy.wait()


def dot(left, right, dims=((1,), (0,))):
    return lax.dot_general(left, right, (dims, ((), ())), preferred_element_type=jnp.float32)


def gelu_value(x):
    return x * (0.5 * (1.0 + jnp.tanh(GELU_SCALE * (x + GELU_CUBE * (x * x * x)))))


def gelu_both(x):
    square = x * x
    level = jnp.tanh(GELU_SCALE * (x + GELU_CUBE * (x * square)))
    half = 0.5 * (1.0 + level)
    slope = half + 0.5 * x * (1.0 - level * level) * (GELU_SCALE * (1.0 + 3.0 * GELU_CUBE * square))
    return x * half, slope


def shifted(cells, step):
    count = cells.shape[0]
    if step == 0:
        return cells
    column = lax.broadcasted_iota(jnp.int32, cells.shape, 0) + step
    rolled = pltpu.roll(cells, (-step) % count, 0)
    return jnp.where((column >= 0) & (column < count), rolled, 0.0)


def spread_pair(pair, cells, shifts_ref, sizes):
    cols, width, pairs = sizes
    for b in range(3):
        moved = shifted(cells, b - 1).astype(jnp.bfloat16)
        shifts_ref[(pair + 1) * cols : (pair + 2) * cols, b * width : (b + 1) * width] = moved[:, width:]
        shifts_ref[pair * cols : (pair + 1) * cols, (3 + b) * width : (4 + b) * width] = moved[:, :width]


def clear_rim(shifts_ref, sizes):
    cols, width, pairs = sizes
    zero = jnp.zeros((cols, 3 * width), jnp.bfloat16)
    shifts_ref[0:cols, 0 : 3 * width] = zero
    shifts_ref[pairs * cols : (pairs + 1) * cols, 3 * width : 6 * width] = zero


def taps_forward(weight_ref, taps_ref, width):
    for k in range(2):
        for rr in range(2):
            for b in range(3):
                for q in range(2):
                    a = 2 * k + rr - q
                    at = (rr * 3 + b) * width
                    if 0 <= a <= 2:
                        block = weight_ref[(a * 3 + b) * width : (a * 3 + b + 1) * width, :]
                    else:
                        block = jnp.zeros((width, width), jnp.bfloat16)
                    taps_ref[k, at : at + width, q * width : (q + 1) * width] = block


def taps_backward(weight_ref, taps_ref, width):
    for k in range(2):
        for rr in range(2):
            for b in range(3):
                for q in range(2):
                    a = 2 - (2 * k + rr - q)
                    at = (rr * 3 + b) * width
                    if 0 <= a <= 2:
                        tap = a * 3 + 2 - b
                        block = weight_ref[tap * width : (tap + 1) * width, :]
                    else:
                        block = jnp.zeros((width, width), jnp.bfloat16)
                    taps_ref[k, q * width : (q + 1) * width, at : at + width] = block


def pair_conv(shifts_ref, taps_ref, group, cols, dims=((1,), (0,))):
    rows = GROUP * cols
    first = shifts_ref[group * rows : (group + 1) * rows, :]
    second = shifts_ref[group * rows + cols : (group + 1) * rows + cols, :]
    return dot(first, taps_ref[0], dims) + dot(second, taps_ref[1], dims)


def folded(sums, width):
    return sums[:, :width] + sums[:, width:]


def total_of(parts_ref):
    return jnp.sum(parts_ref[...], axis=0)


def twice(row):
    return jnp.concatenate([row, row], axis=1)


def norm_of(total, pixel_count):
    average = total[0:1] / pixel_count
    return average, lax.rsqrt(total[1:2] / pixel_count - average * average + NORM_EPSILON)


def conv_and_sums(flags_ref, shifts_ref, taps_ref, fired_ref, slope_ref, sums_ref, sizes, more=None):
    cols, width, pairs = sizes
    total = jnp.zeros((1, 2 * width), jnp.float32)
    squares = jnp.zeros((1, 2 * width), jnp.float32)
    step = GROUP * cols
    for group in range(pairs // GROUP):
        fired, slope = gelu_both(pair_conv(shifts_ref, taps_ref, group, cols))
        rows = pl.ds(group * step, step)
        fired = fired.astype(jnp.bfloat16)
        fired_ref[rows, :] = fired
        slope_ref[rows, :] = slope.astype(jnp.bfloat16)
        wide = fired.astype(jnp.float32)
        total = total + jnp.sum(wide, axis=0, keepdims=True)
        squares = squares + jnp.sum(wide * wide, axis=0, keepdims=True)
    active = flags_ref[0].astype(jnp.float32)
    parts = [folded(total, width) * active, folded(squares, width) * active]
    put_sums(sums_ref, parts + (more or []))


def put_sums(sums_ref, parts):
    shape = sums_ref.shape[1:]
    row = lax.broadcasted_iota(jnp.int32, shape, 0)
    block = jnp.zeros(shape, jnp.float32)
    at = 0
    for part in parts:
        for i in range(part.shape[0]):
            block = jnp.where(row == at, jnp.broadcast_to(part[i : i + 1], shape), block)
            at += 1
    sums_ref[...] = jnp.broadcast_to(block[None], sums_ref.shape)


def field_row(fields_ref, row, tiles):
    nl, no, rows_here, cols_here = tiles
    lat, inner = row // rows_here, row % rows_here
    return jnp.concatenate([fields_ref[lat * no + lon, inner] for lon in range(no)], axis=0)


def wide_shifts(row_of, shifts_ref, sizes, done=None):
    cols, width, pairs = sizes
    rows = 2 * pairs
    for row in range(-3, rows + 3):
        at, rr = (row + 3) // 2, (row + 3) % 2
        if 0 <= row < rows:
            cells = row_of(row).astype(jnp.float32)
        for b in range(7):
            if 0 <= row < rows:
                moved = shifted(cells, b - 3).astype(jnp.bfloat16)
            else:
                moved = jnp.zeros((cols, width), jnp.bfloat16)
            spot = (rr * 7 + b) * width
            shifts_ref[at * cols : (at + 1) * cols, spot : spot + width] = moved
        if rr == 1 and done is not None:
            done(pl.ds(at * cols, cols))


def first_row(device, shard, width):
    return lax.div(device * shard, width)


def frame_rows(shard, devices, width, grain):
    rows = max(-(-(d + 1) * shard // width) - d * shard // width for d in range(devices))
    return -(-rows // grain) * grain


def device_at(flags_ref, lon_step, lat_step, core_step, tiles):
    lat = flags_ref[2] ^ lat_step
    lon = flags_ref[3] ^ lon_step
    return (lat * tiles[1] + lon) * 2 + (flags_ref[1] ^ core_step)


def pack_kernel(fields_ref, targets_ref, weights_ref, packed_ref, pieces_ref, unused_ref, *, in_width):
    samples, rows, cols, unused = fields_ref.shape
    width = packed_ref.shape[3]
    outs = targets_ref.shape[0]
    many = pieces_ref.shape[0]
    pieces_ref[...] = jnp.zeros(pieces_ref.shape, jnp.float32)
    packed_ref[samples:] = jnp.zeros((packed_ref.shape[0] - samples, rows, cols, width), jnp.bfloat16)
    take_from = lax.broadcasted_iota(jnp.int32, (many, width), 0)
    put_to = lax.broadcasted_iota(jnp.int32, (many, width), 1) - in_width
    picks = [
        jnp.where((put_to >= 0) & (take_from == put_to * rows + row), 1.0, 0.0).astype(jnp.bfloat16)
        for row in range(rows)
    ]
    for sample in range(samples):
        for source in range(outs + 1):
            left = targets_ref[source, sample] if source < outs else weights_ref[sample]
            for piece in range(PIECES):
                low = left.astype(jnp.bfloat16).astype(jnp.float32)
                left = left - low
                at = (source * PIECES + piece) * rows
                pieces_ref[at : at + rows, :] = low
        pieces = pieces_ref[...].astype(jnp.bfloat16)
        for row in range(rows):
            placed = dot(pieces, picks[row], ((0,), (0,))).astype(jnp.bfloat16)
            packed_ref[sample, row] = placed
            packed_ref[sample, row, :, 0:in_width] = fields_ref[sample, row]


def place_blocks(part, at, count, rows, device, stage_ref, flat_refs):
    stage_ref[...] = part[at : at + stage_ref.shape[0], :].astype(jnp.float32)
    for index in range(count):
        flat_refs[index][pl.ds(device * rows, rows), :] = stage_ref[index * rows : (index + 1) * rows, :]


def near_kernels(
    flags_ref, parts, taps_ref, flat_ref, stage_ref, flat_block_refs, tiles, shards, in_width
):
    nl, no = tiles[0], tiles[1]
    width = flat_ref.shape[1]
    in_shard, block_rows = shards
    rows = frame_rows(in_shard, 2 * nl * no, width, SPREAD)
    flat_ref[...] = jnp.zeros(flat_ref.shape, jnp.float32)
    for lon_step in range(no):
        for core_step in range(2):
            part = parts[lon_step * 2 + core_step]
            for lat_step in range(nl):
                device = device_at(flags_ref, lon_step, lat_step, core_step, tiles)
                spot = pl.ds(first_row(device, in_shard, width), rows)
                flat_ref[spot, :] += part[lat_step, 0:rows, :].astype(jnp.float32)
                place_blocks(
                    part.at[lat_step], rows, len(flat_block_refs), block_rows, device, stage_ref, flat_block_refs
                )
    inside = lax.broadcasted_iota(jnp.int32, (width, width), 0) < in_width
    zero = jnp.zeros((width, width), jnp.bfloat16)
    for b in range(7):
        taps_ref[3, (7 + b) * width : (8 + b) * width, 0:width] = zero
        taps_ref[0, b * width : (b + 1) * width, width : 2 * width] = zero
        for a in range(7):
            tap = a * 7 + b
            block = flat_ref[tap * in_width : tap * in_width + width, :]
            block = jnp.where(inside, block, 0.0).astype(jnp.bfloat16)
            for q in range(2):
                k, rr = (a + q) // 2, (a + q) % 2
                spot = (rr * 7 + b) * width
                taps_ref[k, spot : spot + width, q * width : (q + 1) * width] = block


def far_kernels_kernel(flags_ref, *refs, tiles, block_rows, count):
    nl, no = tiles[0], tiles[1]
    parts, outs, next_ref, refs = refs[: 2 * no], refs[2 * no : 2 * no + count], refs[2 * no + count], refs[2 * no + count + 1 :]
    near_ref, stage_ref, *flat_refs, whole_ref, semaphores = refs
    mover = Mover(semaphores)
    arrivals = [mover.start(part, near_ref.at[i]) for i, part in enumerate(parts)]
    for lon_step in range(no):
        for core_step in range(2):
            at = lon_step * 2 + core_step
            arrivals[at].wait()
            for lat_step in range(nl):
                device = device_at(flags_ref, lon_step, lat_step, core_step, tiles)
                place_blocks(near_ref.at[at, lat_step], 0, count, block_rows, device, stage_ref, flat_refs)
    for index in range(count):
        weight = flat_refs[index][0 : whole_ref.shape[1], :].astype(jnp.bfloat16)
        whole_ref[index] = weight
        if index == 0:
            next_ref[...] = weight
        mover.send(whole_ref.at[index], outs[index])
    mover.finish()


def wide_kernel(flags_ref, fields_in, wide_out, fields_ref, wide_ref, semaphores, *, sizes):
    cols, width, pairs = sizes
    mover = Mover(semaphores)
    mover.fetch(fields_in, fields_ref)[0].wait()

    def row_of(row):
        pair, q = row // 2, row % 2
        return fields_ref[pair * cols : (pair + 1) * cols, q * width : (q + 1) * width]

    def done(rows):
        mover.send(wide_ref.at[rows], wide_out.at[rows])

    wide_shifts(row_of, wide_ref, sizes, done)
    mover.finish()


def first_kernel(flags_ref, *refs, tiles, sizes, shards, in_width, count):
    cols, width, pairs = sizes
    nl, no = tiles[0], tiles[1]
    near, refs = refs[: 2 * no], refs[2 * no :]
    fields_ref, *refs = refs
    weight_outs, refs = refs[:count], refs[count:]
    pairs_out, slope_in_out, stream_out, source_out, fired_ref, slope_ref, sums_ref, *refs = refs
    flat_block_refs, refs = refs[:count], refs[count:]
    (
        pairs_ref, weights_ref, stage_ref, in_taps_ref, flat_ref, wide_ref,
        slope_in_ref, stream_ref, source_ref, shifts_ref, taps_ref, semaphores,
    ) = refs
    mover = Mover(semaphores)
    clear_rim(shifts_ref, sizes)

    def row_of(row):
        cells = field_row(fields_ref, row, tiles)
        pair, q = row // 2, row % 2
        pairs_ref[pair * cols : (pair + 1) * cols, q * width : (q + 1) * width] = cells
        return cells

    wide_shifts(row_of, wide_ref, sizes)
    mover.send(pairs_ref, pairs_out)
    near_kernels(
        flags_ref, near, in_taps_ref, flat_ref, stage_ref, flat_block_refs, tiles, shards, in_width
    )
    for index in range(count):
        weight = flat_block_refs[index][0 : weights_ref.shape[1], :].astype(jnp.bfloat16)
        weights_ref[index] = weight
        mover.send(weights_ref.at[index], weight_outs[index])
    taps_forward(weights_ref.at[0], taps_ref, width)
    step = GROUP * cols
    for group in range(pairs // GROUP):
        at = group * step
        preact = dot(wide_ref[at : at + step, :], in_taps_ref[0])
        for k in range(1, 4):
            preact += dot(wide_ref[at + k * cols : at + step + k * cols, :], in_taps_ref[k])
        rows = pl.ds(at, step)
        stream, slope = gelu_both(preact)
        slope_in_ref[rows, :] = slope.astype(jnp.bfloat16)
        mover.send(slope_in_ref.at[rows], slope_in_out.at[rows])
        stream_ref[rows, :] = stream
        mover.send(stream_ref.at[rows], stream_out.at[rows])
        source = stream.astype(jnp.bfloat16)
        source_ref[rows, :] = source
        mover.send(source_ref.at[rows], source_out.at[rows])
        for pair in range(GROUP):
            cells = source[pair * cols : (pair + 1) * cols].astype(jnp.float32)
            spread_pair(group * GROUP + pair, cells, shifts_ref, sizes)
    weight_sum = folded(jnp.sum(pairs_ref[...].astype(jnp.float32), axis=0, keepdims=True), width)
    lane = lax.broadcasted_iota(jnp.int32, (1, width), 1) - in_width
    chosen = (lane >= 2 * PIECES) & (lane < 3 * PIECES)
    weight_sum = jnp.sum(jnp.where(chosen, weight_sum, 0.0), axis=1, keepdims=True)
    conv_and_sums(
        flags_ref, shifts_ref, taps_ref, fired_ref, slope_ref, sums_ref, sizes,
        [jnp.broadcast_to(weight_sum, (1, width))],
    )
    mover.finish()


def keep_norm(stats_ref, total, average, inverse_std):
    stats_ref[0:1, :] = average
    stats_ref[1:2, :] = inverse_std
    if total.shape[0] > 2:
        stats_ref[2:3, :] = total[2:3]


def unit_kernel(
    flags_ref, fired_in_ref, parts_ref, norms_ref, weight_ref, slope_in_ref, *refs,
    sizes, pixel_count, index, residual, fetches,
):
    cols, width, pairs = sizes
    if residual:
        stream_in_ref, *refs = refs
    fetched_from, refs = refs[:fetches], refs[fetches:]
    if residual:
        stream_out, *refs = refs
    source_out, stats_out, fired_out, slope_out, fired_ref, slope_ref, sums_ref, *refs = refs
    fetched_to, refs = refs[:fetches], refs[fetches:]
    if residual:
        stream_ref, *refs = refs
    source_ref, stats_ref, shifts_ref, taps_ref, semaphores = refs
    mover = Mover(semaphores)
    mover.send(fired_in_ref, fired_out)
    mover.send(slope_in_ref, slope_out)
    for source, target in zip(fetched_from, fetched_to):
        mover.send(source, target)
    total = total_of(parts_ref)
    average, inverse_std = norm_of(total, pixel_count)
    keep_norm(stats_ref, total, average, inverse_std)
    mover.send(stats_ref, stats_out)
    average, inverse_std = twice(average), twice(inverse_std)
    gain, shift = twice(norms_ref[index, 0:1]), twice(norms_ref[index, 1:2])
    taps_forward(weight_ref, taps_ref, width)
    clear_rim(shifts_ref, sizes)
    for pair in range(pairs):
        rows = pl.ds(pair * cols, cols)
        fired = fired_in_ref[rows, :].astype(jnp.float32)
        normed = (gain * ((fired - average) * inverse_std) + shift).astype(jnp.bfloat16)
        if residual:
            stream = stream_in_ref[rows, :] + normed.astype(jnp.float32)
            stream_ref[rows, :] = stream
            normed = stream.astype(jnp.bfloat16)
        source_ref[rows, :] = normed
        spread_pair(pair, normed.astype(jnp.float32), shifts_ref, sizes)
    mover.send(source_ref, source_out)
    if residual:
        mover.send(stream_ref, stream_out)
    conv_and_sums(flags_ref, shifts_ref, taps_ref, fired_ref, slope_ref, sums_ref, sizes)
    mover.finish()


def head_kernel(
    flags_ref, fired_ref, parts_ref, norms_ref, head_ref, stream_ref, fields_in, first_stats_in,
    grad_ref, sums_ref, stats_ref, head_grad_ref, fields_ref, first_stats_ref, top_ref, semaphores, *,
    sizes, pixel_count, sample_count, in_width, index,
):
    cols, width, pairs = sizes
    mover = Mover(semaphores)
    first_stats = mover.fetch(first_stats_in, first_stats_ref)
    fetched = mover.fetch(fields_in, fields_ref)
    total = total_of(parts_ref)
    average, inverse_std = norm_of(total, pixel_count)
    keep_norm(stats_ref, total, average, inverse_std)
    average, inverse_std = twice(average), twice(inverse_std)
    gain, shift = twice(norms_ref[index, 0:1]), twice(norms_ref[index, 1:2])
    head = head_ref[...]
    outs = 2
    lane_from = lax.broadcasted_iota(jnp.int32, (width, 2 * width), 0) - in_width
    lane_to = lax.broadcasted_iota(jnp.int32, (width, 2 * width), 1)
    within = lane_from - PIECES * lane_to
    picks = (within >= 0) & (within < PIECES) & (lane_to < outs)
    lane_to = lane_to - width
    weighs = (lane_from >= outs * PIECES) & (lane_from < (outs + 1) * PIECES)
    picks = picks | (weighs & (lane_to >= 0) & (lane_to < outs))
    picks = jnp.where(picks, 1.0, 0.0).astype(jnp.bfloat16)
    for pair in range(pairs):
        rows = pl.ds(pair * cols, cols)
        centred = (fired_ref[rows, :].astype(jnp.float32) - average) * inverse_std
        normed = (gain * centred + shift).astype(jnp.bfloat16)
        top_ref[rows, :] = (stream_ref[rows, :] + normed.astype(jnp.float32)).astype(jnp.bfloat16)
    first_stats[0].wait()
    loss_weight = first_stats_ref[2:3, :] / sample_count
    loss = jnp.zeros((1, width), jnp.float32)
    shift_grad = jnp.zeros((1, 2 * width), jnp.float32)
    gain_grad = jnp.zeros((1, 2 * width), jnp.float32)
    head_grad = jnp.zeros((width, width), jnp.float32)
    fetched[0].wait()
    step = GROUP * cols
    for group in range(pairs // GROUP):
        rows = pl.ds(group * step, step)
        for q in range(2):
            lanes = slice(q * width, (q + 1) * width)
            top = top_ref[rows, lanes]
            picked = dot(fields_ref[rows, lanes], picks)
            misfit, weight = dot(top, head) - picked[:, :width], picked[:, width:]
            loss += jnp.sum(weight * misfit * misfit, axis=0, keepdims=True)
            pred_grad = (2.0 * weight * misfit / loss_weight).astype(jnp.bfloat16)
            head_grad += dot(pred_grad, top, ((0,), (0,)))
            grad_ref[rows, lanes] = dot(pred_grad, head, ((1,), (1,)))
        low = grad_ref[rows, :].astype(jnp.bfloat16).astype(jnp.float32)
        centred = (fired_ref[rows, :].astype(jnp.float32) - average) * inverse_std
        shift_grad += jnp.sum(low, axis=0, keepdims=True)
        gain_grad += jnp.sum(low * centred, axis=0, keepdims=True)
    loss = jnp.broadcast_to(jnp.sum(loss, axis=1, keepdims=True), (1, width))
    head_grad_ref[...] = head_grad[0:outs]
    put_sums(sums_ref, [folded(shift_grad, width), folded(gain_grad, width), loss])


def back_to_preact(parts_ref, stats_ref, norms_ref, index, flags_ref, refs, pixel_count, sizes):
    grad_ref, fired_ref, slope_ref, pre_ref, pair_grad_ref, shifts_ref = refs
    cols, width, pairs = sizes
    total = total_of(parts_ref)
    shift_grad, gain_grad = total[0:1], total[1:2]
    pair_grad_ref[0:1, :] = gain_grad
    pair_grad_ref[1:2, :] = shift_grad
    average, inverse_std = twice(stats_ref[0:1, :]), twice(stats_ref[1:2, :])
    scaled = twice(norms_ref[index, 0:1]) * inverse_std * flags_ref[0].astype(jnp.float32)
    shift_mean, gain_mean = twice(shift_grad / pixel_count), twice(gain_grad / pixel_count)
    for pair in range(pairs):
        rows = pl.ds(pair * cols, cols)
        centred = (fired_ref[rows, :].astype(jnp.float32) - average) * inverse_std
        grad = grad_ref[rows, :].astype(jnp.bfloat16).astype(jnp.float32)
        fired_grad = (scaled * (grad - shift_mean - centred * gain_mean)).astype(jnp.bfloat16)
        pre = (fired_grad.astype(jnp.float32) * slope_ref[rows, :].astype(jnp.float32)).astype(jnp.bfloat16)
        pre_ref[rows, :] = pre
        spread_pair(pair, pre.astype(jnp.float32), shifts_ref, sizes)


def back_kernel(
    flags_ref, parts_ref, norms_ref, grad_ref, weight_ref, fired_ref, slope_ref, stats_ref, below_in, below_stats_in,
    *refs, sizes, pixel_count, index, second, top,
):
    cols, width, pairs = sizes
    if not second:
        kept_in, *refs = refs
    if top:
        head_grad_ref, *refs = refs
    pre_out, pair_grad_out, *refs = refs
    if second:
        kept_out, *refs = refs
    out_ref, sums_ref, *refs = refs
    if not second:
        kept_ref, *refs = refs
    below_ref, below_stats_ref, pre_ref, pair_grad_ref, shifts_ref, taps_ref, semaphores = refs
    mover = Mover(semaphores)
    groups = pairs // GROUP
    below_stats = mover.fetch(below_stats_in, below_stats_ref)
    below = mover.fetch(below_in, below_ref)
    if second:
        mover.send(grad_ref, kept_out)
    else:
        kept = mover.fetch(kept_in, kept_ref)
    clear_rim(shifts_ref, sizes)
    taps_backward(weight_ref, taps_ref, width)
    refs = (grad_ref, fired_ref, slope_ref, pre_ref, pair_grad_ref, shifts_ref)
    back_to_preact(parts_ref, stats_ref, norms_ref, index, flags_ref, refs, pixel_count, sizes)
    mover.send(pre_ref, pre_out)
    mover.send(pair_grad_ref, pair_grad_out)
    below_stats[0].wait()
    average, inverse_std = twice(below_stats_ref[0:1, :]), twice(below_stats_ref[1:2, :])
    shift_sum = jnp.zeros((1, 2 * width), jnp.float32)
    gain_sum = jnp.zeros((1, 2 * width), jnp.float32)
    step = GROUP * cols
    if not second:
        kept[0].wait()
    below[0].wait()
    for group in range(groups):
        rows = pl.ds(group * step, step)
        source = pair_conv(shifts_ref, taps_ref, group, cols, ((1,), (1,)))
        if not second:
            source = source + kept_ref[rows, :]
        out_ref[rows, :] = source.astype(out_ref.dtype)
        low = source.astype(jnp.bfloat16).astype(jnp.float32)
        shift_sum += jnp.sum(low, axis=0, keepdims=True)
        gain_sum += jnp.sum(low * ((below_ref[rows, :].astype(jnp.float32) - average) * inverse_std), axis=0, keepdims=True)
    active = flags_ref[0].astype(jnp.float32)
    sums = [folded(shift_sum, width) * active, folded(gain_sum, width) * active]
    put_sums(sums_ref, sums + ([head_grad_ref[...]] if top else []))
    mover.finish()


def cut_frames(flags_ref, flat_ref, mine_ref, theirs_ref, tiles, shard):
    width = flat_ref.shape[1]
    nl, no = tiles[0], tiles[1]
    rows = mine_ref.shape[2]
    for lon_step in range(no):
        for lat_step in range(nl):
            for core_step, target in ((0, mine_ref), (1, theirs_ref)):
                device = device_at(flags_ref, lon_step, lat_step, core_step, tiles)
                start = first_row(device, shard, width)
                target[lon_step, lat_step] = flat_ref[pl.ds(start, rows), :].astype(jnp.bfloat16)


def block_kernel_grad(shifts_ref, pre_ref, flat_ref, sizes):
    cols, width, pairs = sizes
    for a in range(4):
        k, rr = a // 2, a % 2
        block = shifts_ref[k * cols : (k + pairs) * cols, rr * 3 * width : (rr + 1) * 3 * width]
        grad = dot(block, pre_ref[...], ((0,), (0,)))
        if a < 3:
            flat_ref[a * 3 * width : (a + 1) * 3 * width, :] = grad[:, :width]
        if a > 0:
            flat_ref[(a - 1) * 3 * width : a * 3 * width, :] += grad[:, width:]


def kernel_grad_kernel(flags_ref, *refs, tiles, sizes, shard, fetches):
    fetched_from, refs = refs[:fetches], refs[fetches:]
    source_in, pre_in, *refs = refs
    fetched_to, refs = refs[:fetches], refs[fetches:]
    mine_out, theirs_ref, mine_ref, source_ref, pre_ref, shifts_ref, flat_ref, semaphores = refs
    mover = Mover(semaphores)
    source, pre = mover.fetch(source_in, source_ref), mover.fetch(pre_in, pre_ref)
    for wide, near in zip(fetched_from, fetched_to):
        mover.send(wide, near)
    clear_rim(shifts_ref, sizes)
    source[0].wait()
    spread_all_pairs(source_ref, shifts_ref, sizes)
    pre[0].wait()
    block_kernel_grad(shifts_ref, pre_ref, flat_ref, sizes)
    cut_frames(flags_ref, flat_ref, mine_ref, theirs_ref, tiles, shard)
    mover.send(mine_ref, mine_out)
    mover.finish()


def spread_all_pairs(source_ref, shifts_ref, sizes):
    cols, width, pairs = sizes
    for pair in range(pairs):
        cells = source_ref[pair * cols : (pair + 1) * cols, :].astype(jnp.float32)
        spread_pair(pair, cells, shifts_ref, sizes)


def last_kernel(
    flags_ref, parts_ref, norms_ref, grad_ref, fired_in, slope_in, stats_in, weight_in, kept_in, in_slope_in,
    source_in, wide_in, *refs, tiles, sizes, shards, in_width, pixel_count,
):
    cols, width, pairs = sizes
    nl, no = tiles[0], tiles[1]
    near_ins, refs = refs[:2], refs[2:]
    (
        pair_grad_out, mine_ref, theirs_ref,
        fired_ref, slope_ref, stats_ref, weight_ref, kept_ref, in_slope_ref, source_ref, wide_ref, pre_ref, in_pre_ref, pair_grad_ref,
        shifts_ref, first_shifts_ref, taps_ref, flat_ref, flat_first_ref, others_ref, semaphores,
    ) = refs
    mover = Mover(semaphores)
    groups = pairs // GROUP
    source = mover.fetch(source_in, source_ref)
    early = mover.fetch(stats_in, stats_ref) + mover.fetch(weight_in, weight_ref)
    early += mover.fetch(fired_in, fired_ref) + mover.fetch(slope_in, slope_ref)
    clear_rim(shifts_ref, sizes)
    clear_rim(first_shifts_ref, sizes)
    source[0].wait()
    spread_all_pairs(source_ref, first_shifts_ref, sizes)
    for arrival in early:
        arrival.wait()
    kept = mover.fetch(kept_in, kept_ref)
    in_slope = mover.fetch(in_slope_in, in_slope_ref)
    wide = mover.fetch(wide_in, wide_ref)
    arrivals = [mover.start(other, others_ref.at[i]) for i, other in enumerate(near_ins)]
    taps_backward(weight_ref, taps_ref, width)
    refs = (grad_ref, fired_ref, slope_ref, pre_ref, pair_grad_ref, shifts_ref)
    back_to_preact(parts_ref, stats_ref, norms_ref, 0, flags_ref, refs, pixel_count, sizes)
    mover.send(pair_grad_ref, pair_grad_out)
    kept[0].wait()
    in_slope[0].wait()
    step = GROUP * cols
    for group in range(groups):
        rows = pl.ds(group * step, step)
        grad = pair_conv(shifts_ref, taps_ref, group, cols, ((1,), (1,))) + kept_ref[rows, :]
        in_pre_ref[rows, :] = (grad * in_slope_ref[rows, :].astype(jnp.float32)).astype(jnp.bfloat16)
    block_kernel_grad(first_shifts_ref, pre_ref, flat_first_ref, sizes)
    for arrival in arrivals:
        arrival.wait()
    wide[0].wait()
    for a in range(8):
        k, rr = a // 2, a % 2
        block = wide_ref[k * cols : (k + pairs) * cols, rr * 7 * width : (rr + 1) * 7 * width]
        grads = dot(block, in_pre_ref[...], ((0,), (0,)))
        for b in range(7):
            grad = grads[b * width : b * width + in_width]
            if a < 7:
                tap = a * 7 + b
                flat_ref[tap * in_width : (tap + 1) * in_width, :] = grad[:, :width]
            if a > 0:
                tap = (a - 1) * 7 + b
                flat_ref[tap * in_width : (tap + 1) * in_width, :] += grad[:, width:]
    rows = others_ref.shape[3]
    in_rows = mine_ref.shape[2] - 2 * rows
    for lon_step in range(no):
        for lat_step in range(nl):
            for core_step, target in ((0, mine_ref), (1, theirs_ref)):
                device = device_at(flags_ref, lon_step, lat_step, core_step, tiles)
                spot = pl.ds(first_row(device, shards[0], width), in_rows)
                target[lon_step, lat_step, 0:in_rows, :] = flat_ref[spot, :].astype(jnp.bfloat16)
                spot = pl.ds(first_row(device, shards[1], width), rows)
                block = flat_first_ref[spot, :].astype(jnp.bfloat16)
                target[lon_step, lat_step, in_rows : in_rows + rows, :] = block
                at = in_rows + rows
                target[lon_step, lat_step, at : at + rows, :] = others_ref[core_step, lon_step, lat_step]
    mover.finish()


def join_kernel(flags_ref, *refs):
    *ins, joined_ref, frames_ref, semaphores = refs
    mover = Mover(semaphores)
    arrivals = [mover.start(frames, frames_ref.at[i]) for i, frames in enumerate(ins)]
    unused, no, nl, rows, unused = frames_ref.shape
    for index in range(len(ins) // 2):
        arrivals[2 * index].wait()
        arrivals[2 * index + 1].wait()
        for lon_step in range(no):
            for lat_step in range(nl):
                joined_ref[lat_step, lon_step, index * rows : (index + 1) * rows, :] = low_sum(
                    frames_ref[2 * index, lon_step, lat_step], frames_ref[2 * index + 1, lon_step, lat_step]
                )


def swap(values, axis, step):
    return lax.ppermute(values, axis, [(i, i ^ step) for i in range(lax.axis_size(axis))])


def low_sum(*values):
    return sum(part.astype(jnp.float32) for part in values).astype(jnp.bfloat16)


def along(values, axis):
    return [values[0]] + [swap(values[k], axis, k) for k in range(1, values.shape[0])]


def wide_sum(parts):
    return sum(part.astype(jnp.float32) for part in parts)


def spread_all(values, axes):
    return lax.all_to_all(values, axes, 0, 0, tiled=True)


def whole_sample_body(
    fields,
    targets,
    land_mask,
    input_kernel,
    input_first,
    input_second,
    block_kernels,
    block_first,
    block_second,
    head_weight,
    head_first,
    head_second,
    norm_params,
    norm_first,
    norm_second,
):
    samples_here, rows_here, cols_here, in_width = fields.shape
    width = norm_params.shape[2]
    conv_count = block_kernels.shape[0]
    nl, no, nb = (lax.axis_size(axis) for axis in ALL)
    places, devices = nl * no, nl * no * nb
    tiles = (nl, no, rows_here, cols_here)
    cols, pairs = cols_here * no, rows_here * nl // 2
    sizes = (cols, width, pairs)
    pixels = pairs * cols
    sample_count = samples_here * nb
    pixel_count = float(sample_count * 2 * pixels)
    place = lax.axis_index(TILE)
    core = lax.axis_index("batch")
    flags = jnp.stack(
        [
            (place < samples_here).astype(jnp.int32),
            lax.axis_index("batch"),
            lax.axis_index("lat"),
            lax.axis_index("lon"),
        ]
    )
    bf16, f32 = jnp.bfloat16, jnp.float32
    device = lax.axis_index(ALL)
    in_shard, block_shard = input_kernel.shape[0], block_kernels.shape[1]
    in_frame = frame_rows(in_shard, devices, width, SPREAD)
    block_frame = frame_rows(block_shard, devices, width, 8)
    in_offset = device * in_shard % width
    flat_rows = max((devices - 1) * in_shard // width + in_frame, 48 * in_width + width)
    flat_rows = -(-flat_rows // 8) * 8
    block_rows = block_shard // width

    def shard_rows(shards):
        count = shards.shape[0] * block_rows
        rows = shards.astype(bf16).reshape(count, width)
        return jnp.pad(rows, ((0, -count % SPREAD), (0, 0)))

    def from_all(values, axis, count):
        return [values] + [swap(values, axis, k) for k in range(1, count)]

    framed = lax.dynamic_update_slice(
        jnp.zeros((in_frame * width,), bf16), input_kernel.astype(bf16), (in_offset,)
    ).reshape(in_frame, width)
    near = jnp.concatenate([framed, shard_rows(block_kernels[:NEAR])], axis=0)
    near_rows = near.shape[0]
    both = jnp.stack(from_all(jnp.concatenate([near, shard_rows(block_kernels[NEAR:])], axis=0), "lat", nl))

    row_global = (lax.axis_index("lat") * rows_here + jnp.arange(rows_here)).astype(f32)
    latitude = (row_global + 0.5) / (rows_here * nl) * jnp.pi - jnp.pi / 2
    pixel_weight = jnp.cos(latitude)[None, :, None] * land_mask.astype(f32)
    (packed,) = call(
        functools.partial(pack_kernel, in_width=in_width),
        [(fields, VECTOR), (targets.transpose(3, 0, 1, 2), VECTOR), (pixel_weight, VECTOR)],
        [((places, rows_here, cols_here, width), bf16, VECTOR)],
        [pltpu.VMEM((-(-3 * PIECES * rows_here // 16) * 16, cols_here), f32)],
    )
    near, far = both[:, :near_rows], both[:, near_rows:]
    packed, near, far = lax.optimization_barrier((packed, near, far))
    near = from_all(near, "lon", no)
    packed = spread_all(packed, TILE)
    head_low = jnp.pad(head_weight.astype(bf16), ((0, 0), (0, width - head_weight.shape[1])))

    plane = (pixels, 2 * width)
    weight_shape = (9 * width, width)
    flat_weight = pltpu.VMEM((9 * width + block_frame + 8, width), f32)
    wide_shape = ((pairs + 3) * cols, 14 * width)
    shift_shape = ((pairs + 1) * cols, 6 * width)
    shift_scratch = pltpu.VMEM(shift_shape, bf16)
    forward_taps, backward_taps = (2, 6 * width, 2 * width), (2, 2 * width, 6 * width)
    def sums_shape(rows):
        return ((devices, rows, width), f32, VECTOR)

    stats_shape, pair_shape = (8, width), (2, width)
    frame_shape = (no, nl, block_frame, width)
    low_plane, wide_plane = pltpu.VMEM(plane, bf16), pltpu.VMEM(plane, f32)
    weight_scratch, stats_scratch = pltpu.VMEM(weight_shape, bf16), pltpu.VMEM(stats_shape, f32)
    pair_scratch = pltpu.VMEM(pair_shape, f32)
    unit_cost = 2 * 2 * pixels * 9 * width * width

    def kept_outs(*kinds):
        return [(shape, dtype, WIDE) for shape, dtype in kinds]

    far = from_all(far, "lon", no)
    near = [part for values in near for part in (values, swap(values, "batch", 1))]
    near_count, far_count = NEAR, conv_count - NEAR
    out = call(
        functools.partial(
            first_kernel, tiles=tiles, sizes=sizes, shards=[in_shard, block_rows], in_width=in_width, count=near_count
        ),
        [(part, VECTOR) for part in near] + [(packed, VECTOR)],
        kept_outs(*[(weight_shape, bf16)] * near_count, (plane, bf16), (plane, bf16), (plane, f32), (plane, bf16))
        + [(plane, bf16, VECTOR), (plane, bf16, VECTOR), sums_shape(4)],
        [flat_weight] * near_count
        + [low_plane, pltpu.VMEM((near_count, *weight_shape), bf16)]
        + [pltpu.VMEM((-(-near_count * block_rows // SPREAD) * SPREAD, width), f32)]
        + [pltpu.VMEM((4, 14 * width, 2 * width), bf16), pltpu.VMEM((flat_rows, width), f32)]
        + [pltpu.VMEM(wide_shape, bf16), low_plane, wide_plane, low_plane]
        + [shift_scratch, pltpu.VMEM(forward_taps, bf16)],
        flags,
        6 * unit_cost,
        LARGE_ROOM,
    )
    weights, out = list(out[:near_count]), out[near_count:]
    fields, in_slope, stream, source, fired, slope, sums = out
    far, sums = lax.optimization_barrier((far, sums))
    parts = spread_all(sums, ALL)
    far = [part for values in far for part in (values, swap(values, "batch", 1))]
    *far_weights, weight = call(
        functools.partial(far_kernels_kernel, tiles=tiles, block_rows=block_rows, count=far_count),
        [(part, WIDE) for part in far],
        kept_outs(*[(weight_shape, bf16)] * far_count) + [(weight_shape, bf16, VECTOR)],
        [pltpu.VMEM((len(far), *far[0].shape), bf16)]
        + [pltpu.VMEM((-(-far_count * block_rows // SPREAD) * SPREAD, width), f32)]
        + [flat_weight] * far_count
        + [pltpu.VMEM((far_count, *weight_shape), bf16)],
        flags,
        unit_cost,
    )
    weights += far_weights

    sources, fireds, slopes, stats = [source], [], [], []
    fetched = []
    for k in range(1, conv_count):
        residual = k % 2 == 0
        fetches = [weights[k + 1]] if k + 1 < conv_count else []
        if not residual:
            fetches.append(stream)
        out = call(
            functools.partial(
                unit_kernel, sizes=sizes, pixel_count=pixel_count, index=k - 1, residual=residual,
                fetches=len(fetches),
            ),
            [(array, VECTOR) for array in (fired, parts, norm_params, weight, slope, *fetched)]
            + [(array, WIDE) for array in fetches],
            kept_outs(*[(plane, f32)] * residual, (plane, bf16), (stats_shape, f32), (plane, bf16), (plane, bf16))
            + [(plane, bf16, VECTOR), (plane, bf16, VECTOR), sums_shape(2)]
            + [(array.shape, array.dtype, VECTOR) for array in fetches],
            [wide_plane] * residual
            + [low_plane, stats_scratch, shift_scratch, pltpu.VMEM(forward_taps, bf16)],
            flags,
            unit_cost,
        )
        if residual:
            stream, *out = out
        source, stat, saved_fired, saved_slope, fired, slope, sums, *fetched = out
        sources.append(source)
        stats.append(stat)
        fireds.append(saved_fired)
        slopes.append(saved_slope)
        if k + 1 < conv_count:
            weight, *fetched = fetched
        parts = spread_all(sums, ALL)

    (wide,) = call(
        functools.partial(wide_kernel, sizes=sizes),
        [(fields, WIDE)],
        kept_outs((wide_shape, bf16)),
        [low_plane, pltpu.VMEM(wide_shape, bf16)],
        flags,
        unit_cost,
        LARGE_ROOM,
    )
    wide, parts = lax.optimization_barrier((wide, parts))
    grad, sums, stat, head_local = call(
        functools.partial(
            head_kernel, sizes=sizes, pixel_count=pixel_count, sample_count=sample_count, in_width=in_width,
            index=conv_count - 1,
        ),
        [(array, VECTOR) for array in (fired, parts, norm_params, head_low, *fetched)]
        + [(fields, WIDE), (stats[0], WIDE)],
        [(plane, f32, VECTOR), sums_shape(4), (stats_shape, f32, VECTOR), ((2, width), f32, VECTOR)],
        [low_plane, stats_scratch, low_plane],
        flags,
        unit_cost // 4,
    )
    parts = spread_all(sums, ALL)
    loss_parts = parts

    pair_grads, frames = [None] * conv_count, [None] * conv_count
    for k in range(conv_count - 1, 0, -1):
        second, top = k % 2 == 1, k == conv_count - 1
        pre, pair_grads[k], *out = call(
            functools.partial(back_kernel, sizes=sizes, pixel_count=pixel_count, index=k, second=second, top=top),
            [(array, VECTOR) for array in (parts, norm_params, grad, weight, fired, slope, stat)]
            + [(array, WIDE) for array in (fireds[k - 1], stats[k - 1])]
            + [(array, WIDE) for array in (() if second else (kept_grad,))]
            + [(head_local, VECTOR)] * top,
            kept_outs((plane, bf16), (pair_shape, f32), *[(plane, f32)] * second)
            + [(plane, bf16 if second else f32, VECTOR), sums_shape(4 if top else 2)],
            [wide_plane] * (not second)
            + [low_plane, stats_scratch, low_plane, pair_scratch, shift_scratch, pltpu.VMEM(backward_taps, bf16)],
            flags,
            unit_cost,
        )
        if second:
            kept_grad, *out = out
        grad, sums = out
        parts = spread_all(sums, ALL)
        if top:
            head_parts = parts
        fetches = (weights[k - 1], fireds[k - 1], slopes[k - 1], stats[k - 1]) if k > 1 else ()
        *fetched, mine, theirs = call(
            functools.partial(
                kernel_grad_kernel, tiles=tiles, sizes=sizes, shard=block_shard, fetches=len(fetches)
            ),
            [(array, WIDE) for array in (*fetches, sources[k], pre)],
            [(array.shape, array.dtype, VECTOR) for array in fetches]
            + [(frame_shape, bf16, WIDE), (frame_shape, bf16, VECTOR)],
            [pltpu.VMEM(frame_shape, bf16), low_plane, low_plane, shift_scratch, flat_weight],
            flags,
            unit_cost,
        )
        frames[k] = [mine, theirs]
        if k > 1:
            weight, fired, slope, stat = fetched
        if k + 1 < conv_count:
            frames[k + 1][1] = swap(frames[k + 1][1], "batch", 1)
        if k == 1:
            others = [part for pair in frames[2:] for part in pair]
            (early,) = call(
                join_kernel,
                [(part, WIDE) for part in others],
                [((nl, no, (conv_count - 2) * block_frame, width), bf16, VECTOR)],
                [pltpu.VMEM((len(others), *frame_shape), bf16)],
                flags,
                unit_cost // 4,
            )
            parts, early, frames[1] = lax.optimization_barrier((parts, early, frames[1]))
            continue
        parts, frames[k:] = lax.optimization_barrier((parts, frames[k:]))
    pair_grads[0], mine, theirs = call(
        functools.partial(
            last_kernel, tiles=tiles, sizes=sizes, shards=[in_shard, block_shard], in_width=in_width,
            pixel_count=pixel_count,
        ),
        [(array, VECTOR) for array in (parts, norm_params, grad)]
        + [(array, WIDE) for array in (fireds[0], slopes[0], stats[0], weights[0])]
        + [(array, WIDE) for array in (kept_grad, in_slope, sources[0], wide, *frames[1])],
        kept_outs((pair_shape, f32))
        + [((no, nl, in_frame + 2 * block_frame, width), bf16, VECTOR)] * 2,
        [low_plane, low_plane, stats_scratch, weight_scratch, wide_plane, low_plane, low_plane]
        + [pltpu.VMEM(wide_shape, bf16), low_plane, low_plane]
        + [pair_scratch, shift_scratch, shift_scratch, pltpu.VMEM(backward_taps, bf16)]
        + [pltpu.VMEM((flat_rows, width), f32), flat_weight]
        + [pltpu.VMEM((2, *frame_shape), bf16)],
        flags,
        6 * unit_cost,
        LARGE_ROOM,
    )
    theirs, head_parts, loss_parts, first_stats = lax.optimization_barrier(
        (theirs, head_parts, loss_parts, stats[0])
    )
    late, early = lax.optimization_barrier((low_sum(mine, swap(theirs, "batch", 1)), early))
    late = along(late, "lon")
    early = along(early, "lat")
    norm_grad = jnp.stack(pair_grads)
    early, late = lax.optimization_barrier((early, late))
    early, late = low_sum(*early), low_sum(*late)
    early, late = wide_sum(along(early, "lon")), wide_sum(along(late, "lat"))
    input_grad = lax.dynamic_slice(late[:in_frame].reshape(-1), (in_offset,), (in_shard,))
    block_grad = jnp.concatenate([late[in_frame:], early], axis=0)
    block_grad = block_grad.reshape(conv_count, block_frame, width)[:, :block_rows]
    block_grad = block_grad.reshape(conv_count, block_shard)
    head_grad = jnp.sum(head_parts, axis=0)[2:4].T
    loss_sum = jnp.sum(loss_parts, axis=0)[2, 0]
    loss_weight = first_stats[2, 0] / sample_count
    return finished(
        loss_sum, loss_weight, input_grad, block_grad, head_grad, norm_grad,
        (input_kernel, input_first, input_second), (block_kernels, block_first, block_second),
        (head_weight, head_first, head_second), (norm_params, norm_first, norm_second),
    )


def one_device_takes_a_sample(fields, block_kernels, head_weight, norm_params):
    samples_here, rows_here, cols_here, in_width = fields.shape
    nl, no, nb = (lax.axis_size(axis) for axis in ALL)
    rows, cols, width = rows_here * nl, cols_here * no, norm_params.shape[2]
    return (
        samples_here <= nl * no
        and nb == 2
        and nl & (nl - 1) == 0
        and no & (no - 1) == 0
        and rows * cols <= MOST_PIXELS
        and rows % (2 * GROUP) == 0
        and cols % 128 == 0
        and cols_here % 8 == 0
        and width == 128
        and head_weight.shape[1] == 2
        and in_width + 3 * PIECES <= width
        and block_kernels.shape[1] % width == 0
        and block_kernels.shape[0] > NEAR
    )


def body(*args):
    fields, block_kernels, head_weight, norm_params = args[0], args[6], args[9], args[12]
    if one_device_takes_a_sample(fields, block_kernels, head_weight, norm_params):
        return whole_sample_body(*args)
    return tile_body(*args)


def solution(mesh):
    in_specs = (
        P("batch", "lat", "lon", None),
        P("batch", "lat", "lon", None),
        P("batch", "lat", "lon"),
        P(("lat", "lon", "batch")),
        P(("lat", "lon", "batch")),
        P(("lat", "lon", "batch")),
        P(None, ("lat", "lon", "batch")),
        P(None, ("lat", "lon", "batch")),
        P(None, ("lat", "lon", "batch")),
        P(),
        P(),
        P(),
        P(),
        P(),
        P(),
    )
    out_specs = (
        P(),
        P(),
        P(("lat", "lon", "batch")),
        P(("lat", "lon", "batch")),
        P(("lat", "lon", "batch")),
        P(None, ("lat", "lon", "batch")),
        P(None, ("lat", "lon", "batch")),
        P(None, ("lat", "lon", "batch")),
        P(),
        P(),
        P(),
        P(),
        P(),
        P(),
    )
    return jax.shard_map(body, mesh=mesh, in_specs=in_specs, out_specs=out_specs, check_vma=False)
```

```python
import functools

import jax
import jax.numpy as jnp
from jax import lax
from jax.experimental import pallas as pl
from jax.experimental.pallas import tpu as pltpu
from jax.sharding import PartitionSpec as P

STEP = 10


NORM_EPSILON = 1e-05
GELU_SCALE = 0.7978845608028654
GELU_CUBE = 0.044715
GROUP = 4

SMALL_ROOM = 14 << 20
LARGE_ROOM = 36 << 20
COPIES = 32
FORWARD, BACKWARD = 1, 2
NEAR = 1
MOST_PIXELS = 4096


def shortened(shard):

    def short(part):
        return part.astype(jnp.bfloat16) if part.dtype == jnp.float32 else part

    return jax.tree.map(short, shard)


def with_halo(cells, sides, width):
    for axis, dim in sides:
        count = lax.axis_size(axis)
        ends = count - 1
        head = lax.slice_in_dim(cells, 0, width, axis=dim)
        tail = lax.slice_in_dim(cells, cells.shape[dim] - width, cells.shape[dim], axis=dim)
        cells = jnp.concatenate(
            [
                lax.ppermute(tail, axis, [(i, (i + 1) % count) for i in range(ends)]),
                cells,
                lax.ppermute(head, axis, [((i + 1) % count, i) for i in range(ends)]),
            ],
            axis=dim,
        )
    return cells


def conv_valid(padded, kernel):
    return lax.conv_general_dilated(
        padded,
        kernel,
        (1, 1),
        "VALID",
        dimension_numbers=("NHWC", "HWIO", "NHWC"),
        preferred_element_type=jnp.float32,
    )


def kernel_grad(padded, gradient):
    summed = lax.conv_general_dilated(
        padded,
        gradient,
        (1, 1),
        "VALID",
        dimension_numbers=("CHWN", "IHWO", "NHWC"),
        preferred_element_type=jnp.float32,
    )
    return summed.transpose(1, 2, 0, 3)


def rim_cells(values):
    return with_halo(shortened(values), (("lat", 1), ("lon", 2)), 1).astype(values.dtype)


def to_channels(values):
    return jax.tree.map(
        lambda part, own: part.astype(own.dtype),
        lax.all_to_all(shortened(values), "lat", split_axis=3, concat_axis=0, tiled=True),
        values,
    )


def to_pixels(values):
    return lax.all_to_all(values, "lat", split_axis=0, concat_axis=3, tiled=True)


def spread_sums(summed, squares):
    return lax.psum((summed, squares), ("lon", "batch"))


def own_channels(norm_pair, width):
    return lax.dynamic_slice_in_dim(norm_pair, lax.axis_index("lat") * width, width, 1)


def norm_forward(fired, norm_pair, pixel_count):
    values = to_channels(fired)
    norm_pair = own_channels(norm_pair, values.shape[3])
    widened = values.astype(jnp.float32)
    summed, squares = spread_sums(
        jnp.sum(widened, axis=(0, 1, 2)), jnp.sum(widened * widened, axis=(0, 1, 2))
    )
    average = summed / pixel_count
    inverse_std = lax.rsqrt(squares / pixel_count - average * average + NORM_EPSILON)
    centred = (widened - average) * inverse_std
    normed = (norm_pair[0] * centred + norm_pair[1]).astype(jnp.bfloat16)
    normed = to_pixels(normed)
    return (normed, (centred, inverse_std, norm_pair))


def norm_backward(gradient, kept, pixel_count):
    centred, inverse_std, norm_pair = kept
    gradient = to_channels(gradient)
    widened = gradient.astype(jnp.float32)
    shift_grad, gain_grad = spread_sums(
        jnp.sum(widened, axis=(0, 1, 2)), jnp.sum(widened * centred, axis=(0, 1, 2))
    )
    scaled = norm_pair[0] * inverse_std
    fired_grad = (
        scaled * (widened - shift_grad / pixel_count - centred * gain_grad / pixel_count)
    ).astype(jnp.bfloat16)
    fired_grad = to_pixels(fired_grad)
    return (fired_grad, jnp.stack([gain_grad, shift_grad]))


def gelu_pullback(preact, gradient):
    unused, pullback = jax.vjp(jax.nn.gelu, preact)
    return pullback(gradient)[0]


def conv_forward(source, kernel, norm_pair, pixel_count):
    padded = rim_cells(source)
    preact = conv_valid(padded, kernel)
    fired = jax.nn.gelu(preact).astype(jnp.bfloat16)
    normed, kept = norm_forward(fired, norm_pair, pixel_count)
    return (normed, (padded, preact, kept))


def conv_backward(gradient, kernel, record, pixel_count):
    padded, preact, kept = record
    fired_grad, pair_grad = norm_backward(gradient, kept, pixel_count)
    preact_grad = gelu_pullback(preact, fired_grad.astype(jnp.float32)).astype(jnp.bfloat16)
    kernel_gradient = kernel_grad(padded, preact_grad)
    flipped = kernel[::-1, ::-1].transpose(0, 1, 3, 2)
    source_grad = conv_valid(rim_cells(preact_grad), flipped)
    return (source_grad, kernel_gradient, pair_grad)


def block_forward(stream, kernels, norm_pairs, pixel_count):
    middle, first_record = conv_forward(
        stream.astype(jnp.bfloat16), kernels[0], norm_pairs[0], pixel_count
    )
    branch, second_record = conv_forward(middle, kernels[1], norm_pairs[1], pixel_count)
    return (stream + branch.astype(jnp.float32), (first_record, second_record))


def block_backward(stream_grad, stream, kernels, norm_pairs, pixel_count):
    unused, records = block_forward(stream, kernels, norm_pairs, pixel_count)
    middle_grad, second_kernel, second_pair = conv_backward(
        stream_grad.astype(jnp.bfloat16), kernels[1], records[1], pixel_count
    )
    source_grad, first_kernel, first_pair = conv_backward(
        middle_grad.astype(jnp.bfloat16), kernels[0], records[0], pixel_count
    )
    return (stream_grad + source_grad, (first_kernel, second_kernel), (first_pair, second_pair))


def adamw_update(weight, gradient, momentum, variance, step_rate):
    momentum = 0.9 * momentum + 0.1 * gradient
    variance = 0.999 * variance + 0.001 * gradient * gradient
    corrected = momentum / (1.0 - 0.9**STEP)
    scaled = jnp.sqrt(variance / (1.0 - 0.999**STEP)) + 1e-08
    return (momentum, variance, weight - step_rate * (corrected / scaled + 0.01 * weight))


def finished(
    loss_sum, loss_weight, input_grad, block_grad, head_grad, norm_grad,
    input_state, block_state, head_state, norm_state,
):
    outputs = [jnp.reshape(loss_sum, (1,)), jnp.reshape(loss_weight, (1,))]
    for state, gradient, step_rate in (
        (input_state, input_grad, 0.015),
        (block_state, block_grad, 0.03),
        (head_state, head_grad, 0.15),
        (norm_state, norm_grad, 0.8),
    ):
        weight, first, second = state
        outputs.extend(adamw_update(weight, gradient, first, second, step_rate))
    return tuple(outputs)


def tile_body(
    fields,
    targets,
    land_mask,
    input_kernel,
    input_first,
    input_second,
    block_kernels,
    block_first,
    block_second,
    head_weight,
    head_first,
    head_second,
    norm_params,
    norm_first,
    norm_second,
):
    samples_here, rows_here, cols_here, in_width = fields.shape
    channels = norm_params.shape[2]
    conv_count = block_kernels.shape[0]
    full_input, full_blocks = (
        lax.all_gather(
            input_kernel.astype(jnp.bfloat16), ("lat", "lon", "batch"), axis=0, tiled=True
        ),
        lax.all_gather(
            block_kernels.astype(jnp.bfloat16), ("lat", "lon", "batch"), axis=1, tiled=True
        ),
    )
    kernel_in = full_input.reshape(7, 7, in_width, channels)
    kernels = full_blocks.reshape(conv_count, 3, 3, channels, channels)
    head_low = head_weight.astype(jnp.bfloat16)
    sample_count = samples_here * lax.axis_size("batch")
    pixel_count = float(
        sample_count * rows_here * lax.axis_size("lat") * cols_here * lax.axis_size("lon")
    )
    row_global = (lax.axis_index("lat") * rows_here + jnp.arange(rows_here)).astype(jnp.float32)
    latitude = (row_global + 0.5) / (rows_here * lax.axis_size("lat")) * jnp.pi - jnp.pi / 2
    pixel_weight = jnp.cos(latitude)[None, :, None] * land_mask.astype(jnp.float32)
    valid_sum = lax.psum(jnp.sum(pixel_weight), ("lat", "lon", "batch"))
    loss_weight = valid_sum / sample_count
    padded_in = with_halo(fields, (("lat", 1), ("lon", 2)), 3)
    preact_in = conv_valid(padded_in, kernel_in)
    streams = [jax.nn.gelu(preact_in)]
    for layer in range(conv_count // 2):
        advanced, unused = block_forward(
            streams[-1],
            kernels[2 * layer : 2 * layer + 2],
            norm_params[2 * layer : 2 * layer + 2],
            pixel_count,
        )
        streams.append(advanced)
    top_stream = streams[-1].astype(jnp.bfloat16)
    predicted = jnp.einsum(
        "nhwc,co->nhwo", top_stream, head_low, preferred_element_type=jnp.float32
    )
    misfit = predicted - targets
    loss_local = jnp.sum(pixel_weight[..., None] * misfit * misfit)
    pred_grad = (2.0 * pixel_weight[..., None] * misfit / loss_weight).astype(jnp.bfloat16)
    head_local = jnp.einsum(
        "nhwc,nhwo->co", top_stream, pred_grad, preferred_element_type=jnp.float32
    )
    stream_grad = jnp.einsum(
        "nhwo,co->nhwc", pred_grad, head_low, preferred_element_type=jnp.float32
    )
    kernel_grads = [None] * conv_count
    pair_grads = [None] * conv_count
    for layer in reversed(range(conv_count // 2)):
        stream_grad, kernel_pair, norm_pair = block_backward(
            stream_grad,
            streams[layer],
            kernels[2 * layer : 2 * layer + 2],
            norm_params[2 * layer : 2 * layer + 2],
            pixel_count,
        )
        kernel_grads[2 * layer], kernel_grads[2 * layer + 1] = kernel_pair
        pair_grads[2 * layer], pair_grads[2 * layer + 1] = norm_pair
    pre_in_grad = gelu_pullback(preact_in, stream_grad).astype(jnp.bfloat16)
    input_local = kernel_grad(padded_in, pre_in_grad).reshape(-1)
    block_local = jnp.stack(kernel_grads).reshape(conv_count, -1)
    input_grad, block_grad = (
        lax.psum_scatter(input_local, ("lat", "lon", "batch"), scatter_dimension=0, tiled=True),
        lax.psum_scatter(block_local, ("lat", "lon", "batch"), scatter_dimension=1, tiled=True),
    )
    head_grad, loss_sum = lax.psum((head_local, loss_local), ("lat", "lon", "batch"))
    norm_grad = jnp.stack(pair_grads)
    norm_grad = lax.all_gather(norm_grad, "lat", axis=2, tiled=True)
    return finished(
        loss_sum, loss_weight, input_grad, block_grad, head_grad, norm_grad,
        (input_kernel, input_first, input_second), (block_kernels, block_first, block_second),
        (head_weight, head_first, head_second), (norm_params, norm_first, norm_second),
    )


ALL = ("lat", "lon", "batch")
TILE = ("lat", "lon")
PIECES = 3
SPREAD = 16


VECTOR, WIDE = "vector", "wide"
SPACES = {VECTOR: pltpu.VMEM, WIDE: pltpu.HBM}


def call(kernel, ins, outs, scratch=(), flags=None, cost=0, room=SMALL_ROOM, aliases=()):
    specs = [pl.BlockSpec(memory_space=SPACES[space]) for unused, space in ins]
    args = [
        pltpu.with_memory_space_constraint(array, pltpu.HBM) if space == WIDE else array
        for array, space in ins
    ]
    if flags is not None:
        specs, args = [pl.BlockSpec(memory_space=pltpu.SMEM)] + specs, [flags] + args
    return pl.pallas_call(
        kernel,
        out_shape=[
            pltpu.HBM(shape, dtype) if space == WIDE else jax.ShapeDtypeStruct(shape, dtype)
            for shape, dtype, space in outs
        ],
        in_specs=specs,
        out_specs=[pl.BlockSpec(memory_space=SPACES[space]) for *unused, space in outs],
        scratch_shapes=list(scratch) + [pltpu.SemaphoreType.DMA((COPIES,))],
        input_output_aliases=dict(aliases),
        compiler_params=pltpu.CompilerParams(vmem_limit_bytes=room),
        cost_estimate=pl.CostEstimate(flops=cost, bytes_accessed=4 << 20, transcendentals=0),
    )(*args)


class Mover:
    def __init__(self, semaphores):
        self.semaphores, self.used, self.sent = semaphores, 0, []

    def start(self, source, target):
        copy = pltpu.make_async_copy(source, target, self.semaphores.at[self.used])
        self.used += 1
        copy.start()
        return copy

    def fetch(self, source, target, parts=1):
        step = target.shape[0] // parts
        return [
            self.start(source.at[pl.ds(i * step, step)], target.at[pl.ds(i * step, step)])
            for i in range(parts)
        ]

    def send(self, source, target):
        self.sent.append(self.start(source, target))

    def finish(self):
        for copy in self.sent:
            copy.wait()


def dot(left, right, dims=((1,), (0,))):
    return lax.dot_general(left, right, (dims, ((), ())), preferred_element_type=jnp.float32)


def gelu_value(x):
    return x * (0.5 * (1.0 + jnp.tanh(GELU_SCALE * (x + GELU_CUBE * (x * x * x)))))


def gelu_both(x):
    square = x * x
    level = jnp.tanh(GELU_SCALE * (x + GELU_CUBE * (x * square)))
    half = 0.5 * (1.0 + level)
    slope = half + 0.5 * x * (1.0 - level * level) * (GELU_SCALE * (1.0 + 3.0 * GELU_CUBE * square))
    return x * half, slope


def shifted(cells, step):
    count = cells.shape[0]
    if step == 0:
        return cells
    column = lax.broadcasted_iota(jnp.int32, cells.shape, 0) + step
    rolled = pltpu.roll(cells, (-step) % count, 0)
    return jnp.where((column >= 0) & (column < count), rolled, 0.0)


def spread_pair(pair, cells, shifts_ref, sizes):
    cols, width, pairs = sizes
    for b in range(3):
        moved = shifted(cells, b - 1).astype(jnp.bfloat16)
        shifts_ref[(pair + 1) * cols : (pair + 2) * cols, b * width : (b + 1) * width] = moved[:, width:]
        shifts_ref[pair * cols : (pair + 1) * cols, (3 + b) * width : (4 + b) * width] = moved[:, :width]


def clear_rim(shifts_ref, sizes):
    cols, width, pairs = sizes
    zero = jnp.zeros((cols, 3 * width), jnp.bfloat16)
    shifts_ref[0:cols, 0 : 3 * width] = zero
    shifts_ref[pairs * cols : (pairs + 1) * cols, 3 * width : 6 * width] = zero


def taps_forward(weight_ref, taps_ref, width):
    for k in range(2):
        for rr in range(2):
            for b in range(3):
                for q in range(2):
                    a = 2 * k + rr - q
                    at = (rr * 3 + b) * width
                    if 0 <= a <= 2:
                        block = weight_ref[(a * 3 + b) * width : (a * 3 + b + 1) * width, :]
                    else:
                        block = jnp.zeros((width, width), jnp.bfloat16)
                    taps_ref[k, at : at + width, q * width : (q + 1) * width] = block


def taps_backward(weight_ref, taps_ref, width):
    for k in range(2):
        for rr in range(2):
            for b in range(3):
                for q in range(2):
                    a = 2 - (2 * k + rr - q)
                    at = (rr * 3 + b) * width
                    if 0 <= a <= 2:
                        tap = a * 3 + 2 - b
                        block = weight_ref[tap * width : (tap + 1) * width, :]
                    else:
                        block = jnp.zeros((width, width), jnp.bfloat16)
                    taps_ref[k, q * width : (q + 1) * width, at : at + width] = block


def pair_conv(shifts_ref, taps_ref, group, cols, dims=((1,), (0,))):
    rows = GROUP * cols
    first = shifts_ref[group * rows : (group + 1) * rows, :]
    second = shifts_ref[group * rows + cols : (group + 1) * rows + cols, :]
    return dot(first, taps_ref[0], dims) + dot(second, taps_ref[1], dims)


def folded(sums, width):
    return sums[:, :width] + sums[:, width:]


def total_of(parts_ref):
    return jnp.sum(parts_ref[...], axis=0)


def twice(row):
    return jnp.concatenate([row, row], axis=1)


def norm_of(total, pixel_count):
    average = total[0:1] / pixel_count
    return average, lax.rsqrt(total[1:2] / pixel_count - average * average + NORM_EPSILON)


def conv_and_sums(flags_ref, shifts_ref, taps_ref, fired_ref, slope_ref, sums_ref, sizes, more=None):
    cols, width, pairs = sizes
    total = jnp.zeros((1, 2 * width), jnp.float32)
    squares = jnp.zeros((1, 2 * width), jnp.float32)
    step = GROUP * cols
    for group in range(pairs // GROUP):
        fired, slope = gelu_both(pair_conv(shifts_ref, taps_ref, group, cols))
        rows = pl.ds(group * step, step)
        fired = fired.astype(jnp.bfloat16)
        fired_ref[rows, :] = fired
        slope_ref[rows, :] = slope.astype(jnp.bfloat16)
        wide = fired.astype(jnp.float32)
        total = total + jnp.sum(wide, axis=0, keepdims=True)
        squares = squares + jnp.sum(wide * wide, axis=0, keepdims=True)
    active = flags_ref[0].astype(jnp.float32)
    parts = [folded(total, width) * active, folded(squares, width) * active]
    put_sums(sums_ref, parts + (more or []))


def put_sums(sums_ref, parts):
    shape = sums_ref.shape[1:]
    row = lax.broadcasted_iota(jnp.int32, shape, 0)
    block = jnp.zeros(shape, jnp.float32)
    at = 0
    for part in parts:
        for i in range(part.shape[0]):
            block = jnp.where(row == at, jnp.broadcast_to(part[i : i + 1], shape), block)
            at += 1
    sums_ref[...] = jnp.broadcast_to(block[None], sums_ref.shape)


def field_row(fields_ref, row, tiles):
    nl, no, rows_here, cols_here = tiles
    lat, inner = row // rows_here, row % rows_here
    return jnp.concatenate([fields_ref[lat * no + lon, inner] for lon in range(no)], axis=0)


def wide_shifts(row_of, shifts_ref, sizes):
    cols, width, pairs = sizes
    rows = 2 * pairs
    for row in range(-3, rows + 3):
        at, rr = (row + 3) // 2, (row + 3) % 2
        if 0 <= row < rows:
            cells = row_of(row).astype(jnp.float32)
        for b in range(7):
            if 0 <= row < rows:
                moved = shifted(cells, b - 3).astype(jnp.bfloat16)
            else:
                moved = jnp.zeros((cols, width), jnp.bfloat16)
            spot = (rr * 7 + b) * width
            shifts_ref[at * cols : (at + 1) * cols, spot : spot + width] = moved


def first_row(device, shard, width):
    return lax.div(device * shard, width)


def frame_rows(shard, devices, width, grain):
    rows = max(-(-(d + 1) * shard // width) - d * shard // width for d in range(devices))
    return -(-rows // grain) * grain


def device_at(flags_ref, lon_step, lat_step, core_step, tiles):
    lat = flags_ref[2] ^ lat_step
    lon = flags_ref[3] ^ lon_step
    return (lat * tiles[1] + lon) * 2 + (flags_ref[1] ^ core_step)


def pack_kernel(fields_ref, targets_ref, weights_ref, packed_ref, pieces_ref, unused_ref, *, in_width):
    samples, rows, cols, unused = fields_ref.shape
    width = packed_ref.shape[3]
    outs = targets_ref.shape[0]
    many = pieces_ref.shape[0]
    pieces_ref[...] = jnp.zeros(pieces_ref.shape, jnp.float32)
    packed_ref[samples:] = jnp.zeros((packed_ref.shape[0] - samples, rows, cols, width), jnp.bfloat16)
    take_from = lax.broadcasted_iota(jnp.int32, (many, width), 0)
    put_to = lax.broadcasted_iota(jnp.int32, (many, width), 1) - in_width
    picks = [
        jnp.where((put_to >= 0) & (take_from == put_to * rows + row), 1.0, 0.0).astype(jnp.bfloat16)
        for row in range(rows)
    ]
    for sample in range(samples):
        for source in range(outs + 1):
            left = targets_ref[source, sample] if source < outs else weights_ref[sample]
            for piece in range(PIECES):
                low = left.astype(jnp.bfloat16).astype(jnp.float32)
                left = left - low
                at = (source * PIECES + piece) * rows
                pieces_ref[at : at + rows, :] = low
        pieces = pieces_ref[...].astype(jnp.bfloat16)
        for row in range(rows):
            placed = dot(pieces, picks[row], ((0,), (0,))).astype(jnp.bfloat16)
            packed_ref[sample, row] = placed
            packed_ref[sample, row, :, 0:in_width] = fields_ref[sample, row]


def place_blocks(part, at, count, rows, device, stage_ref, flat_refs):
    stage_ref[...] = part[at : at + stage_ref.shape[0], :].astype(jnp.float32)
    for index in range(count):
        flat_refs[index][pl.ds(device * rows, rows), :] = stage_ref[index * rows : (index + 1) * rows, :]


def near_kernels(
    flags_ref, parts, taps_ref, flat_ref, stage_ref, flat_block_refs, tiles, shards, in_width
):
    nl, no = tiles[0], tiles[1]
    width = flat_ref.shape[1]
    in_shard, block_rows = shards
    rows = frame_rows(in_shard, 2 * nl * no, width, SPREAD)
    flat_ref[...] = jnp.zeros(flat_ref.shape, jnp.float32)
    for lon_step in range(no):
        for core_step in range(2):
            part = parts[lon_step * 2 + core_step]
            for lat_step in range(nl):
                device = device_at(flags_ref, lon_step, lat_step, core_step, tiles)
                spot = pl.ds(first_row(device, in_shard, width), rows)
                flat_ref[spot, :] += part[lat_step, 0:rows, :].astype(jnp.float32)
                place_blocks(
                    part.at[lat_step], rows, len(flat_block_refs), block_rows, device, stage_ref, flat_block_refs
                )
    inside = lax.broadcasted_iota(jnp.int32, (width, width), 0) < in_width
    zero = jnp.zeros((width, width), jnp.bfloat16)
    for b in range(7):
        taps_ref[3, (7 + b) * width : (8 + b) * width, 0:width] = zero
        taps_ref[0, b * width : (b + 1) * width, width : 2 * width] = zero
        for a in range(7):
            tap = a * 7 + b
            block = flat_ref[tap * in_width : tap * in_width + width, :]
            block = jnp.where(inside, block, 0.0).astype(jnp.bfloat16)
            for q in range(2):
                k, rr = (a + q) // 2, (a + q) % 2
                spot = (rr * 7 + b) * width
                taps_ref[k, spot : spot + width, q * width : (q + 1) * width] = block


def far_kernels_kernel(flags_ref, *refs, tiles, block_rows, count):
    nl, no = tiles[0], tiles[1]
    parts, outs, next_ref, refs = refs[: 2 * no], refs[2 * no : 2 * no + count], refs[2 * no + count], refs[2 * no + count + 1 :]
    stage_ref, *flat_refs, whole_ref, semaphores = refs
    mover = Mover(semaphores)
    for lon_step in range(no):
        for core_step in range(2):
            at = lon_step * 2 + core_step
            for lat_step in range(nl):
                device = device_at(flags_ref, lon_step, lat_step, core_step, tiles)
                place_blocks(parts[at].at[lat_step], 0, count, block_rows, device, stage_ref, flat_refs)
    for index in range(count):
        weight = flat_refs[index][0 : whole_ref.shape[1], :].astype(jnp.bfloat16)
        whole_ref[index] = weight
        if index == 0:
            next_ref[...] = weight
        mover.send(whole_ref.at[index], outs[index])
    mover.finish()


def first_kernel(flags_ref, *refs, tiles, sizes, shards, in_width, count):
    cols, width, pairs = sizes
    nl, no = tiles[0], tiles[1]
    near, refs = refs[: 2 * no], refs[2 * no :]
    fields_ref, *refs = refs
    weight_outs, refs = refs[:count], refs[count:]
    pairs_out, wide_out, slope_in_out, stream_out, source_out, fired_ref, slope_ref, sums_ref, *refs = refs
    flat_block_refs, refs = refs[:count], refs[count:]
    (
        pairs_ref, weights_ref, stage_ref, in_taps_ref, flat_ref, wide_ref,
        slope_in_ref, stream_ref, source_ref, shifts_ref, taps_ref, semaphores,
    ) = refs
    mover = Mover(semaphores)
    clear_rim(shifts_ref, sizes)

    def row_of(row):
        cells = field_row(fields_ref, row, tiles)
        pair, q = row // 2, row % 2
        pairs_ref[pair * cols : (pair + 1) * cols, q * width : (q + 1) * width] = cells
        return cells

    wide_shifts(row_of, wide_ref, sizes)
    mover.send(pairs_ref, pairs_out)
    mover.send(wide_ref, wide_out)
    near_kernels(
        flags_ref, near, in_taps_ref, flat_ref, stage_ref, flat_block_refs, tiles, shards, in_width
    )
    for index in range(count):
        weight = flat_block_refs[index][0 : weights_ref.shape[1], :].astype(jnp.bfloat16)
        weights_ref[index] = weight
        mover.send(weights_ref.at[index], weight_outs[index])
    taps_forward(weights_ref.at[0], taps_ref, width)
    step = GROUP * cols
    for group in range(pairs // GROUP):
        at = group * step
        preact = dot(wide_ref[at : at + step, :], in_taps_ref[0])
        for k in range(1, 4):
            preact += dot(wide_ref[at + k * cols : at + step + k * cols, :], in_taps_ref[k])
        rows = pl.ds(at, step)
        stream, slope = gelu_both(preact)
        slope_in_ref[rows, :] = slope.astype(jnp.bfloat16)
        mover.send(slope_in_ref.at[rows], slope_in_out.at[rows])
        stream_ref[rows, :] = stream
        mover.send(stream_ref.at[rows], stream_out.at[rows])
        source = stream.astype(jnp.bfloat16)
        source_ref[rows, :] = source
        mover.send(source_ref.at[rows], source_out.at[rows])
        for pair in range(GROUP):
            cells = source[pair * cols : (pair + 1) * cols].astype(jnp.float32)
            spread_pair(group * GROUP + pair, cells, shifts_ref, sizes)
    weight_sum = folded(jnp.sum(pairs_ref[...].astype(jnp.float32), axis=0, keepdims=True), width)
    lane = lax.broadcasted_iota(jnp.int32, (1, width), 1) - in_width
    chosen = (lane >= 2 * PIECES) & (lane < 3 * PIECES)
    weight_sum = jnp.sum(jnp.where(chosen, weight_sum, 0.0), axis=1, keepdims=True)
    conv_and_sums(
        flags_ref, shifts_ref, taps_ref, fired_ref, slope_ref, sums_ref, sizes,
        [jnp.broadcast_to(weight_sum, (1, width))],
    )
    mover.finish()


def keep_norm(stats_ref, total, average, inverse_std):
    stats_ref[0:1, :] = average
    stats_ref[1:2, :] = inverse_std
    if total.shape[0] > 2:
        stats_ref[2:3, :] = total[2:3]


def unit_kernel(
    flags_ref, fired_in_ref, parts_ref, norms_ref, weight_ref, slope_in_ref, *refs,
    sizes, pixel_count, index, residual, fetches,
):
    cols, width, pairs = sizes
    if residual:
        stream_in_ref, *refs = refs
    fetched_from, refs = refs[:fetches], refs[fetches:]
    if residual:
        stream_out, *refs = refs
    source_out, stats_out, fired_out, slope_out, fired_ref, slope_ref, sums_ref, *refs = refs
    fetched_to, refs = refs[:fetches], refs[fetches:]
    if residual:
        stream_ref, *refs = refs
    source_ref, stats_ref, shifts_ref, taps_ref, semaphores = refs
    mover = Mover(semaphores)
    mover.send(fired_in_ref, fired_out)
    mover.send(slope_in_ref, slope_out)
    for source, target in zip(fetched_from, fetched_to):
        mover.send(source, target)
    total = total_of(parts_ref)
    average, inverse_std = norm_of(total, pixel_count)
    keep_norm(stats_ref, total, average, inverse_std)
    mover.send(stats_ref, stats_out)
    average, inverse_std = twice(average), twice(inverse_std)
    gain, shift = twice(norms_ref[index, 0:1]), twice(norms_ref[index, 1:2])
    taps_forward(weight_ref, taps_ref, width)
    clear_rim(shifts_ref, sizes)
    for pair in range(pairs):
        rows = pl.ds(pair * cols, cols)
        fired = fired_in_ref[rows, :].astype(jnp.float32)
        normed = (gain * ((fired - average) * inverse_std) + shift).astype(jnp.bfloat16)
        if residual:
            stream = stream_in_ref[rows, :] + normed.astype(jnp.float32)
            stream_ref[rows, :] = stream
            normed = stream.astype(jnp.bfloat16)
        source_ref[rows, :] = normed
        spread_pair(pair, normed.astype(jnp.float32), shifts_ref, sizes)
    mover.send(source_ref, source_out)
    if residual:
        mover.send(stream_ref, stream_out)
    conv_and_sums(flags_ref, shifts_ref, taps_ref, fired_ref, slope_ref, sums_ref, sizes)
    mover.finish()


def head_kernel(
    flags_ref, fired_ref, parts_ref, norms_ref, head_ref, stream_ref, fields_in, first_stats_in, *refs,
    sizes, pixel_count, sample_count, in_width, index, fetches,
):
    cols, width, pairs = sizes
    fetched_from, refs = refs[:fetches], refs[fetches:]
    fetched_to, refs = refs[:fetches], refs[fetches:]
    grad_ref, sums_ref, stats_ref, head_grad_ref, fields_ref, first_stats_ref, top_ref, semaphores = refs
    mover = Mover(semaphores)
    first_stats = mover.fetch(first_stats_in, first_stats_ref)
    fetched = mover.fetch(fields_in, fields_ref)
    for source, target in zip(fetched_from, fetched_to):
        mover.send(source, target)
    total = total_of(parts_ref)
    average, inverse_std = norm_of(total, pixel_count)
    keep_norm(stats_ref, total, average, inverse_std)
    average, inverse_std = twice(average), twice(inverse_std)
    gain, shift = twice(norms_ref[index, 0:1]), twice(norms_ref[index, 1:2])
    outs = head_ref.shape[0]
    row = lax.broadcasted_iota(jnp.int32, (width, width), 0)
    head = jnp.zeros((width, width), jnp.float32)
    for out in range(outs):
        head = jnp.where(row == out, jnp.broadcast_to(head_ref[out : out + 1, :], head.shape), head)
    head = head.astype(jnp.bfloat16)
    lane_from = lax.broadcasted_iota(jnp.int32, (width, 2 * width), 0) - in_width
    lane_to = lax.broadcasted_iota(jnp.int32, (width, 2 * width), 1)
    within = lane_from - PIECES * lane_to
    picks = (within >= 0) & (within < PIECES) & (lane_to < outs)
    lane_to = lane_to - width
    weighs = (lane_from >= outs * PIECES) & (lane_from < (outs + 1) * PIECES)
    picks = picks | (weighs & (lane_to >= 0) & (lane_to < outs))
    picks = jnp.where(picks, 1.0, 0.0).astype(jnp.bfloat16)
    for pair in range(pairs):
        rows = pl.ds(pair * cols, cols)
        centred = (fired_ref[rows, :].astype(jnp.float32) - average) * inverse_std
        normed = (gain * centred + shift).astype(jnp.bfloat16)
        top_ref[rows, :] = (stream_ref[rows, :] + normed.astype(jnp.float32)).astype(jnp.bfloat16)
    first_stats[0].wait()
    loss_weight = first_stats_ref[2:3, :] / sample_count
    loss = jnp.zeros((1, width), jnp.float32)
    shift_grad = jnp.zeros((1, 2 * width), jnp.float32)
    gain_grad = jnp.zeros((1, 2 * width), jnp.float32)
    head_grad = jnp.zeros((width, width), jnp.float32)
    fetched[0].wait()
    step = GROUP * cols
    for group in range(pairs // GROUP):
        rows = pl.ds(group * step, step)
        for q in range(2):
            lanes = slice(q * width, (q + 1) * width)
            top = top_ref[rows, lanes]
            picked = dot(fields_ref[rows, lanes], picks)
            misfit, weight = dot(top, head, ((1,), (1,))) - picked[:, :width], picked[:, width:]
            loss += jnp.sum(weight * misfit * misfit, axis=0, keepdims=True)
            pred_grad = (2.0 * weight * misfit / loss_weight).astype(jnp.bfloat16)
            head_grad += dot(pred_grad, top, ((0,), (0,)))
            grad_ref[rows, lanes] = dot(pred_grad, head)
        low = grad_ref[rows, :].astype(jnp.bfloat16).astype(jnp.float32)
        centred = (fired_ref[rows, :].astype(jnp.float32) - average) * inverse_std
        shift_grad += jnp.sum(low, axis=0, keepdims=True)
        gain_grad += jnp.sum(low * centred, axis=0, keepdims=True)
    loss = jnp.broadcast_to(jnp.sum(loss, axis=1, keepdims=True), (1, width))
    head_grad_ref[...] = head_grad[0:outs]
    put_sums(sums_ref, [folded(shift_grad, width), folded(gain_grad, width), loss])
    mover.finish()


def back_to_preact(parts_ref, stats_ref, norms_ref, index, flags_ref, refs, pixel_count, sizes):
    grad_ref, fired_ref, slope_ref, pre_ref, pair_grad_ref, shifts_ref = refs
    cols, width, pairs = sizes
    total = total_of(parts_ref)
    shift_grad, gain_grad = total[0:1], total[1:2]
    pair_grad_ref[0:1, :] = gain_grad
    pair_grad_ref[1:2, :] = shift_grad
    average, inverse_std = twice(stats_ref[0:1, :]), twice(stats_ref[1:2, :])
    scaled = twice(norms_ref[index, 0:1]) * inverse_std * flags_ref[0].astype(jnp.float32)
    shift_mean, gain_mean = twice(shift_grad / pixel_count), twice(gain_grad / pixel_count)
    for pair in range(pairs):
        rows = pl.ds(pair * cols, cols)
        centred = (fired_ref[rows, :].astype(jnp.float32) - average) * inverse_std
        grad = grad_ref[rows, :].astype(jnp.bfloat16).astype(jnp.float32)
        fired_grad = (scaled * (grad - shift_mean - centred * gain_mean)).astype(jnp.bfloat16)
        pre = (fired_grad.astype(jnp.float32) * slope_ref[rows, :].astype(jnp.float32)).astype(jnp.bfloat16)
        pre_ref[rows, :] = pre
        spread_pair(pair, pre.astype(jnp.float32), shifts_ref, sizes)


def back_kernel(
    flags_ref, parts_ref, norms_ref, grad_ref, weight_ref, fired_ref, slope_ref, stats_ref, below_in, below_stats_in,
    *refs, sizes, pixel_count, index, second, top,
):
    cols, width, pairs = sizes
    if not second:
        kept_in, *refs = refs
    if top:
        head_grad_ref, *refs = refs
    pre_out, pair_grad_out, *refs = refs
    if second:
        kept_out, *refs = refs
    out_ref, sums_ref, *refs = refs
    if not second:
        kept_ref, *refs = refs
    below_ref, below_stats_ref, pre_ref, pair_grad_ref, shifts_ref, taps_ref, semaphores = refs
    mover = Mover(semaphores)
    groups = pairs // GROUP
    below_stats = mover.fetch(below_stats_in, below_stats_ref)
    below = mover.fetch(below_in, below_ref)
    if second:
        mover.send(grad_ref, kept_out)
    else:
        kept = mover.fetch(kept_in, kept_ref)
    clear_rim(shifts_ref, sizes)
    taps_backward(weight_ref, taps_ref, width)
    refs = (grad_ref, fired_ref, slope_ref, pre_ref, pair_grad_ref, shifts_ref)
    back_to_preact(parts_ref, stats_ref, norms_ref, index, flags_ref, refs, pixel_count, sizes)
    mover.send(pre_ref, pre_out)
    mover.send(pair_grad_ref, pair_grad_out)
    below_stats[0].wait()
    average, inverse_std = twice(below_stats_ref[0:1, :]), twice(below_stats_ref[1:2, :])
    shift_sum = jnp.zeros((1, 2 * width), jnp.float32)
    gain_sum = jnp.zeros((1, 2 * width), jnp.float32)
    step = GROUP * cols
    if not second:
        kept[0].wait()
    below[0].wait()
    for group in range(groups):
        rows = pl.ds(group * step, step)
        source = pair_conv(shifts_ref, taps_ref, group, cols, ((1,), (1,)))
        if not second:
            source = source + kept_ref[rows, :]
        out_ref[rows, :] = source.astype(out_ref.dtype)
        low = source.astype(jnp.bfloat16).astype(jnp.float32)
        shift_sum += jnp.sum(low, axis=0, keepdims=True)
        gain_sum += jnp.sum(low * ((below_ref[rows, :].astype(jnp.float32) - average) * inverse_std), axis=0, keepdims=True)
    active = flags_ref[0].astype(jnp.float32)
    sums = [folded(shift_sum, width) * active, folded(gain_sum, width) * active]
    put_sums(sums_ref, sums + ([head_grad_ref[...]] if top else []))
    mover.finish()


def cut_frames(flags_ref, flat_ref, mine_ref, theirs_ref, tiles, shard):
    width = flat_ref.shape[1]
    nl, no = tiles[0], tiles[1]
    rows = mine_ref.shape[2]
    for lon_step in range(no):
        for lat_step in range(nl):
            for core_step, target in ((0, mine_ref), (1, theirs_ref)):
                device = device_at(flags_ref, lon_step, lat_step, core_step, tiles)
                start = first_row(device, shard, width)
                target[lon_step, lat_step] = flat_ref[pl.ds(start, rows), :].astype(jnp.bfloat16)


def block_kernel_grad(shifts_ref, pre_ref, flat_ref, sizes):
    cols, width, pairs = sizes
    for a in range(4):
        k, rr = a // 2, a % 2
        block = shifts_ref[k * cols : (k + pairs) * cols, rr * 3 * width : (rr + 1) * 3 * width]
        grad = dot(block, pre_ref[...], ((0,), (0,)))
        if a < 3:
            flat_ref[a * 3 * width : (a + 1) * 3 * width, :] = grad[:, :width]
        if a > 0:
            flat_ref[(a - 1) * 3 * width : a * 3 * width, :] += grad[:, width:]


def kernel_grad_kernel(flags_ref, *refs, tiles, sizes, shard, fetches):
    fetched_from, refs = refs[:fetches], refs[fetches:]
    source_in, pre_in, *refs = refs
    fetched_to, refs = refs[:fetches], refs[fetches:]
    mine_out, theirs_ref, mine_ref, source_ref, pre_ref, shifts_ref, flat_ref, semaphores = refs
    mover = Mover(semaphores)
    source, pre = mover.fetch(source_in, source_ref), mover.fetch(pre_in, pre_ref)
    for wide, near in zip(fetched_from, fetched_to):
        mover.send(wide, near)
    clear_rim(shifts_ref, sizes)
    source[0].wait()
    spread_all_pairs(source_ref, shifts_ref, sizes)
    pre[0].wait()
    block_kernel_grad(shifts_ref, pre_ref, flat_ref, sizes)
    cut_frames(flags_ref, flat_ref, mine_ref, theirs_ref, tiles, shard)
    mover.send(mine_ref, mine_out)
    mover.finish()


def spread_all_pairs(source_ref, shifts_ref, sizes):
    cols, width, pairs = sizes
    for pair in range(pairs):
        cells = source_ref[pair * cols : (pair + 1) * cols, :].astype(jnp.float32)
        spread_pair(pair, cells, shifts_ref, sizes)


def last_kernel(
    flags_ref, parts_ref, norms_ref, grad_ref, fired_in, slope_in, stats_in, weight_in, kept_in, in_slope_in,
    source_in, wide_in, *refs, tiles, sizes, shards, in_width, pixel_count,
):
    cols, width, pairs = sizes
    nl, no = tiles[0], tiles[1]
    near_ins, refs = refs[:2], refs[2:]
    (
        pair_grad_out, mine_ref, theirs_ref,
        fired_ref, slope_ref, stats_ref, weight_ref, kept_ref, in_slope_ref, source_ref, wide_ref, pre_ref, in_pre_ref, pair_grad_ref,
        shifts_ref, first_shifts_ref, taps_ref, flat_ref, flat_first_ref, others_ref, semaphores,
    ) = refs
    mover = Mover(semaphores)
    groups = pairs // GROUP
    source = mover.fetch(source_in, source_ref)
    early = mover.fetch(stats_in, stats_ref) + mover.fetch(weight_in, weight_ref)
    early += mover.fetch(fired_in, fired_ref) + mover.fetch(slope_in, slope_ref)
    clear_rim(shifts_ref, sizes)
    clear_rim(first_shifts_ref, sizes)
    source[0].wait()
    spread_all_pairs(source_ref, first_shifts_ref, sizes)
    for arrival in early:
        arrival.wait()
    kept = mover.fetch(kept_in, kept_ref)
    in_slope = mover.fetch(in_slope_in, in_slope_ref)
    wide = mover.fetch(wide_in, wide_ref)
    arrivals = [mover.start(other, others_ref.at[i]) for i, other in enumerate(near_ins)]
    taps_backward(weight_ref, taps_ref, width)
    refs = (grad_ref, fired_ref, slope_ref, pre_ref, pair_grad_ref, shifts_ref)
    back_to_preact(parts_ref, stats_ref, norms_ref, 0, flags_ref, refs, pixel_count, sizes)
    mover.send(pair_grad_ref, pair_grad_out)
    kept[0].wait()
    in_slope[0].wait()
    step = GROUP * cols
    for group in range(groups):
        rows = pl.ds(group * step, step)
        grad = pair_conv(shifts_ref, taps_ref, group, cols, ((1,), (1,))) + kept_ref[rows, :]
        in_pre_ref[rows, :] = (grad * in_slope_ref[rows, :].astype(jnp.float32)).astype(jnp.bfloat16)
    block_kernel_grad(first_shifts_ref, pre_ref, flat_first_ref, sizes)
    for arrival in arrivals:
        arrival.wait()
    wide[0].wait()
    for a in range(8):
        k, rr = a // 2, a % 2
        block = wide_ref[k * cols : (k + pairs) * cols, rr * 7 * width : (rr + 1) * 7 * width]
        grads = dot(block, in_pre_ref[...], ((0,), (0,)))
        for b in range(7):
            grad = grads[b * width : b * width + in_width]
            if a < 7:
                tap = a * 7 + b
                flat_ref[tap * in_width : (tap + 1) * in_width, :] = grad[:, :width]
            if a > 0:
                tap = (a - 1) * 7 + b
                flat_ref[tap * in_width : (tap + 1) * in_width, :] += grad[:, width:]
    rows = others_ref.shape[3]
    in_rows = mine_ref.shape[2] - 2 * rows
    for lon_step in range(no):
        for lat_step in range(nl):
            for core_step, target in ((0, mine_ref), (1, theirs_ref)):
                device = device_at(flags_ref, lon_step, lat_step, core_step, tiles)
                spot = pl.ds(first_row(device, shards[0], width), in_rows)
                target[lon_step, lat_step, 0:in_rows, :] = flat_ref[spot, :].astype(jnp.bfloat16)
                spot = pl.ds(first_row(device, shards[1], width), rows)
                block = flat_first_ref[spot, :].astype(jnp.bfloat16)
                target[lon_step, lat_step, in_rows : in_rows + rows, :] = block
                at = in_rows + rows
                target[lon_step, lat_step, at : at + rows, :] = others_ref[core_step, lon_step, lat_step]
    mover.finish()


def join_kernel(flags_ref, *refs):
    *ins, joined_ref, frames_ref, semaphores = refs
    mover = Mover(semaphores)
    arrivals = [mover.start(frames, frames_ref.at[i]) for i, frames in enumerate(ins)]
    unused, no, nl, rows, unused = frames_ref.shape
    for index in range(len(ins) // 2):
        arrivals[2 * index].wait()
        arrivals[2 * index + 1].wait()
        for lon_step in range(no):
            for lat_step in range(nl):
                joined_ref[lat_step, lon_step, index * rows : (index + 1) * rows, :] = low_sum(
                    frames_ref[2 * index, lon_step, lat_step], frames_ref[2 * index + 1, lon_step, lat_step]
                )


def swap(values, axis, step):
    return lax.ppermute(values, axis, [(i, i ^ step) for i in range(lax.axis_size(axis))])


def low_sum(*values):
    return sum(part.astype(jnp.float32) for part in values).astype(jnp.bfloat16)


def along(values, axis):
    return [values[0]] + [swap(values[k], axis, k) for k in range(1, values.shape[0])]


def wide_sum(parts):
    return sum(part.astype(jnp.float32) for part in parts)


def spread_all(values, axes):
    return lax.all_to_all(values, axes, 0, 0, tiled=True)


def whole_sample_body(
    fields,
    targets,
    land_mask,
    input_kernel,
    input_first,
    input_second,
    block_kernels,
    block_first,
    block_second,
    head_weight,
    head_first,
    head_second,
    norm_params,
    norm_first,
    norm_second,
):
    samples_here, rows_here, cols_here, in_width = fields.shape
    width = norm_params.shape[2]
    conv_count = block_kernels.shape[0]
    nl, no, nb = (lax.axis_size(axis) for axis in ALL)
    places, devices = nl * no, nl * no * nb
    tiles = (nl, no, rows_here, cols_here)
    cols, pairs = cols_here * no, rows_here * nl // 2
    sizes = (cols, width, pairs)
    pixels = pairs * cols
    sample_count = samples_here * nb
    pixel_count = float(sample_count * 2 * pixels)
    place = lax.axis_index(TILE)
    core = lax.axis_index("batch")
    flags = jnp.stack(
        [
            (place < samples_here).astype(jnp.int32),
            lax.axis_index("batch"),
            lax.axis_index("lat"),
            lax.axis_index("lon"),
        ]
    )
    bf16, f32 = jnp.bfloat16, jnp.float32
    device = lax.axis_index(ALL)
    in_shard, block_shard = input_kernel.shape[0], block_kernels.shape[1]
    in_frame = frame_rows(in_shard, devices, width, SPREAD)
    block_frame = frame_rows(block_shard, devices, width, 8)
    in_offset = device * in_shard % width
    flat_rows = max((devices - 1) * in_shard // width + in_frame, 48 * in_width + width)
    flat_rows = -(-flat_rows // 8) * 8
    block_rows = block_shard // width

    def shard_rows(shards):
        count = shards.shape[0] * block_rows
        rows = shards.astype(bf16).reshape(count, width)
        return jnp.pad(rows, ((0, -count % SPREAD), (0, 0)))

    def from_all(values, axis, count):
        return [values] + [swap(values, axis, k) for k in range(1, count)]

    framed = lax.dynamic_update_slice(
        jnp.zeros((in_frame * width,), bf16), input_kernel.astype(bf16), (in_offset,)
    ).reshape(in_frame, width)
    near = jnp.concatenate([framed, shard_rows(block_kernels[:NEAR])], axis=0)
    near_rows = near.shape[0]
    both = jnp.stack(from_all(jnp.concatenate([near, shard_rows(block_kernels[NEAR:])], axis=0), "lat", nl))

    row_global = (lax.axis_index("lat") * rows_here + jnp.arange(rows_here)).astype(f32)
    latitude = (row_global + 0.5) / (rows_here * nl) * jnp.pi - jnp.pi / 2
    pixel_weight = jnp.cos(latitude)[None, :, None] * land_mask.astype(f32)
    (packed,) = call(
        functools.partial(pack_kernel, in_width=in_width),
        [(fields, VECTOR), (targets.transpose(3, 0, 1, 2), VECTOR), (pixel_weight, VECTOR)],
        [((places, rows_here, cols_here, width), bf16, VECTOR)],
        [pltpu.VMEM((-(-3 * PIECES * rows_here // 16) * 16, cols_here), f32)],
    )
    near, far = both[:, :near_rows], both[:, near_rows:]
    packed, near, far = lax.optimization_barrier((packed, near, far))
    near = from_all(near, "lon", no)
    packed = spread_all(packed, TILE)

    plane = (pixels, 2 * width)
    weight_shape = (9 * width, width)
    flat_weight = pltpu.VMEM((9 * width + block_frame + 8, width), f32)
    wide_shape = ((pairs + 3) * cols, 14 * width)
    shift_shape = ((pairs + 1) * cols, 6 * width)
    shift_scratch = pltpu.VMEM(shift_shape, bf16)
    forward_taps, backward_taps = (2, 6 * width, 2 * width), (2, 2 * width, 6 * width)
    def sums_shape(rows):
        return ((devices, rows, width), f32, VECTOR)

    stats_shape, pair_shape = (8, width), (2, width)
    frame_shape = (no, nl, block_frame, width)
    low_plane, wide_plane = pltpu.VMEM(plane, bf16), pltpu.VMEM(plane, f32)
    weight_scratch, stats_scratch = pltpu.VMEM(weight_shape, bf16), pltpu.VMEM(stats_shape, f32)
    pair_scratch = pltpu.VMEM(pair_shape, f32)
    unit_cost = 2 * 2 * pixels * 9 * width * width

    def kept_outs(*kinds):
        return [(shape, dtype, WIDE) for shape, dtype in kinds]

    far = from_all(far, "lon", no)
    near = [part for values in near for part in (values, swap(values, "batch", 1))]
    near_count, far_count = NEAR, conv_count - NEAR
    out = call(
        functools.partial(
            first_kernel, tiles=tiles, sizes=sizes, shards=[in_shard, block_rows], in_width=in_width, count=near_count
        ),
        [(part, VECTOR) for part in near] + [(packed, VECTOR)],
        kept_outs(*[(weight_shape, bf16)] * near_count, (plane, bf16), (wide_shape, bf16), (plane, bf16), (plane, f32), (plane, bf16))
        + [(plane, bf16, VECTOR), (plane, bf16, VECTOR), sums_shape(4)],
        [flat_weight] * near_count
        + [low_plane, pltpu.VMEM((near_count, *weight_shape), bf16)]
        + [pltpu.VMEM((-(-near_count * block_rows // SPREAD) * SPREAD, width), f32)]
        + [pltpu.VMEM((4, 14 * width, 2 * width), bf16), pltpu.VMEM((flat_rows, width), f32)]
        + [pltpu.VMEM(wide_shape, bf16), low_plane, wide_plane, low_plane]
        + [shift_scratch, pltpu.VMEM(forward_taps, bf16)],
        flags,
        6 * unit_cost,
        LARGE_ROOM,
    )
    weights, out = list(out[:near_count]), out[near_count:]
    fields, wide, in_slope, stream, source, fired, slope, sums = out
    far, sums = lax.optimization_barrier((far, sums))
    parts = spread_all(sums, ALL)
    far = [part for values in far for part in (values, swap(values, "batch", 1))]
    *far_weights, weight = call(
        functools.partial(far_kernels_kernel, tiles=tiles, block_rows=block_rows, count=far_count),
        [(part, VECTOR) for part in far],
        kept_outs(*[(weight_shape, bf16)] * far_count) + [(weight_shape, bf16, VECTOR)],
        [pltpu.VMEM((-(-far_count * block_rows // SPREAD) * SPREAD, width), f32)]
        + [flat_weight] * far_count
        + [pltpu.VMEM((far_count, *weight_shape), bf16)],
        flags,
        unit_cost,
    )
    weights += far_weights

    sources, fireds, slopes, stats = [source], [], [], []
    fetched = []
    for k in range(1, conv_count):
        residual = k % 2 == 0
        fetches = [weights[k + 1]] if k + 1 < conv_count else []
        if not residual:
            fetches.append(stream)
        out = call(
            functools.partial(
                unit_kernel, sizes=sizes, pixel_count=pixel_count, index=k - 1, residual=residual,
                fetches=len(fetches),
            ),
            [(array, VECTOR) for array in (fired, parts, norm_params, weight, slope, *fetched)]
            + [(array, WIDE) for array in fetches],
            kept_outs(*[(plane, f32)] * residual, (plane, bf16), (stats_shape, f32), (plane, bf16), (plane, bf16))
            + [(plane, bf16, VECTOR), (plane, bf16, VECTOR), sums_shape(2)]
            + [(array.shape, array.dtype, VECTOR) for array in fetches],
            [wide_plane] * residual
            + [low_plane, stats_scratch, shift_scratch, pltpu.VMEM(forward_taps, bf16)],
            flags,
            unit_cost,
        )
        if residual:
            stream, *out = out
        source, stat, saved_fired, saved_slope, fired, slope, sums, *fetched = out
        sources.append(source)
        stats.append(stat)
        fireds.append(saved_fired)
        slopes.append(saved_slope)
        if k + 1 < conv_count:
            weight, *fetched = fetched
        parts = spread_all(sums, ALL)

    grad, sums, stat, head_local = call(
        functools.partial(
            head_kernel, sizes=sizes, pixel_count=pixel_count, sample_count=sample_count, in_width=in_width,
            index=conv_count - 1, fetches=0,
        ),
        [(array, VECTOR) for array in (fired, parts, norm_params, head_weight.T, *fetched)]
        + [(array, WIDE) for array in (fields, stats[0])],
        [(plane, f32, VECTOR), sums_shape(4), (stats_shape, f32, VECTOR), (head_weight.T.shape, f32, VECTOR)],
        [low_plane, stats_scratch, low_plane],
        flags,
        unit_cost // 4,
    )
    parts = spread_all(sums, ALL)
    loss_parts = parts

    pair_grads, frames = [None] * conv_count, [None] * conv_count
    for k in range(conv_count - 1, 0, -1):
        second, top = k % 2 == 1, k == conv_count - 1
        pre, pair_grads[k], *out = call(
            functools.partial(back_kernel, sizes=sizes, pixel_count=pixel_count, index=k, second=second, top=top),
            [(array, VECTOR) for array in (parts, norm_params, grad, weight, fired, slope, stat)]
            + [(array, WIDE) for array in (fireds[k - 1], stats[k - 1])]
            + [(array, WIDE) for array in (() if second else (kept_grad,))]
            + [(head_local, VECTOR)] * top,
            kept_outs((plane, bf16), (pair_shape, f32), *[(plane, f32)] * second)
            + [(plane, bf16 if second else f32, VECTOR), sums_shape(4 if top else 2)],
            [wide_plane] * (not second)
            + [low_plane, stats_scratch, low_plane, pair_scratch, shift_scratch, pltpu.VMEM(backward_taps, bf16)],
            flags,
            unit_cost,
        )
        if second:
            kept_grad, *out = out
        grad, sums = out
        parts = spread_all(sums, ALL)
        if top:
            head_parts = parts
        fetches = (weights[k - 1], fireds[k - 1], slopes[k - 1], stats[k - 1]) if k > 1 else ()
        *fetched, mine, theirs = call(
            functools.partial(
                kernel_grad_kernel, tiles=tiles, sizes=sizes, shard=block_shard, fetches=len(fetches)
            ),
            [(array, WIDE) for array in (*fetches, sources[k], pre)],
            [(array.shape, array.dtype, VECTOR) for array in fetches]
            + [(frame_shape, bf16, WIDE), (frame_shape, bf16, VECTOR)],
            [pltpu.VMEM(frame_shape, bf16), low_plane, low_plane, shift_scratch, flat_weight],
            flags,
            unit_cost,
        )
        frames[k] = [mine, theirs]
        if k > 1:
            weight, fired, slope, stat = fetched
        if k + 1 < conv_count:
            frames[k + 1][1] = swap(frames[k + 1][1], "batch", 1)
        if k == 1:
            others = [part for pair in frames[2:] for part in pair]
            (early,) = call(
                join_kernel,
                [(part, WIDE) for part in others],
                [((nl, no, (conv_count - 2) * block_frame, width), bf16, VECTOR)],
                [pltpu.VMEM((len(others), *frame_shape), bf16)],
                flags,
                unit_cost // 4,
            )
            parts, early, frames[1] = lax.optimization_barrier((parts, early, frames[1]))
            continue
        parts, frames[k:] = lax.optimization_barrier((parts, frames[k:]))
    pair_grads[0], mine, theirs = call(
        functools.partial(
            last_kernel, tiles=tiles, sizes=sizes, shards=[in_shard, block_shard], in_width=in_width,
            pixel_count=pixel_count,
        ),
        [(array, VECTOR) for array in (parts, norm_params, grad)]
        + [(array, WIDE) for array in (fireds[0], slopes[0], stats[0], weights[0])]
        + [(array, WIDE) for array in (kept_grad, in_slope, sources[0], wide, *frames[1])],
        kept_outs((pair_shape, f32))
        + [((no, nl, in_frame + 2 * block_frame, width), bf16, VECTOR)] * 2,
        [low_plane, low_plane, stats_scratch, weight_scratch, wide_plane, low_plane, low_plane]
        + [pltpu.VMEM(wide_shape, bf16), low_plane, low_plane]
        + [pair_scratch, shift_scratch, shift_scratch, pltpu.VMEM(backward_taps, bf16)]
        + [pltpu.VMEM((flat_rows, width), f32), flat_weight]
        + [pltpu.VMEM((2, *frame_shape), bf16)],
        flags,
        6 * unit_cost,
        LARGE_ROOM,
    )
    theirs, head_parts, loss_parts, first_stats = lax.optimization_barrier(
        (theirs, head_parts, loss_parts, stats[0])
    )
    late, early = lax.optimization_barrier((low_sum(mine, swap(theirs, "batch", 1)), early))
    late = along(late, "lon")
    early = along(early, "lat")
    norm_grad = jnp.stack(pair_grads)
    early, late = lax.optimization_barrier((early, late))
    early, late = low_sum(*early), low_sum(*late)
    early, late = wide_sum(along(early, "lon")), wide_sum(along(late, "lat"))
    input_grad = lax.dynamic_slice(late[:in_frame].reshape(-1), (in_offset,), (in_shard,))
    block_grad = jnp.concatenate([late[in_frame:], early], axis=0)
    block_grad = block_grad.reshape(conv_count, block_frame, width)[:, :block_rows]
    block_grad = block_grad.reshape(conv_count, block_shard)
    head_grad = jnp.sum(head_parts, axis=0)[2:4].T
    loss_sum = jnp.sum(loss_parts, axis=0)[2, 0]
    loss_weight = first_stats[2, 0] / sample_count
    return finished(
        loss_sum, loss_weight, input_grad, block_grad, head_grad, norm_grad,
        (input_kernel, input_first, input_second), (block_kernels, block_first, block_second),
        (head_weight, head_first, head_second), (norm_params, norm_first, norm_second),
    )


def one_device_takes_a_sample(fields, block_kernels, head_weight, norm_params):
    samples_here, rows_here, cols_here, in_width = fields.shape
    nl, no, nb = (lax.axis_size(axis) for axis in ALL)
    rows, cols, width = rows_here * nl, cols_here * no, norm_params.shape[2]
    return (
        samples_here <= nl * no
        and nb == 2
        and nl & (nl - 1) == 0
        and no & (no - 1) == 0
        and rows * cols <= MOST_PIXELS
        and rows % (2 * GROUP) == 0
        and cols % 128 == 0
        and cols_here % 8 == 0
        and width == 128
        and head_weight.shape[1] == 2
        and in_width + 3 * PIECES <= width
        and block_kernels.shape[1] % width == 0
        and block_kernels.shape[0] > NEAR
    )


def body(*args):
    fields, block_kernels, head_weight, norm_params = args[0], args[6], args[9], args[12]
    if one_device_takes_a_sample(fields, block_kernels, head_weight, norm_params):
        return whole_sample_body(*args)
    return tile_body(*args)


def solution(mesh):
    in_specs = (
        P("batch", "lat", "lon", None),
        P("batch", "lat", "lon", None),
        P("batch", "lat", "lon"),
        P(("lat", "lon", "batch")),
        P(("lat", "lon", "batch")),
        P(("lat", "lon", "batch")),
        P(None, ("lat", "lon", "batch")),
        P(None, ("lat", "lon", "batch")),
        P(None, ("lat", "lon", "batch")),
        P(),
        P(),
        P(),
        P(),
        P(),
        P(),
    )
    out_specs = (
        P(),
        P(),
        P(("lat", "lon", "batch")),
        P(("lat", "lon", "batch")),
        P(("lat", "lon", "batch")),
        P(None, ("lat", "lon", "batch")),
        P(None, ("lat", "lon", "batch")),
        P(None, ("lat", "lon", "batch")),
        P(),
        P(),
        P(),
        P(),
        P(),
        P(),
    )
    return jax.shard_map(body, mesh=mesh, in_specs=in_specs, out_specs=out_specs, check_vma=False)
```

```python
import functools

import jax
import jax.numpy as jnp
from jax import lax
from jax.experimental import pallas as pl
from jax.experimental.pallas import tpu as pltpu
from jax.sharding import PartitionSpec as P

STEP = 10


NORM_EPSILON = 1e-05
GELU_SCALE = 0.7978845608028654
GELU_CUBE = 0.044715
GROUP = 4

SMALL_ROOM = 14 << 20
LARGE_ROOM = 36 << 20
COPIES = 32
FORWARD, BACKWARD = 1, 2
NEAR = 1
MOST_PIXELS = 4096


def shortened(shard):

    def short(part):
        return part.astype(jnp.bfloat16) if part.dtype == jnp.float32 else part

    return jax.tree.map(short, shard)


def with_halo(cells, sides, width):
    for axis, dim in sides:
        count = lax.axis_size(axis)
        ends = count - 1
        head = lax.slice_in_dim(cells, 0, width, axis=dim)
        tail = lax.slice_in_dim(cells, cells.shape[dim] - width, cells.shape[dim], axis=dim)
        cells = jnp.concatenate(
            [
                lax.ppermute(tail, axis, [(i, (i + 1) % count) for i in range(ends)]),
                cells,
                lax.ppermute(head, axis, [((i + 1) % count, i) for i in range(ends)]),
            ],
            axis=dim,
        )
    return cells


def conv_valid(padded, kernel):
    return lax.conv_general_dilated(
        padded,
        kernel,
        (1, 1),
        "VALID",
        dimension_numbers=("NHWC", "HWIO", "NHWC"),
        preferred_element_type=jnp.float32,
    )


def kernel_grad(padded, gradient):
    summed = lax.conv_general_dilated(
        padded,
        gradient,
        (1, 1),
        "VALID",
        dimension_numbers=("CHWN", "IHWO", "NHWC"),
        preferred_element_type=jnp.float32,
    )
    return summed.transpose(1, 2, 0, 3)


def rim_cells(values):
    return with_halo(shortened(values), (("lat", 1), ("lon", 2)), 1).astype(values.dtype)


def to_channels(values):
    return jax.tree.map(
        lambda part, own: part.astype(own.dtype),
        lax.all_to_all(shortened(values), "lat", split_axis=3, concat_axis=0, tiled=True),
        values,
    )


def to_pixels(values):
    return lax.all_to_all(values, "lat", split_axis=0, concat_axis=3, tiled=True)


def spread_sums(summed, squares):
    return lax.psum((summed, squares), ("lon", "batch"))


def own_channels(norm_pair, width):
    return lax.dynamic_slice_in_dim(norm_pair, lax.axis_index("lat") * width, width, 1)


def norm_forward(fired, norm_pair, pixel_count):
    values = to_channels(fired)
    norm_pair = own_channels(norm_pair, values.shape[3])
    widened = values.astype(jnp.float32)
    summed, squares = spread_sums(
        jnp.sum(widened, axis=(0, 1, 2)), jnp.sum(widened * widened, axis=(0, 1, 2))
    )
    average = summed / pixel_count
    inverse_std = lax.rsqrt(squares / pixel_count - average * average + NORM_EPSILON)
    centred = (widened - average) * inverse_std
    normed = (norm_pair[0] * centred + norm_pair[1]).astype(jnp.bfloat16)
    normed = to_pixels(normed)
    return (normed, (centred, inverse_std, norm_pair))


def norm_backward(gradient, kept, pixel_count):
    centred, inverse_std, norm_pair = kept
    gradient = to_channels(gradient)
    widened = gradient.astype(jnp.float32)
    shift_grad, gain_grad = spread_sums(
        jnp.sum(widened, axis=(0, 1, 2)), jnp.sum(widened * centred, axis=(0, 1, 2))
    )
    scaled = norm_pair[0] * inverse_std
    fired_grad = (
        scaled * (widened - shift_grad / pixel_count - centred * gain_grad / pixel_count)
    ).astype(jnp.bfloat16)
    fired_grad = to_pixels(fired_grad)
    return (fired_grad, jnp.stack([gain_grad, shift_grad]))


def gelu_pullback(preact, gradient):
    unused, pullback = jax.vjp(jax.nn.gelu, preact)
    return pullback(gradient)[0]


def conv_forward(source, kernel, norm_pair, pixel_count):
    padded = rim_cells(source)
    preact = conv_valid(padded, kernel)
    fired = jax.nn.gelu(preact).astype(jnp.bfloat16)
    normed, kept = norm_forward(fired, norm_pair, pixel_count)
    return (normed, (padded, preact, kept))


def conv_backward(gradient, kernel, record, pixel_count):
    padded, preact, kept = record
    fired_grad, pair_grad = norm_backward(gradient, kept, pixel_count)
    preact_grad = gelu_pullback(preact, fired_grad.astype(jnp.float32)).astype(jnp.bfloat16)
    kernel_gradient = kernel_grad(padded, preact_grad)
    flipped = kernel[::-1, ::-1].transpose(0, 1, 3, 2)
    source_grad = conv_valid(rim_cells(preact_grad), flipped)
    return (source_grad, kernel_gradient, pair_grad)


def block_forward(stream, kernels, norm_pairs, pixel_count):
    middle, first_record = conv_forward(
        stream.astype(jnp.bfloat16), kernels[0], norm_pairs[0], pixel_count
    )
    branch, second_record = conv_forward(middle, kernels[1], norm_pairs[1], pixel_count)
    return (stream + branch.astype(jnp.float32), (first_record, second_record))


def block_backward(stream_grad, stream, kernels, norm_pairs, pixel_count):
    unused, records = block_forward(stream, kernels, norm_pairs, pixel_count)
    middle_grad, second_kernel, second_pair = conv_backward(
        stream_grad.astype(jnp.bfloat16), kernels[1], records[1], pixel_count
    )
    source_grad, first_kernel, first_pair = conv_backward(
        middle_grad.astype(jnp.bfloat16), kernels[0], records[0], pixel_count
    )
    return (stream_grad + source_grad, (first_kernel, second_kernel), (first_pair, second_pair))


def adamw_update(weight, gradient, momentum, variance, step_rate):
    momentum = 0.9 * momentum + 0.1 * gradient
    variance = 0.999 * variance + 0.001 * gradient * gradient
    corrected = momentum / (1.0 - 0.9**STEP)
    scaled = jnp.sqrt(variance / (1.0 - 0.999**STEP)) + 1e-08
    return (momentum, variance, weight - step_rate * (corrected / scaled + 0.01 * weight))


def finished(
    loss_sum, loss_weight, input_grad, block_grad, head_grad, norm_grad,
    input_state, block_state, head_state, norm_state,
):
    outputs = [jnp.reshape(loss_sum, (1,)), jnp.reshape(loss_weight, (1,))]
    for state, gradient, step_rate in (
        (input_state, input_grad, 0.015),
        (block_state, block_grad, 0.03),
        (head_state, head_grad, 0.15),
        (norm_state, norm_grad, 0.8),
    ):
        weight, first, second = state
        outputs.extend(adamw_update(weight, gradient, first, second, step_rate))
    return tuple(outputs)


def tile_body(
    fields,
    targets,
    land_mask,
    input_kernel,
    input_first,
    input_second,
    block_kernels,
    block_first,
    block_second,
    head_weight,
    head_first,
    head_second,
    norm_params,
    norm_first,
    norm_second,
):
    samples_here, rows_here, cols_here, in_width = fields.shape
    channels = norm_params.shape[2]
    conv_count = block_kernels.shape[0]
    full_input, full_blocks = (
        lax.all_gather(
            input_kernel.astype(jnp.bfloat16), ("lat", "lon", "batch"), axis=0, tiled=True
        ),
        lax.all_gather(
            block_kernels.astype(jnp.bfloat16), ("lat", "lon", "batch"), axis=1, tiled=True
        ),
    )
    kernel_in = full_input.reshape(7, 7, in_width, channels)
    kernels = full_blocks.reshape(conv_count, 3, 3, channels, channels)
    head_low = head_weight.astype(jnp.bfloat16)
    sample_count = samples_here * lax.axis_size("batch")
    pixel_count = float(
        sample_count * rows_here * lax.axis_size("lat") * cols_here * lax.axis_size("lon")
    )
    row_global = (lax.axis_index("lat") * rows_here + jnp.arange(rows_here)).astype(jnp.float32)
    latitude = (row_global + 0.5) / (rows_here * lax.axis_size("lat")) * jnp.pi - jnp.pi / 2
    pixel_weight = jnp.cos(latitude)[None, :, None] * land_mask.astype(jnp.float32)
    valid_sum = lax.psum(jnp.sum(pixel_weight), ("lat", "lon", "batch"))
    loss_weight = valid_sum / sample_count
    padded_in = with_halo(fields, (("lat", 1), ("lon", 2)), 3)
    preact_in = conv_valid(padded_in, kernel_in)
    streams = [jax.nn.gelu(preact_in)]
    for layer in range(conv_count // 2):
        advanced, unused = block_forward(
            streams[-1],
            kernels[2 * layer : 2 * layer + 2],
            norm_params[2 * layer : 2 * layer + 2],
            pixel_count,
        )
        streams.append(advanced)
    top_stream = streams[-1].astype(jnp.bfloat16)
    predicted = jnp.einsum(
        "nhwc,co->nhwo", top_stream, head_low, preferred_element_type=jnp.float32
    )
    misfit = predicted - targets
    loss_local = jnp.sum(pixel_weight[..., None] * misfit * misfit)
    pred_grad = (2.0 * pixel_weight[..., None] * misfit / loss_weight).astype(jnp.bfloat16)
    head_local = jnp.einsum(
        "nhwc,nhwo->co", top_stream, pred_grad, preferred_element_type=jnp.float32
    )
    stream_grad = jnp.einsum(
        "nhwo,co->nhwc", pred_grad, head_low, preferred_element_type=jnp.float32
    )
    kernel_grads = [None] * conv_count
    pair_grads = [None] * conv_count
    for layer in reversed(range(conv_count // 2)):
        stream_grad, kernel_pair, norm_pair = block_backward(
            stream_grad,
            streams[layer],
            kernels[2 * layer : 2 * layer + 2],
            norm_params[2 * layer : 2 * layer + 2],
            pixel_count,
        )
        kernel_grads[2 * layer], kernel_grads[2 * layer + 1] = kernel_pair
        pair_grads[2 * layer], pair_grads[2 * layer + 1] = norm_pair
    pre_in_grad = gelu_pullback(preact_in, stream_grad).astype(jnp.bfloat16)
    input_local = kernel_grad(padded_in, pre_in_grad).reshape(-1)
    block_local = jnp.stack(kernel_grads).reshape(conv_count, -1)
    input_grad, block_grad = (
        lax.psum_scatter(input_local, ("lat", "lon", "batch"), scatter_dimension=0, tiled=True),
        lax.psum_scatter(block_local, ("lat", "lon", "batch"), scatter_dimension=1, tiled=True),
    )
    head_grad, loss_sum = lax.psum((head_local, loss_local), ("lat", "lon", "batch"))
    norm_grad = jnp.stack(pair_grads)
    norm_grad = lax.all_gather(norm_grad, "lat", axis=2, tiled=True)
    return finished(
        loss_sum, loss_weight, input_grad, block_grad, head_grad, norm_grad,
        (input_kernel, input_first, input_second), (block_kernels, block_first, block_second),
        (head_weight, head_first, head_second), (norm_params, norm_first, norm_second),
    )


ALL = ("lat", "lon", "batch")
TILE = ("lat", "lon")
PIECES = 3
SPREAD = 16


VECTOR, WIDE = "vector", "wide"
SPACES = {VECTOR: pltpu.VMEM, WIDE: pltpu.HBM}


def call(kernel, ins, outs, scratch=(), flags=None, cost=0, room=SMALL_ROOM, aliases=()):
    specs = [pl.BlockSpec(memory_space=SPACES[space]) for unused, space in ins]
    args = [
        pltpu.with_memory_space_constraint(array, pltpu.HBM) if space == WIDE else array
        for array, space in ins
    ]
    if flags is not None:
        specs, args = [pl.BlockSpec(memory_space=pltpu.SMEM)] + specs, [flags] + args
    return pl.pallas_call(
        kernel,
        out_shape=[
            pltpu.HBM(shape, dtype) if space == WIDE else jax.ShapeDtypeStruct(shape, dtype)
            for shape, dtype, space in outs
        ],
        in_specs=specs,
        out_specs=[pl.BlockSpec(memory_space=SPACES[space]) for *unused, space in outs],
        scratch_shapes=list(scratch) + [pltpu.SemaphoreType.DMA((COPIES,))],
        input_output_aliases=dict(aliases),
        compiler_params=pltpu.CompilerParams(vmem_limit_bytes=room),
        cost_estimate=pl.CostEstimate(flops=cost, bytes_accessed=4 << 20, transcendentals=0),
    )(*args)


class Mover:
    def __init__(self, semaphores):
        self.semaphores, self.used, self.sent = semaphores, 0, []

    def start(self, source, target):
        copy = pltpu.make_async_copy(source, target, self.semaphores.at[self.used])
        self.used += 1
        copy.start()
        return copy

    def fetch(self, source, target, parts=1):
        step = target.shape[0] // parts
        return [
            self.start(source.at[pl.ds(i * step, step)], target.at[pl.ds(i * step, step)])
            for i in range(parts)
        ]

    def send(self, source, target):
        self.sent.append(self.start(source, target))

    def finish(self):
        for copy in self.sent:
            copy.wait()


def dot(left, right, dims=((1,), (0,))):
    return lax.dot_general(left, right, (dims, ((), ())), preferred_element_type=jnp.float32)


def gelu_value(x):
    return x * (0.5 * (1.0 + jnp.tanh(GELU_SCALE * (x + GELU_CUBE * (x * x * x)))))


def gelu_both(x):
    square = x * x
    level = jnp.tanh(GELU_SCALE * (x + GELU_CUBE * (x * square)))
    half = 0.5 * (1.0 + level)
    slope = half + 0.5 * x * (1.0 - level * level) * (GELU_SCALE * (1.0 + 3.0 * GELU_CUBE * square))
    return x * half, slope


def shifted(cells, step):
    count = cells.shape[0]
    if step == 0:
        return cells
    column = lax.broadcasted_iota(jnp.int32, cells.shape, 0) + step
    rolled = pltpu.roll(cells, (-step) % count, 0)
    return jnp.where((column >= 0) & (column < count), rolled, 0.0)


def spread_pair(pair, cells, shifts_ref, sizes):
    cols, width, pairs = sizes
    for b in range(3):
        moved = shifted(cells, b - 1).astype(jnp.bfloat16)
        shifts_ref[(pair + 1) * cols : (pair + 2) * cols, b * width : (b + 1) * width] = moved[:, width:]
        shifts_ref[pair * cols : (pair + 1) * cols, (3 + b) * width : (4 + b) * width] = moved[:, :width]


def clear_rim(shifts_ref, sizes):
    cols, width, pairs = sizes
    zero = jnp.zeros((cols, 3 * width), jnp.bfloat16)
    shifts_ref[0:cols, 0 : 3 * width] = zero
    shifts_ref[pairs * cols : (pairs + 1) * cols, 3 * width : 6 * width] = zero


def taps_forward(weight_ref, taps_ref, width):
    for k in range(2):
        for rr in range(2):
            for b in range(3):
                for q in range(2):
                    a = 2 * k + rr - q
                    at = (rr * 3 + b) * width
                    if 0 <= a <= 2:
                        block = weight_ref[(a * 3 + b) * width : (a * 3 + b + 1) * width, :]
                    else:
                        block = jnp.zeros((width, width), jnp.bfloat16)
                    taps_ref[k, at : at + width, q * width : (q + 1) * width] = block


def taps_backward(weight_ref, taps_ref, width):
    for k in range(2):
        for rr in range(2):
            for b in range(3):
                for q in range(2):
                    a = 2 - (2 * k + rr - q)
                    at = (rr * 3 + b) * width
                    if 0 <= a <= 2:
                        tap = a * 3 + 2 - b
                        block = weight_ref[tap * width : (tap + 1) * width, :]
                    else:
                        block = jnp.zeros((width, width), jnp.bfloat16)
                    taps_ref[k, q * width : (q + 1) * width, at : at + width] = block


def pair_conv(shifts_ref, taps_ref, group, cols, dims=((1,), (0,))):
    rows = GROUP * cols
    first = shifts_ref[group * rows : (group + 1) * rows, :]
    second = shifts_ref[group * rows + cols : (group + 1) * rows + cols, :]
    return dot(first, taps_ref[0], dims) + dot(second, taps_ref[1], dims)


def folded(sums, width):
    return sums[:, :width] + sums[:, width:]


def total_of(parts_ref):
    return jnp.sum(parts_ref[...], axis=0)


def twice(row):
    return jnp.concatenate([row, row], axis=1)


def norm_of(total, pixel_count):
    average = total[0:1] / pixel_count
    return average, lax.rsqrt(total[1:2] / pixel_count - average * average + NORM_EPSILON)


def conv_and_sums(flags_ref, shifts_ref, taps_ref, fired_ref, slope_ref, sums_ref, sizes, more=None):
    cols, width, pairs = sizes
    total = jnp.zeros((1, 2 * width), jnp.float32)
    squares = jnp.zeros((1, 2 * width), jnp.float32)
    step = GROUP * cols
    for group in range(pairs // GROUP):
        fired, slope = gelu_both(pair_conv(shifts_ref, taps_ref, group, cols))
        rows = pl.ds(group * step, step)
        fired = fired.astype(jnp.bfloat16)
        fired_ref[rows, :] = fired
        slope_ref[rows, :] = slope.astype(jnp.bfloat16)
        wide = fired.astype(jnp.float32)
        total = total + jnp.sum(wide, axis=0, keepdims=True)
        squares = squares + jnp.sum(wide * wide, axis=0, keepdims=True)
    active = flags_ref[0].astype(jnp.float32)
    parts = [folded(total, width) * active, folded(squares, width) * active]
    put_sums(sums_ref, parts + (more or []))


def put_sums(sums_ref, parts):
    shape = sums_ref.shape[1:]
    row = lax.broadcasted_iota(jnp.int32, shape, 0)
    block = jnp.zeros(shape, jnp.float32)
    at = 0
    for part in parts:
        for i in range(part.shape[0]):
            block = jnp.where(row == at, jnp.broadcast_to(part[i : i + 1], shape), block)
            at += 1
    sums_ref[...] = jnp.broadcast_to(block[None], sums_ref.shape)


def field_row(fields_ref, row, tiles):
    nl, no, rows_here, cols_here = tiles
    lat, inner = row // rows_here, row % rows_here
    return jnp.concatenate([fields_ref[lat * no + lon, inner] for lon in range(no)], axis=0)


def wide_shifts(row_of, shifts_ref, sizes):
    cols, width, pairs = sizes
    rows = 2 * pairs
    for row in range(-3, rows + 3):
        at, rr = (row + 3) // 2, (row + 3) % 2
        if 0 <= row < rows:
            cells = row_of(row).astype(jnp.float32)
        for b in range(7):
            if 0 <= row < rows:
                moved = shifted(cells, b - 3).astype(jnp.bfloat16)
            else:
                moved = jnp.zeros((cols, width), jnp.bfloat16)
            spot = (rr * 7 + b) * width
            shifts_ref[at * cols : (at + 1) * cols, spot : spot + width] = moved


def first_row(device, shard, width):
    return lax.div(device * shard, width)


def frame_rows(shard, devices, width, grain):
    rows = max(-(-(d + 1) * shard // width) - d * shard // width for d in range(devices))
    return -(-rows // grain) * grain


def device_at(flags_ref, lon_step, lat_step, core_step, tiles):
    lat = flags_ref[2] ^ lat_step
    lon = flags_ref[3] ^ lon_step
    return (lat * tiles[1] + lon) * 2 + (flags_ref[1] ^ core_step)


def pack_kernel(fields_ref, targets_ref, weights_ref, packed_ref, pieces_ref, unused_ref, *, in_width):
    samples, rows, cols, unused = fields_ref.shape
    width = packed_ref.shape[3]
    outs = targets_ref.shape[0]
    many = pieces_ref.shape[0]
    pieces_ref[...] = jnp.zeros(pieces_ref.shape, jnp.float32)
    packed_ref[samples:] = jnp.zeros((packed_ref.shape[0] - samples, rows, cols, width), jnp.bfloat16)
    take_from = lax.broadcasted_iota(jnp.int32, (many, width), 0)
    put_to = lax.broadcasted_iota(jnp.int32, (many, width), 1) - in_width
    picks = [
        jnp.where((put_to >= 0) & (take_from == put_to * rows + row), 1.0, 0.0).astype(jnp.bfloat16)
        for row in range(rows)
    ]
    for sample in range(samples):
        for source in range(outs + 1):
            left = targets_ref[source, sample] if source < outs else weights_ref[sample]
            for piece in range(PIECES):
                low = left.astype(jnp.bfloat16).astype(jnp.float32)
                left = left - low
                at = (source * PIECES + piece) * rows
                pieces_ref[at : at + rows, :] = low
        pieces = pieces_ref[...].astype(jnp.bfloat16)
        for row in range(rows):
            placed = dot(pieces, picks[row], ((0,), (0,))).astype(jnp.bfloat16)
            packed_ref[sample, row] = placed
            packed_ref[sample, row, :, 0:in_width] = fields_ref[sample, row]


def place_blocks(part, at, count, rows, device, stage_ref, flat_refs):
    stage_ref[...] = part[at : at + stage_ref.shape[0], :].astype(jnp.float32)
    for index in range(count):
        flat_refs[index][pl.ds(device * rows, rows), :] = stage_ref[index * rows : (index + 1) * rows, :]


def near_kernels(
    flags_ref, parts, taps_ref, flat_ref, stage_ref, flat_block_refs, tiles, shards, in_width
):
    nl, no = tiles[0], tiles[1]
    width = flat_ref.shape[1]
    in_shard, block_rows = shards
    rows = frame_rows(in_shard, 2 * nl * no, width, SPREAD)
    flat_ref[...] = jnp.zeros(flat_ref.shape, jnp.float32)
    for lon_step in range(no):
        for core_step in range(2):
            part = parts[lon_step * 2 + core_step]
            for lat_step in range(nl):
                device = device_at(flags_ref, lon_step, lat_step, core_step, tiles)
                spot = pl.ds(first_row(device, in_shard, width), rows)
                flat_ref[spot, :] += part[lat_step, 0:rows, :].astype(jnp.float32)
                place_blocks(
                    part.at[lat_step], rows, len(flat_block_refs), block_rows, device, stage_ref, flat_block_refs
                )
    inside = lax.broadcasted_iota(jnp.int32, (width, width), 0) < in_width
    zero = jnp.zeros((width, width), jnp.bfloat16)
    for b in range(7):
        taps_ref[3, (7 + b) * width : (8 + b) * width, 0:width] = zero
        taps_ref[0, b * width : (b + 1) * width, width : 2 * width] = zero
        for a in range(7):
            tap = a * 7 + b
            block = flat_ref[tap * in_width : tap * in_width + width, :]
            block = jnp.where(inside, block, 0.0).astype(jnp.bfloat16)
            for q in range(2):
                k, rr = (a + q) // 2, (a + q) % 2
                spot = (rr * 7 + b) * width
                taps_ref[k, spot : spot + width, q * width : (q + 1) * width] = block


def far_kernels_kernel(flags_ref, *refs, tiles, block_rows, count):
    nl, no = tiles[0], tiles[1]
    parts, outs, next_ref, refs = refs[: 2 * no], refs[2 * no : 2 * no + count], refs[2 * no + count], refs[2 * no + count + 1 :]
    stage_ref, *flat_refs, whole_ref, semaphores = refs
    mover = Mover(semaphores)
    for lon_step in range(no):
        for core_step in range(2):
            at = lon_step * 2 + core_step
            for lat_step in range(nl):
                device = device_at(flags_ref, lon_step, lat_step, core_step, tiles)
                place_blocks(parts[at].at[lat_step], 0, count, block_rows, device, stage_ref, flat_refs)
    for index in range(count):
        weight = flat_refs[index][0 : whole_ref.shape[1], :].astype(jnp.bfloat16)
        whole_ref[index] = weight
        if index == 0:
            next_ref[...] = weight
        mover.send(whole_ref.at[index], outs[index])
    mover.finish()


def first_kernel(flags_ref, *refs, tiles, sizes, shards, in_width, count):
    cols, width, pairs = sizes
    nl, no = tiles[0], tiles[1]
    own_in, near, refs = refs[0], refs[1 : 2 * no], refs[2 * no :]
    fields_ref, *refs = refs
    weight_outs, refs = refs[:count], refs[count:]
    pairs_out, wide_out, slope_in_out, stream_out, source_out, fired_ref, slope_ref, sums_ref, *refs = refs
    flat_block_refs, refs = refs[:count], refs[count:]
    own_ref, *refs = refs
    (
        pairs_ref, weights_ref, stage_ref, in_taps_ref, flat_ref, wide_ref,
        slope_in_ref, stream_ref, source_ref, shifts_ref, taps_ref, semaphores,
    ) = refs
    mover = Mover(semaphores)
    own = mover.fetch(own_in, own_ref)
    clear_rim(shifts_ref, sizes)

    def row_of(row):
        cells = field_row(fields_ref, row, tiles)
        pair, q = row // 2, row % 2
        pairs_ref[pair * cols : (pair + 1) * cols, q * width : (q + 1) * width] = cells
        return cells

    wide_shifts(row_of, wide_ref, sizes)
    mover.send(pairs_ref, pairs_out)
    mover.send(wide_ref, wide_out)
    own[0].wait()
    near_kernels(
        flags_ref, (own_ref, *near), in_taps_ref, flat_ref, stage_ref, flat_block_refs, tiles, shards, in_width
    )
    for index in range(count):
        weight = flat_block_refs[index][0 : weights_ref.shape[1], :].astype(jnp.bfloat16)
        weights_ref[index] = weight
        mover.send(weights_ref.at[index], weight_outs[index])
    taps_forward(weights_ref.at[0], taps_ref, width)
    step = GROUP * cols
    for group in range(pairs // GROUP):
        at = group * step
        preact = dot(wide_ref[at : at + step, :], in_taps_ref[0])
        for k in range(1, 4):
            preact += dot(wide_ref[at + k * cols : at + step + k * cols, :], in_taps_ref[k])
        rows = pl.ds(at, step)
        stream, slope = gelu_both(preact)
        slope_in_ref[rows, :] = slope.astype(jnp.bfloat16)
        mover.send(slope_in_ref.at[rows], slope_in_out.at[rows])
        stream_ref[rows, :] = stream
        mover.send(stream_ref.at[rows], stream_out.at[rows])
        source = stream.astype(jnp.bfloat16)
        source_ref[rows, :] = source
        mover.send(source_ref.at[rows], source_out.at[rows])
        for pair in range(GROUP):
            cells = source[pair * cols : (pair + 1) * cols].astype(jnp.float32)
            spread_pair(group * GROUP + pair, cells, shifts_ref, sizes)
    weight_sum = folded(jnp.sum(pairs_ref[...].astype(jnp.float32), axis=0, keepdims=True), width)
    lane = lax.broadcasted_iota(jnp.int32, (1, width), 1) - in_width
    chosen = (lane >= 2 * PIECES) & (lane < 3 * PIECES)
    weight_sum = jnp.sum(jnp.where(chosen, weight_sum, 0.0), axis=1, keepdims=True)
    conv_and_sums(
        flags_ref, shifts_ref, taps_ref, fired_ref, slope_ref, sums_ref, sizes,
        [jnp.broadcast_to(weight_sum, (1, width))],
    )
    mover.finish()


def keep_norm(stats_ref, total, average, inverse_std):
    stats_ref[0:1, :] = average
    stats_ref[1:2, :] = inverse_std
    if total.shape[0] > 2:
        stats_ref[2:3, :] = total[2:3]


def unit_kernel(
    flags_ref, fired_in_ref, parts_ref, norms_ref, weight_ref, slope_in_ref, *refs,
    sizes, pixel_count, index, residual, fetches,
):
    cols, width, pairs = sizes
    if residual:
        stream_in_ref, *refs = refs
    fetched_from, refs = refs[:fetches], refs[fetches:]
    if residual:
        stream_out, *refs = refs
    source_out, stats_out, fired_out, slope_out, fired_ref, slope_ref, sums_ref, *refs = refs
    fetched_to, refs = refs[:fetches], refs[fetches:]
    if residual:
        stream_ref, *refs = refs
    source_ref, stats_ref, shifts_ref, taps_ref, semaphores = refs
    mover = Mover(semaphores)
    mover.send(fired_in_ref, fired_out)
    mover.send(slope_in_ref, slope_out)
    for source, target in zip(fetched_from, fetched_to):
        mover.send(source, target)
    total = total_of(parts_ref)
    average, inverse_std = norm_of(total, pixel_count)
    keep_norm(stats_ref, total, average, inverse_std)
    mover.send(stats_ref, stats_out)
    average, inverse_std = twice(average), twice(inverse_std)
    gain, shift = twice(norms_ref[index, 0:1]), twice(norms_ref[index, 1:2])
    taps_forward(weight_ref, taps_ref, width)
    clear_rim(shifts_ref, sizes)
    for pair in range(pairs):
        rows = pl.ds(pair * cols, cols)
        fired = fired_in_ref[rows, :].astype(jnp.float32)
        normed = (gain * ((fired - average) * inverse_std) + shift).astype(jnp.bfloat16)
        if residual:
            stream = stream_in_ref[rows, :] + normed.astype(jnp.float32)
            stream_ref[rows, :] = stream
            normed = stream.astype(jnp.bfloat16)
        source_ref[rows, :] = normed
        spread_pair(pair, normed.astype(jnp.float32), shifts_ref, sizes)
    mover.send(source_ref, source_out)
    if residual:
        mover.send(stream_ref, stream_out)
    conv_and_sums(flags_ref, shifts_ref, taps_ref, fired_ref, slope_ref, sums_ref, sizes)
    mover.finish()


def head_kernel(
    flags_ref, fired_ref, parts_ref, norms_ref, head_ref, stream_ref, fields_in, first_stats_in, *refs,
    sizes, pixel_count, sample_count, in_width, index, fetches,
):
    cols, width, pairs = sizes
    fetched_from, refs = refs[:fetches], refs[fetches:]
    fetched_to, refs = refs[:fetches], refs[fetches:]
    grad_ref, sums_ref, stats_ref, head_grad_ref, fields_ref, first_stats_ref, top_ref, semaphores = refs
    mover = Mover(semaphores)
    first_stats = mover.fetch(first_stats_in, first_stats_ref)
    fetched = mover.fetch(fields_in, fields_ref)
    for source, target in zip(fetched_from, fetched_to):
        mover.send(source, target)
    total = total_of(parts_ref)
    average, inverse_std = norm_of(total, pixel_count)
    keep_norm(stats_ref, total, average, inverse_std)
    average, inverse_std = twice(average), twice(inverse_std)
    gain, shift = twice(norms_ref[index, 0:1]), twice(norms_ref[index, 1:2])
    outs = head_ref.shape[0]
    row = lax.broadcasted_iota(jnp.int32, (width, width), 0)
    head = jnp.zeros((width, width), jnp.float32)
    for out in range(outs):
        head = jnp.where(row == out, jnp.broadcast_to(head_ref[out : out + 1, :], head.shape), head)
    head = head.astype(jnp.bfloat16)
    lane_from = lax.broadcasted_iota(jnp.int32, (width, 2 * width), 0) - in_width
    lane_to = lax.broadcasted_iota(jnp.int32, (width, 2 * width), 1)
    within = lane_from - PIECES * lane_to
    picks = (within >= 0) & (within < PIECES) & (lane_to < outs)
    lane_to = lane_to - width
    weighs = (lane_from >= outs * PIECES) & (lane_from < (outs + 1) * PIECES)
    picks = picks | (weighs & (lane_to >= 0) & (lane_to < outs))
    picks = jnp.where(picks, 1.0, 0.0).astype(jnp.bfloat16)
    for pair in range(pairs):
        rows = pl.ds(pair * cols, cols)
        centred = (fired_ref[rows, :].astype(jnp.float32) - average) * inverse_std
        normed = (gain * centred + shift).astype(jnp.bfloat16)
        top_ref[rows, :] = (stream_ref[rows, :] + normed.astype(jnp.float32)).astype(jnp.bfloat16)
    first_stats[0].wait()
    loss_weight = first_stats_ref[2:3, :] / sample_count
    loss = jnp.zeros((1, width), jnp.float32)
    shift_grad = jnp.zeros((1, 2 * width), jnp.float32)
    gain_grad = jnp.zeros((1, 2 * width), jnp.float32)
    head_grad = jnp.zeros((width, width), jnp.float32)
    fetched[0].wait()
    step = GROUP * cols
    for group in range(pairs // GROUP):
        rows = pl.ds(group * step, step)
        for q in range(2):
            lanes = slice(q * width, (q + 1) * width)
            top = top_ref[rows, lanes]
            picked = dot(fields_ref[rows, lanes], picks)
            misfit, weight = dot(top, head, ((1,), (1,))) - picked[:, :width], picked[:, width:]
            loss += jnp.sum(weight * misfit * misfit, axis=0, keepdims=True)
            pred_grad = (2.0 * weight * misfit / loss_weight).astype(jnp.bfloat16)
            head_grad += dot(pred_grad, top, ((0,), (0,)))
            grad_ref[rows, lanes] = dot(pred_grad, head)
        low = grad_ref[rows, :].astype(jnp.bfloat16).astype(jnp.float32)
        centred = (fired_ref[rows, :].astype(jnp.float32) - average) * inverse_std
        shift_grad += jnp.sum(low, axis=0, keepdims=True)
        gain_grad += jnp.sum(low * centred, axis=0, keepdims=True)
    loss = jnp.broadcast_to(jnp.sum(loss, axis=1, keepdims=True), (1, width))
    head_grad_ref[...] = head_grad[0:outs]
    put_sums(sums_ref, [folded(shift_grad, width), folded(gain_grad, width), loss])
    mover.finish()


def back_to_preact(parts_ref, stats_ref, norms_ref, index, flags_ref, refs, pixel_count, sizes):
    grad_ref, fired_ref, slope_ref, pre_ref, pair_grad_ref, shifts_ref = refs
    cols, width, pairs = sizes
    total = total_of(parts_ref)
    shift_grad, gain_grad = total[0:1], total[1:2]
    pair_grad_ref[0:1, :] = gain_grad
    pair_grad_ref[1:2, :] = shift_grad
    average, inverse_std = twice(stats_ref[0:1, :]), twice(stats_ref[1:2, :])
    scaled = twice(norms_ref[index, 0:1]) * inverse_std * flags_ref[0].astype(jnp.float32)
    shift_mean, gain_mean = twice(shift_grad / pixel_count), twice(gain_grad / pixel_count)
    for pair in range(pairs):
        rows = pl.ds(pair * cols, cols)
        centred = (fired_ref[rows, :].astype(jnp.float32) - average) * inverse_std
        grad = grad_ref[rows, :].astype(jnp.bfloat16).astype(jnp.float32)
        fired_grad = (scaled * (grad - shift_mean - centred * gain_mean)).astype(jnp.bfloat16)
        pre = (fired_grad.astype(jnp.float32) * slope_ref[rows, :].astype(jnp.float32)).astype(jnp.bfloat16)
        pre_ref[rows, :] = pre
        spread_pair(pair, pre.astype(jnp.float32), shifts_ref, sizes)


def back_kernel(
    flags_ref, parts_ref, norms_ref, grad_ref, weight_ref, fired_ref, slope_ref, stats_ref, below_in, below_stats_in,
    *refs, sizes, pixel_count, index, second, top,
):
    cols, width, pairs = sizes
    if not second:
        kept_in, *refs = refs
    if top:
        head_grad_ref, *refs = refs
    pre_out, pair_grad_out, *refs = refs
    if second:
        kept_out, *refs = refs
    out_ref, sums_ref, *refs = refs
    if not second:
        kept_ref, *refs = refs
    below_ref, below_stats_ref, pre_ref, pair_grad_ref, shifts_ref, taps_ref, semaphores = refs
    mover = Mover(semaphores)
    groups = pairs // GROUP
    below_stats = mover.fetch(below_stats_in, below_stats_ref)
    below = mover.fetch(below_in, below_ref)
    if second:
        mover.send(grad_ref, kept_out)
    else:
        kept = mover.fetch(kept_in, kept_ref)
    clear_rim(shifts_ref, sizes)
    taps_backward(weight_ref, taps_ref, width)
    refs = (grad_ref, fired_ref, slope_ref, pre_ref, pair_grad_ref, shifts_ref)
    back_to_preact(parts_ref, stats_ref, norms_ref, index, flags_ref, refs, pixel_count, sizes)
    mover.send(pre_ref, pre_out)
    mover.send(pair_grad_ref, pair_grad_out)
    below_stats[0].wait()
    average, inverse_std = twice(below_stats_ref[0:1, :]), twice(below_stats_ref[1:2, :])
    shift_sum = jnp.zeros((1, 2 * width), jnp.float32)
    gain_sum = jnp.zeros((1, 2 * width), jnp.float32)
    step = GROUP * cols
    if not second:
        kept[0].wait()
    below[0].wait()
    for group in range(groups):
        rows = pl.ds(group * step, step)
        source = pair_conv(shifts_ref, taps_ref, group, cols, ((1,), (1,)))
        if not second:
            source = source + kept_ref[rows, :]
        out_ref[rows, :] = source.astype(out_ref.dtype)
        low = source.astype(jnp.bfloat16).astype(jnp.float32)
        shift_sum += jnp.sum(low, axis=0, keepdims=True)
        gain_sum += jnp.sum(low * ((below_ref[rows, :].astype(jnp.float32) - average) * inverse_std), axis=0, keepdims=True)
    active = flags_ref[0].astype(jnp.float32)
    sums = [folded(shift_sum, width) * active, folded(gain_sum, width) * active]
    put_sums(sums_ref, sums + ([head_grad_ref[...]] if top else []))
    mover.finish()


def cut_frames(flags_ref, flat_ref, mine_ref, theirs_ref, tiles, shard):
    width = flat_ref.shape[1]
    nl, no = tiles[0], tiles[1]
    rows = mine_ref.shape[2]
    for lon_step in range(no):
        for lat_step in range(nl):
            for core_step, target in ((0, mine_ref), (1, theirs_ref)):
                device = device_at(flags_ref, lon_step, lat_step, core_step, tiles)
                start = first_row(device, shard, width)
                target[lon_step, lat_step] = flat_ref[pl.ds(start, rows), :].astype(jnp.bfloat16)


def block_kernel_grad(shifts_ref, pre_ref, flat_ref, sizes):
    cols, width, pairs = sizes
    for a in range(4):
        k, rr = a // 2, a % 2
        block = shifts_ref[k * cols : (k + pairs) * cols, rr * 3 * width : (rr + 1) * 3 * width]
        grad = dot(block, pre_ref[...], ((0,), (0,)))
        if a < 3:
            flat_ref[a * 3 * width : (a + 1) * 3 * width, :] = grad[:, :width]
        if a > 0:
            flat_ref[(a - 1) * 3 * width : a * 3 * width, :] += grad[:, width:]


def kernel_grad_kernel(flags_ref, *refs, tiles, sizes, shard, fetches, joins):
    fetched_from, refs = refs[:fetches], refs[fetches:]
    source_in, pre_in, *refs = refs
    others, refs = refs[:joins], refs[joins:]
    fetched_to, refs = refs[:fetches], refs[fetches:]
    mine_out, theirs_ref, *refs = refs
    if joins:
        joined_ref, frames_ref, *refs = refs
    mine_ref, source_ref, pre_ref, shifts_ref, flat_ref, semaphores = refs
    mover = Mover(semaphores)
    source, pre = mover.fetch(source_in, source_ref), mover.fetch(pre_in, pre_ref)
    for wide, near in zip(fetched_from, fetched_to):
        mover.send(wide, near)
    arrivals = [mover.start(frames, frames_ref.at[i]) for i, frames in enumerate(others)]
    clear_rim(shifts_ref, sizes)
    source[0].wait()
    spread_all_pairs(source_ref, shifts_ref, sizes)
    pre[0].wait()
    block_kernel_grad(shifts_ref, pre_ref, flat_ref, sizes)
    cut_frames(flags_ref, flat_ref, mine_ref, theirs_ref, tiles, shard)
    mover.send(mine_ref, mine_out)
    for arrival in arrivals:
        arrival.wait()
    if joins:
        join_frames(frames_ref, joined_ref)
    mover.finish()


def spread_all_pairs(source_ref, shifts_ref, sizes):
    cols, width, pairs = sizes
    for pair in range(pairs):
        cells = source_ref[pair * cols : (pair + 1) * cols, :].astype(jnp.float32)
        spread_pair(pair, cells, shifts_ref, sizes)


def last_kernel(
    flags_ref, parts_ref, norms_ref, grad_ref, fired_in, slope_in, stats_in, weight_in, kept_in, in_slope_in,
    source_in, wide_in, *refs, tiles, sizes, shards, in_width, pixel_count,
):
    cols, width, pairs = sizes
    nl, no = tiles[0], tiles[1]
    near_ins, refs = refs[:2], refs[2:]
    (
        pair_grad_out, mine_ref, theirs_ref,
        fired_ref, slope_ref, stats_ref, weight_ref, kept_ref, in_slope_ref, source_ref, wide_ref, pre_ref, in_pre_ref, pair_grad_ref,
        shifts_ref, first_shifts_ref, taps_ref, flat_ref, flat_first_ref, others_ref, semaphores,
    ) = refs
    mover = Mover(semaphores)
    groups = pairs // GROUP
    source = mover.fetch(source_in, source_ref)
    early = mover.fetch(stats_in, stats_ref) + mover.fetch(weight_in, weight_ref)
    early += mover.fetch(fired_in, fired_ref) + mover.fetch(slope_in, slope_ref)
    clear_rim(shifts_ref, sizes)
    clear_rim(first_shifts_ref, sizes)
    source[0].wait()
    spread_all_pairs(source_ref, first_shifts_ref, sizes)
    for arrival in early:
        arrival.wait()
    kept = mover.fetch(kept_in, kept_ref)
    in_slope = mover.fetch(in_slope_in, in_slope_ref)
    wide = mover.fetch(wide_in, wide_ref)
    arrivals = [mover.start(other, others_ref.at[i]) for i, other in enumerate(near_ins)]
    taps_backward(weight_ref, taps_ref, width)
    refs = (grad_ref, fired_ref, slope_ref, pre_ref, pair_grad_ref, shifts_ref)
    back_to_preact(parts_ref, stats_ref, norms_ref, 0, flags_ref, refs, pixel_count, sizes)
    mover.send(pair_grad_ref, pair_grad_out)
    kept[0].wait()
    in_slope[0].wait()
    step = GROUP * cols
    for group in range(groups):
        rows = pl.ds(group * step, step)
        grad = pair_conv(shifts_ref, taps_ref, group, cols, ((1,), (1,))) + kept_ref[rows, :]
        in_pre_ref[rows, :] = (grad * in_slope_ref[rows, :].astype(jnp.float32)).astype(jnp.bfloat16)
    block_kernel_grad(first_shifts_ref, pre_ref, flat_first_ref, sizes)
    for arrival in arrivals:
        arrival.wait()
    wide[0].wait()
    for a in range(8):
        k, rr = a // 2, a % 2
        block = wide_ref[k * cols : (k + pairs) * cols, rr * 7 * width : (rr + 1) * 7 * width]
        grads = dot(block, in_pre_ref[...], ((0,), (0,)))
        for b in range(7):
            grad = grads[b * width : b * width + in_width]
            if a < 7:
                tap = a * 7 + b
                flat_ref[tap * in_width : (tap + 1) * in_width, :] = grad[:, :width]
            if a > 0:
                tap = (a - 1) * 7 + b
                flat_ref[tap * in_width : (tap + 1) * in_width, :] += grad[:, width:]
    rows = others_ref.shape[3]
    in_rows = mine_ref.shape[2] - 2 * rows
    for lon_step in range(no):
        for lat_step in range(nl):
            for core_step, target in ((0, mine_ref), (1, theirs_ref)):
                device = device_at(flags_ref, lon_step, lat_step, core_step, tiles)
                spot = pl.ds(first_row(device, shards[0], width), in_rows)
                target[lon_step, lat_step, 0:in_rows, :] = flat_ref[spot, :].astype(jnp.bfloat16)
                spot = pl.ds(first_row(device, shards[1], width), rows)
                block = flat_first_ref[spot, :].astype(jnp.bfloat16)
                target[lon_step, lat_step, in_rows : in_rows + rows, :] = block
                at = in_rows + rows
                target[lon_step, lat_step, at : at + rows, :] = others_ref[core_step, lon_step, lat_step]
    mover.finish()


def join_frames(frames_ref, joined_ref):
    count, no, nl, rows, unused = frames_ref.shape
    for index in range(count // 2):
        for lon_step in range(no):
            for lat_step in range(nl):
                joined_ref[lat_step, lon_step, index * rows : (index + 1) * rows, :] = low_sum(
                    frames_ref[2 * index, lon_step, lat_step], frames_ref[2 * index + 1, lon_step, lat_step]
                )


def swap(values, axis, step):
    return lax.ppermute(values, axis, [(i, i ^ step) for i in range(lax.axis_size(axis))])


def low_sum(*values):
    return sum(part.astype(jnp.float32) for part in values).astype(jnp.bfloat16)


def along(values, axis):
    return [values[0]] + [swap(values[k], axis, k) for k in range(1, values.shape[0])]


def wide_sum(parts):
    return sum(part.astype(jnp.float32) for part in parts)


def spread_all(values, axes):
    return lax.all_to_all(values, axes, 0, 0, tiled=True)


def whole_sample_body(
    fields,
    targets,
    land_mask,
    input_kernel,
    input_first,
    input_second,
    block_kernels,
    block_first,
    block_second,
    head_weight,
    head_first,
    head_second,
    norm_params,
    norm_first,
    norm_second,
):
    samples_here, rows_here, cols_here, in_width = fields.shape
    width = norm_params.shape[2]
    conv_count = block_kernels.shape[0]
    nl, no, nb = (lax.axis_size(axis) for axis in ALL)
    places, devices = nl * no, nl * no * nb
    tiles = (nl, no, rows_here, cols_here)
    cols, pairs = cols_here * no, rows_here * nl // 2
    sizes = (cols, width, pairs)
    pixels = pairs * cols
    sample_count = samples_here * nb
    pixel_count = float(sample_count * 2 * pixels)
    place = lax.axis_index(TILE)
    core = lax.axis_index("batch")
    flags = jnp.stack(
        [
            (place < samples_here).astype(jnp.int32),
            lax.axis_index("batch"),
            lax.axis_index("lat"),
            lax.axis_index("lon"),
        ]
    )
    bf16, f32 = jnp.bfloat16, jnp.float32
    device = lax.axis_index(ALL)
    in_shard, block_shard = input_kernel.shape[0], block_kernels.shape[1]
    in_frame = frame_rows(in_shard, devices, width, SPREAD)
    block_frame = frame_rows(block_shard, devices, width, 8)
    in_offset = device * in_shard % width
    flat_rows = max((devices - 1) * in_shard // width + in_frame, 48 * in_width + width)
    flat_rows = -(-flat_rows // 8) * 8
    block_rows = block_shard // width

    def shard_rows(shards):
        count = shards.shape[0] * block_rows
        rows = shards.astype(bf16).reshape(count, width)
        return jnp.pad(rows, ((0, -count % SPREAD), (0, 0)))

    def from_all(values, axis, count):
        return [values] + [swap(values, axis, k) for k in range(1, count)]

    framed = lax.dynamic_update_slice(
        jnp.zeros((in_frame * width,), bf16), input_kernel.astype(bf16), (in_offset,)
    ).reshape(in_frame, width)
    near = jnp.concatenate([framed, shard_rows(block_kernels[:NEAR])], axis=0)
    near_rows = near.shape[0]
    both = jnp.stack(from_all(jnp.concatenate([near, shard_rows(block_kernels[NEAR:])], axis=0), "lat", nl))

    row_global = (lax.axis_index("lat") * rows_here + jnp.arange(rows_here)).astype(f32)
    latitude = (row_global + 0.5) / (rows_here * nl) * jnp.pi - jnp.pi / 2
    pixel_weight = jnp.cos(latitude)[None, :, None] * land_mask.astype(f32)
    (packed,) = call(
        functools.partial(pack_kernel, in_width=in_width),
        [(fields, VECTOR), (targets.transpose(3, 0, 1, 2), VECTOR), (pixel_weight, VECTOR)],
        [((places, rows_here, cols_here, width), bf16, VECTOR)],
        [pltpu.VMEM((-(-3 * PIECES * rows_here // 16) * 16, cols_here), f32)],
    )
    near, far = both[:, :near_rows], both[:, near_rows:]
    packed, near, far = lax.optimization_barrier((packed, near, far))
    near = from_all(near, "lon", no)
    packed = spread_all(packed, TILE)

    plane = (pixels, 2 * width)
    weight_shape = (9 * width, width)
    flat_weight = pltpu.VMEM((9 * width + block_frame + 8, width), f32)
    wide_shape = ((pairs + 3) * cols, 14 * width)
    shift_shape = ((pairs + 1) * cols, 6 * width)
    shift_scratch = pltpu.VMEM(shift_shape, bf16)
    forward_taps, backward_taps = (2, 6 * width, 2 * width), (2, 2 * width, 6 * width)
    def sums_shape(rows):
        return ((devices, rows, width), f32, VECTOR)

    stats_shape, pair_shape = (8, width), (2, width)
    frame_shape = (no, nl, block_frame, width)
    low_plane, wide_plane = pltpu.VMEM(plane, bf16), pltpu.VMEM(plane, f32)
    weight_scratch, stats_scratch = pltpu.VMEM(weight_shape, bf16), pltpu.VMEM(stats_shape, f32)
    pair_scratch = pltpu.VMEM(pair_shape, f32)
    unit_cost = 2 * 2 * pixels * 9 * width * width

    def kept_outs(*kinds):
        return [(shape, dtype, WIDE) for shape, dtype in kinds]

    far = from_all(far, "lon", no)
    near = [part for values in near for part in (values, swap(values, "batch", 1))]
    near_count, far_count = NEAR, conv_count - NEAR
    out = call(
        functools.partial(
            first_kernel, tiles=tiles, sizes=sizes, shards=[in_shard, block_rows], in_width=in_width, count=near_count
        ),
        [(near[0], WIDE)] + [(part, VECTOR) for part in near[1:]] + [(packed, VECTOR)],
        kept_outs(*[(weight_shape, bf16)] * near_count, (plane, bf16), (wide_shape, bf16), (plane, bf16), (plane, f32), (plane, bf16))
        + [(plane, bf16, VECTOR), (plane, bf16, VECTOR), sums_shape(4)],
        [flat_weight] * near_count
        + [pltpu.VMEM(near[0].shape, bf16), low_plane, pltpu.VMEM((near_count, *weight_shape), bf16)]
        + [pltpu.VMEM((-(-near_count * block_rows // SPREAD) * SPREAD, width), f32)]
        + [pltpu.VMEM((4, 14 * width, 2 * width), bf16), pltpu.VMEM((flat_rows, width), f32)]
        + [pltpu.VMEM(wide_shape, bf16), low_plane, wide_plane, low_plane]
        + [shift_scratch, pltpu.VMEM(forward_taps, bf16)],
        flags,
        6 * unit_cost,
        LARGE_ROOM,
    )
    weights, out = list(out[:near_count]), out[near_count:]
    fields, wide, in_slope, stream, source, fired, slope, sums = out
    far, sums = lax.optimization_barrier((far, sums))
    parts = spread_all(sums, ALL)
    far = [part for values in far for part in (values, swap(values, "batch", 1))]
    *far_weights, weight = call(
        functools.partial(far_kernels_kernel, tiles=tiles, block_rows=block_rows, count=far_count),
        [(part, VECTOR) for part in far],
        kept_outs(*[(weight_shape, bf16)] * far_count) + [(weight_shape, bf16, VECTOR)],
        [pltpu.VMEM((-(-far_count * block_rows // SPREAD) * SPREAD, width), f32)]
        + [flat_weight] * far_count
        + [pltpu.VMEM((far_count, *weight_shape), bf16)],
        flags,
        unit_cost,
    )
    weights += far_weights

    sources, fireds, slopes, stats = [source], [], [], []
    fetched = []
    for k in range(1, conv_count):
        residual = k % 2 == 0
        fetches = [weights[k + 1]] if k + 1 < conv_count else []
        if not residual:
            fetches.append(stream)
        out = call(
            functools.partial(
                unit_kernel, sizes=sizes, pixel_count=pixel_count, index=k - 1, residual=residual,
                fetches=len(fetches),
            ),
            [(array, VECTOR) for array in (fired, parts, norm_params, weight, slope, *fetched)]
            + [(array, WIDE) for array in fetches],
            kept_outs(*[(plane, f32)] * residual, (plane, bf16), (stats_shape, f32), (plane, bf16), (plane, bf16))
            + [(plane, bf16, VECTOR), (plane, bf16, VECTOR), sums_shape(2)]
            + [(array.shape, array.dtype, VECTOR) for array in fetches],
            [wide_plane] * residual
            + [low_plane, stats_scratch, shift_scratch, pltpu.VMEM(forward_taps, bf16)],
            flags,
            unit_cost,
        )
        if residual:
            stream, *out = out
        source, stat, saved_fired, saved_slope, fired, slope, sums, *fetched = out
        sources.append(source)
        stats.append(stat)
        fireds.append(saved_fired)
        slopes.append(saved_slope)
        if k + 1 < conv_count:
            weight, *fetched = fetched
        parts = spread_all(sums, ALL)

    grad, sums, stat, head_local = call(
        functools.partial(
            head_kernel, sizes=sizes, pixel_count=pixel_count, sample_count=sample_count, in_width=in_width,
            index=conv_count - 1, fetches=0,
        ),
        [(array, VECTOR) for array in (fired, parts, norm_params, head_weight.T, *fetched)]
        + [(array, WIDE) for array in (fields, stats[0])],
        [(plane, f32, VECTOR), sums_shape(4), (stats_shape, f32, VECTOR), (head_weight.T.shape, f32, VECTOR)],
        [low_plane, stats_scratch, low_plane],
        flags,
        unit_cost // 4,
    )
    parts = spread_all(sums, ALL)
    loss_parts = parts

    pair_grads, frames = [None] * conv_count, [None] * conv_count
    for k in range(conv_count - 1, 0, -1):
        second, top = k % 2 == 1, k == conv_count - 1
        pre, pair_grads[k], *out = call(
            functools.partial(back_kernel, sizes=sizes, pixel_count=pixel_count, index=k, second=second, top=top),
            [(array, VECTOR) for array in (parts, norm_params, grad, weight, fired, slope, stat)]
            + [(array, WIDE) for array in (fireds[k - 1], stats[k - 1])]
            + [(array, WIDE) for array in (() if second else (kept_grad,))]
            + [(head_local, VECTOR)] * top,
            kept_outs((plane, bf16), (pair_shape, f32), *[(plane, f32)] * second)
            + [(plane, bf16 if second else f32, VECTOR), sums_shape(4 if top else 2)],
            [wide_plane] * (not second)
            + [low_plane, stats_scratch, low_plane, pair_scratch, shift_scratch, pltpu.VMEM(backward_taps, bf16)],
            flags,
            unit_cost,
        )
        if second:
            kept_grad, *out = out
        grad, sums = out
        parts = spread_all(sums, ALL)
        if top:
            head_parts = parts
        fetches = (weights[k - 1], fireds[k - 1], slopes[k - 1], stats[k - 1]) if k > 1 else ()
        others = ()
        if k + 1 < conv_count:
            frames[k + 1][1] = swap(frames[k + 1][1], "batch", 1)
        if k == 1:
            others = [part for pair in frames[2:] for part in pair]
        out = call(
            functools.partial(
                kernel_grad_kernel, tiles=tiles, sizes=sizes, shard=block_shard, fetches=len(fetches),
                joins=len(others),
            ),
            [(array, WIDE) for array in (*fetches, sources[k], pre, *others)],
            [(array.shape, array.dtype, VECTOR) for array in fetches]
            + [(frame_shape, bf16, WIDE), (frame_shape, bf16, VECTOR)]
            + [((nl, no, (conv_count - 2) * block_frame, width), bf16, VECTOR)] * (k == 1),
            [pltpu.VMEM((len(others), *frame_shape), bf16)] * (k == 1)
            + [pltpu.VMEM(frame_shape, bf16), low_plane, low_plane, shift_scratch, flat_weight],
            flags,
            unit_cost,
        )
        if k == 1:
            *frames[1], early = out
            parts, early, frames[1] = lax.optimization_barrier((parts, early, frames[1]))
            continue
        weight, fired, slope, stat, *frames[k] = out
        parts, frames[k:] = lax.optimization_barrier((parts, frames[k:]))
    pair_grads[0], mine, theirs = call(
        functools.partial(
            last_kernel, tiles=tiles, sizes=sizes, shards=[in_shard, block_shard], in_width=in_width,
            pixel_count=pixel_count,
        ),
        [(array, VECTOR) for array in (parts, norm_params, grad)]
        + [(array, WIDE) for array in (fireds[0], slopes[0], stats[0], weights[0])]
        + [(array, WIDE) for array in (kept_grad, in_slope, sources[0], wide, *frames[1])],
        kept_outs((pair_shape, f32))
        + [((no, nl, in_frame + 2 * block_frame, width), bf16, VECTOR)] * 2,
        [low_plane, low_plane, stats_scratch, weight_scratch, wide_plane, low_plane, low_plane]
        + [pltpu.VMEM(wide_shape, bf16), low_plane, low_plane]
        + [pair_scratch, shift_scratch, shift_scratch, pltpu.VMEM(backward_taps, bf16)]
        + [pltpu.VMEM((flat_rows, width), f32), flat_weight]
        + [pltpu.VMEM((2, *frame_shape), bf16)],
        flags,
        6 * unit_cost,
        LARGE_ROOM,
    )
    late, early = lax.optimization_barrier((low_sum(mine, swap(theirs, "batch", 1)), early))
    late = along(late, "lon")
    early = along(early, "lat")
    early, late = lax.optimization_barrier((early, late))
    early, late = along(low_sum(*early), "lon"), along(low_sum(*late), "lat")
    early[1], head_parts, loss_parts, first_stats, norm_grad = lax.optimization_barrier(
        (early[1], head_parts, loss_parts, stats[0], jnp.stack(pair_grads))
    )
    early, late = wide_sum(early), wide_sum(late)
    input_grad = lax.dynamic_slice(late[:in_frame].reshape(-1), (in_offset,), (in_shard,))
    block_grad = jnp.concatenate([late[in_frame:], early], axis=0)
    block_grad = block_grad.reshape(conv_count, block_frame, width)[:, :block_rows]
    block_grad = block_grad.reshape(conv_count, block_shard)
    head_grad = jnp.sum(head_parts, axis=0)[2:4].T
    loss_sum = jnp.sum(loss_parts, axis=0)[2, 0]
    loss_weight = first_stats[2, 0] / sample_count
    return finished(
        loss_sum, loss_weight, input_grad, block_grad, head_grad, norm_grad,
        (input_kernel, input_first, input_second), (block_kernels, block_first, block_second),
        (head_weight, head_first, head_second), (norm_params, norm_first, norm_second),
    )


def one_device_takes_a_sample(fields, block_kernels, head_weight, norm_params):
    samples_here, rows_here, cols_here, in_width = fields.shape
    nl, no, nb = (lax.axis_size(axis) for axis in ALL)
    rows, cols, width = rows_here * nl, cols_here * no, norm_params.shape[2]
    return (
        samples_here <= nl * no
        and nb == 2
        and nl & (nl - 1) == 0
        and no & (no - 1) == 0
        and rows * cols <= MOST_PIXELS
        and rows % (2 * GROUP) == 0
        and cols % 128 == 0
        and cols_here % 8 == 0
        and width == 128
        and head_weight.shape[1] == 2
        and in_width + 3 * PIECES <= width
        and block_kernels.shape[1] % width == 0
        and block_kernels.shape[0] > NEAR
    )


def body(*args):
    fields, block_kernels, head_weight, norm_params = args[0], args[6], args[9], args[12]
    if one_device_takes_a_sample(fields, block_kernels, head_weight, norm_params):
        return whole_sample_body(*args)
    return tile_body(*args)


def solution(mesh):
    in_specs = (
        P("batch", "lat", "lon", None),
        P("batch", "lat", "lon", None),
        P("batch", "lat", "lon"),
        P(("lat", "lon", "batch")),
        P(("lat", "lon", "batch")),
        P(("lat", "lon", "batch")),
        P(None, ("lat", "lon", "batch")),
        P(None, ("lat", "lon", "batch")),
        P(None, ("lat", "lon", "batch")),
        P(),
        P(),
        P(),
        P(),
        P(),
        P(),
    )
    out_specs = (
        P(),
        P(),
        P(("lat", "lon", "batch")),
        P(("lat", "lon", "batch")),
        P(("lat", "lon", "batch")),
        P(None, ("lat", "lon", "batch")),
        P(None, ("lat", "lon", "batch")),
        P(None, ("lat", "lon", "batch")),
        P(),
        P(),
        P(),
        P(),
        P(),
        P(),
    )
    return jax.shard_map(body, mesh=mesh, in_specs=in_specs, out_specs=out_specs, check_vma=False)
```

```python
import functools

import jax
import jax.numpy as jnp
from jax import lax
from jax.experimental import pallas as pl
from jax.experimental.pallas import tpu as pltpu
from jax.sharding import PartitionSpec as P

STEP = 10


NORM_EPSILON = 1e-05
GELU_SCALE = 0.7978845608028654
GELU_CUBE = 0.044715
GROUP = 4

SMALL_ROOM = 14 << 20
LARGE_ROOM = 36 << 20
COPIES = 32
FORWARD, BACKWARD = 1, 2
NEAR = 1
LATE = 3
MOST_PIXELS = 4096


def shortened(shard):

    def short(part):
        return part.astype(jnp.bfloat16) if part.dtype == jnp.float32 else part

    return jax.tree.map(short, shard)


def with_halo(cells, sides, width):
    for axis, dim in sides:
        count = lax.axis_size(axis)
        ends = count - 1
        head = lax.slice_in_dim(cells, 0, width, axis=dim)
        tail = lax.slice_in_dim(cells, cells.shape[dim] - width, cells.shape[dim], axis=dim)
        cells = jnp.concatenate(
            [
                lax.ppermute(tail, axis, [(i, (i + 1) % count) for i in range(ends)]),
                cells,
                lax.ppermute(head, axis, [((i + 1) % count, i) for i in range(ends)]),
            ],
            axis=dim,
        )
    return cells


def conv_valid(padded, kernel):
    return lax.conv_general_dilated(
        padded,
        kernel,
        (1, 1),
        "VALID",
        dimension_numbers=("NHWC", "HWIO", "NHWC"),
        preferred_element_type=jnp.float32,
    )


def kernel_grad(padded, gradient):
    summed = lax.conv_general_dilated(
        padded,
        gradient,
        (1, 1),
        "VALID",
        dimension_numbers=("CHWN", "IHWO", "NHWC"),
        preferred_element_type=jnp.float32,
    )
    return summed.transpose(1, 2, 0, 3)


def rim_cells(values):
    return with_halo(shortened(values), (("lat", 1), ("lon", 2)), 1).astype(values.dtype)


def to_channels(values):
    return jax.tree.map(
        lambda part, own: part.astype(own.dtype),
        lax.all_to_all(shortened(values), "lat", split_axis=3, concat_axis=0, tiled=True),
        values,
    )


def to_pixels(values):
    return lax.all_to_all(values, "lat", split_axis=0, concat_axis=3, tiled=True)


def spread_sums(summed, squares):
    return lax.psum((summed, squares), ("lon", "batch"))


def own_channels(norm_pair, width):
    return lax.dynamic_slice_in_dim(norm_pair, lax.axis_index("lat") * width, width, 1)


def norm_forward(fired, norm_pair, pixel_count):
    values = to_channels(fired)
    norm_pair = own_channels(norm_pair, values.shape[3])
    widened = values.astype(jnp.float32)
    summed, squares = spread_sums(
        jnp.sum(widened, axis=(0, 1, 2)), jnp.sum(widened * widened, axis=(0, 1, 2))
    )
    average = summed / pixel_count
    inverse_std = lax.rsqrt(squares / pixel_count - average * average + NORM_EPSILON)
    centred = (widened - average) * inverse_std
    normed = (norm_pair[0] * centred + norm_pair[1]).astype(jnp.bfloat16)
    normed = to_pixels(normed)
    return (normed, (centred, inverse_std, norm_pair))


def norm_backward(gradient, kept, pixel_count):
    centred, inverse_std, norm_pair = kept
    gradient = to_channels(gradient)
    widened = gradient.astype(jnp.float32)
    shift_grad, gain_grad = spread_sums(
        jnp.sum(widened, axis=(0, 1, 2)), jnp.sum(widened * centred, axis=(0, 1, 2))
    )
    scaled = norm_pair[0] * inverse_std
    fired_grad = (
        scaled * (widened - shift_grad / pixel_count - centred * gain_grad / pixel_count)
    ).astype(jnp.bfloat16)
    fired_grad = to_pixels(fired_grad)
    return (fired_grad, jnp.stack([gain_grad, shift_grad]))


def gelu_pullback(preact, gradient):
    unused, pullback = jax.vjp(jax.nn.gelu, preact)
    return pullback(gradient)[0]


def conv_forward(source, kernel, norm_pair, pixel_count):
    padded = rim_cells(source)
    preact = conv_valid(padded, kernel)
    fired = jax.nn.gelu(preact).astype(jnp.bfloat16)
    normed, kept = norm_forward(fired, norm_pair, pixel_count)
    return (normed, (padded, preact, kept))


def conv_backward(gradient, kernel, record, pixel_count):
    padded, preact, kept = record
    fired_grad, pair_grad = norm_backward(gradient, kept, pixel_count)
    preact_grad = gelu_pullback(preact, fired_grad.astype(jnp.float32)).astype(jnp.bfloat16)
    kernel_gradient = kernel_grad(padded, preact_grad)
    flipped = kernel[::-1, ::-1].transpose(0, 1, 3, 2)
    source_grad = conv_valid(rim_cells(preact_grad), flipped)
    return (source_grad, kernel_gradient, pair_grad)


def block_forward(stream, kernels, norm_pairs, pixel_count):
    middle, first_record = conv_forward(
        stream.astype(jnp.bfloat16), kernels[0], norm_pairs[0], pixel_count
    )
    branch, second_record = conv_forward(middle, kernels[1], norm_pairs[1], pixel_count)
    return (stream + branch.astype(jnp.float32), (first_record, second_record))


def block_backward(stream_grad, stream, kernels, norm_pairs, pixel_count):
    unused, records = block_forward(stream, kernels, norm_pairs, pixel_count)
    middle_grad, second_kernel, second_pair = conv_backward(
        stream_grad.astype(jnp.bfloat16), kernels[1], records[1], pixel_count
    )
    source_grad, first_kernel, first_pair = conv_backward(
        middle_grad.astype(jnp.bfloat16), kernels[0], records[0], pixel_count
    )
    return (stream_grad + source_grad, (first_kernel, second_kernel), (first_pair, second_pair))


def adamw_update(weight, gradient, momentum, variance, step_rate):
    momentum = 0.9 * momentum + 0.1 * gradient
    variance = 0.999 * variance + 0.001 * gradient * gradient
    corrected = momentum / (1.0 - 0.9**STEP)
    scaled = jnp.sqrt(variance / (1.0 - 0.999**STEP)) + 1e-08
    return (momentum, variance, weight - step_rate * (corrected / scaled + 0.01 * weight))


def finished(
    loss_sum, loss_weight, input_grad, block_grad, head_grad, norm_grad,
    input_state, block_state, head_state, norm_state,
):
    outputs = [jnp.reshape(loss_sum, (1,)), jnp.reshape(loss_weight, (1,))]
    for state, gradient, step_rate in (
        (input_state, input_grad, 0.015),
        (block_state, block_grad, 0.03),
        (head_state, head_grad, 0.15),
        (norm_state, norm_grad, 0.8),
    ):
        weight, first, second = state
        outputs.extend(adamw_update(weight, gradient, first, second, step_rate))
    return tuple(outputs)


def tile_body(
    fields,
    targets,
    land_mask,
    input_kernel,
    input_first,
    input_second,
    block_kernels,
    block_first,
    block_second,
    head_weight,
    head_first,
    head_second,
    norm_params,
    norm_first,
    norm_second,
):
    samples_here, rows_here, cols_here, in_width = fields.shape
    channels = norm_params.shape[2]
    conv_count = block_kernels.shape[0]
    full_input, full_blocks = (
        lax.all_gather(
            input_kernel.astype(jnp.bfloat16), ("lat", "lon", "batch"), axis=0, tiled=True
        ),
        lax.all_gather(
            block_kernels.astype(jnp.bfloat16), ("lat", "lon", "batch"), axis=1, tiled=True
        ),
    )
    kernel_in = full_input.reshape(7, 7, in_width, channels)
    kernels = full_blocks.reshape(conv_count, 3, 3, channels, channels)
    head_low = head_weight.astype(jnp.bfloat16)
    sample_count = samples_here * lax.axis_size("batch")
    pixel_count = float(
        sample_count * rows_here * lax.axis_size("lat") * cols_here * lax.axis_size("lon")
    )
    row_global = (lax.axis_index("lat") * rows_here + jnp.arange(rows_here)).astype(jnp.float32)
    latitude = (row_global + 0.5) / (rows_here * lax.axis_size("lat")) * jnp.pi - jnp.pi / 2
    pixel_weight = jnp.cos(latitude)[None, :, None] * land_mask.astype(jnp.float32)
    valid_sum = lax.psum(jnp.sum(pixel_weight), ("lat", "lon", "batch"))
    loss_weight = valid_sum / sample_count
    padded_in = with_halo(fields, (("lat", 1), ("lon", 2)), 3)
    preact_in = conv_valid(padded_in, kernel_in)
    streams = [jax.nn.gelu(preact_in)]
    for layer in range(conv_count // 2):
        advanced, unused = block_forward(
            streams[-1],
            kernels[2 * layer : 2 * layer + 2],
            norm_params[2 * layer : 2 * layer + 2],
            pixel_count,
        )
        streams.append(advanced)
    top_stream = streams[-1].astype(jnp.bfloat16)
    predicted = jnp.einsum(
        "nhwc,co->nhwo", top_stream, head_low, preferred_element_type=jnp.float32
    )
    misfit = predicted - targets
    loss_local = jnp.sum(pixel_weight[..., None] * misfit * misfit)
    pred_grad = (2.0 * pixel_weight[..., None] * misfit / loss_weight).astype(jnp.bfloat16)
    head_local = jnp.einsum(
        "nhwc,nhwo->co", top_stream, pred_grad, preferred_element_type=jnp.float32
    )
    stream_grad = jnp.einsum(
        "nhwo,co->nhwc", pred_grad, head_low, preferred_element_type=jnp.float32
    )
    kernel_grads = [None] * conv_count
    pair_grads = [None] * conv_count
    for layer in reversed(range(conv_count // 2)):
        stream_grad, kernel_pair, norm_pair = block_backward(
            stream_grad,
            streams[layer],
            kernels[2 * layer : 2 * layer + 2],
            norm_params[2 * layer : 2 * layer + 2],
            pixel_count,
        )
        kernel_grads[2 * layer], kernel_grads[2 * layer + 1] = kernel_pair
        pair_grads[2 * layer], pair_grads[2 * layer + 1] = norm_pair
    pre_in_grad = gelu_pullback(preact_in, stream_grad).astype(jnp.bfloat16)
    input_local = kernel_grad(padded_in, pre_in_grad).reshape(-1)
    block_local = jnp.stack(kernel_grads).reshape(conv_count, -1)
    input_grad, block_grad = (
        lax.psum_scatter(input_local, ("lat", "lon", "batch"), scatter_dimension=0, tiled=True),
        lax.psum_scatter(block_local, ("lat", "lon", "batch"), scatter_dimension=1, tiled=True),
    )
    head_grad, loss_sum = lax.psum((head_local, loss_local), ("lat", "lon", "batch"))
    norm_grad = jnp.stack(pair_grads)
    norm_grad = lax.all_gather(norm_grad, "lat", axis=2, tiled=True)
    return finished(
        loss_sum, loss_weight, input_grad, block_grad, head_grad, norm_grad,
        (input_kernel, input_first, input_second), (block_kernels, block_first, block_second),
        (head_weight, head_first, head_second), (norm_params, norm_first, norm_second),
    )


ALL = ("lat", "lon", "batch")
TILE = ("lat", "lon")
PIECES = 3
SPREAD = 16


VECTOR, WIDE = "vector", "wide"
SPACES = {VECTOR: pltpu.VMEM, WIDE: pltpu.HBM}


def call(kernel, ins, outs, scratch=(), flags=None, cost=0, room=SMALL_ROOM, aliases=()):
    specs = [pl.BlockSpec(memory_space=SPACES[space]) for unused, space in ins]
    args = [
        pltpu.with_memory_space_constraint(array, pltpu.HBM) if space == WIDE else array
        for array, space in ins
    ]
    if flags is not None:
        specs, args = [pl.BlockSpec(memory_space=pltpu.SMEM)] + specs, [flags] + args
    return pl.pallas_call(
        kernel,
        out_shape=[
            pltpu.HBM(shape, dtype) if space == WIDE else jax.ShapeDtypeStruct(shape, dtype)
            for shape, dtype, space in outs
        ],
        in_specs=specs,
        out_specs=[pl.BlockSpec(memory_space=SPACES[space]) for *unused, space in outs],
        scratch_shapes=list(scratch) + [pltpu.SemaphoreType.DMA((COPIES,))],
        input_output_aliases=dict(aliases),
        compiler_params=pltpu.CompilerParams(vmem_limit_bytes=room),
        cost_estimate=pl.CostEstimate(flops=cost, bytes_accessed=4 << 20, transcendentals=0),
    )(*args)


class Mover:
    def __init__(self, semaphores):
        self.semaphores, self.used, self.sent = semaphores, 0, []

    def start(self, source, target):
        copy = pltpu.make_async_copy(source, target, self.semaphores.at[self.used])
        self.used += 1
        copy.start()
        return copy

    def fetch(self, source, target, parts=1):
        step = target.shape[0] // parts
        return [
            self.start(source.at[pl.ds(i * step, step)], target.at[pl.ds(i * step, step)])
            for i in range(parts)
        ]

    def send(self, source, target):
        self.sent.append(self.start(source, target))

    def finish(self):
        for copy in self.sent:
            copy.wait()


def dot(left, right, dims=((1,), (0,))):
    return lax.dot_general(left, right, (dims, ((), ())), preferred_element_type=jnp.float32)


def gelu_value(x):
    return x * (0.5 * (1.0 + jnp.tanh(GELU_SCALE * (x + GELU_CUBE * (x * x * x)))))


def gelu_both(x):
    square = x * x
    level = jnp.tanh(GELU_SCALE * (x + GELU_CUBE * (x * square)))
    half = 0.5 * (1.0 + level)
    slope = half + 0.5 * x * (1.0 - level * level) * (GELU_SCALE * (1.0 + 3.0 * GELU_CUBE * square))
    return x * half, slope


def shifted(cells, step):
    count = cells.shape[0]
    if step == 0:
        return cells
    column = lax.broadcasted_iota(jnp.int32, cells.shape, 0) + step
    rolled = pltpu.roll(cells, (-step) % count, 0)
    return jnp.where((column >= 0) & (column < count), rolled, 0.0)


def spread_pair(pair, cells, shifts_ref, sizes):
    cols, width, pairs = sizes
    for b in range(3):
        moved = shifted(cells, b - 1).astype(jnp.bfloat16)
        shifts_ref[(pair + 1) * cols : (pair + 2) * cols, b * width : (b + 1) * width] = moved[:, width:]
        shifts_ref[pair * cols : (pair + 1) * cols, (3 + b) * width : (4 + b) * width] = moved[:, :width]


def clear_rim(shifts_ref, sizes):
    cols, width, pairs = sizes
    zero = jnp.zeros((cols, 3 * width), jnp.bfloat16)
    shifts_ref[0:cols, 0 : 3 * width] = zero
    shifts_ref[pairs * cols : (pairs + 1) * cols, 3 * width : 6 * width] = zero


def taps_forward(weight_ref, taps_ref, width):
    for k in range(2):
        for rr in range(2):
            for b in range(3):
                for q in range(2):
                    a = 2 * k + rr - q
                    at = (rr * 3 + b) * width
                    if 0 <= a <= 2:
                        block = weight_ref[(a * 3 + b) * width : (a * 3 + b + 1) * width, :]
                    else:
                        block = jnp.zeros((width, width), jnp.bfloat16)
                    taps_ref[k, at : at + width, q * width : (q + 1) * width] = block


def taps_backward(weight_ref, taps_ref, width):
    for k in range(2):
        for rr in range(2):
            for b in range(3):
                for q in range(2):
                    a = 2 - (2 * k + rr - q)
                    at = (rr * 3 + b) * width
                    if 0 <= a <= 2:
                        tap = a * 3 + 2 - b
                        block = weight_ref[tap * width : (tap + 1) * width, :]
                    else:
                        block = jnp.zeros((width, width), jnp.bfloat16)
                    taps_ref[k, q * width : (q + 1) * width, at : at + width] = block


def pair_conv(shifts_ref, taps_ref, group, cols, dims=((1,), (0,)), size=GROUP):
    rows = size * cols
    first = shifts_ref[group * rows : (group + 1) * rows, :]
    second = shifts_ref[group * rows + cols : (group + 1) * rows + cols, :]
    return dot(first, taps_ref[0], dims) + dot(second, taps_ref[1], dims)


def folded(sums, width):
    return sums[:, :width] + sums[:, width:]


def total_of(parts_ref):
    return jnp.sum(parts_ref[...], axis=0)


def twice(row):
    return jnp.concatenate([row, row], axis=1)


def norm_of(total, pixel_count):
    average = total[0:1] / pixel_count
    return average, lax.rsqrt(total[1:2] / pixel_count - average * average + NORM_EPSILON)


def conv_and_sums(flags_ref, shifts_ref, taps_ref, fired_ref, slope_ref, sums_ref, sizes, more=None, size=GROUP):
    cols, width, pairs = sizes
    total = jnp.zeros((1, 2 * width), jnp.float32)
    squares = jnp.zeros((1, 2 * width), jnp.float32)
    step = size * cols
    for group in range(pairs // size):
        fired, slope = gelu_both(pair_conv(shifts_ref, taps_ref, group, cols, size=size))
        rows = pl.ds(group * step, step)
        fired = fired.astype(jnp.bfloat16)
        fired_ref[rows, :] = fired
        slope_ref[rows, :] = slope.astype(jnp.bfloat16)
        wide = fired.astype(jnp.float32)
        total = total + jnp.sum(wide, axis=0, keepdims=True)
        squares = squares + jnp.sum(wide * wide, axis=0, keepdims=True)
    active = flags_ref[0].astype(jnp.float32)
    parts = [folded(total, width) * active, folded(squares, width) * active]
    put_sums(sums_ref, parts + (more or []))


def put_sums(sums_ref, parts):
    shape = sums_ref.shape[1:]
    row = lax.broadcasted_iota(jnp.int32, shape, 0)
    block = jnp.zeros(shape, jnp.float32)
    at = 0
    for part in parts:
        for i in range(part.shape[0]):
            block = jnp.where(row == at, jnp.broadcast_to(part[i : i + 1], shape), block)
            at += 1
    sums_ref[...] = jnp.broadcast_to(block[None], sums_ref.shape)


def field_row(fields_ref, row, tiles):
    nl, no, rows_here, cols_here = tiles
    lat, inner = row // rows_here, row % rows_here
    return jnp.concatenate([fields_ref[lat * no + lon, inner] for lon in range(no)], axis=0)


def wide_shifts(row_of, shifts_ref, sizes):
    cols, width, pairs = sizes
    rows = 2 * pairs
    for row in range(-3, rows + 3):
        at, rr = (row + 3) // 2, (row + 3) % 2
        if 0 <= row < rows:
            cells = row_of(row).astype(jnp.float32)
        for b in range(7):
            if 0 <= row < rows:
                moved = shifted(cells, b - 3).astype(jnp.bfloat16)
            else:
                moved = jnp.zeros((cols, width), jnp.bfloat16)
            spot = (rr * 7 + b) * width
            shifts_ref[at * cols : (at + 1) * cols, spot : spot + width] = moved


def first_row(device, shard, width):
    return lax.div(device * shard, width)


def frame_rows(shard, devices, width, grain):
    rows = max(-(-(d + 1) * shard // width) - d * shard // width for d in range(devices))
    return -(-rows // grain) * grain


def device_at(flags_ref, lon_step, lat_step, core_step, tiles):
    lat = flags_ref[2] ^ lat_step
    lon = flags_ref[3] ^ lon_step
    return (lat * tiles[1] + lon) * 2 + (flags_ref[1] ^ core_step)


def pack_kernel(fields_ref, targets_ref, weights_ref, packed_ref, pieces_ref, unused_ref, *, in_width):
    samples, rows, cols, unused = fields_ref.shape
    width = packed_ref.shape[3]
    outs = targets_ref.shape[0]
    many = pieces_ref.shape[0]
    pieces_ref[...] = jnp.zeros(pieces_ref.shape, jnp.float32)
    packed_ref[samples:] = jnp.zeros((packed_ref.shape[0] - samples, rows, cols, width), jnp.bfloat16)
    take_from = lax.broadcasted_iota(jnp.int32, (many, width), 0)
    put_to = lax.broadcasted_iota(jnp.int32, (many, width), 1) - in_width
    picks = [
        jnp.where((put_to >= 0) & (take_from == put_to * rows + row), 1.0, 0.0).astype(jnp.bfloat16)
        for row in range(rows)
    ]
    for sample in range(samples):
        for source in range(outs + 1):
            left = targets_ref[source, sample] if source < outs else weights_ref[sample]
            for piece in range(PIECES):
                low = left.astype(jnp.bfloat16).astype(jnp.float32)
                left = left - low
                at = (source * PIECES + piece) * rows
                pieces_ref[at : at + rows, :] = low
        pieces = pieces_ref[...].astype(jnp.bfloat16)
        for row in range(rows):
            placed = dot(pieces, picks[row], ((0,), (0,))).astype(jnp.bfloat16)
            packed_ref[sample, row] = placed
            packed_ref[sample, row, :, 0:in_width] = fields_ref[sample, row]


def place_blocks(part, at, count, rows, device, stage_ref, flat_refs):
    stage_ref[...] = part[at : at + stage_ref.shape[0], :].astype(jnp.float32)
    for index in range(count):
        flat_refs[index][pl.ds(device * rows, rows), :] = stage_ref[index * rows : (index + 1) * rows, :]


def near_kernels(
    flags_ref, parts, taps_ref, flat_ref, stage_ref, flat_block_refs, tiles, shards, in_width
):
    nl, no = tiles[0], tiles[1]
    width = flat_ref.shape[1]
    in_shard, block_rows = shards
    rows = frame_rows(in_shard, 2 * nl * no, width, SPREAD)
    flat_ref[...] = jnp.zeros(flat_ref.shape, jnp.float32)
    for lon_step in range(no):
        for core_step in range(2):
            part = parts[lon_step * 2 + core_step]
            for lat_step in range(nl):
                device = device_at(flags_ref, lon_step, lat_step, core_step, tiles)
                spot = pl.ds(first_row(device, in_shard, width), rows)
                flat_ref[spot, :] += part[lat_step, 0:rows, :].astype(jnp.float32)
                place_blocks(
                    part.at[lat_step], rows, len(flat_block_refs), block_rows, device, stage_ref, flat_block_refs
                )
    inside = lax.broadcasted_iota(jnp.int32, (width, width), 0) < in_width
    zero = jnp.zeros((width, width), jnp.bfloat16)
    for b in range(7):
        taps_ref[3, (7 + b) * width : (8 + b) * width, 0:width] = zero
        taps_ref[0, b * width : (b + 1) * width, width : 2 * width] = zero
        for a in range(7):
            tap = a * 7 + b
            block = flat_ref[tap * in_width : tap * in_width + width, :]
            block = jnp.where(inside, block, 0.0).astype(jnp.bfloat16)
            for q in range(2):
                k, rr = (a + q) // 2, (a + q) % 2
                spot = (rr * 7 + b) * width
                taps_ref[k, spot : spot + width, q * width : (q + 1) * width] = block


def far_kernels_kernel(flags_ref, *refs, tiles, block_rows, count):
    nl, no = tiles[0], tiles[1]
    parts, outs, next_ref, refs = refs[: 2 * no], refs[2 * no : 2 * no + count], refs[2 * no + count], refs[2 * no + count + 1 :]
    stage_ref, *flat_refs, whole_ref, semaphores = refs
    mover = Mover(semaphores)
    for lon_step in range(no):
        for core_step in range(2):
            at = lon_step * 2 + core_step
            for lat_step in range(nl):
                device = device_at(flags_ref, lon_step, lat_step, core_step, tiles)
                place_blocks(parts[at].at[lat_step], 0, count, block_rows, device, stage_ref, flat_refs)
    for index in range(count):
        weight = flat_refs[index][0 : whole_ref.shape[1], :].astype(jnp.bfloat16)
        whole_ref[index] = weight
        if index == 0:
            next_ref[...] = weight
        mover.send(whole_ref.at[index], outs[index])
    mover.finish()


def first_kernel(flags_ref, *refs, tiles, sizes, shards, in_width, count):
    cols, width, pairs = sizes
    nl, no = tiles[0], tiles[1]
    own_in, near, refs = refs[0], refs[1 : 2 * no], refs[2 * no :]
    fields_ref, *refs = refs
    weight_outs, refs = refs[:count], refs[count:]
    pairs_out, wide_out, slope_in_out, stream_out, source_out, fired_ref, slope_ref, sums_ref, *refs = refs
    flat_block_refs, refs = refs[:count], refs[count:]
    own_ref, *refs = refs
    (
        pairs_ref, weights_ref, stage_ref, in_taps_ref, flat_ref, wide_ref,
        slope_in_ref, stream_ref, source_ref, shifts_ref, taps_ref, semaphores,
    ) = refs
    mover = Mover(semaphores)
    own = mover.fetch(own_in, own_ref)
    clear_rim(shifts_ref, sizes)

    def row_of(row):
        cells = field_row(fields_ref, row, tiles)
        pair, q = row // 2, row % 2
        pairs_ref[pair * cols : (pair + 1) * cols, q * width : (q + 1) * width] = cells
        return cells

    wide_shifts(row_of, wide_ref, sizes)
    mover.send(pairs_ref, pairs_out)
    mover.send(wide_ref, wide_out)
    own[0].wait()
    near_kernels(
        flags_ref, (own_ref, *near), in_taps_ref, flat_ref, stage_ref, flat_block_refs, tiles, shards, in_width
    )
    for index in range(count):
        weight = flat_block_refs[index][0 : weights_ref.shape[1], :].astype(jnp.bfloat16)
        weights_ref[index] = weight
        mover.send(weights_ref.at[index], weight_outs[index])
    taps_forward(weights_ref.at[0], taps_ref, width)
    step = GROUP * cols
    for group in range(pairs // GROUP):
        at = group * step
        preact = dot(wide_ref[at : at + step, :], in_taps_ref[0])
        for k in range(1, 4):
            preact += dot(wide_ref[at + k * cols : at + step + k * cols, :], in_taps_ref[k])
        rows = pl.ds(at, step)
        stream, slope = gelu_both(preact)
        slope_in_ref[rows, :] = slope.astype(jnp.bfloat16)
        mover.send(slope_in_ref.at[rows], slope_in_out.at[rows])
        stream_ref[rows, :] = stream
        mover.send(stream_ref.at[rows], stream_out.at[rows])
        source = stream.astype(jnp.bfloat16)
        source_ref[rows, :] = source
        mover.send(source_ref.at[rows], source_out.at[rows])
        for pair in range(GROUP):
            cells = source[pair * cols : (pair + 1) * cols].astype(jnp.float32)
            spread_pair(group * GROUP + pair, cells, shifts_ref, sizes)
    weight_sum = folded(jnp.sum(pairs_ref[...].astype(jnp.float32), axis=0, keepdims=True), width)
    lane = lax.broadcasted_iota(jnp.int32, (1, width), 1) - in_width
    chosen = (lane >= 2 * PIECES) & (lane < 3 * PIECES)
    weight_sum = jnp.sum(jnp.where(chosen, weight_sum, 0.0), axis=1, keepdims=True)
    conv_and_sums(
        flags_ref, shifts_ref, taps_ref, fired_ref, slope_ref, sums_ref, sizes,
        [jnp.broadcast_to(weight_sum, (1, width))],
    )
    mover.finish()


def keep_norm(stats_ref, total, average, inverse_std):
    stats_ref[0:1, :] = average
    stats_ref[1:2, :] = inverse_std
    if total.shape[0] > 2:
        stats_ref[2:3, :] = total[2:3]


def unit_kernel(
    flags_ref, fired_in_ref, parts_ref, norms_ref, weight_ref, slope_in_ref, *refs,
    sizes, pixel_count, index, residual, fetches,
):
    cols, width, pairs = sizes
    if residual:
        stream_in_ref, *refs = refs
    fetched_from, refs = refs[:fetches], refs[fetches:]
    if residual:
        stream_out, *refs = refs
    source_out, stats_out, fired_out, slope_out, fired_ref, slope_ref, sums_ref, *refs = refs
    fetched_to, refs = refs[:fetches], refs[fetches:]
    if residual:
        stream_ref, *refs = refs
    source_ref, stats_ref, shifts_ref, taps_ref, semaphores = refs
    mover = Mover(semaphores)
    mover.send(fired_in_ref, fired_out)
    mover.send(slope_in_ref, slope_out)
    for source, target in zip(fetched_from, fetched_to):
        mover.send(source, target)
    total = total_of(parts_ref)
    average, inverse_std = norm_of(total, pixel_count)
    keep_norm(stats_ref, total, average, inverse_std)
    mover.send(stats_ref, stats_out)
    average, inverse_std = twice(average), twice(inverse_std)
    gain, shift = twice(norms_ref[index, 0:1]), twice(norms_ref[index, 1:2])
    taps_forward(weight_ref, taps_ref, width)
    clear_rim(shifts_ref, sizes)
    for pair in range(pairs):
        rows = pl.ds(pair * cols, cols)
        fired = fired_in_ref[rows, :].astype(jnp.float32)
        normed = (gain * ((fired - average) * inverse_std) + shift).astype(jnp.bfloat16)
        if residual:
            stream = stream_in_ref[rows, :] + normed.astype(jnp.float32)
            stream_ref[rows, :] = stream
            normed = stream.astype(jnp.bfloat16)
        source_ref[rows, :] = normed
        spread_pair(pair, normed.astype(jnp.float32), shifts_ref, sizes)
    mover.send(source_ref, source_out)
    if residual:
        mover.send(stream_ref, stream_out)
    conv_and_sums(flags_ref, shifts_ref, taps_ref, fired_ref, slope_ref, sums_ref, sizes, size=pairs)
    mover.finish()


def head_kernel(
    flags_ref, fired_ref, parts_ref, norms_ref, head_ref, stream_ref, fields_in, first_stats_in, *refs,
    sizes, pixel_count, sample_count, in_width, index, fetches,
):
    cols, width, pairs = sizes
    fetched_from, refs = refs[:fetches], refs[fetches:]
    fetched_to, refs = refs[:fetches], refs[fetches:]
    grad_ref, sums_ref, stats_ref, head_grad_ref, fields_ref, first_stats_ref, top_ref, semaphores = refs
    mover = Mover(semaphores)
    first_stats = mover.fetch(first_stats_in, first_stats_ref)
    fetched = mover.fetch(fields_in, fields_ref)
    for source, target in zip(fetched_from, fetched_to):
        mover.send(source, target)
    total = total_of(parts_ref)
    average, inverse_std = norm_of(total, pixel_count)
    keep_norm(stats_ref, total, average, inverse_std)
    average, inverse_std = twice(average), twice(inverse_std)
    gain, shift = twice(norms_ref[index, 0:1]), twice(norms_ref[index, 1:2])
    outs = head_ref.shape[0]
    row = lax.broadcasted_iota(jnp.int32, (width, width), 0)
    head = jnp.zeros((width, width), jnp.float32)
    for out in range(outs):
        head = jnp.where(row == out, jnp.broadcast_to(head_ref[out : out + 1, :], head.shape), head)
    head = head.astype(jnp.bfloat16)
    lane_from = lax.broadcasted_iota(jnp.int32, (width, 2 * width), 0) - in_width
    lane_to = lax.broadcasted_iota(jnp.int32, (width, 2 * width), 1)
    within = lane_from - PIECES * lane_to
    picks = (within >= 0) & (within < PIECES) & (lane_to < outs)
    lane_to = lane_to - width
    weighs = (lane_from >= outs * PIECES) & (lane_from < (outs + 1) * PIECES)
    picks = picks | (weighs & (lane_to >= 0) & (lane_to < outs))
    picks = jnp.where(picks, 1.0, 0.0).astype(jnp.bfloat16)
    for pair in range(pairs):
        rows = pl.ds(pair * cols, cols)
        centred = (fired_ref[rows, :].astype(jnp.float32) - average) * inverse_std
        normed = (gain * centred + shift).astype(jnp.bfloat16)
        top_ref[rows, :] = (stream_ref[rows, :] + normed.astype(jnp.float32)).astype(jnp.bfloat16)
    first_stats[0].wait()
    loss_weight = first_stats_ref[2:3, :] / sample_count
    loss = jnp.zeros((1, width), jnp.float32)
    shift_grad = jnp.zeros((1, 2 * width), jnp.float32)
    gain_grad = jnp.zeros((1, 2 * width), jnp.float32)
    head_grad = jnp.zeros((width, width), jnp.float32)
    fetched[0].wait()
    step = GROUP * cols
    for group in range(pairs // GROUP):
        rows = pl.ds(group * step, step)
        for q in range(2):
            lanes = slice(q * width, (q + 1) * width)
            top = top_ref[rows, lanes]
            picked = dot(fields_ref[rows, lanes], picks)
            misfit, weight = dot(top, head, ((1,), (1,))) - picked[:, :width], picked[:, width:]
            loss += jnp.sum(weight * misfit * misfit, axis=0, keepdims=True)
            pred_grad = (2.0 * weight * misfit / loss_weight).astype(jnp.bfloat16)
            head_grad += dot(pred_grad, top, ((0,), (0,)))
            grad_ref[rows, lanes] = dot(pred_grad, head)
        low = grad_ref[rows, :].astype(jnp.bfloat16).astype(jnp.float32)
        centred = (fired_ref[rows, :].astype(jnp.float32) - average) * inverse_std
        shift_grad += jnp.sum(low, axis=0, keepdims=True)
        gain_grad += jnp.sum(low * centred, axis=0, keepdims=True)
    loss = jnp.broadcast_to(jnp.sum(loss, axis=1, keepdims=True), (1, width))
    head_grad_ref[...] = head_grad[0:outs]
    put_sums(sums_ref, [folded(shift_grad, width), folded(gain_grad, width), loss])
    mover.finish()


def back_to_preact(parts_ref, stats_ref, norms_ref, index, flags_ref, refs, pixel_count, sizes):
    grad_ref, fired_ref, slope_ref, pre_ref, pair_grad_ref, shifts_ref = refs
    cols, width, pairs = sizes
    total = total_of(parts_ref)
    shift_grad, gain_grad = total[0:1], total[1:2]
    pair_grad_ref[0:1, :] = gain_grad
    pair_grad_ref[1:2, :] = shift_grad
    average, inverse_std = twice(stats_ref[0:1, :]), twice(stats_ref[1:2, :])
    scaled = twice(norms_ref[index, 0:1]) * inverse_std * flags_ref[0].astype(jnp.float32)
    shift_mean, gain_mean = twice(shift_grad / pixel_count), twice(gain_grad / pixel_count)
    for pair in range(pairs):
        rows = pl.ds(pair * cols, cols)
        centred = (fired_ref[rows, :].astype(jnp.float32) - average) * inverse_std
        grad = grad_ref[rows, :].astype(jnp.bfloat16).astype(jnp.float32)
        fired_grad = (scaled * (grad - shift_mean - centred * gain_mean)).astype(jnp.bfloat16)
        pre = (fired_grad.astype(jnp.float32) * slope_ref[rows, :].astype(jnp.float32)).astype(jnp.bfloat16)
        pre_ref[rows, :] = pre
        spread_pair(pair, pre.astype(jnp.float32), shifts_ref, sizes)


def back_kernel(
    flags_ref, parts_ref, norms_ref, grad_ref, weight_ref, fired_ref, slope_ref, stats_ref, below_in, below_stats_in,
    *refs, sizes, pixel_count, index, second, top,
):
    cols, width, pairs = sizes
    if not second:
        kept_in, *refs = refs
    if top:
        head_grad_ref, *refs = refs
    pre_out, pair_grad_out, *refs = refs
    if second:
        kept_out, *refs = refs
    out_ref, sums_ref, *refs = refs
    if not second:
        kept_ref, *refs = refs
    below_ref, below_stats_ref, pre_ref, pair_grad_ref, shifts_ref, taps_ref, semaphores = refs
    mover = Mover(semaphores)
    groups = pairs // GROUP
    below_stats = mover.fetch(below_stats_in, below_stats_ref)
    below = mover.fetch(below_in, below_ref)
    if second:
        mover.send(grad_ref, kept_out)
    else:
        kept = mover.fetch(kept_in, kept_ref)
    clear_rim(shifts_ref, sizes)
    taps_backward(weight_ref, taps_ref, width)
    refs = (grad_ref, fired_ref, slope_ref, pre_ref, pair_grad_ref, shifts_ref)
    back_to_preact(parts_ref, stats_ref, norms_ref, index, flags_ref, refs, pixel_count, sizes)
    mover.send(pre_ref, pre_out)
    mover.send(pair_grad_ref, pair_grad_out)
    below_stats[0].wait()
    average, inverse_std = twice(below_stats_ref[0:1, :]), twice(below_stats_ref[1:2, :])
    shift_sum = jnp.zeros((1, 2 * width), jnp.float32)
    gain_sum = jnp.zeros((1, 2 * width), jnp.float32)
    step = GROUP * cols
    if not second:
        kept[0].wait()
    below[0].wait()
    for group in range(groups):
        rows = pl.ds(group * step, step)
        source = pair_conv(shifts_ref, taps_ref, group, cols, ((1,), (1,)))
        if not second:
            source = source + kept_ref[rows, :]
        out_ref[rows, :] = source.astype(out_ref.dtype)
        low = source.astype(jnp.bfloat16).astype(jnp.float32)
        shift_sum += jnp.sum(low, axis=0, keepdims=True)
        gain_sum += jnp.sum(low * ((below_ref[rows, :].astype(jnp.float32) - average) * inverse_std), axis=0, keepdims=True)
    active = flags_ref[0].astype(jnp.float32)
    sums = [folded(shift_sum, width) * active, folded(gain_sum, width) * active]
    put_sums(sums_ref, sums + ([head_grad_ref[...]] if top else []))
    mover.finish()


def cut_frames(flags_ref, flat_ref, mine_ref, theirs_ref, tiles, shard):
    width = flat_ref.shape[1]
    nl, no = tiles[0], tiles[1]
    rows = mine_ref.shape[2]
    for lon_step in range(no):
        for lat_step in range(nl):
            for core_step, target in ((0, mine_ref), (1, theirs_ref)):
                device = device_at(flags_ref, lon_step, lat_step, core_step, tiles)
                start = first_row(device, shard, width)
                target[lon_step, lat_step] = flat_ref[pl.ds(start, rows), :].astype(jnp.bfloat16)


def block_kernel_grad(shifts_ref, pre_ref, flat_ref, sizes):
    cols, width, pairs = sizes
    for a in range(4):
        k, rr = a // 2, a % 2
        block = shifts_ref[k * cols : (k + pairs) * cols, rr * 3 * width : (rr + 1) * 3 * width]
        grad = dot(block, pre_ref[...], ((0,), (0,)))
        if a < 3:
            flat_ref[a * 3 * width : (a + 1) * 3 * width, :] = grad[:, :width]
        if a > 0:
            flat_ref[(a - 1) * 3 * width : a * 3 * width, :] += grad[:, width:]


def kernel_grad_kernel(flags_ref, *refs, tiles, sizes, shard, fetches, joins):
    fetched_from, refs = refs[:fetches], refs[fetches:]
    source_in, pre_in, *refs = refs
    others, refs = refs[:joins], refs[joins:]
    fetched_to, refs = refs[:fetches], refs[fetches:]
    mine_out, theirs_ref, *refs = refs
    if joins:
        joined_ref, frames_ref, *refs = refs
    mine_ref, source_ref, pre_ref, shifts_ref, flat_ref, semaphores = refs
    mover = Mover(semaphores)
    source, pre = mover.fetch(source_in, source_ref), mover.fetch(pre_in, pre_ref)
    for wide, near in zip(fetched_from, fetched_to):
        mover.send(wide, near)
    arrivals = [mover.start(frames, frames_ref.at[i]) for i, frames in enumerate(others)]
    clear_rim(shifts_ref, sizes)
    source[0].wait()
    spread_all_pairs(source_ref, shifts_ref, sizes)
    pre[0].wait()
    block_kernel_grad(shifts_ref, pre_ref, flat_ref, sizes)
    cut_frames(flags_ref, flat_ref, mine_ref, theirs_ref, tiles, shard)
    mover.send(mine_ref, mine_out)
    for arrival in arrivals:
        arrival.wait()
    if joins:
        join_frames(frames_ref, joined_ref)
    mover.finish()


def spread_all_pairs(source_ref, shifts_ref, sizes):
    cols, width, pairs = sizes
    for pair in range(pairs):
        cells = source_ref[pair * cols : (pair + 1) * cols, :].astype(jnp.float32)
        spread_pair(pair, cells, shifts_ref, sizes)


def last_kernel(
    flags_ref, parts_ref, norms_ref, grad_ref, fired_in, slope_in, stats_in, weight_in, kept_in, in_slope_in,
    source_in, wide_in, *refs, tiles, sizes, shards, in_width, pixel_count, others,
):
    cols, width, pairs = sizes
    nl, no = tiles[0], tiles[1]
    near_ins, refs = refs[: 2 * others], refs[2 * others :]
    (
        pair_grad_out, mine_ref, theirs_ref,
        fired_ref, slope_ref, stats_ref, weight_ref, kept_ref, in_slope_ref, source_ref, wide_ref, pre_ref, in_pre_ref, pair_grad_ref,
        shifts_ref, first_shifts_ref, taps_ref, flat_ref, flat_first_ref, others_ref, semaphores,
    ) = refs
    mover = Mover(semaphores)
    groups = pairs // GROUP
    source = mover.fetch(source_in, source_ref)
    early = mover.fetch(stats_in, stats_ref) + mover.fetch(weight_in, weight_ref)
    early += mover.fetch(fired_in, fired_ref) + mover.fetch(slope_in, slope_ref)
    clear_rim(shifts_ref, sizes)
    clear_rim(first_shifts_ref, sizes)
    source[0].wait()
    spread_all_pairs(source_ref, first_shifts_ref, sizes)
    for arrival in early:
        arrival.wait()
    kept = mover.fetch(kept_in, kept_ref)
    in_slope = mover.fetch(in_slope_in, in_slope_ref)
    wide = mover.fetch(wide_in, wide_ref)
    arrivals = [mover.start(other, others_ref.at[i]) for i, other in enumerate(near_ins)]
    taps_backward(weight_ref, taps_ref, width)
    refs = (grad_ref, fired_ref, slope_ref, pre_ref, pair_grad_ref, shifts_ref)
    back_to_preact(parts_ref, stats_ref, norms_ref, 0, flags_ref, refs, pixel_count, sizes)
    mover.send(pair_grad_ref, pair_grad_out)
    kept[0].wait()
    in_slope[0].wait()
    step = GROUP * cols
    for group in range(groups):
        rows = pl.ds(group * step, step)
        grad = pair_conv(shifts_ref, taps_ref, group, cols, ((1,), (1,))) + kept_ref[rows, :]
        in_pre_ref[rows, :] = (grad * in_slope_ref[rows, :].astype(jnp.float32)).astype(jnp.bfloat16)
    block_kernel_grad(first_shifts_ref, pre_ref, flat_first_ref, sizes)
    for arrival in arrivals:
        arrival.wait()
    wide[0].wait()
    for a in range(8):
        k, rr = a // 2, a % 2
        block = wide_ref[k * cols : (k + pairs) * cols, rr * 7 * width : (rr + 1) * 7 * width]
        grads = dot(block, in_pre_ref[...], ((0,), (0,)))
        for b in range(7):
            grad = grads[b * width : b * width + in_width]
            if a < 7:
                tap = a * 7 + b
                flat_ref[tap * in_width : (tap + 1) * in_width, :] = grad[:, :width]
            if a > 0:
                tap = (a - 1) * 7 + b
                flat_ref[tap * in_width : (tap + 1) * in_width, :] += grad[:, width:]
    rows = others_ref.shape[3]
    in_rows = mine_ref.shape[2] - (others + 1) * rows
    for lon_step in range(no):
        for lat_step in range(nl):
            for core_step, target in ((0, mine_ref), (1, theirs_ref)):
                device = device_at(flags_ref, lon_step, lat_step, core_step, tiles)
                spot = pl.ds(first_row(device, shards[0], width), in_rows)
                target[lon_step, lat_step, 0:in_rows, :] = flat_ref[spot, :].astype(jnp.bfloat16)
                spot = pl.ds(first_row(device, shards[1], width), rows)
                block = flat_first_ref[spot, :].astype(jnp.bfloat16)
                target[lon_step, lat_step, in_rows : in_rows + rows, :] = block
                for other in range(others):
                    at = in_rows + (other + 1) * rows
                    target[lon_step, lat_step, at : at + rows, :] = others_ref[
                        2 * other + core_step, lon_step, lat_step
                    ]
    mover.finish()


def join_frames(frames_ref, joined_ref):
    count, no, nl, rows, unused = frames_ref.shape
    for index in range(count // 2):
        for lon_step in range(no):
            for lat_step in range(nl):
                joined_ref[lat_step, lon_step, index * rows : (index + 1) * rows, :] = low_sum(
                    frames_ref[2 * index, lon_step, lat_step], frames_ref[2 * index + 1, lon_step, lat_step]
                )


def swap(values, axis, step):
    return lax.ppermute(values, axis, [(i, i ^ step) for i in range(lax.axis_size(axis))])


def low_sum(*values):
    return sum(part.astype(jnp.float32) for part in values).astype(jnp.bfloat16)


def along(values, axis):
    return [values[0]] + [swap(values[k], axis, k) for k in range(1, values.shape[0])]


def wide_sum(parts):
    return sum(part.astype(jnp.float32) for part in parts)


def spread_all(values, axes):
    return lax.all_to_all(values, axes, 0, 0, tiled=True)


def whole_sample_body(
    fields,
    targets,
    land_mask,
    input_kernel,
    input_first,
    input_second,
    block_kernels,
    block_first,
    block_second,
    head_weight,
    head_first,
    head_second,
    norm_params,
    norm_first,
    norm_second,
):
    samples_here, rows_here, cols_here, in_width = fields.shape
    width = norm_params.shape[2]
    conv_count = block_kernels.shape[0]
    nl, no, nb = (lax.axis_size(axis) for axis in ALL)
    places, devices = nl * no, nl * no * nb
    tiles = (nl, no, rows_here, cols_here)
    cols, pairs = cols_here * no, rows_here * nl // 2
    sizes = (cols, width, pairs)
    pixels = pairs * cols
    sample_count = samples_here * nb
    pixel_count = float(sample_count * 2 * pixels)
    place = lax.axis_index(TILE)
    core = lax.axis_index("batch")
    flags = jnp.stack(
        [
            (place < samples_here).astype(jnp.int32),
            lax.axis_index("batch"),
            lax.axis_index("lat"),
            lax.axis_index("lon"),
        ]
    )
    bf16, f32 = jnp.bfloat16, jnp.float32
    device = lax.axis_index(ALL)
    in_shard, block_shard = input_kernel.shape[0], block_kernels.shape[1]
    in_frame = frame_rows(in_shard, devices, width, SPREAD)
    block_frame = frame_rows(block_shard, devices, width, 8)
    in_offset = device * in_shard % width
    flat_rows = max((devices - 1) * in_shard // width + in_frame, 48 * in_width + width)
    flat_rows = -(-flat_rows // 8) * 8
    block_rows = block_shard // width

    def shard_rows(shards):
        count = shards.shape[0] * block_rows
        rows = shards.astype(bf16).reshape(count, width)
        return jnp.pad(rows, ((0, -count % SPREAD), (0, 0)))

    def from_all(values, axis, count):
        return [values] + [swap(values, axis, k) for k in range(1, count)]

    framed = lax.dynamic_update_slice(
        jnp.zeros((in_frame * width,), bf16), input_kernel.astype(bf16), (in_offset,)
    ).reshape(in_frame, width)
    near = jnp.concatenate([framed, shard_rows(block_kernels[:NEAR])], axis=0)
    near_rows = near.shape[0]
    both = jnp.stack(from_all(jnp.concatenate([near, shard_rows(block_kernels[NEAR:])], axis=0), "lat", nl))

    row_global = (lax.axis_index("lat") * rows_here + jnp.arange(rows_here)).astype(f32)
    latitude = (row_global + 0.5) / (rows_here * nl) * jnp.pi - jnp.pi / 2
    pixel_weight = jnp.cos(latitude)[None, :, None] * land_mask.astype(f32)
    (packed,) = call(
        functools.partial(pack_kernel, in_width=in_width),
        [(fields, VECTOR), (targets.transpose(3, 0, 1, 2), VECTOR), (pixel_weight, VECTOR)],
        [((places, rows_here, cols_here, width), bf16, VECTOR)],
        [pltpu.VMEM((-(-3 * PIECES * rows_here // 16) * 16, cols_here), f32)],
    )
    near, far = both[:, :near_rows], both[:, near_rows:]
    packed, near, far = lax.optimization_barrier((packed, near, far))
    near = from_all(near, "lon", no)
    packed = spread_all(packed, TILE)

    plane = (pixels, 2 * width)
    weight_shape = (9 * width, width)
    flat_weight = pltpu.VMEM((9 * width + block_frame + 8, width), f32)
    wide_shape = ((pairs + 3) * cols, 14 * width)
    shift_shape = ((pairs + 1) * cols, 6 * width)
    shift_scratch = pltpu.VMEM(shift_shape, bf16)
    forward_taps, backward_taps = (2, 6 * width, 2 * width), (2, 2 * width, 6 * width)
    def sums_shape(rows):
        return ((devices, rows, width), f32, VECTOR)

    stats_shape, pair_shape = (8, width), (2, width)
    frame_shape = (no, nl, block_frame, width)
    low_plane, wide_plane = pltpu.VMEM(plane, bf16), pltpu.VMEM(plane, f32)
    weight_scratch, stats_scratch = pltpu.VMEM(weight_shape, bf16), pltpu.VMEM(stats_shape, f32)
    pair_scratch = pltpu.VMEM(pair_shape, f32)
    unit_cost = 2 * 2 * pixels * 9 * width * width

    def kept_outs(*kinds):
        return [(shape, dtype, WIDE) for shape, dtype in kinds]

    far = from_all(far, "lon", no)
    near = [part for values in near for part in (values, swap(values, "batch", 1))]
    near_count, far_count = NEAR, conv_count - NEAR
    out = call(
        functools.partial(
            first_kernel, tiles=tiles, sizes=sizes, shards=[in_shard, block_rows], in_width=in_width, count=near_count
        ),
        [(near[0], WIDE)] + [(part, VECTOR) for part in near[1:]] + [(packed, VECTOR)],
        kept_outs(*[(weight_shape, bf16)] * near_count, (plane, bf16), (wide_shape, bf16), (plane, bf16), (plane, f32), (plane, bf16))
        + [(plane, bf16, VECTOR), (plane, bf16, VECTOR), sums_shape(4)],
        [flat_weight] * near_count
        + [pltpu.VMEM(near[0].shape, bf16), low_plane, pltpu.VMEM((near_count, *weight_shape), bf16)]
        + [pltpu.VMEM((-(-near_count * block_rows // SPREAD) * SPREAD, width), f32)]
        + [pltpu.VMEM((4, 14 * width, 2 * width), bf16), pltpu.VMEM((flat_rows, width), f32)]
        + [pltpu.VMEM(wide_shape, bf16), low_plane, wide_plane, low_plane]
        + [shift_scratch, pltpu.VMEM(forward_taps, bf16)],
        flags,
        6 * unit_cost,
        LARGE_ROOM,
    )
    weights, out = list(out[:near_count]), out[near_count:]
    fields, wide, in_slope, stream, source, fired, slope, sums = out
    far, sums = lax.optimization_barrier((far, sums))
    parts = spread_all(sums, ALL)
    far = [part for values in far for part in (values, swap(values, "batch", 1))]
    *far_weights, weight = call(
        functools.partial(far_kernels_kernel, tiles=tiles, block_rows=block_rows, count=far_count),
        [(part, VECTOR) for part in far],
        kept_outs(*[(weight_shape, bf16)] * far_count) + [(weight_shape, bf16, VECTOR)],
        [pltpu.VMEM((-(-far_count * block_rows // SPREAD) * SPREAD, width), f32)]
        + [flat_weight] * far_count
        + [pltpu.VMEM((far_count, *weight_shape), bf16)],
        flags,
        unit_cost,
    )
    weights += far_weights

    sources, fireds, slopes, stats = [source], [], [], []
    fetched = []
    for k in range(1, conv_count):
        residual = k % 2 == 0
        fetches = [weights[k + 1]] if k + 1 < conv_count else []
        if not residual:
            fetches.append(stream)
        out = call(
            functools.partial(
                unit_kernel, sizes=sizes, pixel_count=pixel_count, index=k - 1, residual=residual,
                fetches=len(fetches),
            ),
            [(array, VECTOR) for array in (fired, parts, norm_params, weight, slope, *fetched)]
            + [(array, WIDE) for array in fetches],
            kept_outs(*[(plane, f32)] * residual, (plane, bf16), (stats_shape, f32), (plane, bf16), (plane, bf16))
            + [(plane, bf16, VECTOR), (plane, bf16, VECTOR), sums_shape(2)]
            + [(array.shape, array.dtype, VECTOR) for array in fetches],
            [wide_plane] * residual
            + [low_plane, stats_scratch, shift_scratch, pltpu.VMEM(forward_taps, bf16)],
            flags,
            unit_cost,
        )
        if residual:
            stream, *out = out
        source, stat, saved_fired, saved_slope, fired, slope, sums, *fetched = out
        sources.append(source)
        stats.append(stat)
        fireds.append(saved_fired)
        slopes.append(saved_slope)
        if k + 1 < conv_count:
            weight, *fetched = fetched
        parts = spread_all(sums, ALL)

    grad, sums, stat, head_local = call(
        functools.partial(
            head_kernel, sizes=sizes, pixel_count=pixel_count, sample_count=sample_count, in_width=in_width,
            index=conv_count - 1, fetches=0,
        ),
        [(array, VECTOR) for array in (fired, parts, norm_params, head_weight.T, *fetched)]
        + [(array, WIDE) for array in (fields, stats[0])],
        [(plane, f32, VECTOR), sums_shape(4), (stats_shape, f32, VECTOR), (head_weight.T.shape, f32, VECTOR)],
        [low_plane, stats_scratch, low_plane],
        flags,
        unit_cost // 4,
    )
    parts = spread_all(sums, ALL)
    loss_parts = parts

    pair_grads, frames = [None] * conv_count, [None] * conv_count
    for k in range(conv_count - 1, 0, -1):
        second, top = k % 2 == 1, k == conv_count - 1
        pre, pair_grads[k], *out = call(
            functools.partial(back_kernel, sizes=sizes, pixel_count=pixel_count, index=k, second=second, top=top),
            [(array, VECTOR) for array in (parts, norm_params, grad, weight, fired, slope, stat)]
            + [(array, WIDE) for array in (fireds[k - 1], stats[k - 1])]
            + [(array, WIDE) for array in (() if second else (kept_grad,))]
            + [(head_local, VECTOR)] * top,
            kept_outs((plane, bf16), (pair_shape, f32), *[(plane, f32)] * second)
            + [(plane, bf16 if second else f32, VECTOR), sums_shape(4 if top else 2)],
            [wide_plane] * (not second)
            + [low_plane, stats_scratch, low_plane, pair_scratch, shift_scratch, pltpu.VMEM(backward_taps, bf16)],
            flags,
            unit_cost,
        )
        if second:
            kept_grad, *out = out
        grad, sums = out
        parts = spread_all(sums, ALL)
        if top:
            head_parts = parts
        fetches = (weights[k - 1], fireds[k - 1], slopes[k - 1], stats[k - 1]) if k > 1 else ()
        others = ()
        if LATE <= k + 1 < conv_count:
            frames[k + 1][1] = swap(frames[k + 1][1], "batch", 1)
        if k == 1:
            others = [part for pair in frames[LATE:] for part in pair]
        out = call(
            functools.partial(
                kernel_grad_kernel, tiles=tiles, sizes=sizes, shard=block_shard, fetches=len(fetches),
                joins=len(others),
            ),
            [(array, WIDE) for array in (*fetches, sources[k], pre, *others)],
            [(array.shape, array.dtype, VECTOR) for array in fetches]
            + [(frame_shape, bf16, WIDE), (frame_shape, bf16, VECTOR)]
            + [((nl, no, (conv_count - LATE) * block_frame, width), bf16, VECTOR)] * (k == 1),
            [pltpu.VMEM((len(others), *frame_shape), bf16)] * (k == 1)
            + [pltpu.VMEM(frame_shape, bf16), low_plane, low_plane, shift_scratch, flat_weight],
            flags,
            unit_cost,
        )
        if k == 1:
            *frames[1], early = out
            parts, early, frames[1:LATE] = lax.optimization_barrier((parts, early, frames[1:LATE]))
            continue
        weight, fired, slope, stat, *frames[k] = out
        parts, frames[k:] = lax.optimization_barrier((parts, frames[k:]))
    pair_grads[0], mine, theirs = call(
        functools.partial(
            last_kernel, tiles=tiles, sizes=sizes, shards=[in_shard, block_shard], in_width=in_width,
            pixel_count=pixel_count, others=LATE - 1,
        ),
        [(array, VECTOR) for array in (parts, norm_params, grad)]
        + [(array, WIDE) for array in (fireds[0], slopes[0], stats[0], weights[0])]
        + [(array, WIDE) for array in (kept_grad, in_slope, sources[0], wide)]
        + [(part, WIDE) for pair in frames[1:LATE] for part in pair],
        kept_outs((pair_shape, f32))
        + [((no, nl, in_frame + LATE * block_frame, width), bf16, VECTOR)] * 2,
        [low_plane, low_plane, stats_scratch, weight_scratch, wide_plane, low_plane, low_plane]
        + [pltpu.VMEM(wide_shape, bf16), low_plane, low_plane]
        + [pair_scratch, shift_scratch, shift_scratch, pltpu.VMEM(backward_taps, bf16)]
        + [pltpu.VMEM((flat_rows, width), f32), flat_weight]
        + [pltpu.VMEM((2 * (LATE - 1), *frame_shape), bf16)],
        flags,
        6 * unit_cost,
        LARGE_ROOM,
    )
    late, early = lax.optimization_barrier((low_sum(mine, swap(theirs, "batch", 1)), early))
    late = along(late, "lon")
    early = along(early, "lat")
    early, late = lax.optimization_barrier((early, late))
    early, late = along(low_sum(*early), "lon"), along(low_sum(*late), "lat")
    early[1], head_parts, loss_parts, first_stats, norm_grad = lax.optimization_barrier(
        (early[1], head_parts, loss_parts, stats[0], jnp.stack(pair_grads))
    )
    early, late = wide_sum(early), wide_sum(late)
    input_grad = lax.dynamic_slice(late[:in_frame].reshape(-1), (in_offset,), (in_shard,))
    block_grad = jnp.concatenate([late[in_frame:], early], axis=0)
    block_grad = block_grad.reshape(conv_count, block_frame, width)[:, :block_rows]
    block_grad = block_grad.reshape(conv_count, block_shard)
    head_grad = jnp.sum(head_parts, axis=0)[2:4].T
    loss_sum = jnp.sum(loss_parts, axis=0)[2, 0]
    loss_weight = first_stats[2, 0] / sample_count
    return finished(
        loss_sum, loss_weight, input_grad, block_grad, head_grad, norm_grad,
        (input_kernel, input_first, input_second), (block_kernels, block_first, block_second),
        (head_weight, head_first, head_second), (norm_params, norm_first, norm_second),
    )


def one_device_takes_a_sample(fields, block_kernels, head_weight, norm_params):
    samples_here, rows_here, cols_here, in_width = fields.shape
    nl, no, nb = (lax.axis_size(axis) for axis in ALL)
    rows, cols, width = rows_here * nl, cols_here * no, norm_params.shape[2]
    return (
        samples_here <= nl * no
        and nb == 2
        and nl & (nl - 1) == 0
        and no & (no - 1) == 0
        and rows * cols <= MOST_PIXELS
        and rows % (2 * GROUP) == 0
        and cols % 128 == 0
        and cols_here % 8 == 0
        and width == 128
        and head_weight.shape[1] == 2
        and in_width + 3 * PIECES <= width
        and block_kernels.shape[1] % width == 0
        and block_kernels.shape[0] > max(NEAR, LATE)
    )


def body(*args):
    fields, block_kernels, head_weight, norm_params = args[0], args[6], args[9], args[12]
    if one_device_takes_a_sample(fields, block_kernels, head_weight, norm_params):
        return whole_sample_body(*args)
    return tile_body(*args)


def solution(mesh):
    in_specs = (
        P("batch", "lat", "lon", None),
        P("batch", "lat", "lon", None),
        P("batch", "lat", "lon"),
        P(("lat", "lon", "batch")),
        P(("lat", "lon", "batch")),
        P(("lat", "lon", "batch")),
        P(None, ("lat", "lon", "batch")),
        P(None, ("lat", "lon", "batch")),
        P(None, ("lat", "lon", "batch")),
        P(),
        P(),
        P(),
        P(),
        P(),
        P(),
    )
    out_specs = (
        P(),
        P(),
        P(("lat", "lon", "batch")),
        P(("lat", "lon", "batch")),
        P(("lat", "lon", "batch")),
        P(None, ("lat", "lon", "batch")),
        P(None, ("lat", "lon", "batch")),
        P(None, ("lat", "lon", "batch")),
        P(),
        P(),
        P(),
        P(),
        P(),
        P(),
    )
    return jax.shard_map(body, mesh=mesh, in_specs=in_specs, out_specs=out_specs, check_vma=False)
```

```python
import functools

import jax
import jax.numpy as jnp
from jax import lax
from jax.experimental import pallas as pl
from jax.experimental.pallas import tpu as pltpu
from jax.sharding import PartitionSpec as P

STEP = 10


NORM_EPSILON = 1e-05
GELU_SCALE = 0.7978845608028654
GELU_CUBE = 0.044715
GROUP = 4

SMALL_ROOM = 14 << 20
LARGE_ROOM = 36 << 20
COPIES = 32
FORWARD, BACKWARD = 1, 2
NEAR = 1
LATE = 3
MOST_PIXELS = 4096


def shortened(shard):

    def short(part):
        return part.astype(jnp.bfloat16) if part.dtype == jnp.float32 else part

    return jax.tree.map(short, shard)


def with_halo(cells, sides, width):
    for axis, dim in sides:
        count = lax.axis_size(axis)
        ends = count - 1
        head = lax.slice_in_dim(cells, 0, width, axis=dim)
        tail = lax.slice_in_dim(cells, cells.shape[dim] - width, cells.shape[dim], axis=dim)
        cells = jnp.concatenate(
            [
                lax.ppermute(tail, axis, [(i, (i + 1) % count) for i in range(ends)]),
                cells,
                lax.ppermute(head, axis, [((i + 1) % count, i) for i in range(ends)]),
            ],
            axis=dim,
        )
    return cells


def conv_valid(padded, kernel):
    return lax.conv_general_dilated(
        padded,
        kernel,
        (1, 1),
        "VALID",
        dimension_numbers=("NHWC", "HWIO", "NHWC"),
        preferred_element_type=jnp.float32,
    )


def kernel_grad(padded, gradient):
    summed = lax.conv_general_dilated(
        padded,
        gradient,
        (1, 1),
        "VALID",
        dimension_numbers=("CHWN", "IHWO", "NHWC"),
        preferred_element_type=jnp.float32,
    )
    return summed.transpose(1, 2, 0, 3)


def rim_cells(values):
    return with_halo(shortened(values), (("lat", 1), ("lon", 2)), 1).astype(values.dtype)


def to_channels(values):
    return jax.tree.map(
        lambda part, own: part.astype(own.dtype),
        lax.all_to_all(shortened(values), "lat", split_axis=3, concat_axis=0, tiled=True),
        values,
    )


def to_pixels(values):
    return lax.all_to_all(values, "lat", split_axis=0, concat_axis=3, tiled=True)


def spread_sums(summed, squares):
    return lax.psum((summed, squares), ("lon", "batch"))


def own_channels(norm_pair, width):
    return lax.dynamic_slice_in_dim(norm_pair, lax.axis_index("lat") * width, width, 1)


def norm_forward(fired, norm_pair, pixel_count):
    values = to_channels(fired)
    norm_pair = own_channels(norm_pair, values.shape[3])
    widened = values.astype(jnp.float32)
    summed, squares = spread_sums(
        jnp.sum(widened, axis=(0, 1, 2)), jnp.sum(widened * widened, axis=(0, 1, 2))
    )
    average = summed / pixel_count
    inverse_std = lax.rsqrt(squares / pixel_count - average * average + NORM_EPSILON)
    centred = (widened - average) * inverse_std
    normed = (norm_pair[0] * centred + norm_pair[1]).astype(jnp.bfloat16)
    normed = to_pixels(normed)
    return (normed, (centred, inverse_std, norm_pair))


def norm_backward(gradient, kept, pixel_count):
    centred, inverse_std, norm_pair = kept
    gradient = to_channels(gradient)
    widened = gradient.astype(jnp.float32)
    shift_grad, gain_grad = spread_sums(
        jnp.sum(widened, axis=(0, 1, 2)), jnp.sum(widened * centred, axis=(0, 1, 2))
    )
    scaled = norm_pair[0] * inverse_std
    fired_grad = (
        scaled * (widened - shift_grad / pixel_count - centred * gain_grad / pixel_count)
    ).astype(jnp.bfloat16)
    fired_grad = to_pixels(fired_grad)
    return (fired_grad, jnp.stack([gain_grad, shift_grad]))


def gelu_pullback(preact, gradient):
    unused, pullback = jax.vjp(jax.nn.gelu, preact)
    return pullback(gradient)[0]


def conv_forward(source, kernel, norm_pair, pixel_count):
    padded = rim_cells(source)
    preact = conv_valid(padded, kernel)
    fired = jax.nn.gelu(preact).astype(jnp.bfloat16)
    normed, kept = norm_forward(fired, norm_pair, pixel_count)
    return (normed, (padded, preact, kept))


def conv_backward(gradient, kernel, record, pixel_count):
    padded, preact, kept = record
    fired_grad, pair_grad = norm_backward(gradient, kept, pixel_count)
    preact_grad = gelu_pullback(preact, fired_grad.astype(jnp.float32)).astype(jnp.bfloat16)
    kernel_gradient = kernel_grad(padded, preact_grad)
    flipped = kernel[::-1, ::-1].transpose(0, 1, 3, 2)
    source_grad = conv_valid(rim_cells(preact_grad), flipped)
    return (source_grad, kernel_gradient, pair_grad)


def block_forward(stream, kernels, norm_pairs, pixel_count):
    middle, first_record = conv_forward(
        stream.astype(jnp.bfloat16), kernels[0], norm_pairs[0], pixel_count
    )
    branch, second_record = conv_forward(middle, kernels[1], norm_pairs[1], pixel_count)
    return (stream + branch.astype(jnp.float32), (first_record, second_record))


def block_backward(stream_grad, stream, kernels, norm_pairs, pixel_count):
    unused, records = block_forward(stream, kernels, norm_pairs, pixel_count)
    middle_grad, second_kernel, second_pair = conv_backward(
        stream_grad.astype(jnp.bfloat16), kernels[1], records[1], pixel_count
    )
    source_grad, first_kernel, first_pair = conv_backward(
        middle_grad.astype(jnp.bfloat16), kernels[0], records[0], pixel_count
    )
    return (stream_grad + source_grad, (first_kernel, second_kernel), (first_pair, second_pair))


def adamw_update(weight, gradient, momentum, variance, step_rate):
    momentum = 0.9 * momentum + 0.1 * gradient
    variance = 0.999 * variance + 0.001 * gradient * gradient
    corrected = momentum / (1.0 - 0.9**STEP)
    scaled = jnp.sqrt(variance / (1.0 - 0.999**STEP)) + 1e-08
    return (momentum, variance, weight - step_rate * (corrected / scaled + 0.01 * weight))


def finished(
    loss_sum, loss_weight, input_grad, block_grad, head_grad, norm_grad,
    input_state, block_state, head_state, norm_state,
):
    outputs = [jnp.reshape(loss_sum, (1,)), jnp.reshape(loss_weight, (1,))]
    for state, gradient, step_rate in (
        (input_state, input_grad, 0.015),
        (block_state, block_grad, 0.03),
        (head_state, head_grad, 0.15),
        (norm_state, norm_grad, 0.8),
    ):
        weight, first, second = state
        outputs.extend(adamw_update(weight, gradient, first, second, step_rate))
    return tuple(outputs)


def tile_body(
    fields,
    targets,
    land_mask,
    input_kernel,
    input_first,
    input_second,
    block_kernels,
    block_first,
    block_second,
    head_weight,
    head_first,
    head_second,
    norm_params,
    norm_first,
    norm_second,
):
    samples_here, rows_here, cols_here, in_width = fields.shape
    channels = norm_params.shape[2]
    conv_count = block_kernels.shape[0]
    full_input, full_blocks = (
        lax.all_gather(
            input_kernel.astype(jnp.bfloat16), ("lat", "lon", "batch"), axis=0, tiled=True
        ),
        lax.all_gather(
            block_kernels.astype(jnp.bfloat16), ("lat", "lon", "batch"), axis=1, tiled=True
        ),
    )
    kernel_in = full_input.reshape(7, 7, in_width, channels)
    kernels = full_blocks.reshape(conv_count, 3, 3, channels, channels)
    head_low = head_weight.astype(jnp.bfloat16)
    sample_count = samples_here * lax.axis_size("batch")
    pixel_count = float(
        sample_count * rows_here * lax.axis_size("lat") * cols_here * lax.axis_size("lon")
    )
    row_global = (lax.axis_index("lat") * rows_here + jnp.arange(rows_here)).astype(jnp.float32)
    latitude = (row_global + 0.5) / (rows_here * lax.axis_size("lat")) * jnp.pi - jnp.pi / 2
    pixel_weight = jnp.cos(latitude)[None, :, None] * land_mask.astype(jnp.float32)
    valid_sum = lax.psum(jnp.sum(pixel_weight), ("lat", "lon", "batch"))
    loss_weight = valid_sum / sample_count
    padded_in = with_halo(fields, (("lat", 1), ("lon", 2)), 3)
    preact_in = conv_valid(padded_in, kernel_in)
    streams = [jax.nn.gelu(preact_in)]
    for layer in range(conv_count // 2):
        advanced, unused = block_forward(
            streams[-1],
            kernels[2 * layer : 2 * layer + 2],
            norm_params[2 * layer : 2 * layer + 2],
            pixel_count,
        )
        streams.append(advanced)
    top_stream = streams[-1].astype(jnp.bfloat16)
    predicted = jnp.einsum(
        "nhwc,co->nhwo", top_stream, head_low, preferred_element_type=jnp.float32
    )
    misfit = predicted - targets
    loss_local = jnp.sum(pixel_weight[..., None] * misfit * misfit)
    pred_grad = (2.0 * pixel_weight[..., None] * misfit / loss_weight).astype(jnp.bfloat16)
    head_local = jnp.einsum(
        "nhwc,nhwo->co", top_stream, pred_grad, preferred_element_type=jnp.float32
    )
    stream_grad = jnp.einsum(
        "nhwo,co->nhwc", pred_grad, head_low, preferred_element_type=jnp.float32
    )
    kernel_grads = [None] * conv_count
    pair_grads = [None] * conv_count
    for layer in reversed(range(conv_count // 2)):
        stream_grad, kernel_pair, norm_pair = block_backward(
            stream_grad,
            streams[layer],
            kernels[2 * layer : 2 * layer + 2],
            norm_params[2 * layer : 2 * layer + 2],
            pixel_count,
        )
        kernel_grads[2 * layer], kernel_grads[2 * layer + 1] = kernel_pair
        pair_grads[2 * layer], pair_grads[2 * layer + 1] = norm_pair
    pre_in_grad = gelu_pullback(preact_in, stream_grad).astype(jnp.bfloat16)
    input_local = kernel_grad(padded_in, pre_in_grad).reshape(-1)
    block_local = jnp.stack(kernel_grads).reshape(conv_count, -1)
    input_grad, block_grad = (
        lax.psum_scatter(input_local, ("lat", "lon", "batch"), scatter_dimension=0, tiled=True),
        lax.psum_scatter(block_local, ("lat", "lon", "batch"), scatter_dimension=1, tiled=True),
    )
    head_grad, loss_sum = lax.psum((head_local, loss_local), ("lat", "lon", "batch"))
    norm_grad = jnp.stack(pair_grads)
    norm_grad = lax.all_gather(norm_grad, "lat", axis=2, tiled=True)
    return finished(
        loss_sum, loss_weight, input_grad, block_grad, head_grad, norm_grad,
        (input_kernel, input_first, input_second), (block_kernels, block_first, block_second),
        (head_weight, head_first, head_second), (norm_params, norm_first, norm_second),
    )


ALL = ("lat", "lon", "batch")
TILE = ("lat", "lon")
PIECES = 3
SPREAD = 16


VECTOR, WIDE = "vector", "wide"
SPACES = {VECTOR: pltpu.VMEM, WIDE: pltpu.HBM}


def call(kernel, ins, outs, scratch=(), flags=None, cost=0, room=SMALL_ROOM, aliases=()):
    specs = [pl.BlockSpec(memory_space=SPACES[space]) for unused, space in ins]
    args = [
        pltpu.with_memory_space_constraint(array, pltpu.HBM) if space == WIDE else array
        for array, space in ins
    ]
    if flags is not None:
        specs, args = [pl.BlockSpec(memory_space=pltpu.SMEM)] + specs, [flags] + args
    return pl.pallas_call(
        kernel,
        out_shape=[
            pltpu.HBM(shape, dtype) if space == WIDE else jax.ShapeDtypeStruct(shape, dtype)
            for shape, dtype, space in outs
        ],
        in_specs=specs,
        out_specs=[pl.BlockSpec(memory_space=SPACES[space]) for *unused, space in outs],
        scratch_shapes=list(scratch) + [pltpu.SemaphoreType.DMA((COPIES,))],
        input_output_aliases=dict(aliases),
        compiler_params=pltpu.CompilerParams(vmem_limit_bytes=room),
        cost_estimate=pl.CostEstimate(flops=cost, bytes_accessed=4 << 20, transcendentals=0),
    )(*args)


class Mover:
    def __init__(self, semaphores):
        self.semaphores, self.used, self.sent = semaphores, 0, []

    def start(self, source, target):
        copy = pltpu.make_async_copy(source, target, self.semaphores.at[self.used])
        self.used += 1
        copy.start()
        return copy

    def fetch(self, source, target, parts=1):
        step = target.shape[0] // parts
        return [
            self.start(source.at[pl.ds(i * step, step)], target.at[pl.ds(i * step, step)])
            for i in range(parts)
        ]

    def send(self, source, target):
        self.sent.append(self.start(source, target))

    def finish(self):
        for copy in self.sent:
            copy.wait()


def dot(left, right, dims=((1,), (0,))):
    return lax.dot_general(left, right, (dims, ((), ())), preferred_element_type=jnp.float32)


def gelu_value(x):
    return x * (0.5 * (1.0 + jnp.tanh(GELU_SCALE * (x + GELU_CUBE * (x * x * x)))))


def gelu_both(x):
    square = x * x
    level = jnp.tanh(GELU_SCALE * (x + GELU_CUBE * (x * square)))
    half = 0.5 * (1.0 + level)
    slope = half + 0.5 * x * (1.0 - level * level) * (GELU_SCALE * (1.0 + 3.0 * GELU_CUBE * square))
    return x * half, slope


def shifted(cells, step):
    count = cells.shape[0]
    if step == 0:
        return cells
    column = lax.broadcasted_iota(jnp.int32, cells.shape, 0) + step
    rolled = pltpu.roll(cells, (-step) % count, 0)
    return jnp.where((column >= 0) & (column < count), rolled, 0.0)


def spread_pair(pair, cells, shifts_ref, sizes):
    cols, width, pairs = sizes
    for b in range(3):
        moved = shifted(cells, b - 1).astype(jnp.bfloat16)
        shifts_ref[(pair + 1) * cols : (pair + 2) * cols, b * width : (b + 1) * width] = moved[:, width:]
        shifts_ref[pair * cols : (pair + 1) * cols, (3 + b) * width : (4 + b) * width] = moved[:, :width]


def clear_rim(shifts_ref, sizes):
    cols, width, pairs = sizes
    zero = jnp.zeros((cols, 3 * width), jnp.bfloat16)
    shifts_ref[0:cols, 0 : 3 * width] = zero
    shifts_ref[pairs * cols : (pairs + 1) * cols, 3 * width : 6 * width] = zero


def taps_forward(weight_ref, taps_ref, width):
    for k in range(2):
        for rr in range(2):
            for b in range(3):
                for q in range(2):
                    a = 2 * k + rr - q
                    at = (rr * 3 + b) * width
                    if 0 <= a <= 2:
                        block = weight_ref[(a * 3 + b) * width : (a * 3 + b + 1) * width, :]
                    else:
                        block = jnp.zeros((width, width), jnp.bfloat16)
                    taps_ref[k, at : at + width, q * width : (q + 1) * width] = block


def taps_backward(weight_ref, taps_ref, width):
    for k in range(2):
        for rr in range(2):
            for b in range(3):
                for q in range(2):
                    a = 2 - (2 * k + rr - q)
                    at = (rr * 3 + b) * width
                    if 0 <= a <= 2:
                        tap = a * 3 + 2 - b
                        block = weight_ref[tap * width : (tap + 1) * width, :]
                    else:
                        block = jnp.zeros((width, width), jnp.bfloat16)
                    taps_ref[k, q * width : (q + 1) * width, at : at + width] = block


def pair_conv(shifts_ref, taps_ref, group, cols, dims=((1,), (0,)), size=GROUP):
    rows = size * cols
    first = shifts_ref[group * rows : (group + 1) * rows, :]
    second = shifts_ref[group * rows + cols : (group + 1) * rows + cols, :]
    return dot(first, taps_ref[0], dims) + dot(second, taps_ref[1], dims)


def folded(sums, width):
    return sums[:, :width] + sums[:, width:]


def total_of(parts_ref):
    return jnp.sum(parts_ref[...], axis=0)


def twice(row):
    return jnp.concatenate([row, row], axis=1)


def norm_of(total, pixel_count):
    average = total[0:1] / pixel_count
    return average, lax.rsqrt(total[1:2] / pixel_count - average * average + NORM_EPSILON)


def conv_and_sums(flags_ref, shifts_ref, taps_ref, fired_ref, slope_ref, sums_ref, sizes, more=None, size=GROUP):
    cols, width, pairs = sizes
    total = jnp.zeros((1, 2 * width), jnp.float32)
    squares = jnp.zeros((1, 2 * width), jnp.float32)
    step = size * cols
    for group in range(pairs // size):
        fired, slope = gelu_both(pair_conv(shifts_ref, taps_ref, group, cols, size=size))
        rows = pl.ds(group * step, step)
        fired = fired.astype(jnp.bfloat16)
        fired_ref[rows, :] = fired
        slope_ref[rows, :] = slope.astype(jnp.bfloat16)
        wide = fired.astype(jnp.float32)
        total = total + jnp.sum(wide, axis=0, keepdims=True)
        squares = squares + jnp.sum(wide * wide, axis=0, keepdims=True)
    active = flags_ref[0].astype(jnp.float32)
    parts = [folded(total, width) * active, folded(squares, width) * active]
    put_sums(sums_ref, parts + (more or []))


def put_sums(sums_ref, parts):
    shape = sums_ref.shape[1:]
    row = lax.broadcasted_iota(jnp.int32, shape, 0)
    block = jnp.zeros(shape, jnp.float32)
    at = 0
    for part in parts:
        for i in range(part.shape[0]):
            block = jnp.where(row == at, jnp.broadcast_to(part[i : i + 1], shape), block)
            at += 1
    sums_ref[...] = jnp.broadcast_to(block[None], sums_ref.shape)


def field_row(fields_ref, row, tiles):
    nl, no, rows_here, cols_here = tiles
    lat, inner = row // rows_here, row % rows_here
    return jnp.concatenate([fields_ref[lat * no + lon, inner] for lon in range(no)], axis=0)


def wide_shifts(row_of, shifts_ref, sizes):
    cols, width, pairs = sizes
    rows = 2 * pairs
    for row in range(-3, rows + 3):
        at, rr = (row + 3) // 2, (row + 3) % 2
        if 0 <= row < rows:
            cells = row_of(row).astype(jnp.float32)
        for b in range(7):
            if 0 <= row < rows:
                moved = shifted(cells, b - 3).astype(jnp.bfloat16)
            else:
                moved = jnp.zeros((cols, width), jnp.bfloat16)
            spot = (rr * 7 + b) * width
            shifts_ref[at * cols : (at + 1) * cols, spot : spot + width] = moved


def first_row(device, shard, width):
    return lax.div(device * shard, width)


def frame_rows(shard, devices, width, grain):
    rows = max(-(-(d + 1) * shard // width) - d * shard // width for d in range(devices))
    return -(-rows // grain) * grain


def device_at(flags_ref, lon_step, lat_step, core_step, tiles):
    lat = flags_ref[2] ^ lat_step
    lon = flags_ref[3] ^ lon_step
    return (lat * tiles[1] + lon) * 2 + (flags_ref[1] ^ core_step)


def pack_kernel(fields_ref, targets_ref, weights_ref, packed_ref, pieces_ref, unused_ref, *, in_width):
    samples, rows, cols, unused = fields_ref.shape
    width = packed_ref.shape[3]
    outs = targets_ref.shape[0]
    many = pieces_ref.shape[0]
    pieces_ref[...] = jnp.zeros(pieces_ref.shape, jnp.float32)
    packed_ref[samples:] = jnp.zeros((packed_ref.shape[0] - samples, rows, cols, width), jnp.bfloat16)
    take_from = lax.broadcasted_iota(jnp.int32, (many, width), 0)
    put_to = lax.broadcasted_iota(jnp.int32, (many, width), 1) - in_width
    picks = [
        jnp.where((put_to >= 0) & (take_from == put_to * rows + row), 1.0, 0.0).astype(jnp.bfloat16)
        for row in range(rows)
    ]
    for sample in range(samples):
        for source in range(outs + 1):
            left = targets_ref[source, sample] if source < outs else weights_ref[sample]
            for piece in range(PIECES):
                low = left.astype(jnp.bfloat16).astype(jnp.float32)
                left = left - low
                at = (source * PIECES + piece) * rows
                pieces_ref[at : at + rows, :] = low
        pieces = pieces_ref[...].astype(jnp.bfloat16)
        for row in range(rows):
            placed = dot(pieces, picks[row], ((0,), (0,))).astype(jnp.bfloat16)
            packed_ref[sample, row] = placed
            packed_ref[sample, row, :, 0:in_width] = fields_ref[sample, row]


def place_blocks(part, at, count, rows, device, stage_ref, flat_refs):
    stage_ref[...] = part[at : at + stage_ref.shape[0], :].astype(jnp.float32)
    for index in range(count):
        flat_refs[index][pl.ds(device * rows, rows), :] = stage_ref[index * rows : (index + 1) * rows, :]


def near_kernels(
    flags_ref, parts, taps_ref, flat_ref, stage_ref, flat_block_refs, tiles, shards, in_width
):
    nl, no = tiles[0], tiles[1]
    width = flat_ref.shape[1]
    in_shard, block_rows = shards
    rows = frame_rows(in_shard, 2 * nl * no, width, SPREAD)
    flat_ref[...] = jnp.zeros(flat_ref.shape, jnp.float32)
    for lon_step in range(no):
        for core_step in range(2):
            part = parts[lon_step * 2 + core_step]
            for lat_step in range(nl):
                device = device_at(flags_ref, lon_step, lat_step, core_step, tiles)
                spot = pl.ds(first_row(device, in_shard, width), rows)
                flat_ref[spot, :] += part[lat_step, 0:rows, :].astype(jnp.float32)
                place_blocks(
                    part.at[lat_step], rows, len(flat_block_refs), block_rows, device, stage_ref, flat_block_refs
                )
    inside = lax.broadcasted_iota(jnp.int32, (width, width), 0) < in_width
    zero = jnp.zeros((width, width), jnp.bfloat16)
    for b in range(7):
        taps_ref[3, (7 + b) * width : (8 + b) * width, 0:width] = zero
        taps_ref[0, b * width : (b + 1) * width, width : 2 * width] = zero
        for a in range(7):
            tap = a * 7 + b
            block = flat_ref[tap * in_width : tap * in_width + width, :]
            block = jnp.where(inside, block, 0.0).astype(jnp.bfloat16)
            for q in range(2):
                k, rr = (a + q) // 2, (a + q) % 2
                spot = (rr * 7 + b) * width
                taps_ref[k, spot : spot + width, q * width : (q + 1) * width] = block


def far_kernels_kernel(flags_ref, *refs, tiles, block_rows, count):
    nl, no = tiles[0], tiles[1]
    parts, outs, next_ref, refs = refs[: 2 * no], refs[2 * no : 2 * no + count], refs[2 * no + count], refs[2 * no + count + 1 :]
    stage_ref, *flat_refs, whole_ref, semaphores = refs
    mover = Mover(semaphores)
    for lon_step in range(no):
        for core_step in range(2):
            at = lon_step * 2 + core_step
            for lat_step in range(nl):
                device = device_at(flags_ref, lon_step, lat_step, core_step, tiles)
                place_blocks(parts[at].at[lat_step], 0, count, block_rows, device, stage_ref, flat_refs)
    for index in range(count):
        weight = flat_refs[index][0 : whole_ref.shape[1], :].astype(jnp.bfloat16)
        whole_ref[index] = weight
        if index == 0:
            next_ref[...] = weight
        mover.send(whole_ref.at[index], outs[index])
    mover.finish()


def first_kernel(flags_ref, *refs, tiles, sizes, shards, in_width, count):
    cols, width, pairs = sizes
    nl, no = tiles[0], tiles[1]
    own_in, near, refs = refs[0], refs[1 : 2 * no], refs[2 * no :]
    fields_ref, *refs = refs
    weight_outs, refs = refs[:count], refs[count:]
    pairs_out, wide_out, slope_in_out, stream_out, source_out, fired_ref, slope_ref, sums_ref, *refs = refs
    flat_block_refs, refs = refs[:count], refs[count:]
    own_ref, *refs = refs
    (
        pairs_ref, weights_ref, stage_ref, in_taps_ref, flat_ref, wide_ref,
        slope_in_ref, stream_ref, source_ref, shifts_ref, taps_ref, semaphores,
    ) = refs
    mover = Mover(semaphores)
    own = mover.fetch(own_in, own_ref)
    clear_rim(shifts_ref, sizes)

    def row_of(row):
        cells = field_row(fields_ref, row, tiles)
        pair, q = row // 2, row % 2
        pairs_ref[pair * cols : (pair + 1) * cols, q * width : (q + 1) * width] = cells
        return cells

    wide_shifts(row_of, wide_ref, sizes)
    mover.send(pairs_ref, pairs_out)
    mover.send(wide_ref, wide_out)
    own[0].wait()
    near_kernels(
        flags_ref, (own_ref, *near), in_taps_ref, flat_ref, stage_ref, flat_block_refs, tiles, shards, in_width
    )
    for index in range(count):
        weight = flat_block_refs[index][0 : weights_ref.shape[1], :].astype(jnp.bfloat16)
        weights_ref[index] = weight
        mover.send(weights_ref.at[index], weight_outs[index])
    taps_forward(weights_ref.at[0], taps_ref, width)
    step = GROUP * cols
    for group in range(pairs // GROUP):
        at = group * step
        preact = dot(wide_ref[at : at + step, :], in_taps_ref[0])
        for k in range(1, 4):
            preact += dot(wide_ref[at + k * cols : at + step + k * cols, :], in_taps_ref[k])
        rows = pl.ds(at, step)
        stream, slope = gelu_both(preact)
        slope_in_ref[rows, :] = slope.astype(jnp.bfloat16)
        mover.send(slope_in_ref.at[rows], slope_in_out.at[rows])
        stream_ref[rows, :] = stream
        mover.send(stream_ref.at[rows], stream_out.at[rows])
        source = stream.astype(jnp.bfloat16)
        source_ref[rows, :] = source
        mover.send(source_ref.at[rows], source_out.at[rows])
        for pair in range(GROUP):
            cells = source[pair * cols : (pair + 1) * cols].astype(jnp.float32)
            spread_pair(group * GROUP + pair, cells, shifts_ref, sizes)
    weight_sum = folded(jnp.sum(pairs_ref[...].astype(jnp.float32), axis=0, keepdims=True), width)
    lane = lax.broadcasted_iota(jnp.int32, (1, width), 1) - in_width
    chosen = (lane >= 2 * PIECES) & (lane < 3 * PIECES)
    weight_sum = jnp.sum(jnp.where(chosen, weight_sum, 0.0), axis=1, keepdims=True)
    conv_and_sums(
        flags_ref, shifts_ref, taps_ref, fired_ref, slope_ref, sums_ref, sizes,
        [jnp.broadcast_to(weight_sum, (1, width))],
    )
    mover.finish()


def keep_norm(stats_ref, total, average, inverse_std):
    stats_ref[0:1, :] = average
    stats_ref[1:2, :] = inverse_std
    if total.shape[0] > 2:
        stats_ref[2:3, :] = total[2:3]


def unit_kernel(
    flags_ref, fired_in_ref, parts_ref, norms_ref, weight_ref, slope_in_ref, *refs,
    sizes, pixel_count, index, residual, fetches,
):
    cols, width, pairs = sizes
    if residual:
        stream_in_ref, *refs = refs
    fetched_from, refs = refs[:fetches], refs[fetches:]
    if residual:
        stream_out, *refs = refs
    source_out, stats_out, fired_out, slope_out, fired_ref, slope_ref, sums_ref, *refs = refs
    fetched_to, refs = refs[:fetches], refs[fetches:]
    if residual:
        stream_ref, *refs = refs
    source_ref, stats_ref, shifts_ref, taps_ref, semaphores = refs
    mover = Mover(semaphores)
    mover.send(fired_in_ref, fired_out)
    mover.send(slope_in_ref, slope_out)
    for source, target in zip(fetched_from, fetched_to):
        mover.send(source, target)
    total = total_of(parts_ref)
    average, inverse_std = norm_of(total, pixel_count)
    keep_norm(stats_ref, total, average, inverse_std)
    mover.send(stats_ref, stats_out)
    average, inverse_std = twice(average), twice(inverse_std)
    gain, shift = twice(norms_ref[index, 0:1]), twice(norms_ref[index, 1:2])
    taps_forward(weight_ref, taps_ref, width)
    clear_rim(shifts_ref, sizes)
    for pair in range(pairs):
        rows = pl.ds(pair * cols, cols)
        fired = fired_in_ref[rows, :].astype(jnp.float32)
        normed = (gain * ((fired - average) * inverse_std) + shift).astype(jnp.bfloat16)
        if residual:
            stream = stream_in_ref[rows, :] + normed.astype(jnp.float32)
            stream_ref[rows, :] = stream
            normed = stream.astype(jnp.bfloat16)
        source_ref[rows, :] = normed
        spread_pair(pair, normed.astype(jnp.float32), shifts_ref, sizes)
    mover.send(source_ref, source_out)
    if residual:
        mover.send(stream_ref, stream_out)
    conv_and_sums(flags_ref, shifts_ref, taps_ref, fired_ref, slope_ref, sums_ref, sizes, size=pairs)
    mover.finish()


def head_kernel(
    flags_ref, fired_ref, parts_ref, norms_ref, head_ref, stream_ref, fields_in, first_stats_in, *refs,
    sizes, pixel_count, sample_count, in_width, index, fetches,
):
    cols, width, pairs = sizes
    fetched_from, refs = refs[:fetches], refs[fetches:]
    fetched_to, refs = refs[:fetches], refs[fetches:]
    grad_ref, sums_ref, stats_ref, head_grad_ref, fields_ref, first_stats_ref, top_ref, semaphores = refs
    mover = Mover(semaphores)
    first_stats = mover.fetch(first_stats_in, first_stats_ref)
    fetched = mover.fetch(fields_in, fields_ref)
    for source, target in zip(fetched_from, fetched_to):
        mover.send(source, target)
    total = total_of(parts_ref)
    average, inverse_std = norm_of(total, pixel_count)
    keep_norm(stats_ref, total, average, inverse_std)
    average, inverse_std = twice(average), twice(inverse_std)
    gain, shift = twice(norms_ref[index, 0:1]), twice(norms_ref[index, 1:2])
    outs = head_ref.shape[0]
    row = lax.broadcasted_iota(jnp.int32, (width, width), 0)
    head = jnp.zeros((width, width), jnp.float32)
    for out in range(outs):
        head = jnp.where(row == out, jnp.broadcast_to(head_ref[out : out + 1, :], head.shape), head)
    head = head.astype(jnp.bfloat16)
    lane_from = lax.broadcasted_iota(jnp.int32, (width, 2 * width), 0) - in_width
    lane_to = lax.broadcasted_iota(jnp.int32, (width, 2 * width), 1)
    within = lane_from - PIECES * lane_to
    picks = (within >= 0) & (within < PIECES) & (lane_to < outs)
    lane_to = lane_to - width
    weighs = (lane_from >= outs * PIECES) & (lane_from < (outs + 1) * PIECES)
    picks = picks | (weighs & (lane_to >= 0) & (lane_to < outs))
    picks = jnp.where(picks, 1.0, 0.0).astype(jnp.bfloat16)
    for pair in range(pairs):
        rows = pl.ds(pair * cols, cols)
        centred = (fired_ref[rows, :].astype(jnp.float32) - average) * inverse_std
        normed = (gain * centred + shift).astype(jnp.bfloat16)
        top_ref[rows, :] = (stream_ref[rows, :] + normed.astype(jnp.float32)).astype(jnp.bfloat16)
    first_stats[0].wait()
    loss_weight = first_stats_ref[2:3, :] / sample_count
    loss = jnp.zeros((1, width), jnp.float32)
    shift_grad = jnp.zeros((1, 2 * width), jnp.float32)
    gain_grad = jnp.zeros((1, 2 * width), jnp.float32)
    head_grad = jnp.zeros((width, width), jnp.float32)
    fetched[0].wait()
    step = GROUP * cols
    for group in range(pairs // GROUP):
        rows = pl.ds(group * step, step)
        for q in range(2):
            lanes = slice(q * width, (q + 1) * width)
            top = top_ref[rows, lanes]
            picked = dot(fields_ref[rows, lanes], picks)
            misfit, weight = dot(top, head, ((1,), (1,))) - picked[:, :width], picked[:, width:]
            loss += jnp.sum(weight * misfit * misfit, axis=0, keepdims=True)
            pred_grad = (2.0 * weight * misfit / loss_weight).astype(jnp.bfloat16)
            head_grad += dot(pred_grad, top, ((0,), (0,)))
            grad_ref[rows, lanes] = dot(pred_grad, head)
        low = grad_ref[rows, :].astype(jnp.bfloat16).astype(jnp.float32)
        centred = (fired_ref[rows, :].astype(jnp.float32) - average) * inverse_std
        shift_grad += jnp.sum(low, axis=0, keepdims=True)
        gain_grad += jnp.sum(low * centred, axis=0, keepdims=True)
    loss = jnp.broadcast_to(jnp.sum(loss, axis=1, keepdims=True), (1, width))
    head_grad_ref[...] = head_grad[0:outs]
    put_sums(sums_ref, [folded(shift_grad, width), folded(gain_grad, width), loss])
    mover.finish()


def back_to_preact(parts_ref, stats_ref, norms_ref, index, flags_ref, refs, pixel_count, sizes):
    grad_ref, fired_ref, slope_ref, pre_ref, pair_grad_ref, shifts_ref = refs
    cols, width, pairs = sizes
    total = total_of(parts_ref)
    shift_grad, gain_grad = total[0:1], total[1:2]
    pair_grad_ref[0:1, :] = gain_grad
    pair_grad_ref[1:2, :] = shift_grad
    average, inverse_std = twice(stats_ref[0:1, :]), twice(stats_ref[1:2, :])
    scaled = twice(norms_ref[index, 0:1]) * inverse_std * flags_ref[0].astype(jnp.float32)
    shift_mean, gain_mean = twice(shift_grad / pixel_count), twice(gain_grad / pixel_count)
    for pair in range(pairs):
        rows = pl.ds(pair * cols, cols)
        centred = (fired_ref[rows, :].astype(jnp.float32) - average) * inverse_std
        grad = grad_ref[rows, :].astype(jnp.bfloat16).astype(jnp.float32)
        fired_grad = (scaled * (grad - shift_mean - centred * gain_mean)).astype(jnp.bfloat16)
        pre = (fired_grad.astype(jnp.float32) * slope_ref[rows, :].astype(jnp.float32)).astype(jnp.bfloat16)
        pre_ref[rows, :] = pre
        spread_pair(pair, pre.astype(jnp.float32), shifts_ref, sizes)


def back_kernel(
    flags_ref, parts_ref, norms_ref, grad_ref, weight_ref, fired_ref, slope_ref, stats_ref, below_in, below_stats_in,
    *refs, sizes, pixel_count, index, second, top,
):
    cols, width, pairs = sizes
    if not second:
        kept_in, *refs = refs
    if top:
        head_grad_ref, *refs = refs
    pre_out, pair_grad_out, *refs = refs
    if second:
        kept_out, *refs = refs
    out_ref, sums_ref, *refs = refs
    if not second:
        kept_ref, *refs = refs
    below_ref, below_stats_ref, pre_ref, pair_grad_ref, shifts_ref, taps_ref, semaphores = refs
    mover = Mover(semaphores)
    groups = 1
    below_stats = mover.fetch(below_stats_in, below_stats_ref)
    below = mover.fetch(below_in, below_ref)
    if second:
        mover.send(grad_ref, kept_out)
    else:
        kept = mover.fetch(kept_in, kept_ref)
    clear_rim(shifts_ref, sizes)
    taps_backward(weight_ref, taps_ref, width)
    refs = (grad_ref, fired_ref, slope_ref, pre_ref, pair_grad_ref, shifts_ref)
    back_to_preact(parts_ref, stats_ref, norms_ref, index, flags_ref, refs, pixel_count, sizes)
    mover.send(pre_ref, pre_out)
    mover.send(pair_grad_ref, pair_grad_out)
    below_stats[0].wait()
    average, inverse_std = twice(below_stats_ref[0:1, :]), twice(below_stats_ref[1:2, :])
    shift_sum = jnp.zeros((1, 2 * width), jnp.float32)
    gain_sum = jnp.zeros((1, 2 * width), jnp.float32)
    step = pairs * cols
    if not second:
        kept[0].wait()
    below[0].wait()
    for group in range(groups):
        rows = pl.ds(group * step, step)
        source = pair_conv(shifts_ref, taps_ref, group, cols, ((1,), (1,)), pairs)
        if not second:
            source = source + kept_ref[rows, :]
        out_ref[rows, :] = source.astype(out_ref.dtype)
        low = source.astype(jnp.bfloat16).astype(jnp.float32)
        shift_sum += jnp.sum(low, axis=0, keepdims=True)
        gain_sum += jnp.sum(low * ((below_ref[rows, :].astype(jnp.float32) - average) * inverse_std), axis=0, keepdims=True)
    active = flags_ref[0].astype(jnp.float32)
    sums = [folded(shift_sum, width) * active, folded(gain_sum, width) * active]
    put_sums(sums_ref, sums + ([head_grad_ref[...]] if top else []))
    mover.finish()


def cut_frames(flags_ref, flat_ref, mine_ref, theirs_ref, tiles, shard):
    width = flat_ref.shape[1]
    nl, no = tiles[0], tiles[1]
    rows = mine_ref.shape[2]
    for lon_step in range(no):
        for lat_step in range(nl):
            for core_step, target in ((0, mine_ref), (1, theirs_ref)):
                device = device_at(flags_ref, lon_step, lat_step, core_step, tiles)
                start = first_row(device, shard, width)
                target[lon_step, lat_step] = flat_ref[pl.ds(start, rows), :].astype(jnp.bfloat16)


def block_kernel_grad(shifts_ref, pre_ref, flat_ref, sizes):
    cols, width, pairs = sizes
    for a in range(4):
        k, rr = a // 2, a % 2
        block = shifts_ref[k * cols : (k + pairs) * cols, rr * 3 * width : (rr + 1) * 3 * width]
        grad = dot(block, pre_ref[...], ((0,), (0,)))
        if a < 3:
            flat_ref[a * 3 * width : (a + 1) * 3 * width, :] = grad[:, :width]
        if a > 0:
            flat_ref[(a - 1) * 3 * width : a * 3 * width, :] += grad[:, width:]


def kernel_grad_kernel(flags_ref, *refs, tiles, sizes, shard, fetches, joins):
    fetched_from, refs = refs[:fetches], refs[fetches:]
    source_in, pre_in, *refs = refs
    others, refs = refs[:joins], refs[joins:]
    fetched_to, refs = refs[:fetches], refs[fetches:]
    mine_out, theirs_ref, *refs = refs
    if joins:
        joined_ref, frames_ref, *refs = refs
    mine_ref, source_ref, pre_ref, shifts_ref, flat_ref, semaphores = refs
    mover = Mover(semaphores)
    source, pre = mover.fetch(source_in, source_ref), mover.fetch(pre_in, pre_ref)
    for wide, near in zip(fetched_from, fetched_to):
        mover.send(wide, near)
    arrivals = [mover.start(frames, frames_ref.at[i]) for i, frames in enumerate(others)]
    clear_rim(shifts_ref, sizes)
    source[0].wait()
    spread_all_pairs(source_ref, shifts_ref, sizes)
    pre[0].wait()
    block_kernel_grad(shifts_ref, pre_ref, flat_ref, sizes)
    cut_frames(flags_ref, flat_ref, mine_ref, theirs_ref, tiles, shard)
    mover.send(mine_ref, mine_out)
    for arrival in arrivals:
        arrival.wait()
    if joins:
        join_frames(frames_ref, joined_ref)
    mover.finish()


def spread_all_pairs(source_ref, shifts_ref, sizes):
    cols, width, pairs = sizes
    for pair in range(pairs):
        cells = source_ref[pair * cols : (pair + 1) * cols, :].astype(jnp.float32)
        spread_pair(pair, cells, shifts_ref, sizes)


def last_kernel(
    flags_ref, parts_ref, norms_ref, grad_ref, fired_in, slope_in, stats_in, weight_in, kept_in, in_slope_in,
    source_in, wide_in, *refs, tiles, sizes, shards, in_width, pixel_count, others,
):
    cols, width, pairs = sizes
    nl, no = tiles[0], tiles[1]
    near_ins, refs = refs[: 2 * others], refs[2 * others :]
    (
        pair_grad_out, mine_ref, theirs_ref,
        fired_ref, slope_ref, stats_ref, weight_ref, kept_ref, in_slope_ref, source_ref, wide_ref, pre_ref, in_pre_ref, pair_grad_ref,
        shifts_ref, first_shifts_ref, taps_ref, flat_ref, flat_first_ref, others_ref, semaphores,
    ) = refs
    mover = Mover(semaphores)
    groups = pairs // GROUP
    source = mover.fetch(source_in, source_ref)
    early = mover.fetch(stats_in, stats_ref) + mover.fetch(weight_in, weight_ref)
    early += mover.fetch(fired_in, fired_ref) + mover.fetch(slope_in, slope_ref)
    clear_rim(shifts_ref, sizes)
    clear_rim(first_shifts_ref, sizes)
    source[0].wait()
    spread_all_pairs(source_ref, first_shifts_ref, sizes)
    for arrival in early:
        arrival.wait()
    kept = mover.fetch(kept_in, kept_ref)
    in_slope = mover.fetch(in_slope_in, in_slope_ref)
    wide = mover.fetch(wide_in, wide_ref)
    arrivals = [mover.start(other, others_ref.at[i]) for i, other in enumerate(near_ins)]
    taps_backward(weight_ref, taps_ref, width)
    refs = (grad_ref, fired_ref, slope_ref, pre_ref, pair_grad_ref, shifts_ref)
    back_to_preact(parts_ref, stats_ref, norms_ref, 0, flags_ref, refs, pixel_count, sizes)
    mover.send(pair_grad_ref, pair_grad_out)
    kept[0].wait()
    in_slope[0].wait()
    step = GROUP * cols
    for group in range(groups):
        rows = pl.ds(group * step, step)
        grad = pair_conv(shifts_ref, taps_ref, group, cols, ((1,), (1,))) + kept_ref[rows, :]
        in_pre_ref[rows, :] = (grad * in_slope_ref[rows, :].astype(jnp.float32)).astype(jnp.bfloat16)
    block_kernel_grad(first_shifts_ref, pre_ref, flat_first_ref, sizes)
    for arrival in arrivals:
        arrival.wait()
    wide[0].wait()
    for a in range(8):
        k, rr = a // 2, a % 2
        block = wide_ref[k * cols : (k + pairs) * cols, rr * 7 * width : (rr + 1) * 7 * width]
        grads = dot(block, in_pre_ref[...], ((0,), (0,)))
        for b in range(7):
            grad = grads[b * width : b * width + in_width]
            if a < 7:
                tap = a * 7 + b
                flat_ref[tap * in_width : (tap + 1) * in_width, :] = grad[:, :width]
            if a > 0:
                tap = (a - 1) * 7 + b
                flat_ref[tap * in_width : (tap + 1) * in_width, :] += grad[:, width:]
    rows = others_ref.shape[3]
    in_rows = mine_ref.shape[2] - (others + 1) * rows
    for lon_step in range(no):
        for lat_step in range(nl):
            for core_step, target in ((0, mine_ref), (1, theirs_ref)):
                device = device_at(flags_ref, lon_step, lat_step, core_step, tiles)
                spot = pl.ds(first_row(device, shards[0], width), in_rows)
                target[lon_step, lat_step, 0:in_rows, :] = flat_ref[spot, :].astype(jnp.bfloat16)
                spot = pl.ds(first_row(device, shards[1], width), rows)
                block = flat_first_ref[spot, :].astype(jnp.bfloat16)
                target[lon_step, lat_step, in_rows : in_rows + rows, :] = block
                for other in range(others):
                    at = in_rows + (other + 1) * rows
                    target[lon_step, lat_step, at : at + rows, :] = others_ref[
                        2 * other + core_step, lon_step, lat_step
                    ]
    mover.finish()


def join_frames(frames_ref, joined_ref):
    count, no, nl, rows, unused = frames_ref.shape
    for index in range(count // 2):
        for lon_step in range(no):
            for lat_step in range(nl):
                joined_ref[lat_step, lon_step, index * rows : (index + 1) * rows, :] = low_sum(
                    frames_ref[2 * index, lon_step, lat_step], frames_ref[2 * index + 1, lon_step, lat_step]
                )


def swap(values, axis, step):
    return lax.ppermute(values, axis, [(i, i ^ step) for i in range(lax.axis_size(axis))])


def low_sum(*values):
    return sum(part.astype(jnp.float32) for part in values).astype(jnp.bfloat16)


def along(values, axis):
    return [values[0]] + [swap(values[k], axis, k) for k in range(1, values.shape[0])]


def wide_sum(parts):
    return sum(part.astype(jnp.float32) for part in parts)


def spread_all(values, axes):
    return lax.all_to_all(values, axes, 0, 0, tiled=True)


def whole_sample_body(
    fields,
    targets,
    land_mask,
    input_kernel,
    input_first,
    input_second,
    block_kernels,
    block_first,
    block_second,
    head_weight,
    head_first,
    head_second,
    norm_params,
    norm_first,
    norm_second,
):
    samples_here, rows_here, cols_here, in_width = fields.shape
    width = norm_params.shape[2]
    conv_count = block_kernels.shape[0]
    nl, no, nb = (lax.axis_size(axis) for axis in ALL)
    places, devices = nl * no, nl * no * nb
    tiles = (nl, no, rows_here, cols_here)
    cols, pairs = cols_here * no, rows_here * nl // 2
    sizes = (cols, width, pairs)
    pixels = pairs * cols
    sample_count = samples_here * nb
    pixel_count = float(sample_count * 2 * pixels)
    place = lax.axis_index(TILE)
    core = lax.axis_index("batch")
    flags = jnp.stack(
        [
            (place < samples_here).astype(jnp.int32),
            lax.axis_index("batch"),
            lax.axis_index("lat"),
            lax.axis_index("lon"),
        ]
    )
    bf16, f32 = jnp.bfloat16, jnp.float32
    device = lax.axis_index(ALL)
    in_shard, block_shard = input_kernel.shape[0], block_kernels.shape[1]
    in_frame = frame_rows(in_shard, devices, width, SPREAD)
    block_frame = frame_rows(block_shard, devices, width, 8)
    in_offset = device * in_shard % width
    flat_rows = max((devices - 1) * in_shard // width + in_frame, 48 * in_width + width)
    flat_rows = -(-flat_rows // 8) * 8
    block_rows = block_shard // width

    def shard_rows(shards):
        count = shards.shape[0] * block_rows
        rows = shards.astype(bf16).reshape(count, width)
        return jnp.pad(rows, ((0, -count % SPREAD), (0, 0)))

    def from_all(values, axis, count):
        return [values] + [swap(values, axis, k) for k in range(1, count)]

    framed = lax.dynamic_update_slice(
        jnp.zeros((in_frame * width,), bf16), input_kernel.astype(bf16), (in_offset,)
    ).reshape(in_frame, width)
    near = jnp.concatenate([framed, shard_rows(block_kernels[:NEAR])], axis=0)
    near_rows = near.shape[0]
    both = jnp.stack(from_all(jnp.concatenate([near, shard_rows(block_kernels[NEAR:])], axis=0), "lat", nl))

    row_global = (lax.axis_index("lat") * rows_here + jnp.arange(rows_here)).astype(f32)
    latitude = (row_global + 0.5) / (rows_here * nl) * jnp.pi - jnp.pi / 2
    pixel_weight = jnp.cos(latitude)[None, :, None] * land_mask.astype(f32)
    (packed,) = call(
        functools.partial(pack_kernel, in_width=in_width),
        [(fields, VECTOR), (targets.transpose(3, 0, 1, 2), VECTOR), (pixel_weight, VECTOR)],
        [((places, rows_here, cols_here, width), bf16, VECTOR)],
        [pltpu.VMEM((-(-3 * PIECES * rows_here // 16) * 16, cols_here), f32)],
    )
    near, far = both[:, :near_rows], both[:, near_rows:]
    packed, near, far = lax.optimization_barrier((packed, near, far))
    near = from_all(near, "lon", no)
    packed = spread_all(packed, TILE)

    plane = (pixels, 2 * width)
    weight_shape = (9 * width, width)
    flat_weight = pltpu.VMEM((9 * width + block_frame + 8, width), f32)
    wide_shape = ((pairs + 3) * cols, 14 * width)
    shift_shape = ((pairs + 1) * cols, 6 * width)
    shift_scratch = pltpu.VMEM(shift_shape, bf16)
    forward_taps, backward_taps = (2, 6 * width, 2 * width), (2, 2 * width, 6 * width)
    def sums_shape(rows):
        return ((devices, rows, width), f32, VECTOR)

    stats_shape, pair_shape = (8, width), (2, width)
    frame_shape = (no, nl, block_frame, width)
    low_plane, wide_plane = pltpu.VMEM(plane, bf16), pltpu.VMEM(plane, f32)
    weight_scratch, stats_scratch = pltpu.VMEM(weight_shape, bf16), pltpu.VMEM(stats_shape, f32)
    pair_scratch = pltpu.VMEM(pair_shape, f32)
    unit_cost = 2 * 2 * pixels * 9 * width * width

    def kept_outs(*kinds):
        return [(shape, dtype, WIDE) for shape, dtype in kinds]

    far = from_all(far, "lon", no)
    near = [part for values in near for part in (values, swap(values, "batch", 1))]
    near_count, far_count = NEAR, conv_count - NEAR
    out = call(
        functools.partial(
            first_kernel, tiles=tiles, sizes=sizes, shards=[in_shard, block_rows], in_width=in_width, count=near_count
        ),
        [(near[0], WIDE)] + [(part, VECTOR) for part in near[1:]] + [(packed, VECTOR)],
        kept_outs(*[(weight_shape, bf16)] * near_count, (plane, bf16), (wide_shape, bf16), (plane, bf16), (plane, f32), (plane, bf16))
        + [(plane, bf16, VECTOR), (plane, bf16, VECTOR), sums_shape(4)],
        [flat_weight] * near_count
        + [pltpu.VMEM(near[0].shape, bf16), low_plane, pltpu.VMEM((near_count, *weight_shape), bf16)]
        + [pltpu.VMEM((-(-near_count * block_rows // SPREAD) * SPREAD, width), f32)]
        + [pltpu.VMEM((4, 14 * width, 2 * width), bf16), pltpu.VMEM((flat_rows, width), f32)]
        + [pltpu.VMEM(wide_shape, bf16), low_plane, wide_plane, low_plane]
        + [shift_scratch, pltpu.VMEM(forward_taps, bf16)],
        flags,
        6 * unit_cost,
        LARGE_ROOM,
    )
    weights, out = list(out[:near_count]), out[near_count:]
    fields, wide, in_slope, stream, source, fired, slope, sums = out
    far, sums = lax.optimization_barrier((far, sums))
    parts = spread_all(sums, ALL)
    far = [part for values in far for part in (values, swap(values, "batch", 1))]
    *far_weights, weight = call(
        functools.partial(far_kernels_kernel, tiles=tiles, block_rows=block_rows, count=far_count),
        [(part, VECTOR) for part in far],
        kept_outs(*[(weight_shape, bf16)] * far_count) + [(weight_shape, bf16, VECTOR)],
        [pltpu.VMEM((-(-far_count * block_rows // SPREAD) * SPREAD, width), f32)]
        + [flat_weight] * far_count
        + [pltpu.VMEM((far_count, *weight_shape), bf16)],
        flags,
        unit_cost,
    )
    weights += far_weights

    sources, fireds, slopes, stats = [source], [], [], []
    fetched = []
    for k in range(1, conv_count):
        residual = k % 2 == 0
        fetches = [weights[k + 1]] if k + 1 < conv_count else []
        if not residual:
            fetches.append(stream)
        out = call(
            functools.partial(
                unit_kernel, sizes=sizes, pixel_count=pixel_count, index=k - 1, residual=residual,
                fetches=len(fetches),
            ),
            [(array, VECTOR) for array in (fired, parts, norm_params, weight, slope, *fetched)]
            + [(array, WIDE) for array in fetches],
            kept_outs(*[(plane, f32)] * residual, (plane, bf16), (stats_shape, f32), (plane, bf16), (plane, bf16))
            + [(plane, bf16, VECTOR), (plane, bf16, VECTOR), sums_shape(2)]
            + [(array.shape, array.dtype, VECTOR) for array in fetches],
            [wide_plane] * residual
            + [low_plane, stats_scratch, shift_scratch, pltpu.VMEM(forward_taps, bf16)],
            flags,
            unit_cost,
        )
        if residual:
            stream, *out = out
        source, stat, saved_fired, saved_slope, fired, slope, sums, *fetched = out
        sources.append(source)
        stats.append(stat)
        fireds.append(saved_fired)
        slopes.append(saved_slope)
        if k + 1 < conv_count:
            weight, *fetched = fetched
        parts = spread_all(sums, ALL)

    grad, sums, stat, head_local = call(
        functools.partial(
            head_kernel, sizes=sizes, pixel_count=pixel_count, sample_count=sample_count, in_width=in_width,
            index=conv_count - 1, fetches=0,
        ),
        [(array, VECTOR) for array in (fired, parts, norm_params, head_weight.T, *fetched)]
        + [(array, WIDE) for array in (fields, stats[0])],
        [(plane, f32, VECTOR), sums_shape(4), (stats_shape, f32, VECTOR), (head_weight.T.shape, f32, VECTOR)],
        [low_plane, stats_scratch, low_plane],
        flags,
        unit_cost // 4,
    )
    parts = spread_all(sums, ALL)
    loss_parts = parts

    pair_grads, frames = [None] * conv_count, [None] * conv_count
    for k in range(conv_count - 1, 0, -1):
        second, top = k % 2 == 1, k == conv_count - 1
        pre, pair_grads[k], *out = call(
            functools.partial(back_kernel, sizes=sizes, pixel_count=pixel_count, index=k, second=second, top=top),
            [(array, VECTOR) for array in (parts, norm_params, grad, weight, fired, slope, stat)]
            + [(array, WIDE) for array in (fireds[k - 1], stats[k - 1])]
            + [(array, WIDE) for array in (() if second else (kept_grad,))]
            + [(head_local, VECTOR)] * top,
            kept_outs((plane, bf16), (pair_shape, f32), *[(plane, f32)] * second)
            + [(plane, bf16 if second else f32, VECTOR), sums_shape(4 if top else 2)],
            [wide_plane] * (not second)
            + [low_plane, stats_scratch, low_plane, pair_scratch, shift_scratch, pltpu.VMEM(backward_taps, bf16)],
            flags,
            unit_cost,
        )
        if second:
            kept_grad, *out = out
        grad, sums = out
        parts = spread_all(sums, ALL)
        if top:
            head_parts = parts
        fetches = (weights[k - 1], fireds[k - 1], slopes[k - 1], stats[k - 1]) if k > 1 else ()
        others = ()
        if LATE <= k + 1 < conv_count:
            frames[k + 1][1] = swap(frames[k + 1][1], "batch", 1)
        if k == 1:
            others = [part for pair in frames[LATE:] for part in pair]
        out = call(
            functools.partial(
                kernel_grad_kernel, tiles=tiles, sizes=sizes, shard=block_shard, fetches=len(fetches),
                joins=len(others),
            ),
            [(array, WIDE) for array in (*fetches, sources[k], pre, *others)],
            [(array.shape, array.dtype, VECTOR) for array in fetches]
            + [(frame_shape, bf16, WIDE), (frame_shape, bf16, VECTOR)]
            + [((nl, no, (conv_count - LATE) * block_frame, width), bf16, VECTOR)] * (k == 1),
            [pltpu.VMEM((len(others), *frame_shape), bf16)] * (k == 1)
            + [pltpu.VMEM(frame_shape, bf16), low_plane, low_plane, shift_scratch, flat_weight],
            flags,
            unit_cost,
        )
        if k == 1:
            *frames[1], early = out
            parts, early, frames[1:LATE] = lax.optimization_barrier((parts, early, frames[1:LATE]))
            continue
        weight, fired, slope, stat, *frames[k] = out
        parts, frames[k:] = lax.optimization_barrier((parts, frames[k:]))
    pair_grads[0], mine, theirs = call(
        functools.partial(
            last_kernel, tiles=tiles, sizes=sizes, shards=[in_shard, block_shard], in_width=in_width,
            pixel_count=pixel_count, others=LATE - 1,
        ),
        [(array, VECTOR) for array in (parts, norm_params, grad)]
        + [(array, WIDE) for array in (fireds[0], slopes[0], stats[0], weights[0])]
        + [(array, WIDE) for array in (kept_grad, in_slope, sources[0], wide)]
        + [(part, WIDE) for pair in frames[1:LATE] for part in pair],
        kept_outs((pair_shape, f32))
        + [((no, nl, in_frame + LATE * block_frame, width), bf16, VECTOR)] * 2,
        [low_plane, low_plane, stats_scratch, weight_scratch, wide_plane, low_plane, low_plane]
        + [pltpu.VMEM(wide_shape, bf16), low_plane, low_plane]
        + [pair_scratch, shift_scratch, shift_scratch, pltpu.VMEM(backward_taps, bf16)]
        + [pltpu.VMEM((flat_rows, width), f32), flat_weight]
        + [pltpu.VMEM((2 * (LATE - 1), *frame_shape), bf16)],
        flags,
        6 * unit_cost,
        LARGE_ROOM,
    )
    late, early = lax.optimization_barrier((low_sum(mine, swap(theirs, "batch", 1)), early))
    late = along(late, "lon")
    early = along(early, "lat")
    early, late = lax.optimization_barrier((early, late))
    early, late = along(low_sum(*early), "lon"), along(low_sum(*late), "lat")
    early[1], head_parts, loss_parts, first_stats, norm_grad = lax.optimization_barrier(
        (early[1], head_parts, loss_parts, stats[0], jnp.stack(pair_grads))
    )
    early, late = wide_sum(early), wide_sum(late)
    input_grad = lax.dynamic_slice(late[:in_frame].reshape(-1), (in_offset,), (in_shard,))
    block_grad = jnp.concatenate([late[in_frame:], early], axis=0)
    block_grad = block_grad.reshape(conv_count, block_frame, width)[:, :block_rows]
    block_grad = block_grad.reshape(conv_count, block_shard)
    head_grad = jnp.sum(head_parts, axis=0)[2:4].T
    loss_sum = jnp.sum(loss_parts, axis=0)[2, 0]
    loss_weight = first_stats[2, 0] / sample_count
    return finished(
        loss_sum, loss_weight, input_grad, block_grad, head_grad, norm_grad,
        (input_kernel, input_first, input_second), (block_kernels, block_first, block_second),
        (head_weight, head_first, head_second), (norm_params, norm_first, norm_second),
    )


def one_device_takes_a_sample(fields, block_kernels, head_weight, norm_params):
    samples_here, rows_here, cols_here, in_width = fields.shape
    nl, no, nb = (lax.axis_size(axis) for axis in ALL)
    rows, cols, width = rows_here * nl, cols_here * no, norm_params.shape[2]
    return (
        samples_here <= nl * no
        and nb == 2
        and nl & (nl - 1) == 0
        and no & (no - 1) == 0
        and rows * cols <= MOST_PIXELS
        and rows % (2 * GROUP) == 0
        and cols % 128 == 0
        and cols_here % 8 == 0
        and width == 128
        and head_weight.shape[1] == 2
        and in_width + 3 * PIECES <= width
        and block_kernels.shape[1] % width == 0
        and block_kernels.shape[0] > max(NEAR, LATE)
    )


def body(*args):
    fields, block_kernels, head_weight, norm_params = args[0], args[6], args[9], args[12]
    if one_device_takes_a_sample(fields, block_kernels, head_weight, norm_params):
        return whole_sample_body(*args)
    return tile_body(*args)


def solution(mesh):
    in_specs = (
        P("batch", "lat", "lon", None),
        P("batch", "lat", "lon", None),
        P("batch", "lat", "lon"),
        P(("lat", "lon", "batch")),
        P(("lat", "lon", "batch")),
        P(("lat", "lon", "batch")),
        P(None, ("lat", "lon", "batch")),
        P(None, ("lat", "lon", "batch")),
        P(None, ("lat", "lon", "batch")),
        P(),
        P(),
        P(),
        P(),
        P(),
        P(),
    )
    out_specs = (
        P(),
        P(),
        P(("lat", "lon", "batch")),
        P(("lat", "lon", "batch")),
        P(("lat", "lon", "batch")),
        P(None, ("lat", "lon", "batch")),
        P(None, ("lat", "lon", "batch")),
        P(None, ("lat", "lon", "batch")),
        P(),
        P(),
        P(),
        P(),
        P(),
        P(),
    )
    return jax.shard_map(body, mesh=mesh, in_specs=in_specs, out_specs=out_specs, check_vma=False)
```
